32 devices in a mesh: section: 4 (over y, core), expert: 8 (over z, x).
Axes of the slice: x: 2, y: 2, z: 4, core: 2. Of those that a mesh axis runs over, the one named last changes fastest.
Arguments:
- tokens: bfloat16 [4, 512, 2560], P('section', 'expert'), may hold values from -6 to 6
- norm_gain: float32 [4, 2560], P('section'), may hold values from 0.25 to 1.75
- w_gate: bfloat16 [4, 8, 2560, 192], P('section', 'expert'), may hold values from -0.125 to 0.125
- w_up: bfloat16 [4, 8, 2560, 192], P('section', 'expert'), may hold values from -0.125 to 0.125
- w_down: bfloat16 [4, 8, 192, 2560], P('section', 'expert'), may hold values from -0.21875 to 0.21875
- routes: int32 [4, 2, 512, 1], P('section', None, 'expert'), may hold values from 0 to 1; in each aligned block of 64 rows (0 to 63, 64 to 127, ..., all dimensions but the last counted through in order) at most 34 rows name the same one
- mix_weights: float32 [4, 2, 512, 1], P('section', None, 'expert'), may hold values from 0.1 to 1
- cotangent: bfloat16 [4, 512, 2560], P('section', 'expert'), may hold values from -6 to 6
Outputs:
- final: bfloat16 [4, 512, 2560], P('section', 'expert')
- input_grads: bfloat16 [4, 512, 2560], P('section', 'expert')
The draws below stay inside these ranges and needn't reach their ends.
Inputs may be any that keep to these rules, and one draw needn't show every extreme that they name: `routes`: the 1 ids of a token differ. In the rows of one device (aligned blocks of 64 tokens of one layer and step) no id is named by more than 34 tokens, a bound that some block reaches.
All inputs are finite; a program needn't handle non-finite values.
Results may differ from the reference program's by a relative error of at most 0.011.
Values may be sent and summed in bfloat16 or wider, within the bound.
No kernel may reach another device: no remote copies, remote signals or barrier semaphores. Data moves between devices by JAX's collectives and lax.ppermute only.
A program may use at most 64 MiB of HBM per device.

```python
import math
import jax
import jax.numpy as jnp
import numpy as np
from jax import lax

D = 2560
HID = 768
SPLIT = 4
TOPK = 1
STEPS = 2
TOK_DEV = 64
HID_DEV = 192
LAYERS = 4
EXPERTS = 2
CAP = 34
MB_TOK = 512
N_EXPERT = 8


def steps_of(own_key, extent, cuts, low, top_value):
    def one(axis_at, shards_of):
        draws = jax.random.uniform(jax.random.fold_in(jax.random.fold_in(own_key, 6), axis_at), (shards_of,), jnp.float32, low / len(cuts), top_value / len(cuts))
        return jnp.repeat(jnp.exp(draws), extent[axis_at] // shards_of).reshape((-1,) + (1,) * (len(extent) - axis_at - 1))

    loudness = one(*cuts[0])
    for cut in cuts[1:]:
        loudness = loudness * one(*cut)
    return loudness


def assign_block(rng, own, number, rows, number_of, top, limit, slope):
    sequence = jax.random.permutation(rng, number_of)
    heavy_load, ordinary = shares(number_of, rows * top, limit, slope, True), shares(number_of, rows * top, limit, slope, False)
    places = jnp.arange(number_of)

    def named(sizes, rotation):
        used = int((sizes > 0).sum())
        fixed = max(1, used // 4)
        passed = fixed + (places - fixed + rotation * (used - fixed)) % max(1, number_of - fixed)
        return jnp.zeros((number_of,), jnp.int32).at[sequence[jnp.where(places < fixed, places, passed)]].set(jnp.asarray(sizes, jnp.int32))

    sizes = jnp.where(number % 4 == 0, named(heavy_load, number // 4), named(ordinary, number - number // 4 - 1))
    mixed = jax.random.permutation(jax.random.fold_in(own, 3), number_of)
    giver, taker = mixed[0:number_of // 2 * 2:2], mixed[1:number_of // 2 * 2:2]
    margin = jnp.minimum(sizes[giver] - 1, limit - sizes[taker]) // 2
    margin = jnp.where((giver == sequence[0]) | (taker == sequence[0]) | (sizes[taker] == 0), 0, jnp.maximum(margin, 0))
    passed = jax.random.randint(jax.random.fold_in(own, 4), (number_of // 2,), 0, 1 << 20) % (margin + 1)
    sizes = sizes.at[giver].add(-passed).at[taker].add(passed)
    items = jnp.searchsorted(jnp.cumsum(sizes), jnp.arange(rows * top), side="right").astype(jnp.int32)
    grid = items.reshape(top, rows).T
    grid = grid[jax.random.permutation(jax.random.fold_in(own, 1), rows)]
    rotation = jax.random.randint(jax.random.fold_in(own, 2), (rows, 1), 0, top)
    return jnp.take_along_axis(grid, (jnp.arange(top)[None, :] + rotation) % top, axis=1)


def shares(number_of, total, reach, lean, full):
    weights = [(1 << 20) // math.isqrt(grade ** lean) + 1 for grade in range(1, number_of + 1)]
    largest = reach if full else min(reach, max(-(-total // number_of), total * weights[0] // sum(weights)))
    least = 1 if total - largest >= number_of - 1 else 0
    counts, rest = [largest] + [least] * (number_of - 1), total - largest - least * (number_of - 1)
    while rest > 0:
        free = [i for i in range(1, number_of) if counts[i] < largest] or [i for i in range(1, number_of) if counts[i] < reach]
        whole, left = sum([weights[i] for i in free]), rest
        for i in free:
            more = min(reach - counts[i], max(1, left * weights[i] // whole), rest)
            counts[i] = counts[i] + more
            rest = rest - more
    return np.array(counts)


def gaussian(key, dims, deviation, limit, cuts=(), held_as=jnp.bfloat16):
    factor_of = steps_of(key, dims, cuts, -0.22, 0.18) if cuts else 1.0
    array = jax.random.normal(key, dims, jnp.float32) * deviation * factor_of
    return jnp.minimum(jnp.maximum(array, -limit), limit).astype(held_as)


def setup_inputs(seed: int = 0) -> dict:
    seeds = jax.random.split(jax.random.key(seed), 9)
    tokens = gaussian(seeds[0], (LAYERS, MB_TOK, D), 1.0, 6.0, ((0, 4), (1, 8)))
    norm_gain = jnp.clip(1.0 + 0.15 * jax.random.normal(seeds[1], (LAYERS, D), jnp.float32), 0.25, 1.75)
    w_gate = gaussian(seeds[2], (LAYERS, N_EXPERT, D, HID_DEV), D ** -0.5, 0.125, ((0, 4), (1, 8)))
    w_up = gaussian(seeds[3], (LAYERS, N_EXPERT, D, HID_DEV), D ** -0.5, 0.125, ((0, 4), (1, 8)))
    w_down = gaussian(seeds[4], (LAYERS, N_EXPERT, HID_DEV, D), HID ** -0.5, 0.21875, ((0, 4), (1, 8)))
    routes_keys = jax.random.split(jax.random.fold_in(seeds[5], 1), LAYERS * STEPS * MB_TOK // TOK_DEV)
    routes_turns = jax.random.permutation(jax.random.fold_in(seeds[5], 3), LAYERS * STEPS * MB_TOK // TOK_DEV)
    routes = jax.vmap(lambda own, number: assign_block(jax.random.fold_in(seeds[5], 2), own, number, TOK_DEV, EXPERTS, TOPK, CAP, 1))(routes_keys, routes_turns).reshape((LAYERS, STEPS, MB_TOK, TOPK))
    mix_weights = jnp.clip(jnp.exp(math.log(1.0) - 2.3025851 * jax.random.uniform(seeds[6], (LAYERS, STEPS, MB_TOK, TOPK), jnp.float32) ** steps_of(seeds[6], (LAYERS, STEPS, MB_TOK, TOPK), ((0, 4), (2, 8)), -0.2, 0.2)), 0.1, 1.0)
    cotangent = gaussian(seeds[7], (LAYERS, MB_TOK, D), 1.0, 6.0, ((0, 4), (1, 8)))
    return {"tokens": tokens, "norm_gain": norm_gain, "w_gate": w_gate, "w_up": w_up, "w_down": w_down, "routes": routes, "mix_weights": mix_weights, "cotangent": cotangent}


EPSILON = 1e-06
HIGHEST = lax.Precision.HIGHEST

def norm_apply(hidden_f, gain_row):
    inv_scale = lax.rsqrt(lax.optimization_barrier(jnp.mean(hidden_f * hidden_f, axis=-1, keepdims=True)) + EPSILON)
    return hidden_f * inv_scale * gain_row

def slot_index(route_ids, experts, capacity):
    labels = jnp.arange(experts, dtype=jnp.int32)
    chosen = lax.optimization_barrier(jnp.sum((route_ids[:, :, None] == labels[None, None, :]).astype(jnp.int32), axis=1))
    before = jnp.cumsum(chosen, axis=0) - chosen
    within = jnp.take_along_axis(before, route_ids, axis=1)
    return (route_ids * capacity + within).astype(jnp.int32)

def blocks_slots(route_ids):
    return jax.vmap(lambda part_ids: slot_index(part_ids, EXPERTS, CAP))(route_ids.reshape(N_EXPERT, TOK_DEV, TOPK))

def dispatch(values, slot_ids):

    def one_block(block_values, places):
        repeated = jnp.repeat(block_values, TOPK, axis=0)
        empty = jnp.zeros((EXPERTS * CAP, block_values.shape[1]), block_values.dtype)
        return empty.at[places.reshape(-1)].set(repeated)
    send_boxes = jax.vmap(one_block)(values, slot_ids)
    return jnp.swapaxes(send_boxes.reshape(N_EXPERT, EXPERTS, CAP, values.shape[2]), 0, 1)

def collect(slot_rows, slot_ids):
    returned = jnp.swapaxes(slot_rows, 0, 1).reshape(N_EXPERT, EXPERTS * CAP, slot_rows.shape[3])
    return jax.vmap(lambda block_rows, places: block_rows[places])(returned, slot_ids)

def round_trip(values):
    return lax.optimization_barrier(values.astype(jnp.bfloat16)).astype(jnp.float32)

def split_weights(gate_w, up_w, down_w):
    gate_s = gate_w.astype(jnp.float32).reshape(EXPERTS, SPLIT, D, HID_DEV)
    up_s = up_w.astype(jnp.float32).reshape(EXPERTS, SPLIT, D, HID_DEV)
    down_s = down_w.astype(jnp.float32).reshape(EXPERTS, SPLIT, HID_DEV, D)
    return (gate_s, up_s, down_s)

def gate_up(slot_rows, gate_s, up_s):
    gate_act = jnp.einsum('enrd,esdh->esnrh', slot_rows, gate_s, precision=HIGHEST)
    upper = jnp.einsum('enrd,esdh->esnrh', slot_rows, up_s, precision=HIGHEST)
    return (gate_act, upper)

def normed_rows(hidden, gain_row):
    return norm_apply(hidden.astype(jnp.float32), gain_row).astype(jnp.bfloat16).reshape(N_EXPERT, TOK_DEV, D)

def layer_forward(hidden, gain_row, gate_w, up_w, down_w, route_ids, mix_row):
    gate_s, up_s, down_s = split_weights(gate_w, up_w, down_w)
    slot_ids = blocks_slots(route_ids)
    slot_rows = dispatch(normed_rows(hidden, gain_row), slot_ids).astype(jnp.float32)
    gate_act, upper = gate_up(slot_rows, gate_s, up_s)
    inner_act = round_trip(jax.nn.silu(gate_act) * upper)
    partial_value = round_trip(jnp.einsum('esnrh,eshd->esnrd', inner_act, down_s, precision=HIGHEST))
    outputs = round_trip(lax.optimization_barrier(jnp.sum(partial_value, axis=1)))
    picked = collect(outputs, slot_ids)
    combined = lax.optimization_barrier(jnp.sum(mix_row.reshape(N_EXPERT, TOK_DEV, TOPK)[..., None] * picked, axis=2)).reshape(MB_TOK, D)
    return (hidden.astype(jnp.float32) + combined).astype(jnp.bfloat16)

def layer_backward(hidden, grad_now, gain_row, gate_w, up_w, down_w, route_ids, mix_row):
    gate_s, up_s, down_s = split_weights(gate_w, up_w, down_w)
    slot_ids = blocks_slots(route_ids)
    slot_rows = dispatch(normed_rows(hidden, gain_row), slot_ids).astype(jnp.float32)
    grad_rows = dispatch(grad_now.reshape(N_EXPERT, TOK_DEV, D), slot_ids).astype(jnp.float32)
    gate_act, upper = gate_up(slot_rows, gate_s, up_s)
    sigmoid_gate = jax.nn.sigmoid(gate_act)
    d_inner = jnp.einsum('enrd,eshd->esnrh', grad_rows, down_s, precision=HIGHEST)
    d_gate = round_trip(d_inner * upper * sigmoid_gate * (1.0 + gate_act * (1.0 - sigmoid_gate)))
    d_upper = round_trip(d_inner * gate_act * sigmoid_gate)
    part_rows = jnp.einsum('esnrh,esdh->esnrd', d_gate, gate_s, precision=HIGHEST)
    part_rows = round_trip(part_rows + jnp.einsum('esnrh,esdh->esnrd', d_upper, up_s, precision=HIGHEST))
    picked = collect(round_trip(lax.optimization_barrier(jnp.sum(part_rows, axis=1))), slot_ids)
    d_normed = lax.optimization_barrier(jnp.sum(mix_row.reshape(N_EXPERT, TOK_DEV, TOPK)[..., None] * picked, axis=2)).reshape(MB_TOK, D)
    _, pullback = jax.vjp(lambda values: norm_apply(values, gain_row), hidden.astype(jnp.float32))
    return (grad_now.astype(jnp.float32) + pullback(d_normed)[0]).astype(jnp.bfloat16)

def reference(tokens, norm_gain, w_gate, w_up, w_down, routes, mix_weights, cotangent):
    layers = tokens.shape[0]
    finals = [None] * layers
    input_grads = [None] * layers
    for micro_batch in range(layers):
        hidden = tokens[micro_batch]
        states = []
        for step_index in range(STEPS):
            layer_index = (micro_batch + step_index) % layers
            states.append(hidden)
            hidden = layer_forward(hidden, norm_gain[layer_index], w_gate[layer_index], w_up[layer_index], w_down[layer_index], routes[layer_index, step_index], mix_weights[layer_index, step_index])
        last_layer = (micro_batch + STEPS - 1) % layers
        finals[last_layer] = hidden
        grad_now = cotangent[last_layer]
        for step_index in reversed(range(STEPS)):
            layer_index = (micro_batch + step_index) % layers
            grad_now = layer_backward(states[step_index], grad_now, norm_gain[layer_index], w_gate[layer_index], w_up[layer_index], w_down[layer_index], routes[layer_index, step_index], mix_weights[layer_index, step_index])
        input_grads[micro_batch] = grad_now
    return (jnp.stack(finals), jnp.stack(input_grads))
```

```python
import jax
import jax.numpy as jnp
from jax import lax
from jax.sharding import PartitionSpec as P

SPLIT = 4
EPSILON = 1e-06
BF = jnp.bfloat16
F32 = jnp.float32


def dot(left, right, dims):
    return lax.dot_general(left, right, (dims, ((), ())), preferred_element_type=F32)


def inv_rms(rows):
    return lax.rsqrt(jnp.mean(rows * rows, axis=-1, keepdims=True) + EPSILON)


def shift(value, sections=0, experts=0, flip=0):
    n_sec, n_own = lax.axis_size("section"), lax.axis_size("expert")
    n_exp = n_own // SPLIT
    if sections % n_sec == 0 and experts % n_exp == 0 and flip == 0:
        return value
    pairs = []
    for sec in range(n_sec):
        for own in range(n_own):
            exp, sl = own // SPLIT, own % SPLIT
            to = ((exp + experts) % n_exp) * SPLIT + (sl ^ flip)
            pairs.append((sec * n_own + own, ((sec + sections) % n_sec) * n_own + to))
    return lax.ppermute(value, ("section", "expert"), pairs)


def selectors(ids, experts, capacity):
    mine = lax.axis_index("expert") // SPLIT
    count = ids.shape[0]
    same = ids[:, None] == ids[None, :]
    earlier = lax.broadcasted_iota(jnp.int32, (count, count), 0) < lax.broadcasted_iota(
        jnp.int32, (count, count), 1
    )
    rank = jnp.sum((same & earlier).astype(jnp.int32), axis=0)
    slot = lax.broadcasted_iota(jnp.int32, (capacity, count), 0)
    hit = slot == rank[None, :]
    return [
        (hit & (ids == (mine + j) % experts)[None, :]).astype(BF) for j in range(experts)
    ]


def local(tokens, norm_gain, w_gate, w_up, w_down, routes, mix_weights, cotangent):
    experts = lax.axis_size("expert") // SPLIT
    count = tokens.shape[1]
    capacity = count // experts + max(1, count // (16 * experts))
    gain = norm_gain
    gate_w, up_w, down_w = w_gate[0, 0], w_up[0, 0], w_down[0, 0]

    def dispatch(values, sel):
        boxes = [dot(one, values, ((1,), (0,))).astype(BF) for one in sel]
        crossed = [shift(boxes[j], experts=j) for j in range(1, experts)]
        own = [shift(boxes[0], flip=i) for i in range(SPLIT)]
        cross = jnp.concatenate(crossed, axis=0)
        cross = [shift(cross, flip=i) for i in range(SPLIT)]
        return [jnp.concatenate(own, axis=0), jnp.concatenate(cross, axis=0)]

    def give_back(parts, sections):
        own, cross = parts
        rows = own.shape[0] // SPLIT
        others = cross.shape[0] // SPLIT
        cross_sum = sum(
            shift(cross[i * others : (i + 1) * others], flip=i).astype(F32) for i in range(SPLIT)
        ).astype(BF)
        back = [
            shift(cross_sum[(j - 1) * rows : j * rows], sections=sections, experts=-j)
            for j in range(1, experts)
        ]
        own_sum = sum(
            shift(own[i * rows : (i + 1) * rows], sections=sections, flip=i).astype(F32)
            for i in range(SPLIT)
        ).astype(BF)
        return [own_sum] + back

    def combine(returned, sel, mix):
        picked = sum(dot(one, rows, ((0,), (0,))) for one, rows in zip(sel, returned))
        return mix * picked

    def gate_up(rows):
        return [
            (dot(part, gate_w, ((1,), (0,))), dot(part, up_w, ((1,), (0,)))) for part in rows
        ]

    def forward_rows(gate_ups):
        return [
            dot((jax.nn.silu(g) * u).astype(BF), down_w, ((1,), (0,))).astype(BF)
            for g, u in gate_ups
        ]

    def backward_rows(gate_ups, grads):
        outs = []
        for (g, u), rows in zip(gate_ups, grads):
            r = jax.nn.sigmoid(g)
            d_inner = dot(rows, down_w, ((1,), (1,)))
            d_gate = (d_inner * u * r * (1.0 + g * (1.0 - r))).astype(BF)
            d_up = (d_inner * g * r).astype(BF)
            part = dot(d_gate, gate_w, ((1,), (1,))) + dot(d_up, up_w, ((1,), (1,)))
            outs.append(part.astype(BF))
        return outs

    def normed(hidden, gain_row):
        wide = hidden.astype(F32)
        return (wide * inv_rms(wide) * gain_row).astype(BF)

    def norm_back(hidden, gain_row, grad):
        wide = hidden.astype(F32)
        inv = inv_rms(wide)
        scaled = grad * gain_row
        along = jnp.mean(scaled * wide, axis=-1, keepdims=True)
        return inv * scaled - wide * (inv * inv * inv * along)

    ids = routes[0, :, :, 0]
    mix = mix_weights[0]
    ids_prev, mix_prev = shift(ids[0], sections=1), shift(mix[0], sections=1)
    ids_next, mix_next = shift(ids[1], sections=-1), shift(mix[1], sections=-1)
    gain_next = shift(gain, sections=-1)
    tokens_prev = shift(tokens[0], sections=1)
    cot_next = shift(cotangent[0], sections=-1)

    sel0 = selectors(ids[0], experts, capacity)
    sel1 = selectors(ids[1], experts, capacity)
    sel0_prev = selectors(ids_prev, experts, capacity)
    sel1_next = selectors(ids_next, experts, capacity)

    rows0 = dispatch(normed(tokens[0], gain), sel0)
    cots = dispatch(cotangent[0], sel1)
    gu0 = gate_up(rows0)
    back0 = give_back(forward_rows(gu0), 1)
    h1 = (tokens_prev.astype(F32) + combine(back0, sel0_prev, mix_prev)).astype(BF)
    h1_home = shift(h1, sections=-1)
    rows1 = dispatch(normed(h1, gain), sel1)
    gu1 = gate_up(rows1)
    grad1 = give_back(backward_rows(gu1, cots), -1)
    fin = give_back(forward_rows(gu1), 0)
    g1 = (
        cot_next.astype(F32)
        + norm_back(h1_home, gain_next, combine(grad1, sel1_next, mix_next))
    ).astype(BF)
    grads = dispatch(g1, sel0)
    grad0 = give_back(backward_rows(gu0, grads), 0)
    final = (h1.astype(F32) + combine(fin, sel1, mix[1])).astype(BF)
    g0 = (g1.astype(F32) + norm_back(tokens[0], gain, combine(grad0, sel0, mix[0]))).astype(BF)
    return (final[None], g0[None])


def solution(mesh):
    in_specs = (
        P("section", "expert", None),
        P("section", None),
        P("section", "expert", None, None),
        P("section", "expert", None, None),
        P("section", "expert", None, None),
        P("section", None, "expert", None),
        P("section", None, "expert", None),
        P("section", "expert", None),
    )
    out_specs = (P("section", "expert", None), P("section", "expert", None))
    return jax.shard_map(local, mesh=mesh, in_specs=in_specs, out_specs=out_specs, check_vma=False)
```

```python
import jax
import jax.numpy as jnp
from jax import lax
from jax.sharding import PartitionSpec as P

SPLIT = 4
EPSILON = 1e-06
BF = jnp.bfloat16
F32 = jnp.float32


def dot(left, right, dims):
    return lax.dot_general(left, right, (dims, ((), ())), preferred_element_type=F32)


def inv_rms(rows):
    return lax.rsqrt(jnp.mean(rows * rows, axis=-1, keepdims=True) + EPSILON)


def shift(value, sections=0, experts=0, flip=0):
    n_sec, n_own = lax.axis_size("section"), lax.axis_size("expert")
    n_exp = n_own // SPLIT
    if sections % n_sec == 0 and experts % n_exp == 0 and flip == 0:
        return value
    pairs = []
    for sec in range(n_sec):
        for own in range(n_own):
            exp, sl = own // SPLIT, own % SPLIT
            to = ((exp + experts) % n_exp) * SPLIT + (sl ^ flip)
            pairs.append((sec * n_own + own, ((sec + sections) % n_sec) * n_own + to))
    return lax.ppermute(value, ("section", "expert"), pairs)


def selectors(ids, experts, capacity):
    mine = lax.axis_index("expert") // SPLIT
    count = ids.shape[0]
    same = ids[:, None] == ids[None, :]
    earlier = lax.broadcasted_iota(jnp.int32, (count, count), 0) < lax.broadcasted_iota(
        jnp.int32, (count, count), 1
    )
    rank = jnp.sum((same & earlier).astype(jnp.int32), axis=0)
    slot = lax.broadcasted_iota(jnp.int32, (capacity, count), 0)
    hit = slot == rank[None, :]
    return [
        (hit & (ids == (mine + j) % experts)[None, :]).astype(BF) for j in range(experts)
    ]


def local(tokens, norm_gain, w_gate, w_up, w_down, routes, mix_weights, cotangent):
    experts = lax.axis_size("expert") // SPLIT
    count = tokens.shape[1]
    capacity = count // experts + max(1, count // (16 * experts))
    gain = norm_gain
    gate_w, up_w, down_w = w_gate[0, 0], w_up[0, 0], w_down[0, 0]

    def dispatch(values, sel):
        boxes = [dot(one, values, ((1,), (0,))).astype(BF) for one in sel]
        crossed = [shift(boxes[j], experts=j) for j in range(1, experts)]
        return [whole(boxes[0]), whole(jnp.concatenate(crossed, axis=0))]

    def whole(rows):
        groups = [[e * SPLIT + i for i in range(SPLIT)] for e in range(experts)]
        every = lax.all_gather(rows, "expert", axis_index_groups=groups)
        me = lax.axis_index("expert") % SPLIT
        return jnp.concatenate([every[me ^ i] for i in range(SPLIT)], axis=0)

    def give_back(parts, sections):
        own, cross = parts
        rows = own.shape[0] // SPLIT
        others = cross.shape[0] // SPLIT
        cross_sum = sum(
            shift(cross[i * others : (i + 1) * others], flip=i).astype(F32) for i in range(SPLIT)
        ).astype(BF)
        back = [
            shift(cross_sum[(j - 1) * rows : j * rows], sections=sections, experts=-j)
            for j in range(1, experts)
        ]
        own_sum = sum(
            shift(own[i * rows : (i + 1) * rows], sections=sections, flip=i).astype(F32)
            for i in range(SPLIT)
        ).astype(BF)
        return [own_sum] + back

    def combine(returned, sel, mix):
        picked = sum(dot(one, rows, ((0,), (0,))) for one, rows in zip(sel, returned))
        return mix * picked

    def gate_up(rows):
        return [
            (dot(part, gate_w, ((1,), (0,))), dot(part, up_w, ((1,), (0,)))) for part in rows
        ]

    def forward_rows(gate_ups):
        return [
            dot((jax.nn.silu(g) * u).astype(BF), down_w, ((1,), (0,))).astype(BF)
            for g, u in gate_ups
        ]

    def backward_rows(gate_ups, grads):
        outs = []
        for (g, u), rows in zip(gate_ups, grads):
            r = jax.nn.sigmoid(g)
            d_inner = dot(rows, down_w, ((1,), (1,)))
            d_gate = (d_inner * u * r * (1.0 + g * (1.0 - r))).astype(BF)
            d_up = (d_inner * g * r).astype(BF)
            part = dot(d_gate, gate_w, ((1,), (1,))) + dot(d_up, up_w, ((1,), (1,)))
            outs.append(part.astype(BF))
        return outs

    def normed(hidden, gain_row):
        wide = hidden.astype(F32)
        return (wide * inv_rms(wide) * gain_row).astype(BF)

    def norm_back(hidden, gain_row, grad):
        wide = hidden.astype(F32)
        inv = inv_rms(wide)
        scaled = grad * gain_row
        along = jnp.mean(scaled * wide, axis=-1, keepdims=True)
        return inv * scaled - wide * (inv * inv * inv * along)

    ids = routes[0, :, :, 0]
    mix = mix_weights[0]
    ids_prev, mix_prev = shift(ids[0], sections=1), shift(mix[0], sections=1)
    ids_next, mix_next = shift(ids[1], sections=-1), shift(mix[1], sections=-1)
    gain_next = shift(gain, sections=-1)
    tokens_prev = shift(tokens[0], sections=1)
    cot_next = shift(cotangent[0], sections=-1)

    sel0 = selectors(ids[0], experts, capacity)
    sel1 = selectors(ids[1], experts, capacity)
    sel0_prev = selectors(ids_prev, experts, capacity)
    sel1_next = selectors(ids_next, experts, capacity)

    rows0 = dispatch(normed(tokens[0], gain), sel0)
    cots = dispatch(cotangent[0], sel1)
    gu0 = gate_up(rows0)
    back0 = give_back(forward_rows(gu0), 1)
    h1 = (tokens_prev.astype(F32) + combine(back0, sel0_prev, mix_prev)).astype(BF)
    h1_home = shift(h1, sections=-1)
    rows1 = dispatch(normed(h1, gain), sel1)
    gu1 = gate_up(rows1)
    grad1 = give_back(backward_rows(gu1, cots), -1)
    fin = give_back(forward_rows(gu1), 0)
    g1 = (
        cot_next.astype(F32)
        + norm_back(h1_home, gain_next, combine(grad1, sel1_next, mix_next))
    ).astype(BF)
    grads = dispatch(g1, sel0)
    grad0 = give_back(backward_rows(gu0, grads), 0)
    final = (h1.astype(F32) + combine(fin, sel1, mix[1])).astype(BF)
    g0 = (g1.astype(F32) + norm_back(tokens[0], gain, combine(grad0, sel0, mix[0]))).astype(BF)
    return (final[None], g0[None])


def solution(mesh):
    in_specs = (
        P("section", "expert", None),
        P("section", None),
        P("section", "expert", None, None),
        P("section", "expert", None, None),
        P("section", "expert", None, None),
        P("section", None, "expert", None),
        P("section", None, "expert", None),
        P("section", "expert", None),
    )
    out_specs = (P("section", "expert", None), P("section", "expert", None))
    return jax.shard_map(local, mesh=mesh, in_specs=in_specs, out_specs=out_specs, check_vma=False)
```

```python
import functools

import jax
import jax.numpy as jnp
from jax import lax
from jax.experimental import pallas as pl
from jax.experimental.pallas import tpu as pltpu
from jax.sharding import PartitionSpec as P

SPLIT = 4
EPSILON = 1e-06
BF = jnp.bfloat16
F32 = jnp.float32
ROWS = 16
LANES = 128


def dot(left, right, dims=((1,), (0,))):
    return lax.dot_general(left, right, (dims, ((), ())), preferred_element_type=F32)


def iota(shape, axis):
    return lax.broadcasted_iota(jnp.int32, shape, axis)


class Box:
    def __init__(self, capacity, width):
        self.capacity, self.width = capacity, width
        self.groups, self.extra = capacity // ROWS, capacity % ROWS
        self.cuts = ROWS // self.extra if self.extra else 1
        self.wide = -(-width // (LANES * self.cuts)) * LANES if self.extra else 0
        self.lanes = self.groups * width + self.wide
        self.pieces = -(-width // self.wide) if self.extra else 0

    def group(self, g):
        return pl.ds(g * self.width, self.width)

    def tail(self):
        return pl.ds(self.groups * self.width, self.wide)

    def piece(self, i):
        return i * self.wide, min(self.wide, self.width - i * self.wide)


def shift(value, sections=0, experts=0, flip=0):
    n_sec, n_own = lax.axis_size("section"), lax.axis_size("expert")
    n_exp = n_own // SPLIT
    if sections % n_sec == 0 and experts % n_exp == 0 and flip == 0:
        return value
    pairs = []
    for sec in range(n_sec):
        for own in range(n_own):
            exp, sl = own // SPLIT, own % SPLIT
            to = ((exp + experts) % n_exp) * SPLIT + (sl ^ flip)
            pairs.append((sec * n_own + own, ((sec + sections) % n_sec) * n_own + to))
    return lax.ppermute(value, ("section", "expert"), pairs)


def call(body, outs, *operands, scratch=(), flops=0):
    moved = sum(a.size * a.dtype.itemsize for a in operands)
    moved += sum(o.size * o.dtype.itemsize for o in outs)
    vmem = pl.BlockSpec(memory_space=pltpu.VMEM)
    return pl.pallas_call(
        body,
        out_shape=list(outs),
        in_specs=[vmem] * len(operands),
        out_specs=[vmem] * len(outs),
        scratch_shapes=list(scratch),
        compiler_params=pltpu.CompilerParams(vmem_limit_bytes=32 * 2**20),
        cost_estimate=pl.CostEstimate(flops=flops, bytes_accessed=moved, transcendentals=0),
    )(*operands)


def row_of(column):
    n = column.shape[0]
    eye = iota((n, n), 0) == iota((n, n), 1)
    return jnp.sum(jnp.where(eye, column, 0.0), axis=0, keepdims=True)


def slots_of(rel, experts, capacity):
    n = rel.shape[0]
    same = jnp.broadcast_to(rel, (n, n)) == jnp.broadcast_to(row_of(rel), (n, n))
    before = iota((n, n), 1) < iota((n, n), 0)
    rank = jnp.sum(jnp.where(same & before, 1.0, 0.0), axis=1, keepdims=True)
    return rel * capacity + rank


def pack_rows(box, slots, values, out_refs):
    n = values.shape[0]
    line = jnp.broadcast_to(row_of(slots).astype(jnp.int32), (ROWS, n))
    r = iota((ROWS, n), 0)
    for j, out in enumerate(out_refs):
        first = j * box.capacity
        for g in range(box.groups):
            sel = jnp.where(line == first + g * ROWS + r, 1.0, 0.0).astype(BF)
            out[:, box.group(g)] = dot(sel, values).astype(BF)
        if box.extra:
            total = jnp.zeros((ROWS, box.wide), F32)
            for i in range(box.pieces):
                at, size = box.piece(i)
                hit = (line == first + box.groups * ROWS + r // box.cuts) & (r % box.cuts == i)
                hit &= r // box.cuts < box.extra
                got = dot(jnp.where(hit, 1.0, 0.0).astype(BF), values[:, at : at + size])
                if size < box.wide:
                    got = jnp.concatenate([got, jnp.zeros((ROWS, box.wide - size), F32)], axis=1)
                total = total + got
            out[:, box.tail()] = total.astype(BF)


def pick_rows(box, slots, boxes, n, picked):
    count = len(boxes)
    if box.groups:
        stack = jnp.concatenate(
            [b[:, g * box.width : (g + 1) * box.width] for b in boxes for g in range(box.groups)],
            axis=0,
        )
        tall = count * box.groups * ROWS
        c = iota((n, tall), 1)
        slot = c // (box.groups * ROWS) * box.capacity + c % (box.groups * ROWS)
        sel = jnp.where(slots.astype(jnp.int32) == slot, 1.0, 0.0).astype(BF)
        picked[...] = dot(sel, stack)
    else:
        picked[...] = jnp.zeros(picked.shape, F32)
    if box.extra:
        tails = jnp.concatenate([b[:, box.groups * box.width :] for b in boxes], axis=0)
        c = iota((n, count * ROWS), 1)
        r = c % ROWS
        slot = c // ROWS * box.capacity + box.groups * ROWS + r // box.cuts
        mine = (slots.astype(jnp.int32) == slot) & (r // box.cuts < box.extra)
        for i in range(box.pieces):
            at, size = box.piece(i)
            sel = jnp.where(mine & (r % box.cuts == i), 1.0, 0.0).astype(BF)
            picked[:, at : at + size] += dot(sel, tails[:, :size])


def heights(box, count):
    extra = -(-count * box.extra // ROWS) * ROWS
    return count * box.groups * ROWS, extra


def unpack(box, refs, stack, tails):
    at = 0
    count = 0
    for ref in refs:
        for p in range(ref.shape[0] // ROWS):
            for g in range(box.groups):
                stack[at : at + ROWS, :] = ref[p * ROWS : (p + 1) * ROWS, box.group(g)]
                at += ROWS
            if box.extra:
                tails[count * ROWS : (count + 1) * ROWS, :] = ref[
                    p * ROWS : (p + 1) * ROWS, box.tail()
                ]
            count += 1
    if box.extra:
        extra = heights(box, count)[1]
        r = iota((extra, count * ROWS), 0)
        c = iota((extra, count * ROWS), 1)
        mine = (r // box.extra == c // ROWS) & (r % box.extra == c % ROWS // box.cuts)
        for i in range(box.pieces):
            start, size = box.piece(i)
            sel = jnp.where(mine & (c % ROWS % box.cuts == i), 1.0, 0.0).astype(BF)
            stack[at : at + extra, start : start + size] = dot(sel, tails[:, :size]).astype(BF)


def repack(box, rows, refs):
    rows = rows.astype(BF)
    at = 0
    count = 0
    for ref in refs:
        for p in range(ref.shape[0] // ROWS):
            for g in range(box.groups):
                ref[p * ROWS : (p + 1) * ROWS, box.group(g)] = rows[at : at + ROWS]
                at += ROWS
            count += 1
    if box.extra:
        extra = heights(box, count)[1]
        r = iota((count * ROWS, extra), 0)
        c = iota((count * ROWS, extra), 1)
        mine = (c // box.extra == r // ROWS) & (c % box.extra == r % ROWS // box.cuts)
        total = jnp.zeros((count * ROWS, box.wide), F32)
        for i in range(box.pieces):
            start, size = box.piece(i)
            sel = jnp.where(mine & (r % ROWS % box.cuts == i), 1.0, 0.0).astype(BF)
            got = dot(sel, rows[at:, start : start + size])
            if size < box.wide:
                pad = jnp.zeros((count * ROWS, box.wide - size), F32)
                got = jnp.concatenate([got, pad], axis=1)
            total = total + got
        total = total.astype(BF)
        count = 0
        for ref in refs:
            tall = ref.shape[0]
            ref[:, box.tail()] = total[count : count + tall]
            count += tall


def inv_rms(wide):
    return lax.rsqrt(jnp.mean(wide * wide, axis=-1, keepdims=True) + EPSILON)


def total_of(refs):
    return sum(ref[...].astype(F32) for ref in refs).astype(BF)


def start_kernel(box, experts, tokens, gain, rel, mix, meta0, meta1, *boxes):
    n = tokens.shape[0]
    lane = iota((n, LANES), 1)
    for k, meta in enumerate((meta0, meta1)):
        slots = slots_of(rel[k].astype(F32), experts, box.capacity)
        meta[:n] = jnp.where(lane == 0, slots, jnp.where(lane == 1, mix[k], 0.0))
    for b in range(box.width // LANES):
        meta1[n + b : n + b + 1] = gain[:, b * LANES : (b + 1) * LANES]
    wide = tokens[...].astype(F32)
    normed = (wide * inv_rms(wide) * gain[...]).astype(BF)
    pack_rows(box, meta0[:n, 0:1], normed, boxes)


def pack_kernel(box, values, meta, *boxes):
    pack_rows(box, meta[: values.shape[0], 0:1], values[...], boxes)


def combine(box, meta, n, own, back, picked):
    sums = [total_of(own)] + [ref[...] for ref in back]
    pick_rows(box, meta[:n, 0:1], sums, n, picked)
    return meta[:n, 1:2] * picked[...]


def middle_kernel(box, experts, hidden, meta, meta_out, gain, *refs):
    own, back = refs[:3], refs[3 : 2 + experts]
    after, boxes, picked = refs[2 + experts], refs[3 + experts : -1], refs[-1]
    n = hidden.shape[0]
    later = (hidden[...].astype(F32) + combine(box, meta, n, own, back, picked)).astype(BF)
    after[...] = later
    wide = later.astype(F32)
    normed = (wide * inv_rms(wide) * gain[...]).astype(BF)
    pack_rows(box, meta_out[:n, 0:1], normed, boxes)


def final_kernel(box, experts, hidden, meta, *refs):
    own, back = refs[:3], refs[3 : 2 + experts]
    out, picked = refs[-2:]
    n = hidden.shape[0]
    out[...] = (hidden[...].astype(F32) + combine(box, meta, n, own, back, picked)).astype(BF)


def norm_back(hidden, gain, grad):
    wide = hidden.astype(F32)
    inv = inv_rms(wide)
    scaled = grad * gain
    along = jnp.mean(scaled * wide, axis=-1, keepdims=True)
    return inv * scaled - wide * (inv * inv * inv * along)


def gradient_kernel(box, experts, packs, grad, hidden, meta, meta_out, gain, *refs):
    own, back = refs[:3], refs[3 : 2 + experts]
    out, boxes, picked = refs[2 + experts], refs[3 + experts : -1], refs[-1]
    n = hidden.shape[0]
    d_normed = combine(box, meta, n, own, back, picked)
    if packs:
        row = jnp.concatenate([meta[n + b : n + b + 1] for b in range(box.width // LANES)], axis=1)
    else:
        row = gain[...]
    now = (grad[...].astype(F32) + norm_back(hidden[...], row, d_normed)).astype(BF)
    out[...] = now
    if packs:
        pack_rows(box, meta_out[:n, 0:1], now, boxes)


def forward_kernel(box, gate_w, up_w, down_w, *refs):
    rows, outs = refs[:SPLIT], refs[SPLIT : 2 * SPLIT]
    gate, up, stack, tails = refs[2 * SPLIT :]
    unpack(box, rows, stack, tails)
    g = dot(stack[...], gate_w[...])
    u = dot(stack[...], up_w[...])
    gate[...] = g
    up[...] = u
    inner = (jax.nn.silu(g) * u).astype(BF)
    repack(box, dot(inner, down_w[...]), outs)


def gate_kernel(box, gate_w, up_w, *refs):
    rows = refs[:SPLIT]
    gate, up, stack, tails = refs[SPLIT:]
    unpack(box, rows, stack, tails)
    gate[...] = dot(stack[...], gate_w[...])
    up[...] = dot(stack[...], up_w[...])


def down_kernel(box, gate, up, down_w, *outs):
    inner = (jax.nn.silu(gate[...]) * up[...]).astype(BF)
    repack(box, dot(inner, down_w[...]), outs)


def inner_kernel(box, down_w, *refs):
    rows = refs[:SPLIT]
    d_inner, stack, tails = refs[SPLIT:]
    unpack(box, rows, stack, tails)
    d_inner[...] = dot(stack[...], down_w[...], ((1,), (1,)))


def part_rows(box, d_inner, gate, up, gate_w, up_w, outs):
    g = gate[...]
    r = jax.nn.sigmoid(g)
    d_gate = (d_inner * up[...] * r * (1.0 + g * (1.0 - r))).astype(BF)
    d_up = (d_inner * g * r).astype(BF)
    part = dot(d_gate, gate_w[...], ((1,), (1,))) + dot(d_up, up_w[...], ((1,), (1,)))
    repack(box, part, outs)


def gate_back_kernel(box, gate_w, up_w, d_inner, *refs):
    rows, outs = refs[:SPLIT], refs[SPLIT : 2 * SPLIT]
    gate, up, stack, tails = refs[2 * SPLIT :]
    unpack(box, rows, stack, tails)
    gate[...] = dot(stack[...], gate_w[...])
    up[...] = dot(stack[...], up_w[...])
    part_rows(box, d_inner[...], gate, up, gate_w, up_w, outs)


def back_kernel(box, gate_w, up_w, down_w, gate, up, *refs):
    rows, outs = refs[:SPLIT], refs[SPLIT : 2 * SPLIT]
    stack, tails = refs[2 * SPLIT :]
    unpack(box, rows, stack, tails)
    d_inner = dot(stack[...], down_w[...], ((1,), (1,)))
    part_rows(box, d_inner, gate, up, gate_w, up_w, outs)


def local(tokens, norm_gain, w_gate, w_up, w_down, routes, mix_weights, cotangent):
    experts = lax.axis_size("expert") // SPLIT
    n, width = tokens.shape[1:]
    hid = w_gate.shape[3]
    capacity = n // experts + max(1, n // (16 * experts))
    box = Box(capacity, width)
    gain = norm_gain
    gate_w, up_w, down_w = w_gate[0, 0], w_up[0, 0], w_down[0, 0]
    boxed = jax.ShapeDtypeStruct((ROWS, box.lanes), BF)
    rows_bf = jax.ShapeDtypeStruct((n, width), BF)
    picked = pltpu.VMEM((n, width), F32)
    bind = functools.partial

    def like(array):
        return jax.ShapeDtypeStruct(array.shape, array.dtype)

    def expert_call(kernel, weights, rows, saved=(), outs=False, keep=0):
        count = sum(a.shape[0] for a in rows) // ROWS
        tall = sum(heights(box, count))
        result = [like(a) for a in rows] if outs else []
        result += [jax.ShapeDtypeStruct((tall, hid), F32)] * keep
        scratch = [
            pltpu.VMEM((tall, width), BF),
            pltpu.VMEM((count * ROWS, max(box.wide, LANES)), BF),
        ]
        mats = len(weights) + (1 if keep == 0 else 0)
        return call(
            bind(kernel, box),
            result,
            *weights,
            *saved,
            *rows,
            scratch=scratch,
            flops=2 * tall * width * hid * mats,
        )

    def dispatch(boxes):
        crossed = [shift(boxes[j], experts=j) for j in range(1, experts)]
        cross = crossed[0] if experts == 2 else jnp.concatenate(crossed, axis=0)
        along = shift(boxes[0], flip=2)
        own = [boxes[0], shift(boxes[0], flip=1), along, shift(along, flip=1)]
        return own, [shift(cross, flip=i) for i in range(SPLIT)]

    def add(*values):
        return sum(v.astype(F32) for v in values).astype(BF)

    def give_back(own, cross, sections):
        total = add(*[shift(cross[i], flip=i) for i in range(SPLIT)])
        back = [
            shift(total[(j - 1) * ROWS : j * ROWS], sections=sections, experts=-j)
            for j in range(1, experts)
        ]
        along = add(own[2], shift(own[3], flip=1))
        return [
            shift(own[0], sections=sections),
            shift(own[1], sections=sections, flip=1),
            shift(along, sections=sections, flip=2),
        ] + back

    rel = (routes[0] - lax.axis_index("expert") // SPLIT) % experts
    meta_shape = jax.ShapeDtypeStruct((n, LANES), F32)
    meta_long = jax.ShapeDtypeStruct((n + -(-width // LANES // 8) * 8, LANES), F32)
    meta0, meta1, *boxes0 = call(
        bind(start_kernel, box, experts),
        [meta_shape, meta_long] + [boxed] * experts,
        tokens[0],
        gain,
        rel,
        mix_weights[0],
    )
    own0, cross0 = dispatch(boxes0)
    meta0_prev = shift(meta0, sections=1)
    meta1_next = shift(meta1, sections=-1)
    tokens_prev = shift(tokens[0], sections=1)
    cot_next = shift(cotangent[0], sections=-1)
    cot_boxes = call(bind(pack_kernel, box), [boxed] * experts, cotangent[0], meta1)
    cot_own, cot_cross = dispatch(cot_boxes)

    forward = bind(expert_call, forward_kernel, (gate_w, up_w, down_w), outs=True, keep=2)
    *own_out, own_g0, own_u0 = forward(own0)
    *cross_out, cross_g0, cross_u0 = forward(cross0)
    got = give_back(own_out, cross_out, 1)
    h1, *boxes1 = call(
        bind(middle_kernel, box, experts),
        [rows_bf] + [boxed] * experts,
        tokens_prev,
        meta0_prev,
        meta1,
        gain,
        *got,
        scratch=[picked],
    )
    h1_home = shift(h1, sections=-1)
    own1, cross1 = dispatch(boxes1)

    inner = bind(expert_call, inner_kernel, (down_w,), keep=1)
    (own_di,), (cross_di,) = inner(cot_own), inner(cot_cross)
    gate_back = bind(expert_call, gate_back_kernel, (gate_w, up_w), outs=True, keep=2)
    *own_grad, own_g1, own_u1 = gate_back(own1, (own_di,))
    *cross_grad, cross_g1, cross_u1 = gate_back(cross1, (cross_di,))
    got = give_back(own_grad, cross_grad, -1)
    g1, *boxes_g = call(
        bind(gradient_kernel, box, experts, True),
        [rows_bf] + [boxed] * experts,
        cot_next,
        h1_home,
        meta1_next,
        meta0,
        gain,
        *got,
        scratch=[picked],
    )

    def down(g, u, rows):
        return call(bind(down_kernel, box), [like(a) for a in rows], g, u, down_w)

    own_fin, cross_fin = down(own_g1, own_u1, own1), down(cross_g1, cross_u1, cross1)
    fin = give_back(own_fin, cross_fin, 0)

    own_g, cross_g = dispatch(boxes_g)
    back = bind(expert_call, back_kernel, (gate_w, up_w, down_w), outs=True)
    own_grad = back(own_g, (own_g0, own_u0))
    cross_grad = back(cross_g, (cross_g0, cross_u0))
    got = give_back(own_grad, cross_grad, 0)
    (g0,) = call(
        bind(gradient_kernel, box, experts, False),
        [rows_bf],
        g1,
        tokens[0],
        meta0,
        meta0,
        gain,
        *got,
        scratch=[picked],
    )
    (final,) = call(
        bind(final_kernel, box, experts), [rows_bf], h1, meta1, *fin, scratch=[picked]
    )
    return (final[None], g0[None])


def solution(mesh):
    in_specs = (
        P("section", "expert", None),
        P("section", None),
        P("section", "expert", None, None),
        P("section", "expert", None, None),
        P("section", "expert", None, None),
        P("section", None, "expert", None),
        P("section", None, "expert", None),
        P("section", "expert", None),
    )
    out_specs = (P("section", "expert", None), P("section", "expert", None))
    return jax.shard_map(local, mesh=mesh, in_specs=in_specs, out_specs=out_specs, check_vma=False)
```

```python
import functools

import jax
import jax.numpy as jnp
from jax import lax
from jax.experimental import pallas as pl
from jax.experimental.pallas import tpu as pltpu
from jax.sharding import PartitionSpec as P

SPLIT = 4
EPSILON = 1e-06
BF = jnp.bfloat16
F32 = jnp.float32
ROWS = 16
LANES = 128


def dot(left, right, dims=((1,), (0,))):
    return lax.dot_general(left, right, (dims, ((), ())), preferred_element_type=F32)


def iota(shape, axis):
    return lax.broadcasted_iota(jnp.int32, shape, axis)


class Box:
    def __init__(self, capacity, width):
        self.capacity, self.width = capacity, width
        self.groups, self.extra = capacity // ROWS, capacity % ROWS
        self.cuts = ROWS // self.extra if self.extra else 1
        self.wide = -(-width // (LANES * self.cuts)) * LANES if self.extra else 0
        self.lanes = self.groups * width + self.wide
        self.pieces = -(-width // self.wide) if self.extra else 0

    def group(self, g):
        return pl.ds(g * self.width, self.width)

    def tail(self):
        return pl.ds(self.groups * self.width, self.wide)

    def piece(self, i):
        return i * self.wide, min(self.wide, self.width - i * self.wide)


def shift(value, sections=0, experts=0, flip=0):
    n_sec, n_own = lax.axis_size("section"), lax.axis_size("expert")
    n_exp = n_own // SPLIT
    if sections % n_sec == 0 and experts % n_exp == 0 and flip == 0:
        return value
    pairs = []
    for sec in range(n_sec):
        for own in range(n_own):
            exp, sl = own // SPLIT, own % SPLIT
            to = ((exp + experts) % n_exp) * SPLIT + (sl ^ flip)
            pairs.append((sec * n_own + own, ((sec + sections) % n_sec) * n_own + to))
    return lax.ppermute(value, ("section", "expert"), pairs)


def call(body, outs, *operands, scratch=(), flops=0):
    moved = sum(a.size * a.dtype.itemsize for a in operands)
    moved += sum(o.size * o.dtype.itemsize for o in outs)
    vmem = pl.BlockSpec(memory_space=pltpu.VMEM)
    return pl.pallas_call(
        body,
        out_shape=list(outs),
        in_specs=[vmem] * len(operands),
        out_specs=[vmem] * len(outs),
        scratch_shapes=list(scratch),
        compiler_params=pltpu.CompilerParams(vmem_limit_bytes=32 * 2**20),
        cost_estimate=pl.CostEstimate(flops=flops, bytes_accessed=moved, transcendentals=0),
    )(*operands)


def row_of(column):
    n = column.shape[0]
    eye = iota((n, n), 0) == iota((n, n), 1)
    return jnp.sum(jnp.where(eye, column, 0.0), axis=0, keepdims=True)


def column_of(row):
    n = row.shape[1]
    eye = iota((n, n), 0) == iota((n, n), 1)
    return jnp.sum(jnp.where(eye, row, 0.0), axis=1, keepdims=True)


def slots_of(rel, experts, capacity):
    n = rel.shape[1]
    column = column_of(rel)
    same = jnp.broadcast_to(column, (n, n)) == jnp.broadcast_to(rel, (n, n))
    before = iota((n, n), 1) < iota((n, n), 0)
    rank = jnp.sum(jnp.where(same & before, 1.0, 0.0), axis=1, keepdims=True)
    return column * capacity + rank


def pack_rows(box, slots, values, out_refs):
    n = values.shape[0]
    line = jnp.broadcast_to(row_of(slots).astype(jnp.int32), (ROWS, n))
    r = iota((ROWS, n), 0)
    for j, out in enumerate(out_refs):
        first = j * box.capacity
        for g in range(box.groups):
            sel = jnp.where(line == first + g * ROWS + r, 1.0, 0.0).astype(BF)
            out[:, box.group(g)] = dot(sel, values).astype(BF)
        if box.extra:
            total = jnp.zeros((ROWS, box.wide), F32)
            for i in range(box.pieces):
                at, size = box.piece(i)
                hit = (line == first + box.groups * ROWS + r // box.cuts) & (r % box.cuts == i)
                hit &= r // box.cuts < box.extra
                got = dot(jnp.where(hit, 1.0, 0.0).astype(BF), values[:, at : at + size])
                if size < box.wide:
                    got = jnp.concatenate([got, jnp.zeros((ROWS, box.wide - size), F32)], axis=1)
                total = total + got
            out[:, box.tail()] = total.astype(BF)


def pick_rows(box, slots, boxes, n, picked):
    count = len(boxes)
    if box.groups:
        stack = jnp.concatenate(
            [b[:, g * box.width : (g + 1) * box.width] for b in boxes for g in range(box.groups)],
            axis=0,
        )
        tall = count * box.groups * ROWS
        c = iota((n, tall), 1)
        slot = c // (box.groups * ROWS) * box.capacity + c % (box.groups * ROWS)
        sel = jnp.where(slots.astype(jnp.int32) == slot, 1.0, 0.0).astype(BF)
        picked[...] = dot(sel, stack)
    else:
        picked[...] = jnp.zeros(picked.shape, F32)
    if box.extra:
        tails = jnp.concatenate([b[:, box.groups * box.width :] for b in boxes], axis=0)
        c = iota((n, count * ROWS), 1)
        r = c % ROWS
        slot = c // ROWS * box.capacity + box.groups * ROWS + r // box.cuts
        mine = (slots.astype(jnp.int32) == slot) & (r // box.cuts < box.extra)
        for i in range(box.pieces):
            at, size = box.piece(i)
            sel = jnp.where(mine & (r % box.cuts == i), 1.0, 0.0).astype(BF)
            picked[:, at : at + size] += dot(sel, tails[:, :size])


def heights(box, count):
    extra = -(-count * box.extra // ROWS) * ROWS
    return count * box.groups * ROWS, extra


def unpack(box, refs, stack, tails):
    at = 0
    count = 0
    for ref in refs:
        for p in range(ref.shape[0] // ROWS):
            for g in range(box.groups):
                stack[at : at + ROWS, :] = ref[p * ROWS : (p + 1) * ROWS, box.group(g)]
                at += ROWS
            if box.extra:
                tails[count * ROWS : (count + 1) * ROWS, :] = ref[
                    p * ROWS : (p + 1) * ROWS, box.tail()
                ]
            count += 1
    if box.extra:
        extra = heights(box, count)[1]
        r = iota((extra, count * ROWS), 0)
        c = iota((extra, count * ROWS), 1)
        mine = (r // box.extra == c // ROWS) & (r % box.extra == c % ROWS // box.cuts)
        for i in range(box.pieces):
            start, size = box.piece(i)
            sel = jnp.where(mine & (c % ROWS % box.cuts == i), 1.0, 0.0).astype(BF)
            stack[at : at + extra, start : start + size] = dot(sel, tails[:, :size]).astype(BF)


def repack(box, rows, refs):
    rows = rows.astype(BF)
    at = 0
    count = 0
    for ref in refs:
        for p in range(ref.shape[0] // ROWS):
            for g in range(box.groups):
                ref[p * ROWS : (p + 1) * ROWS, box.group(g)] = rows[at : at + ROWS]
                at += ROWS
            count += 1
    if box.extra:
        extra = heights(box, count)[1]
        r = iota((count * ROWS, extra), 0)
        c = iota((count * ROWS, extra), 1)
        mine = (c // box.extra == r // ROWS) & (c % box.extra == r % ROWS // box.cuts)
        total = jnp.zeros((count * ROWS, box.wide), F32)
        for i in range(box.pieces):
            start, size = box.piece(i)
            sel = jnp.where(mine & (r % ROWS % box.cuts == i), 1.0, 0.0).astype(BF)
            got = dot(sel, rows[at:, start : start + size])
            if size < box.wide:
                pad = jnp.zeros((count * ROWS, box.wide - size), F32)
                got = jnp.concatenate([got, pad], axis=1)
            total = total + got
        total = total.astype(BF)
        count = 0
        for ref in refs:
            tall = ref.shape[0]
            ref[:, box.tail()] = total[count : count + tall]
            count += tall


def inv_rms(wide):
    return lax.rsqrt(jnp.mean(wide * wide, axis=-1, keepdims=True) + EPSILON)


def total_of(refs):
    return sum(ref[...].astype(F32) for ref in refs).astype(BF)


def start_kernel(box, experts, tokens, gain, ids, mix, meta0, meta1, *boxes):
    n = tokens.shape[0]
    lane = iota((n, LANES), 1)
    mine = lax.axis_index("expert") // SPLIT
    for k, meta in enumerate((meta0, meta1)):
        rel = ids[k : k + 1, :] - mine
        rel = jnp.where(rel < 0, rel + experts, rel).astype(F32)
        slots = slots_of(rel, experts, box.capacity)
        mixes = column_of(mix[k : k + 1, :])
        meta[:n] = jnp.where(lane == 0, slots, jnp.where(lane == 1, mixes, 0.0))
    for b in range(box.width // LANES):
        meta1[n + b : n + b + 1] = gain[:, b * LANES : (b + 1) * LANES]
    wide = tokens[...].astype(F32)
    normed = (wide * inv_rms(wide) * gain[...]).astype(BF)
    pack_rows(box, meta0[:n, 0:1], normed, boxes)


def pack_kernel(box, values, meta, *boxes):
    pack_rows(box, meta[: values.shape[0], 0:1], values[...], boxes)


def combine(box, meta, n, own, back, picked):
    sums = [total_of(own)] + [ref[...] for ref in back]
    pick_rows(box, meta[:n, 0:1], sums, n, picked)
    return meta[:n, 1:2] * picked[...]


def split_refs(refs, experts, outs):
    ins = refs[:-outs]
    return ins[: len(ins) + 1 - experts], ins[len(ins) + 1 - experts :], refs[-outs:]


def middle_kernel(box, experts, hidden, meta, meta_out, gain, *refs):
    boxes, picked = refs[-1 - experts : -1], refs[-1]
    own, back, (after,) = split_refs(refs[: -1 - experts], experts, 1)
    n = hidden.shape[0]
    later = (hidden[...].astype(F32) + combine(box, meta, n, own, back, picked)).astype(BF)
    after[...] = later
    wide = later.astype(F32)
    normed = (wide * inv_rms(wide) * gain[...]).astype(BF)
    pack_rows(box, meta_out[:n, 0:1], normed, boxes)


def final_kernel(box, experts, hidden, meta, *refs):
    picked = refs[-1]
    own, back, (out,) = split_refs(refs[:-1], experts, 1)
    n = hidden.shape[0]
    out[...] = (hidden[...].astype(F32) + combine(box, meta, n, own, back, picked)).astype(BF)


def norm_back(hidden, gain, grad):
    wide = hidden.astype(F32)
    inv = inv_rms(wide)
    scaled = grad * gain
    along = jnp.mean(scaled * wide, axis=-1, keepdims=True)
    return inv * scaled - wide * (inv * inv * inv * along)


def gradient_kernel(box, experts, packs, grad, hidden, meta, meta_out, gain, *refs):
    boxes, picked = (refs[-1 - experts : -1] if packs else ()), refs[-1]
    own, back, (out,) = split_refs(refs[: len(refs) - 1 - len(boxes)], experts, 1)
    n = hidden.shape[0]
    d_normed = combine(box, meta, n, own, back, picked)
    if packs:
        row = jnp.concatenate([meta[n + b : n + b + 1] for b in range(box.width // LANES)], axis=1)
    else:
        row = gain[...]
    now = (grad[...].astype(F32) + norm_back(hidden[...], row, d_normed)).astype(BF)
    out[...] = now
    if packs:
        pack_rows(box, meta_out[:n, 0:1], now, boxes)


def halves(refs):
    return refs[: len(refs) // 2], refs[len(refs) // 2 :]


def forward_kernel(box, gate_w, up_w, down_w, *refs):
    gate, up, stack, tails = refs[-4:]
    rows, outs = halves(refs[:-4])
    unpack(box, rows, stack, tails)
    g = dot(stack[...], gate_w[...], ((1,), (1,)))
    u = dot(stack[...], up_w[...], ((1,), (1,)))
    gate[...] = g
    up[...] = u
    inner = (jax.nn.silu(g) * u).astype(BF)
    repack(box, dot(inner, down_w[...]), outs)


def gate_kernel(box, gate_w, up_w, *refs):
    rows = refs[:-4]
    gate, up, stack, tails = refs[-4:]
    unpack(box, rows, stack, tails)
    gate[...] = dot(stack[...], gate_w[...], ((1,), (1,)))
    up[...] = dot(stack[...], up_w[...], ((1,), (1,)))


def down_kernel(box, gate, up, down_w, *outs):
    inner = (jax.nn.silu(gate[...]) * up[...]).astype(BF)
    repack(box, dot(inner, down_w[...]), outs)


def inner_kernel(box, down_w, *refs):
    rows = refs[:-3]
    d_inner, stack, tails = refs[-3:]
    unpack(box, rows, stack, tails)
    d_inner[...] = dot(stack[...], down_w[...], ((1,), (1,)))


def part_rows(box, d_inner, gate, up, gate_w, up_w, outs):
    g = gate[...]
    r = jax.nn.sigmoid(g)
    d_gate = (d_inner * up[...] * r * (1.0 + g * (1.0 - r))).astype(BF)
    d_up = (d_inner * g * r).astype(BF)
    part = dot(d_gate, gate_w[...]) + dot(d_up, up_w[...])
    repack(box, part, outs)


def gate_back_kernel(box, gate_w, up_w, d_inner, *refs):
    gate, up, stack, tails = refs[-4:]
    rows, outs = halves(refs[:-4])
    unpack(box, rows, stack, tails)
    gate[...] = dot(stack[...], gate_w[...], ((1,), (1,)))
    up[...] = dot(stack[...], up_w[...], ((1,), (1,)))
    part_rows(box, d_inner[...], gate, up, gate_w, up_w, outs)


def back_kernel(box, gate_w, up_w, down_w, gate, up, *refs):
    stack, tails = refs[-2:]
    rows, outs = halves(refs[:-2])
    unpack(box, rows, stack, tails)
    d_inner = dot(stack[...], down_w[...], ((1,), (1,)))
    part_rows(box, d_inner, gate, up, gate_w, up_w, outs)


def local(tokens, norm_gain, w_gate, w_up, w_down, routes, mix_weights, cotangent):
    experts = lax.axis_size("expert") // SPLIT
    n, width = tokens.shape[1:]
    hid = w_gate.shape[3]
    capacity = n // experts + max(1, n // (16 * experts))
    box = Box(capacity, width)
    gain = norm_gain
    gate_w, up_w, down_w = w_gate[0, 0].T, w_up[0, 0].T, w_down[0, 0]
    boxed = jax.ShapeDtypeStruct((ROWS, box.lanes), BF)
    rows_bf = jax.ShapeDtypeStruct((n, width), BF)
    picked = pltpu.VMEM((n, width), F32)
    bind = functools.partial

    def like(array):
        return jax.ShapeDtypeStruct(array.shape, array.dtype)

    def expert_call(kernel, weights, rows, saved=(), outs=False, keep=0):
        count = sum(a.shape[0] for a in rows) // ROWS
        tall = sum(heights(box, count))
        result = [like(a) for a in rows] if outs else []
        result += [jax.ShapeDtypeStruct((tall, hid), F32)] * keep
        scratch = [
            pltpu.VMEM((tall, width), BF),
            pltpu.VMEM((count * ROWS, max(box.wide, LANES)), BF),
        ]
        mats = len(weights) + (1 if keep == 0 else 0)
        return call(
            bind(kernel, box),
            result,
            *weights,
            *saved,
            *rows,
            scratch=scratch,
            flops=2 * tall * width * hid * mats,
        )

    groups = [[e * SPLIT + i for i in range(SPLIT)] for e in range(experts)]
    others = (experts - 1) * ROWS

    def exchange(parts):
        return lax.all_to_all(
            parts, "expert", split_axis=0, concat_axis=0, axis_index_groups=groups, tiled=True
        )

    def dispatch(boxes):
        crossed = [shift(boxes[j], experts=j) for j in range(1, experts)]
        cross = crossed[0] if experts == 2 else jnp.concatenate(crossed, axis=0)
        along = shift(boxes[0], flip=2)
        pair = shift(jnp.concatenate([boxes[0], along], axis=0), flip=1)
        every = jnp.broadcast_to(cross[None], (SPLIT,) + cross.shape)
        return [boxes[0], along, pair], [exchange(every.reshape(SPLIT * others, -1))]

    def add(*values):
        return sum(v.astype(F32) for v in values).astype(BF)

    def give_back(own, cross, sections):
        parts = exchange(cross[0]).reshape(SPLIT, others, box.lanes)
        total = add(*[parts[i] for i in range(SPLIT)])
        back = [
            shift(total[(j - 1) * ROWS : j * ROWS], sections=sections, experts=-j)
            for j in range(1, experts)
        ]
        here, along, pair = own
        pair = shift(pair, flip=1)
        along = shift(add(along, pair[ROWS:]), sections=sections, flip=2)
        if sections:
            return [shift(add(here, pair[:ROWS]), sections=sections), along] + back
        return [here, pair[:ROWS], along] + back

    meta_shape = jax.ShapeDtypeStruct((n, LANES), F32)
    meta_long = jax.ShapeDtypeStruct((n + -(-width // LANES // 8) * 8, LANES), F32)
    meta0, meta1, *boxes0 = call(
        bind(start_kernel, box, experts),
        [meta_shape, meta_long] + [boxed] * experts,
        tokens[0],
        gain,
        routes[0, :, :, 0],
        mix_weights[0, :, :, 0],
    )
    own0, cross0 = dispatch(boxes0)
    meta0_prev = shift(meta0, sections=1)
    meta1_next = shift(meta1, sections=-1)
    tokens_prev = shift(tokens[0], sections=1)
    cot_next = shift(cotangent[0], sections=-1)
    cot_boxes = call(bind(pack_kernel, box), [boxed] * experts, cotangent[0], meta1)
    cot_own, cot_cross = dispatch(cot_boxes)

    forward = bind(expert_call, forward_kernel, (gate_w, up_w, down_w), outs=True, keep=2)
    *own_out, own_g0, own_u0 = forward(own0)
    *cross_out, cross_g0, cross_u0 = forward(cross0)
    got = give_back(own_out, cross_out, 1)
    h1, *boxes1 = call(
        bind(middle_kernel, box, experts),
        [rows_bf] + [boxed] * experts,
        tokens_prev,
        meta0_prev,
        meta1,
        gain,
        *got,
        scratch=[picked],
    )
    h1_home = shift(h1, sections=-1)
    own1, cross1 = dispatch(boxes1)

    inner = bind(expert_call, inner_kernel, (down_w,), keep=1)
    (own_di,), (cross_di,) = inner(cot_own), inner(cot_cross)
    gate_back = bind(expert_call, gate_back_kernel, (gate_w, up_w), outs=True, keep=2)
    *own_grad, own_g1, own_u1 = gate_back(own1, (own_di,))
    *cross_grad, cross_g1, cross_u1 = gate_back(cross1, (cross_di,))
    got = give_back(own_grad, cross_grad, -1)
    g1, *boxes_g = call(
        bind(gradient_kernel, box, experts, True),
        [rows_bf] + [boxed] * experts,
        cot_next,
        h1_home,
        meta1_next,
        meta0,
        gain,
        *got,
        scratch=[picked],
    )

    def down(g, u, rows):
        return call(bind(down_kernel, box), [like(a) for a in rows], g, u, down_w)

    own_fin, cross_fin = down(own_g1, own_u1, own1), down(cross_g1, cross_u1, cross1)
    fin = give_back(own_fin, cross_fin, 0)

    own_g, cross_g = dispatch(boxes_g)
    back = bind(expert_call, back_kernel, (gate_w, up_w, down_w), outs=True)
    own_grad = back(own_g, (own_g0, own_u0))
    cross_grad = back(cross_g, (cross_g0, cross_u0))
    got = give_back(own_grad, cross_grad, 0)
    (g0,) = call(
        bind(gradient_kernel, box, experts, False),
        [rows_bf],
        g1,
        tokens[0],
        meta0,
        meta0,
        gain,
        *got,
        scratch=[picked],
    )
    (final,) = call(
        bind(final_kernel, box, experts), [rows_bf], h1, meta1, *fin, scratch=[picked]
    )
    return (final[None], g0[None])


def solution(mesh):
    in_specs = (
        P("section", "expert", None),
        P("section", None),
        P("section", "expert", None, None),
        P("section", "expert", None, None),
        P("section", "expert", None, None),
        P("section", None, "expert", None),
        P("section", None, "expert", None),
        P("section", "expert", None),
    )
    out_specs = (P("section", "expert", None), P("section", "expert", None))
    return jax.shard_map(local, mesh=mesh, in_specs=in_specs, out_specs=out_specs, check_vma=False)
```

```python
import functools

import jax
import jax.numpy as jnp
from jax import lax
from jax.experimental import pallas as pl
from jax.experimental.pallas import tpu as pltpu
from jax.sharding import PartitionSpec as P

SPLIT = 4
EPSILON = 1e-06
BF = jnp.bfloat16
F32 = jnp.float32
ROWS = 16
LANES = 128


def dot(left, right, dims=((1,), (0,))):
    return lax.dot_general(left, right, (dims, ((), ())), preferred_element_type=F32)


NT = ((1,), (1,))


def iota(shape, axis):
    return lax.broadcasted_iota(jnp.int32, shape, axis)


class Box:
    def __init__(self, capacity, width):
        self.capacity, self.width = capacity, width
        self.groups, self.extra = capacity // ROWS, capacity % ROWS
        self.cuts = ROWS // self.extra if self.extra else 1
        self.wide = -(-width // (LANES * self.cuts)) * LANES if self.extra else 0
        self.lanes = self.groups * width + self.wide
        self.pieces = -(-width // self.wide) if self.extra else 0

    def group(self, g):
        return pl.ds(g * self.width, self.width)

    def tail(self):
        return pl.ds(self.groups * self.width, self.wide)

    def piece(self, i):
        return i * self.wide, min(self.wide, self.width - i * self.wide)


def shift(value, sections=0, experts=0, flip=0):
    n_sec, n_own = lax.axis_size("section"), lax.axis_size("expert")
    n_exp = n_own // SPLIT
    if sections % n_sec == 0 and experts % n_exp == 0 and flip == 0:
        return value
    pairs = []
    for sec in range(n_sec):
        for own in range(n_own):
            exp, sl = own // SPLIT, own % SPLIT
            to = ((exp + experts) % n_exp) * SPLIT + (sl ^ flip)
            pairs.append((sec * n_own + own, ((sec + sections) % n_sec) * n_own + to))
    return lax.ppermute(value, ("section", "expert"), pairs)


def call(body, outs, *operands, scratch=(), flops=0):
    moved = sum(a.size * a.dtype.itemsize for a in operands)
    moved += sum(o.size * o.dtype.itemsize for o in outs)
    vmem = pl.BlockSpec(memory_space=pltpu.VMEM)
    return pl.pallas_call(
        body,
        out_shape=list(outs),
        in_specs=[vmem] * len(operands),
        out_specs=[vmem] * len(outs),
        scratch_shapes=list(scratch),
        compiler_params=pltpu.CompilerParams(vmem_limit_bytes=32 * 2**20),
        cost_estimate=pl.CostEstimate(flops=flops, bytes_accessed=moved, transcendentals=0),
    )(*operands)


def row_of(column):
    n = column.shape[0]
    eye = iota((n, n), 0) == iota((n, n), 1)
    return jnp.sum(jnp.where(eye, column, 0.0), axis=0, keepdims=True)


def column_of(row):
    n = row.shape[1]
    eye = iota((n, n), 0) == iota((n, n), 1)
    return jnp.sum(jnp.where(eye, row, 0.0), axis=1, keepdims=True)


def slots_of(rel, experts, capacity):
    n = rel.shape[1]
    column = column_of(rel)
    same = jnp.broadcast_to(column, (n, n)) == jnp.broadcast_to(rel, (n, n))
    before = iota((n, n), 1) < iota((n, n), 0)
    rank = jnp.sum(jnp.where(same & before, 1.0, 0.0), axis=1, keepdims=True)
    return column * capacity + rank


def pack_rows(box, slots, values, out_refs):
    n = values.shape[0]
    line = jnp.broadcast_to(row_of(slots).astype(jnp.int32), (ROWS, n))
    r = iota((ROWS, n), 0)
    for j, out in enumerate(out_refs):
        first = j * box.capacity
        for g in range(box.groups):
            sel = jnp.where(line == first + g * ROWS + r, 1.0, 0.0).astype(BF)
            out[:, box.group(g)] = dot(sel, values).astype(BF)
        if box.extra:
            total = jnp.zeros((ROWS, box.wide), F32)
            for i in range(box.pieces):
                at, size = box.piece(i)
                hit = (line == first + box.groups * ROWS + r // box.cuts) & (r % box.cuts == i)
                hit &= r // box.cuts < box.extra
                got = dot(jnp.where(hit, 1.0, 0.0).astype(BF), values[:, at : at + size])
                if size < box.wide:
                    got = jnp.concatenate([got, jnp.zeros((ROWS, box.wide - size), F32)], axis=1)
                total = total + got
            out[:, box.tail()] = total.astype(BF)


def pick_rows(box, slots, boxes, n, picked):
    count = len(boxes)
    if box.groups:
        stack = jnp.concatenate(
            [b[:, g * box.width : (g + 1) * box.width] for b in boxes for g in range(box.groups)],
            axis=0,
        )
        tall = count * box.groups * ROWS
        c = iota((n, tall), 1)
        slot = c // (box.groups * ROWS) * box.capacity + c % (box.groups * ROWS)
        sel = jnp.where(slots.astype(jnp.int32) == slot, 1.0, 0.0).astype(BF)
        picked[...] = dot(sel, stack)
    else:
        picked[...] = jnp.zeros(picked.shape, F32)
    if box.extra:
        tails = jnp.concatenate([b[:, box.groups * box.width :] for b in boxes], axis=0)
        c = iota((n, count * ROWS), 1)
        r = c % ROWS
        slot = c // ROWS * box.capacity + box.groups * ROWS + r // box.cuts
        mine = (slots.astype(jnp.int32) == slot) & (r // box.cuts < box.extra)
        for i in range(box.pieces):
            at, size = box.piece(i)
            sel = jnp.where(mine & (r % box.cuts == i), 1.0, 0.0).astype(BF)
            picked[:, at : at + size] += dot(sel, tails[:, :size])


def heights(box, count):
    extra = -(-count * box.extra // ROWS) * ROWS
    return count * box.groups * ROWS, extra


def unpack(box, refs, stack, tails):
    at = 0
    count = 0
    for ref in refs:
        for p in range(ref.shape[0] // ROWS):
            for g in range(box.groups):
                stack[at : at + ROWS, :] = ref[p * ROWS : (p + 1) * ROWS, box.group(g)]
                at += ROWS
            if box.extra:
                tails[count * ROWS : (count + 1) * ROWS, :] = ref[
                    p * ROWS : (p + 1) * ROWS, box.tail()
                ]
            count += 1
    if box.extra:
        extra = heights(box, count)[1]
        r = iota((extra, count * ROWS), 0)
        c = iota((extra, count * ROWS), 1)
        mine = (r // box.extra == c // ROWS) & (r % box.extra == c % ROWS // box.cuts)
        for i in range(box.pieces):
            start, size = box.piece(i)
            sel = jnp.where(mine & (c % ROWS % box.cuts == i), 1.0, 0.0).astype(BF)
            stack[at : at + extra, start : start + size] = dot(sel, tails[:, :size]).astype(BF)


def repack(box, rows, refs):
    rows = rows.astype(BF)
    at = 0
    count = 0
    for ref in refs:
        for p in range(ref.shape[0] // ROWS):
            for g in range(box.groups):
                ref[p * ROWS : (p + 1) * ROWS, box.group(g)] = rows[at : at + ROWS]
                at += ROWS
            count += 1
    if box.extra:
        extra = heights(box, count)[1]
        r = iota((count * ROWS, extra), 0)
        c = iota((count * ROWS, extra), 1)
        mine = (c // box.extra == r // ROWS) & (c % box.extra == r % ROWS // box.cuts)
        total = jnp.zeros((count * ROWS, box.wide), F32)
        for i in range(box.pieces):
            start, size = box.piece(i)
            sel = jnp.where(mine & (r % ROWS % box.cuts == i), 1.0, 0.0).astype(BF)
            got = dot(sel, rows[at:, start : start + size])
            if size < box.wide:
                pad = jnp.zeros((count * ROWS, box.wide - size), F32)
                got = jnp.concatenate([got, pad], axis=1)
            total = total + got
        total = total.astype(BF)
        count = 0
        for ref in refs:
            tall = ref.shape[0]
            ref[:, box.tail()] = total[count : count + tall]
            count += tall


def inv_rms(wide):
    return lax.rsqrt(jnp.mean(wide * wide, axis=-1, keepdims=True) + EPSILON)


def total_of(refs):
    return sum(ref[...].astype(F32) for ref in refs).astype(BF)


def start_kernel(box, experts, tokens, gain, ids, mix, meta0, meta1, *boxes):
    n = tokens.shape[0]
    lane = iota((n, LANES), 1)
    mine = lax.axis_index("expert") // SPLIT
    for k, meta in enumerate((meta0, meta1)):
        rel = ids[k : k + 1, :] - mine
        rel = jnp.where(rel < 0, rel + experts, rel).astype(F32)
        slots = slots_of(rel, experts, box.capacity)
        mixes = column_of(mix[k : k + 1, :])
        meta[:n] = jnp.where(lane == 0, slots, jnp.where(lane == 1, mixes, 0.0))
    for b in range(box.width // LANES):
        meta1[n + b : n + b + 1] = gain[:, b * LANES : (b + 1) * LANES]
    wide = tokens[...].astype(F32)
    normed = (wide * inv_rms(wide) * gain[...]).astype(BF)
    pack_rows(box, meta0[:n, 0:1], normed, boxes)


def pack_kernel(box, values, meta, *boxes):
    pack_rows(box, meta[: values.shape[0], 0:1], values[...], boxes)


def combine(box, meta, n, own, back, picked):
    sums = [total_of(own)] + [ref[...] for ref in back]
    pick_rows(box, meta[:n, 0:1], sums, n, picked)
    return meta[:n, 1:2] * picked[...]


def split_refs(refs, experts, outs):
    ins = refs[:-outs]
    return ins[: len(ins) + 1 - experts], ins[len(ins) + 1 - experts :], refs[-outs:]


def middle_kernel(box, experts, hidden, meta, meta_out, gain, *refs):
    boxes, picked = refs[-1 - experts : -1], refs[-1]
    own, back, (after,) = split_refs(refs[: -1 - experts], experts, 1)
    n = hidden.shape[0]
    later = (hidden[...].astype(F32) + combine(box, meta, n, own, back, picked)).astype(BF)
    after[...] = later
    wide = later.astype(F32)
    normed = (wide * inv_rms(wide) * gain[...]).astype(BF)
    pack_rows(box, meta_out[:n, 0:1], normed, boxes)


def final_kernel(box, experts, hidden, meta, *refs):
    picked = refs[-1]
    own, back, (out,) = split_refs(refs[:-1], experts, 1)
    n = hidden.shape[0]
    out[...] = (hidden[...].astype(F32) + combine(box, meta, n, own, back, picked)).astype(BF)


def norm_back(hidden, gain, grad):
    wide = hidden.astype(F32)
    inv = inv_rms(wide)
    scaled = grad * gain
    along = jnp.mean(scaled * wide, axis=-1, keepdims=True)
    return inv * scaled - wide * (inv * inv * inv * along)


def gradient_kernel(box, experts, packs, grad, hidden, meta, meta_out, gain, *refs):
    boxes, picked = (refs[-1 - experts : -1] if packs else ()), refs[-1]
    own, back, (out,) = split_refs(refs[: len(refs) - 1 - len(boxes)], experts, 1)
    n = hidden.shape[0]
    d_normed = combine(box, meta, n, own, back, picked)
    if packs:
        row = jnp.concatenate([meta[n + b : n + b + 1] for b in range(box.width // LANES)], axis=1)
    else:
        row = gain[...]
    now = (grad[...].astype(F32) + norm_back(hidden[...], row, d_normed)).astype(BF)
    out[...] = now
    if packs:
        pack_rows(box, meta_out[:n, 0:1], now, boxes)


def halves(refs):
    return refs[: len(refs) // 2], refs[len(refs) // 2 :]


def gate_up(stack, gates, ups):
    rows = stack[...]
    return [(dot(rows, g[...], NT), dot(rows, u[...], NT)) for g, u in zip(gates, ups)]


def down_rows(saved, downs):
    return sum(
        dot((jax.nn.silu(g) * u).astype(BF), down[...]) for (g, u), down in zip(saved, downs)
    )


def part_rows(inners, saved, gates, ups):
    total = 0.0
    for d_inner, (g, u), gate_w, up_w in zip(inners, saved, gates, ups):
        r = jax.nn.sigmoid(g)
        d_gate = (d_inner * u * r * (1.0 + g * (1.0 - r))).astype(BF)
        d_up = (d_inner * g * r).astype(BF)
        total = total + dot(d_gate, gate_w[...]) + dot(d_up, up_w[...])
    return total


def keep(saved, refs):
    for at, (g, u) in enumerate(saved):
        refs[2 * at][...] = g
        refs[2 * at + 1][...] = u


def kept(refs):
    return [(refs[2 * at][...], refs[2 * at + 1][...]) for at in range(len(refs) // 2)]


def forward_kernel(box, held, weights, saved, rows, outs, kept_refs, stack, tails):
    gates, ups, downs = weights
    unpack(box, rows, stack, tails)
    now = gate_up(stack, gates, ups)
    keep(now, kept_refs)
    repack(box, down_rows(now, downs), outs)


def inner_kernel(box, held, weights, saved, rows, outs, kept_refs, stack, tails):
    (downs,) = weights
    unpack(box, rows, stack, tails)
    for ref, down in zip(kept_refs, downs):
        ref[...] = dot(stack[...], down[...], NT)


def gate_back_kernel(box, held, weights, saved, rows, outs, kept_refs, stack, tails):
    gates, ups = weights
    unpack(box, rows, stack, tails)
    now = gate_up(stack, gates, ups)
    keep(now, kept_refs)
    repack(box, part_rows([ref[...] for ref in saved], now, gates, ups), outs)


def back_kernel(box, held, weights, saved, rows, outs, kept_refs, stack, tails):
    gates, ups, downs = weights
    unpack(box, rows, stack, tails)
    inners = [dot(stack[...], down[...], NT) for down in downs]
    repack(box, part_rows(inners, kept(saved), gates, ups), outs)


def down_kernel(box, held, weights, saved, rows, outs, kept_refs, stack, tails):
    (downs,) = weights
    repack(box, down_rows(kept(saved), downs), outs)


def expert_call(kernel, box, weights, rows, saved=(), outs=True, kept_count=0, reads=True):
    held = len(weights[0])
    hid, width = weights[0][0].shape
    count = sum(a.shape[0] for a in rows) // ROWS
    tall = sum(heights(box, count))
    results = [jax.ShapeDtypeStruct(a.shape, a.dtype) for a in rows] if outs else []
    results += [jax.ShapeDtypeStruct((tall, hid), F32)] * kept_count
    inputs = [w for kind in weights for w in kind] + list(saved) + (list(rows) if reads else [])
    n_in, n_w, n_saved = len(inputs), held * len(weights), len(saved)
    n_out = len(rows) if outs else 0

    def body(*refs):
        kinds = [refs[i * held : (i + 1) * held] for i in range(len(weights))]
        results_refs = refs[n_in:-2]
        kernel(
            box,
            held,
            kinds,
            refs[n_w : n_w + n_saved],
            refs[n_w + n_saved : n_in],
            results_refs[:n_out],
            results_refs[n_out:],
            refs[-2],
            refs[-1],
        )

    scratch = [
        pltpu.VMEM((tall, width), BF),
        pltpu.VMEM((count * ROWS, max(box.wide, LANES)), BF),
    ]
    flops = 2 * tall * width * hid * held * (len(weights) + 1)
    return call(body, results, *inputs, scratch=scratch, flops=flops)


def local(tokens, norm_gain, w_gate, w_up, w_down, routes, mix_weights, cotangent):
    experts = lax.axis_size("expert") // SPLIT
    n, width = tokens.shape[1:]
    capacity = n // experts + max(1, n // (16 * experts))
    box = Box(capacity, width)
    gain = norm_gain
    gate_w, up_w, down_w = w_gate[0, 0].T, w_up[0, 0].T, w_down[0, 0]
    boxed = jax.ShapeDtypeStruct((ROWS, box.lanes), BF)
    rows_bf = jax.ShapeDtypeStruct((n, width), BF)
    picked = pltpu.VMEM((n, width), F32)
    bind = functools.partial

    def like(array):
        return jax.ShapeDtypeStruct(array.shape, array.dtype)

    def dispatch(boxes):
        crossed = [shift(boxes[j], experts=j) for j in range(1, experts)]
        cross = crossed[0] if experts == 2 else jnp.concatenate(crossed, axis=0)
        return [boxes[0], shift(boxes[0], flip=2)], [cross, shift(cross, flip=2)]

    def parted(results):
        return results[:2], results[2:]

    def add(*values):
        return sum(v.astype(F32) for v in values).astype(BF)

    def give_back(own, cross, sections):
        total = add(cross[0], shift(cross[1], flip=2))
        back = [
            shift(total[(j - 1) * ROWS : j * ROWS], sections=sections, experts=-j)
            for j in range(1, experts)
        ]
        here, along = own
        here = shift(here, sections=sections)
        return [here, shift(along, sections=sections, flip=2)] + back

    meta_shape = jax.ShapeDtypeStruct((n, LANES), F32)
    meta_long = jax.ShapeDtypeStruct((n + -(-width // LANES // 8) * 8, LANES), F32)
    meta0, meta1, *boxes0 = call(
        bind(start_kernel, box, experts),
        [meta_shape, meta_long] + [boxed] * experts,
        tokens[0],
        gain,
        routes[0, :, :, 0],
        mix_weights[0, :, :, 0],
    )
    own0, cross0 = dispatch(boxes0)
    meta0_prev = shift(meta0, sections=1)
    meta1_next = shift(meta1, sections=-1)
    tokens_prev = shift(tokens[0], sections=1)
    cot_next = shift(cotangent[0], sections=-1)
    cot_boxes = call(bind(pack_kernel, box), [boxed] * experts, cotangent[0], meta1)
    cot_own, cot_cross = dispatch(cot_boxes)

    gates, ups, downs = ([w, shift(w, flip=1)] for w in (gate_w, up_w, down_w))
    every = (gates, ups, downs)

    forward = bind(expert_call, forward_kernel, box, every, kept_count=4)
    own_out, own_kept0 = parted(forward(own0))
    cross_out, cross_kept0 = parted(forward(cross0))
    got = give_back(own_out, cross_out, 1)
    h1, *boxes1 = call(
        bind(middle_kernel, box, experts),
        [rows_bf] + [boxed] * experts,
        tokens_prev,
        meta0_prev,
        meta1,
        gain,
        *got,
        scratch=[picked],
    )
    h1_home = shift(h1, sections=-1)
    own1, cross1 = dispatch(boxes1)

    inner = bind(expert_call, inner_kernel, box, (downs,), outs=False, kept_count=2)
    own_di, cross_di = inner(cot_own), inner(cot_cross)
    gate_back = bind(expert_call, gate_back_kernel, box, (gates, ups), kept_count=4)
    own_grad, own_kept1 = parted(gate_back(own1, own_di))
    cross_grad, cross_kept1 = parted(gate_back(cross1, cross_di))
    got = give_back(own_grad, cross_grad, -1)
    g1, *boxes_g = call(
        bind(gradient_kernel, box, experts, True),
        [rows_bf] + [boxed] * experts,
        cot_next,
        h1_home,
        meta1_next,
        meta0,
        gain,
        *got,
        scratch=[picked],
    )

    down = bind(expert_call, down_kernel, box, (downs,), reads=False)
    own_fin, cross_fin = down(own1, own_kept1), down(cross1, cross_kept1)
    fin = give_back(own_fin, cross_fin, 0)

    own_g, cross_g = dispatch(boxes_g)
    back = bind(expert_call, back_kernel, box, every)
    own_grad = back(own_g, own_kept0)
    cross_grad = back(cross_g, cross_kept0)
    got = give_back(own_grad, cross_grad, 0)
    (g0,) = call(
        bind(gradient_kernel, box, experts, False),
        [rows_bf],
        g1,
        tokens[0],
        meta0,
        meta0,
        gain,
        *got,
        scratch=[picked],
    )
    (final,) = call(
        bind(final_kernel, box, experts), [rows_bf], h1, meta1, *fin, scratch=[picked]
    )
    return (final[None], g0[None])


def solution(mesh):
    in_specs = (
        P("section", "expert", None),
        P("section", None),
        P("section", "expert", None, None),
        P("section", "expert", None, None),
        P("section", "expert", None, None),
        P("section", None, "expert", None),
        P("section", None, "expert", None),
        P("section", "expert", None),
    )
    out_specs = (P("section", "expert", None), P("section", "expert", None))
    return jax.shard_map(local, mesh=mesh, in_specs=in_specs, out_specs=out_specs, check_vma=False)
```

```python
import functools

import jax
import jax.numpy as jnp
from jax import lax
from jax.experimental import pallas as pl
from jax.experimental.pallas import tpu as pltpu
from jax.sharding import PartitionSpec as P

SPLIT = 4
EPSILON = 1e-06
BF = jnp.bfloat16
F32 = jnp.float32
ROWS = 16
LANES = 128


def dot(left, right, dims=((1,), (0,))):
    return lax.dot_general(left, right, (dims, ((), ())), preferred_element_type=F32)


NT = ((1,), (1,))


def iota(shape, axis):
    return lax.broadcasted_iota(jnp.int32, shape, axis)


class Box:
    def __init__(self, capacity, width):
        self.capacity, self.width = capacity, width
        self.groups, self.extra = capacity // ROWS, capacity % ROWS
        self.cuts = ROWS // self.extra if self.extra else 1
        self.wide = -(-width // (LANES * self.cuts)) * LANES if self.extra else 0
        self.lanes = self.groups * width + self.wide
        self.pieces = -(-width // self.wide) if self.extra else 0

    def group(self, g):
        return pl.ds(g * self.width, self.width)

    def tail(self):
        return pl.ds(self.groups * self.width, self.wide)

    def piece(self, i):
        return i * self.wide, min(self.wide, self.width - i * self.wide)


def shift(value, sections=0, experts=0, flip=0):
    n_sec, n_own = lax.axis_size("section"), lax.axis_size("expert")
    n_exp = n_own // SPLIT
    if sections % n_sec == 0 and experts % n_exp == 0 and flip == 0:
        return value
    pairs = []
    for sec in range(n_sec):
        for own in range(n_own):
            exp, sl = own // SPLIT, own % SPLIT
            to = ((exp + experts) % n_exp) * SPLIT + (sl ^ flip)
            pairs.append((sec * n_own + own, ((sec + sections) % n_sec) * n_own + to))
    return lax.ppermute(value, ("section", "expert"), pairs)


def call(body, outs, *operands, scratch=(), flops=0, after=()):
    moved = sum(a.size * a.dtype.itemsize for a in operands)
    moved += sum(o.size * o.dtype.itemsize for o in outs)
    vmem = pl.BlockSpec(memory_space=pltpu.VMEM)
    read = len(operands)

    def reading(*refs):
        body(*refs[:read], *refs[read + len(after) :])

    return pl.pallas_call(
        reading,
        out_shape=list(outs),
        in_specs=[vmem] * read + [pl.BlockSpec(memory_space=pl.ANY)] * len(after),
        out_specs=[vmem] * len(outs),
        scratch_shapes=list(scratch),
        compiler_params=pltpu.CompilerParams(vmem_limit_bytes=40 * 2**20),
        cost_estimate=pl.CostEstimate(flops=flops, bytes_accessed=moved, transcendentals=0),
    )(*operands, *after)


def row_of(column):
    n = column.shape[0]
    eye = iota((n, n), 0) == iota((n, n), 1)
    return jnp.sum(jnp.where(eye, column, 0.0), axis=0, keepdims=True)


def column_of(row):
    n = row.shape[1]
    eye = iota((n, n), 0) == iota((n, n), 1)
    return jnp.sum(jnp.where(eye, row, 0.0), axis=1, keepdims=True)


def slots_of(rel, experts, capacity):
    n = rel.shape[1]
    column = column_of(rel)
    same = jnp.broadcast_to(column, (n, n)) == jnp.broadcast_to(rel, (n, n))
    before = iota((n, n), 1) < iota((n, n), 0)
    rank = jnp.sum(jnp.where(same & before, 1.0, 0.0), axis=1, keepdims=True)
    return column * capacity + rank


def pack_rows(box, slots, values, out_refs):
    n = values.shape[0]
    line = jnp.broadcast_to(row_of(slots).astype(jnp.int32), (ROWS, n))
    r = iota((ROWS, n), 0)
    for j, out in enumerate(out_refs):
        first = j * box.capacity
        for g in range(box.groups):
            sel = jnp.where(line == first + g * ROWS + r, 1.0, 0.0).astype(BF)
            out[:, box.group(g)] = dot(sel, values).astype(BF)
        if box.extra:
            total = jnp.zeros((ROWS, box.wide), F32)
            for i in range(box.pieces):
                at, size = box.piece(i)
                hit = (line == first + box.groups * ROWS + r // box.cuts) & (r % box.cuts == i)
                hit &= r // box.cuts < box.extra
                got = dot(jnp.where(hit, 1.0, 0.0).astype(BF), values[:, at : at + size])
                if size < box.wide:
                    got = jnp.concatenate([got, jnp.zeros((ROWS, box.wide - size), F32)], axis=1)
                total = total + got
            out[:, box.tail()] = total.astype(BF)


def pick_rows(box, slots, boxes, n, picked):
    count = len(boxes)
    if box.groups:
        stack = jnp.concatenate(
            [b[:, g * box.width : (g + 1) * box.width] for b in boxes for g in range(box.groups)],
            axis=0,
        )
        tall = count * box.groups * ROWS
        c = iota((n, tall), 1)
        slot = c // (box.groups * ROWS) * box.capacity + c % (box.groups * ROWS)
        sel = jnp.where(slots.astype(jnp.int32) == slot, 1.0, 0.0).astype(BF)
        picked[...] = dot(sel, stack)
    else:
        picked[...] = jnp.zeros(picked.shape, F32)
    if box.extra:
        tails = jnp.concatenate([b[:, box.groups * box.width :] for b in boxes], axis=0)
        c = iota((n, count * ROWS), 1)
        r = c % ROWS
        slot = c // ROWS * box.capacity + box.groups * ROWS + r // box.cuts
        mine = (slots.astype(jnp.int32) == slot) & (r // box.cuts < box.extra)
        for i in range(box.pieces):
            at, size = box.piece(i)
            sel = jnp.where(mine & (r % box.cuts == i), 1.0, 0.0).astype(BF)
            picked[:, at : at + size] += dot(sel, tails[:, :size])


def heights(box, count):
    extra = -(-count * box.extra // ROWS) * ROWS
    return count * box.groups * ROWS, extra


def unpack(box, refs, stack, tails, at=0):
    count = 0
    for ref in refs:
        for p in range(ref.shape[0] // ROWS):
            for g in range(box.groups):
                stack[at : at + ROWS, :] = ref[p * ROWS : (p + 1) * ROWS, box.group(g)]
                at += ROWS
            if box.extra:
                tails[count * ROWS : (count + 1) * ROWS, :] = ref[
                    p * ROWS : (p + 1) * ROWS, box.tail()
                ]
            count += 1
    if box.extra:
        extra = heights(box, count)[1]
        r = iota((extra, count * ROWS), 0)
        c = iota((extra, count * ROWS), 1)
        mine = (r // box.extra == c // ROWS) & (r % box.extra == c % ROWS // box.cuts)
        for i in range(box.pieces):
            start, size = box.piece(i)
            sel = jnp.where(mine & (c % ROWS % box.cuts == i), 1.0, 0.0).astype(BF)
            stack[at : at + extra, start : start + size] = dot(sel, tails[:, :size]).astype(BF)


def repack(box, rows, refs):
    rows = rows.astype(BF)
    at = 0
    count = 0
    for ref in refs:
        for p in range(ref.shape[0] // ROWS):
            for g in range(box.groups):
                ref[p * ROWS : (p + 1) * ROWS, box.group(g)] = rows[at : at + ROWS]
                at += ROWS
            count += 1
    if box.extra:
        extra = heights(box, count)[1]
        r = iota((count * ROWS, extra), 0)
        c = iota((count * ROWS, extra), 1)
        mine = (c // box.extra == r // ROWS) & (c % box.extra == r % ROWS // box.cuts)
        total = jnp.zeros((count * ROWS, box.wide), F32)
        for i in range(box.pieces):
            start, size = box.piece(i)
            sel = jnp.where(mine & (r % ROWS % box.cuts == i), 1.0, 0.0).astype(BF)
            got = dot(sel, rows[at:, start : start + size])
            if size < box.wide:
                pad = jnp.zeros((count * ROWS, box.wide - size), F32)
                got = jnp.concatenate([got, pad], axis=1)
            total = total + got
        total = total.astype(BF)
        count = 0
        for ref in refs:
            tall = ref.shape[0]
            ref[:, box.tail()] = total[count : count + tall]
            count += tall


def inv_rms(wide):
    return lax.rsqrt(jnp.mean(wide * wide, axis=-1, keepdims=True) + EPSILON)


def total_of(refs):
    return sum(ref[...].astype(F32) for ref in refs).astype(BF)


def start_kernel(box, experts, tokens, gain, ids, mix, meta0, meta1, *boxes):
    n = tokens.shape[0]
    lane = iota((n, LANES), 1)
    mine = lax.axis_index("expert") // SPLIT
    for k, meta in enumerate((meta0, meta1)):
        rel = ids[k : k + 1, :] - mine
        rel = jnp.where(rel < 0, rel + experts, rel).astype(F32)
        slots = slots_of(rel, experts, box.capacity)
        mixes = column_of(mix[k : k + 1, :])
        meta[:n] = jnp.where(lane == 0, slots, jnp.where(lane == 1, mixes, 0.0))
    for b in range(box.width // LANES):
        meta1[n + b : n + b + 1] = gain[:, b * LANES : (b + 1) * LANES]
    wide = tokens[...].astype(F32)
    normed = (wide * inv_rms(wide) * gain[...]).astype(BF)
    pack_rows(box, meta0[:n, 0:1], normed, boxes)


def pack_kernel(box, values, meta, *boxes):
    pack_rows(box, meta[: values.shape[0], 0:1], values[...], boxes)


def combine(box, meta, n, own, back, picked):
    sums = [total_of(own)] + [ref[...] for ref in back]
    pick_rows(box, meta[:n, 0:1], sums, n, picked)
    return meta[:n, 1:2] * picked[...]


def split_refs(refs, experts, outs):
    ins = refs[:-outs]
    return ins[: len(ins) + 1 - experts], ins[len(ins) + 1 - experts :], refs[-outs:]


def middle_kernel(box, experts, hidden, meta, meta_out, gain, *refs):
    boxes, picked = refs[-1 - experts : -1], refs[-1]
    own, back, (after,) = split_refs(refs[: -1 - experts], experts, 1)
    n = hidden.shape[0]
    later = (hidden[...].astype(F32) + combine(box, meta, n, own, back, picked)).astype(BF)
    after[...] = later
    wide = later.astype(F32)
    normed = (wide * inv_rms(wide) * gain[...]).astype(BF)
    pack_rows(box, meta_out[:n, 0:1], normed, boxes)


def final_kernel(box, experts, hidden, meta, *refs):
    picked = refs[-1]
    own, back, (out,) = split_refs(refs[:-1], experts, 1)
    n = hidden.shape[0]
    out[...] = (hidden[...].astype(F32) + combine(box, meta, n, own, back, picked)).astype(BF)


def norm_back(hidden, gain, grad):
    wide = hidden.astype(F32)
    inv = inv_rms(wide)
    scaled = grad * gain
    along = jnp.mean(scaled * wide, axis=-1, keepdims=True)
    return inv * scaled - wide * (inv * inv * inv * along)


def gradient_kernel(box, experts, packs, grad, hidden, meta, meta_out, gain, *refs):
    boxes, picked = (refs[-1 - experts : -1] if packs else ()), refs[-1]
    own, back, (out,) = split_refs(refs[: len(refs) - 1 - len(boxes)], experts, 1)
    n = hidden.shape[0]
    d_normed = combine(box, meta, n, own, back, picked)
    if packs:
        row = jnp.concatenate([meta[n + b : n + b + 1] for b in range(box.width // LANES)], axis=1)
    else:
        row = gain[...]
    now = (grad[...].astype(F32) + norm_back(hidden[...], row, d_normed)).astype(BF)
    out[...] = now
    if packs:
        pack_rows(box, meta_out[:n, 0:1], now, boxes)


def spans(tall):
    return pl.ds(0, 2 * tall), pl.ds(tall, 2 * tall)


def gate_up(rows, pack):
    half = pack.shape[0] // 3
    return dot(rows, pack[: 2 * half], NT)


def parts_of(both):
    half = both.shape[1] // 2
    return both[:, :half], both[:, half:]


def down_rows(both, pack):
    g, u = parts_of(both)
    return dot((jax.nn.silu(g) * u).astype(BF), pack[2 * g.shape[1] :])


def inner_of(rows, pack):
    return dot(rows, pack[2 * (pack.shape[0] // 3) :], NT)


def part_rows(d_inner, both, pack):
    half = d_inner.shape[1]
    g, u = parts_of(both)
    r = jax.nn.sigmoid(g)
    d_gate = (d_inner * u * r * (1.0 + g * (1.0 - r))).astype(BF)
    d_up = (d_inner * g * r).astype(BF)
    return dot(d_gate, pack[:half]) + dot(d_up, pack[half : 2 * half])


def read_rows(box, rows, stack, tails):
    tall = stack.shape[0] // 3
    for at, ref in enumerate(rows):
        unpack(box, [ref], stack, tails, at * tall)
    return [stack[span, :] for span in spans(tall)]


def write_rows(box, top, bottom, outs):
    tall = top.shape[0] // 2
    for ref, value in zip(outs, (top[:tall], top[tall:] + bottom[:tall], bottom[tall:])):
        repack(box, value, [ref])


def forward_kernel(box, packs, saved, rows, outs, kept, stack, tails):
    sides = read_rows(box, rows, stack, tails)
    total = []
    for side, values in enumerate(sides):
        total.append(0.0)
        for at in (2 * side, 2 * side + 1):
            both = gate_up(values, packs[at])
            kept[at][...] = both
            total[side] = total[side] + down_rows(both, packs[at])
    write_rows(box, *total, outs)


def inner_kernel(box, packs, saved, rows, outs, kept, stack, tails):
    for side, values in enumerate(read_rows(box, rows, stack, tails)):
        for at in (2 * side, 2 * side + 1):
            kept[at][...] = inner_of(values, packs[at])


def gate_back_kernel(box, packs, saved, rows, outs, kept, stack, tails):
    sides = read_rows(box, rows, stack, tails)
    total = []
    for side, values in enumerate(sides):
        total.append(0.0)
        for at in (2 * side, 2 * side + 1):
            both = gate_up(values, packs[at])
            kept[at][...] = both
            total[side] = total[side] + part_rows(saved[at][...], both, packs[at])
    write_rows(box, *total, outs)


def back_kernel(box, packs, saved, rows, outs, kept, stack, tails):
    sides = read_rows(box, rows, stack, tails)
    total = []
    for side, values in enumerate(sides):
        total.append(0.0)
        for at in (2 * side, 2 * side + 1):
            d_inner = inner_of(values, packs[at])
            total[side] = total[side] + part_rows(d_inner, saved[at][...], packs[at])
    write_rows(box, *total, outs)


def down_kernel(box, packs, saved, rows, outs, kept, stack, tails):
    total = []
    for side in range(2):
        at = 2 * side
        total.append(sum(down_rows(saved[i][...], packs[i]) for i in (at, at + 1)))
    write_rows(box, *total, outs)


def expert_call(kernel, box, packs, rows, saved=(), outs=True, kept=0, reads=True, after=()):
    width = packs[0].shape[1]
    half = packs[0].shape[0] // 3
    count = rows[0].shape[0] // ROWS
    tall = sum(heights(box, count))
    results = [jax.ShapeDtypeStruct(a.shape, a.dtype) for a in rows] if outs else []
    results += [jax.ShapeDtypeStruct((2 * tall, kept * half), F32)] * (4 if kept else 0)
    inputs = list(packs) + list(saved) + (list(rows) if reads else [])
    n_in, n_p, n_s, n_out = len(inputs), len(packs), len(saved), len(rows) if outs else 0

    def body(*refs):
        results_refs = refs[n_in:-2]
        kernel(
            box,
            refs[:n_p],
            refs[n_p : n_p + n_s],
            refs[n_p + n_s : n_in],
            results_refs[:n_out],
            results_refs[n_out:],
            refs[-2],
            refs[-1],
        )

    scratch = [
        pltpu.VMEM((3 * tall, width), BF),
        pltpu.VMEM((count * ROWS, max(box.wide, LANES)), BF),
    ]
    flops = 2 * 2 * tall * width * half * 4 * 3
    results = call(body, results, *inputs, scratch=scratch, flops=flops, after=after)
    return results[:n_out], results[n_out:]


def local(tokens, norm_gain, w_gate, w_up, w_down, routes, mix_weights, cotangent):
    experts = lax.axis_size("expert") // SPLIT
    n, width = tokens.shape[1:]
    capacity = n // experts + max(1, n // (16 * experts))
    box = Box(capacity, width)
    gain = norm_gain
    gate_w, up_w, down_w = w_gate[0, 0].T, w_up[0, 0].T, w_down[0, 0]
    boxed = jax.ShapeDtypeStruct((ROWS, box.lanes), BF)
    rows_bf = jax.ShapeDtypeStruct((n, width), BF)
    picked = pltpu.VMEM((n, width), F32)
    bind = functools.partial

    def dispatch(boxes):
        crossed = [shift(boxes[j], experts=j) for j in range(1, experts)]
        cross = crossed[0] if experts == 2 else jnp.concatenate(crossed, axis=0)
        own_z, own_x = shift(boxes[0], flip=2), shift(boxes[0], flip=1)
        cross, own_z, own_x = lax.optimization_barrier((cross, own_z, own_x))
        cross_z, cross_x = shift(cross, flip=2), shift(cross, flip=1)
        return [own_z, boxes[0], own_x], [cross_z, cross, cross_x]

    def add(*values):
        return sum(v.astype(F32) for v in values).astype(BF)

    def give_back(own, cross, sections):
        total = add(cross[1], shift(cross[0], flip=2), shift(cross[2], flip=1))
        back = [
            shift(total[(j - 1) * ROWS : j * ROWS], sections=sections, experts=-j)
            for j in range(1, experts)
        ]
        return [
            shift(own[1], sections=sections),
            shift(own[0], sections=sections, flip=2),
            shift(own[2], sections=sections, flip=1),
        ] + back

    half = w_gate.shape[3] // 2
    kinds = (gate_w, up_w, down_w)
    top = jnp.concatenate([w[:half] for w in kinds], axis=0)
    bottom = jnp.concatenate([w[half:] for w in kinds], axis=0)
    packs = [top, shift(top, flip=1), bottom, shift(bottom, flip=2)]

    meta_shape = jax.ShapeDtypeStruct((n, LANES), F32)
    meta_long = jax.ShapeDtypeStruct((n + -(-width // LANES // 8) * 8, LANES), F32)
    meta0, meta1, *boxes0 = call(
        bind(start_kernel, box, experts),
        [meta_shape, meta_long] + [boxed] * experts,
        tokens[0],
        gain,
        routes[0, :, :, 0],
        mix_weights[0, :, :, 0],
    )
    own0, cross0 = dispatch(boxes0)
    meta0_prev = shift(meta0, sections=1)
    meta1_next = shift(meta1, sections=-1)
    tokens_prev = shift(tokens[0], sections=1)
    cot_next = shift(cotangent[0], sections=-1)
    cot_boxes = call(bind(pack_kernel, box), [boxed] * experts, cotangent[0], meta1)
    cot_own, cot_cross = dispatch(cot_boxes)

    early = cot_own + cot_cross + [meta0_prev, meta1_next, tokens_prev, cot_next]
    own_out, own_kept0 = expert_call(forward_kernel, box, packs, own0, kept=2, after=early)
    cross_out, cross_kept0 = expert_call(
        forward_kernel, box, packs, cross0, kept=2, after=own_out[:1]
    )
    got = give_back(own_out, cross_out, 1)
    h1, *boxes1 = call(
        bind(middle_kernel, box, experts),
        [rows_bf] + [boxed] * experts,
        tokens_prev,
        meta0_prev,
        meta1,
        gain,
        *got,
        scratch=[picked],
    )
    h1_home = shift(h1, sections=-1)
    own1, cross1 = dispatch(boxes1)

    inner = bind(expert_call, inner_kernel, box, packs, outs=False, kept=1)
    own_di, cross_di = inner(cot_own)[1], inner(cot_cross)[1]
    gate_back = bind(expert_call, gate_back_kernel, box, packs, kept=2)
    own_grad, own_kept1 = gate_back(own1, own_di)
    cross_grad, cross_kept1 = gate_back(cross1, cross_di, after=own_grad[:1])
    got = give_back(own_grad, cross_grad, -1)
    g1, *boxes_g = call(
        bind(gradient_kernel, box, experts, True),
        [rows_bf] + [boxed] * experts,
        cot_next,
        h1_home,
        meta1_next,
        meta0,
        gain,
        *got,
        scratch=[picked],
    )

    down = bind(expert_call, down_kernel, box, packs, reads=False)
    own_fin, cross_fin = down(own1, own_kept1)[0], down(cross1, cross_kept1)[0]
    fin = give_back(own_fin, cross_fin, 0)

    own_g, cross_g = dispatch(boxes_g)
    back = bind(expert_call, back_kernel, box, packs)
    own_grad = back(own_g, own_kept0)[0]
    cross_grad = back(cross_g, cross_kept0, after=own_grad[:1])[0]
    got = give_back(own_grad, cross_grad, 0)
    (g0,) = call(
        bind(gradient_kernel, box, experts, False),
        [rows_bf],
        g1,
        tokens[0],
        meta0,
        meta0,
        gain,
        *got,
        scratch=[picked],
    )
    (final,) = call(
        bind(final_kernel, box, experts), [rows_bf], h1, meta1, *fin, scratch=[picked]
    )
    return (final[None], g0[None])


def solution(mesh):
    in_specs = (
        P("section", "expert", None),
        P("section", None),
        P("section", "expert", None, None),
        P("section", "expert", None, None),
        P("section", "expert", None, None),
        P("section", None, "expert", None),
        P("section", None, "expert", None),
        P("section", "expert", None),
    )
    out_specs = (P("section", "expert", None), P("section", "expert", None))
    return jax.shard_map(local, mesh=mesh, in_specs=in_specs, out_specs=out_specs, check_vma=False)
```

```python
import functools

import jax
import jax.numpy as jnp
from jax import lax
from jax.experimental import pallas as pl
from jax.experimental.pallas import tpu as pltpu
from jax.sharding import PartitionSpec as P

SPLIT = 4
EPSILON = 1e-06
BF = jnp.bfloat16
F32 = jnp.float32
ROWS = 16
LANES = 128


def dot(left, right, dims=((1,), (0,))):
    return lax.dot_general(left, right, (dims, ((), ())), preferred_element_type=F32)


NT = ((1,), (1,))


def iota(shape, axis):
    return lax.broadcasted_iota(jnp.int32, shape, axis)


class Box:
    def __init__(self, capacity, width):
        self.capacity, self.width = capacity, width
        self.groups, self.extra = capacity // ROWS, capacity % ROWS
        self.cuts = ROWS // self.extra if self.extra else 1
        self.wide = -(-width // (LANES * self.cuts)) * LANES if self.extra else 0
        self.lanes = self.groups * width + self.wide
        self.pieces = -(-width // self.wide) if self.extra else 0

    def group(self, g):
        return pl.ds(g * self.width, self.width)

    def tail(self):
        return pl.ds(self.groups * self.width, self.wide)

    def piece(self, i):
        return i * self.wide, min(self.wide, self.width - i * self.wide)


def shift(value, sections=0, experts=0, flip=0):
    n_sec, n_own = lax.axis_size("section"), lax.axis_size("expert")
    n_exp = n_own // SPLIT
    if sections % n_sec == 0 and experts % n_exp == 0 and flip == 0:
        return value
    pairs = []
    for sec in range(n_sec):
        for own in range(n_own):
            exp, sl = own // SPLIT, own % SPLIT
            to = ((exp + experts) % n_exp) * SPLIT + (sl ^ flip)
            pairs.append((sec * n_own + own, ((sec + sections) % n_sec) * n_own + to))
    return lax.ppermute(value, ("section", "expert"), pairs)


def call(body, outs, *operands, scratch=(), flops=0, after=()):
    moved = sum(a.size * a.dtype.itemsize for a in operands)
    moved += sum(o.size * o.dtype.itemsize for o in outs)
    vmem = pl.BlockSpec(memory_space=pltpu.VMEM)
    read = len(operands)

    def reading(*refs):
        body(*refs[:read], *refs[read + len(after) :])

    return pl.pallas_call(
        reading,
        out_shape=list(outs),
        in_specs=[vmem] * read + [pl.BlockSpec(memory_space=pl.ANY)] * len(after),
        out_specs=[vmem] * len(outs),
        scratch_shapes=list(scratch),
        compiler_params=pltpu.CompilerParams(vmem_limit_bytes=40 * 2**20),
        cost_estimate=pl.CostEstimate(flops=flops, bytes_accessed=moved, transcendentals=0),
    )(*operands, *after)


def row_of(column):
    n = column.shape[0]
    eye = iota((n, n), 0) == iota((n, n), 1)
    return jnp.sum(jnp.where(eye, column, 0.0), axis=0, keepdims=True)


def column_of(row):
    n = row.shape[1]
    eye = iota((n, n), 0) == iota((n, n), 1)
    return jnp.sum(jnp.where(eye, row, 0.0), axis=1, keepdims=True)


def slots_of(rel, experts, capacity):
    n = rel.shape[1]
    column = column_of(rel)
    same = jnp.broadcast_to(column, (n, n)) == jnp.broadcast_to(rel, (n, n))
    before = iota((n, n), 1) < iota((n, n), 0)
    rank = jnp.sum(jnp.where(same & before, 1.0, 0.0), axis=1, keepdims=True)
    return column * capacity + rank


def pack_rows(box, slots, values, out_refs):
    n = values.shape[0]
    line = jnp.broadcast_to(row_of(slots).astype(jnp.int32), (ROWS, n))
    r = iota((ROWS, n), 0)
    for j, out in enumerate(out_refs):
        first = j * box.capacity
        for g in range(box.groups):
            sel = jnp.where(line == first + g * ROWS + r, 1.0, 0.0).astype(BF)
            out[:, box.group(g)] = dot(sel, values).astype(BF)
        if box.extra:
            total = jnp.zeros((ROWS, box.wide), F32)
            for i in range(box.pieces):
                at, size = box.piece(i)
                hit = (line == first + box.groups * ROWS + r // box.cuts) & (r % box.cuts == i)
                hit &= r // box.cuts < box.extra
                got = dot(jnp.where(hit, 1.0, 0.0).astype(BF), values[:, at : at + size])
                if size < box.wide:
                    got = jnp.concatenate([got, jnp.zeros((ROWS, box.wide - size), F32)], axis=1)
                total = total + got
            out[:, box.tail()] = total.astype(BF)


def pick_rows(box, slots, boxes, n, picked):
    count = len(boxes)
    if box.groups:
        stack = jnp.concatenate(
            [b[:, g * box.width : (g + 1) * box.width] for b in boxes for g in range(box.groups)],
            axis=0,
        )
        tall = count * box.groups * ROWS
        c = iota((n, tall), 1)
        slot = c // (box.groups * ROWS) * box.capacity + c % (box.groups * ROWS)
        sel = jnp.where(slots.astype(jnp.int32) == slot, 1.0, 0.0).astype(BF)
        picked[...] = dot(sel, stack)
    else:
        picked[...] = jnp.zeros(picked.shape, F32)
    if box.extra:
        tails = jnp.concatenate([b[:, box.groups * box.width :] for b in boxes], axis=0)
        c = iota((n, count * ROWS), 1)
        r = c % ROWS
        slot = c // ROWS * box.capacity + box.groups * ROWS + r // box.cuts
        mine = (slots.astype(jnp.int32) == slot) & (r // box.cuts < box.extra)
        for i in range(box.pieces):
            at, size = box.piece(i)
            sel = jnp.where(mine & (r % box.cuts == i), 1.0, 0.0).astype(BF)
            picked[:, at : at + size] += dot(sel, tails[:, :size])


def heights(box, count):
    extra = -(-count * box.extra // ROWS) * ROWS
    return count * box.groups * ROWS, extra


def unpack(box, refs, stack, tails, at=0):
    count = 0
    for ref in refs:
        for p in range(ref.shape[0] // ROWS):
            for g in range(box.groups):
                stack[at : at + ROWS, :] = ref[p * ROWS : (p + 1) * ROWS, box.group(g)]
                at += ROWS
            if box.extra:
                tails[count * ROWS : (count + 1) * ROWS, :] = ref[
                    p * ROWS : (p + 1) * ROWS, box.tail()
                ]
            count += 1
    if box.extra:
        extra = heights(box, count)[1]
        r = iota((extra, count * ROWS), 0)
        c = iota((extra, count * ROWS), 1)
        mine = (r // box.extra == c // ROWS) & (r % box.extra == c % ROWS // box.cuts)
        for i in range(box.pieces):
            start, size = box.piece(i)
            sel = jnp.where(mine & (c % ROWS % box.cuts == i), 1.0, 0.0).astype(BF)
            stack[at : at + extra, start : start + size] = dot(sel, tails[:, :size]).astype(BF)


def repack(box, rows, refs):
    rows = rows.astype(BF)
    at = 0
    count = 0
    for ref in refs:
        for p in range(ref.shape[0] // ROWS):
            for g in range(box.groups):
                ref[p * ROWS : (p + 1) * ROWS, box.group(g)] = rows[at : at + ROWS]
                at += ROWS
            count += 1
    if box.extra:
        extra = heights(box, count)[1]
        r = iota((count * ROWS, extra), 0)
        c = iota((count * ROWS, extra), 1)
        mine = (c // box.extra == r // ROWS) & (c % box.extra == r % ROWS // box.cuts)
        total = jnp.zeros((count * ROWS, box.wide), F32)
        for i in range(box.pieces):
            start, size = box.piece(i)
            sel = jnp.where(mine & (r % ROWS % box.cuts == i), 1.0, 0.0).astype(BF)
            got = dot(sel, rows[at:, start : start + size])
            if size < box.wide:
                pad = jnp.zeros((count * ROWS, box.wide - size), F32)
                got = jnp.concatenate([got, pad], axis=1)
            total = total + got
        total = total.astype(BF)
        count = 0
        for ref in refs:
            tall = ref.shape[0]
            ref[:, box.tail()] = total[count : count + tall]
            count += tall


def inv_rms(wide):
    return lax.rsqrt(jnp.mean(wide * wide, axis=-1, keepdims=True) + EPSILON)


def total_of(refs):
    return sum(ref[...].astype(F32) for ref in refs).astype(BF)


def start_kernel(box, experts, tokens, gain, ids, mix, meta0, meta1, *boxes):
    n = tokens.shape[0]
    lane = iota((n, LANES), 1)
    mine = lax.axis_index("expert") // SPLIT
    for k, meta in enumerate((meta0, meta1)):
        rel = ids[k : k + 1, :] - mine
        rel = jnp.where(rel < 0, rel + experts, rel).astype(F32)
        slots = slots_of(rel, experts, box.capacity)
        mixes = column_of(mix[k : k + 1, :])
        meta[:n] = jnp.where(lane == 0, slots, jnp.where(lane == 1, mixes, 0.0))
    for b in range(box.width // LANES):
        meta1[n + b : n + b + 1] = gain[:, b * LANES : (b + 1) * LANES]
    wide = tokens[...].astype(F32)
    normed = (wide * inv_rms(wide) * gain[...]).astype(BF)
    pack_rows(box, meta0[:n, 0:1], normed, boxes)


def pack_kernel(box, values, meta, *boxes):
    pack_rows(box, meta[: values.shape[0], 0:1], values[...], boxes)


def combine(box, meta, n, own, back, picked):
    sums = [total_of(own)] + [ref[...] for ref in back]
    pick_rows(box, meta[:n, 0:1], sums, n, picked)
    return meta[:n, 1:2] * picked[...]


def split_refs(refs, experts, outs):
    ins = refs[:-outs]
    return ins[: len(ins) + 1 - experts], ins[len(ins) + 1 - experts :], refs[-outs:]


def middle_kernel(box, experts, hidden, meta, meta_out, gain, *refs):
    boxes, picked = refs[-1 - experts : -1], refs[-1]
    own, back, (after,) = split_refs(refs[: -1 - experts], experts, 1)
    n = hidden.shape[0]
    later = (hidden[...].astype(F32) + combine(box, meta, n, own, back, picked)).astype(BF)
    after[...] = later
    wide = later.astype(F32)
    normed = (wide * inv_rms(wide) * gain[...]).astype(BF)
    pack_rows(box, meta_out[:n, 0:1], normed, boxes)


def final_kernel(box, experts, hidden, meta, *refs):
    picked = refs[-1]
    own, back, (out,) = split_refs(refs[:-1], experts, 1)
    n = hidden.shape[0]
    out[...] = (hidden[...].astype(F32) + combine(box, meta, n, own, back, picked)).astype(BF)


def norm_back(hidden, gain, grad):
    wide = hidden.astype(F32)
    inv = inv_rms(wide)
    scaled = grad * gain
    along = jnp.mean(scaled * wide, axis=-1, keepdims=True)
    return inv * scaled - wide * (inv * inv * inv * along)


def gradient_kernel(box, experts, packs, grad, hidden, meta, meta_out, gain, *refs):
    boxes, picked = (refs[-1 - experts : -1] if packs else ()), refs[-1]
    own, back, (out,) = split_refs(refs[: len(refs) - 1 - len(boxes)], experts, 1)
    n = hidden.shape[0]
    d_normed = combine(box, meta, n, own, back, picked)
    if packs:
        row = jnp.concatenate([meta[n + b : n + b + 1] for b in range(box.width // LANES)], axis=1)
    else:
        row = gain[...]
    now = (grad[...].astype(F32) + norm_back(hidden[...], row, d_normed)).astype(BF)
    out[...] = now
    if packs:
        pack_rows(box, meta_out[:n, 0:1], now, boxes)


def spans(tall):
    return pl.ds(0, 2 * tall), pl.ds(tall, 2 * tall)


def gate_up(rows, pack):
    return dot(rows, pack[0][...], NT)


def parts_of(both):
    units = both.shape[1] // 2
    return both[:, :units], both[:, units:]


def down_rows(both, pack):
    g, u = parts_of(both)
    return dot((jax.nn.silu(g) * u).astype(BF), pack[1][...])


def inner_of(rows, pack):
    return dot(rows, pack[1][...], NT)


def part_rows(d_inner, both, pack):
    g, u = parts_of(both)
    r = jax.nn.sigmoid(g)
    d_gate = d_inner * u * r * (1.0 + g * (1.0 - r))
    d_up = d_inner * g * r
    return dot(jnp.concatenate([d_gate, d_up], axis=1).astype(BF), pack[0][...])


def read_rows(box, rows, stack, tails):
    tall = stack.shape[0] // 3
    for at, ref in enumerate(rows):
        unpack(box, [ref], stack, tails, at * tall)
    return [stack[span, :] for span in spans(tall)]


def write_rows(box, top, bottom, outs):
    tall = top.shape[0] // 2
    for ref, value in zip(outs, (top[:tall], top[tall:] + bottom[:tall], bottom[tall:])):
        repack(box, value, [ref])


def forward_kernel(box, packs, saved, rows, outs, kept, stack, tails):
    sides = read_rows(box, rows, stack, tails)
    total = []
    for side, values in enumerate(sides):
        total.append(0.0)
        for at in (2 * side, 2 * side + 1):
            both = gate_up(values, packs[at])
            kept[at][...] = both
            total[side] = total[side] + down_rows(both, packs[at])
    write_rows(box, *total, outs)


def inner_kernel(box, packs, saved, rows, outs, kept, stack, tails):
    for side, values in enumerate(read_rows(box, rows, stack, tails)):
        for at in (2 * side, 2 * side + 1):
            kept[at][...] = inner_of(values, packs[at])


def gate_back_kernel(box, packs, saved, rows, outs, kept, stack, tails):
    sides = read_rows(box, rows, stack, tails)
    total = []
    for side, values in enumerate(sides):
        total.append(0.0)
        for at in (2 * side, 2 * side + 1):
            both = gate_up(values, packs[at])
            kept[at][...] = both
            total[side] = total[side] + part_rows(saved[at][...], both, packs[at])
    write_rows(box, *total, outs)


def back_kernel(box, packs, saved, rows, outs, kept, stack, tails):
    sides = read_rows(box, rows, stack, tails)
    total = []
    for side, values in enumerate(sides):
        total.append(0.0)
        for at in (2 * side, 2 * side + 1):
            d_inner = inner_of(values, packs[at])
            total[side] = total[side] + part_rows(d_inner, saved[at][...], packs[at])
    write_rows(box, *total, outs)


def down_kernel(box, packs, saved, rows, outs, kept, stack, tails):
    total = []
    for side in range(2):
        at = 2 * side
        total.append(sum(down_rows(saved[i][...], packs[i]) for i in (at, at + 1)))
    write_rows(box, *total, outs)


def expert_call(kernel, box, packs, rows, saved=(), outs=True, kept=0, reads=True, after=()):
    width = packs[0][0].shape[1]
    count = rows[0].shape[0] // ROWS
    tall = sum(heights(box, count))
    results = [jax.ShapeDtypeStruct(a.shape, a.dtype) for a in rows] if outs else []
    if kept:
        results += [jax.ShapeDtypeStruct((2 * tall, kept * dn.shape[0]), F32) for _, dn in packs]
    inputs = [w for pack in packs for w in pack] + list(saved) + (list(rows) if reads else [])
    n_in, n_p, n_s, n_out = len(inputs), 2 * len(packs), len(saved), len(rows) if outs else 0

    def body(*refs):
        results_refs = refs[n_in:-2]
        kernel(
            box,
            [refs[at : at + 2] for at in range(0, n_p, 2)],
            refs[n_p : n_p + n_s],
            refs[n_p + n_s : n_in],
            results_refs[:n_out],
            results_refs[n_out:],
            refs[-2],
            refs[-1],
        )

    scratch = [
        pltpu.VMEM((3 * tall, width), BF),
        pltpu.VMEM((count * ROWS, max(box.wide, LANES)), BF),
    ]
    flops = sum(2 * 2 * tall * width * 3 * dn.shape[0] for _, dn in packs)
    results = call(body, results, *inputs, scratch=scratch, flops=flops, after=after)
    return results[:n_out], results[n_out:]


def local(tokens, norm_gain, w_gate, w_up, w_down, routes, mix_weights, cotangent):
    experts = lax.axis_size("expert") // SPLIT
    n, width = tokens.shape[1:]
    capacity = n // experts + max(1, n // (16 * experts))
    box = Box(capacity, width)
    gain = norm_gain
    gate_w, up_w, down_w = w_gate[0, 0].T, w_up[0, 0].T, w_down[0, 0]
    boxed = jax.ShapeDtypeStruct((ROWS, box.lanes), BF)
    rows_bf = jax.ShapeDtypeStruct((n, width), BF)
    picked = pltpu.VMEM((n, width), F32)
    bind = functools.partial

    def first_hop(boxes):
        crossed = [shift(boxes[j], experts=j) for j in range(1, experts)]
        cross = crossed[0] if experts == 2 else jnp.concatenate(crossed, axis=0)
        return shift(boxes[0], flip=2), shift(boxes[0], flip=1), cross

    def second_hop(boxes, own_z, own_x, cross):
        return [own_z, boxes[0], own_x], [shift(cross, flip=2), cross, shift(cross, flip=1)]

    def dispatch(boxes):
        return second_hop(boxes, *lax.optimization_barrier(first_hop(boxes)))

    def add(*values):
        return sum(v.astype(F32) for v in values).astype(BF)

    def give_back(own, cross, sections, wait=None):
        total = add(cross[1], shift(cross[0], flip=2), shift(cross[2], flip=1))
        if wait is not None:
            (total, own), wait = lax.optimization_barrier(((total, own), wait))
        back = [
            shift(total[(j - 1) * ROWS : j * ROWS], sections=sections, experts=-j)
            for j in range(1, experts)
        ]
        got = [
            shift(own[1], sections=sections),
            shift(own[0], sections=sections, flip=2),
            shift(own[2], sections=sections, flip=1),
        ] + back
        return got if wait is None else (got, wait)

    meta_shape = jax.ShapeDtypeStruct((n, LANES), F32)
    meta_long = jax.ShapeDtypeStruct((n + -(-width // LANES // 8) * 8, LANES), F32)
    meta0, meta1, *boxes0 = call(
        bind(start_kernel, box, experts),
        [meta_shape, meta_long] + [boxed] * experts,
        tokens[0],
        gain,
        routes[0, :, :, 0],
        mix_weights[0, :, :, 0],
    )
    cot_boxes = call(bind(pack_kernel, box), [boxed] * experts, cotangent[0], meta1)
    units = w_gate.shape[3]
    cut = -(-units * 7 // 12 // ROWS) * ROWS
    top_dn, bottom_dn = down_w[:cut], down_w[cut:]
    top_gu = jnp.concatenate([gate_w[:cut], up_w[:cut]], axis=0)
    bottom_gu = jnp.concatenate([gate_w[cut:], up_w[cut:]], axis=0)
    first, later = lax.optimization_barrier(
        (
            (
                first_hop(boxes0),
                first_hop(cot_boxes),
                shift(top_dn, flip=1),
                shift(bottom_dn, flip=2),
            ),
            (top_gu, bottom_gu, meta0, meta1, tokens[0], cotangent[0]),
        )
    )
    hop0, hop_cot, x_dn, z_dn = first
    top_gu, bottom_gu, meta0, meta1, tokens0, cot = later
    own0, cross0 = second_hop(boxes0, *hop0)
    cot_own, cot_cross = second_hop(cot_boxes, *hop_cot)
    packs = [
        (top_gu, top_dn),
        (shift(top_gu, flip=1), x_dn),
        (bottom_gu, bottom_dn),
        (shift(bottom_gu, flip=2), z_dn),
    ]
    meta0_prev = shift(meta0, sections=1)
    meta1_next = shift(meta1, sections=-1)
    tokens_prev = shift(tokens0, sections=1)
    cot_next = shift(cot, sections=-1)

    early = cot_own + cot_cross + [meta0_prev, meta1_next, tokens_prev, cot_next]
    own_out, own_kept0 = expert_call(forward_kernel, box, packs, own0, kept=2, after=early)
    cross_out, cross_kept0 = expert_call(
        forward_kernel, box, packs, cross0, kept=2, after=own_out[:1]
    )
    got = give_back(own_out, cross_out, 1)
    inner = bind(expert_call, inner_kernel, box, packs, outs=False, kept=1)
    own_di, cross_di = inner(cot_own)[1], inner(cot_cross)[1]
    h1, *boxes1 = call(
        bind(middle_kernel, box, experts),
        [rows_bf] + [boxed] * experts,
        tokens_prev,
        meta0_prev,
        meta1,
        gain,
        *got,
        scratch=[picked],
        after=[own_di[0], cross_di[0]],
    )
    h1_home = shift(h1, sections=-1)
    own1, cross1 = dispatch(boxes1)

    gate_back = bind(expert_call, gate_back_kernel, box, packs, kept=2)
    own_grad, own_kept1 = gate_back(own1, own_di)
    cross_grad, cross_kept1 = gate_back(cross1, cross_di, after=own_grad[:1])
    got = give_back(own_grad, cross_grad, -1)
    g1, *boxes_g = call(
        bind(gradient_kernel, box, experts, True),
        [rows_bf] + [boxed] * experts,
        cot_next,
        h1_home,
        meta1_next,
        meta0,
        gain,
        *got,
        scratch=[picked],
    )

    down = bind(expert_call, down_kernel, box, packs, reads=False)
    own_fin, cross_fin = down(own1, own_kept1)[0], down(cross1, cross_kept1)[0]
    hop_g = first_hop(boxes_g)
    fin, hop_g = give_back(own_fin, cross_fin, 0, wait=hop_g)
    own_g, cross_g = second_hop(boxes_g, *hop_g)
    back = bind(expert_call, back_kernel, box, packs)
    own_grad = back(own_g, own_kept0)[0]
    cross_grad = back(cross_g, cross_kept0, after=own_grad[:1])[0]
    got = give_back(own_grad, cross_grad, 0)
    (g0,) = call(
        bind(gradient_kernel, box, experts, False),
        [rows_bf],
        g1,
        tokens[0],
        meta0,
        meta0,
        gain,
        *got,
        scratch=[picked],
    )
    (final,) = call(
        bind(final_kernel, box, experts), [rows_bf], h1, meta1, *fin, scratch=[picked]
    )
    return (final[None], g0[None])


def solution(mesh):
    in_specs = (
        P("section", "expert", None),
        P("section", None),
        P("section", "expert", None, None),
        P("section", "expert", None, None),
        P("section", "expert", None, None),
        P("section", None, "expert", None),
        P("section", None, "expert", None),
        P("section", "expert", None),
    )
    out_specs = (P("section", "expert", None), P("section", "expert", None))
    return jax.shard_map(local, mesh=mesh, in_specs=in_specs, out_specs=out_specs, check_vma=False)
```

```python
import functools

import jax
import jax.numpy as jnp
from jax import lax
from jax.experimental import pallas as pl
from jax.experimental.pallas import tpu as pltpu
from jax.sharding import PartitionSpec as P

SPLIT = 4
EPSILON = 1e-06
BF = jnp.bfloat16
F32 = jnp.float32
ROWS = 16
LANES = 128


def dot(left, right, dims=((1,), (0,))):
    return lax.dot_general(left, right, (dims, ((), ())), preferred_element_type=F32)


NT = ((1,), (1,))


def iota(shape, axis):
    return lax.broadcasted_iota(jnp.int32, shape, axis)


class Box:
    def __init__(self, capacity, width):
        self.capacity, self.width = capacity, width
        self.groups, self.extra = capacity // ROWS, capacity % ROWS
        self.cuts = ROWS // self.extra if self.extra else 1
        self.wide = -(-width // (LANES * self.cuts)) * LANES if self.extra else 0
        self.lanes = self.groups * width + self.wide
        self.pieces = -(-width // self.wide) if self.extra else 0

    def group(self, g):
        return pl.ds(g * self.width, self.width)

    def tail(self):
        return pl.ds(self.groups * self.width, self.wide)

    def piece(self, i):
        return i * self.wide, min(self.wide, self.width - i * self.wide)


def shift(value, sections=0, experts=0, flip=0):
    n_sec, n_own = lax.axis_size("section"), lax.axis_size("expert")
    n_exp = n_own // SPLIT
    if sections % n_sec == 0 and experts % n_exp == 0 and flip == 0:
        return value
    pairs = []
    for sec in range(n_sec):
        for own in range(n_own):
            exp, sl = own // SPLIT, own % SPLIT
            to = ((exp + experts) % n_exp) * SPLIT + (sl ^ flip)
            pairs.append((sec * n_own + own, ((sec + sections) % n_sec) * n_own + to))
    return lax.ppermute(value, ("section", "expert"), pairs)


def call(body, outs, *operands, scratch=(), flops=0, after=()):
    moved = sum(a.size * a.dtype.itemsize for a in operands)
    moved += sum(o.size * o.dtype.itemsize for o in outs)
    vmem = pl.BlockSpec(memory_space=pltpu.VMEM)
    read = len(operands)

    def reading(*refs):
        body(*refs[:read], *refs[read + len(after) :])

    return pl.pallas_call(
        reading,
        out_shape=list(outs),
        in_specs=[vmem] * read + [pl.BlockSpec(memory_space=pl.ANY)] * len(after),
        out_specs=[vmem] * len(outs),
        scratch_shapes=list(scratch),
        compiler_params=pltpu.CompilerParams(vmem_limit_bytes=40 * 2**20),
        cost_estimate=pl.CostEstimate(flops=flops, bytes_accessed=moved, transcendentals=0),
    )(*operands, *after)


def row_of(column):
    n = column.shape[0]
    eye = iota((n, n), 0) == iota((n, n), 1)
    return jnp.sum(jnp.where(eye, column, 0.0), axis=0, keepdims=True)


def column_of(row):
    n = row.shape[1]
    eye = iota((n, n), 0) == iota((n, n), 1)
    return jnp.sum(jnp.where(eye, row, 0.0), axis=1, keepdims=True)


def slots_of(rel, experts, capacity):
    n = rel.shape[1]
    column = column_of(rel)
    same = jnp.broadcast_to(column, (n, n)) == jnp.broadcast_to(rel, (n, n))
    before = iota((n, n), 1) < iota((n, n), 0)
    rank = jnp.sum(jnp.where(same & before, 1.0, 0.0), axis=1, keepdims=True)
    return column * capacity + rank


def pack_rows(box, slots, values, out_refs):
    n = values.shape[0]
    line = jnp.broadcast_to(row_of(slots).astype(jnp.int32), (ROWS, n))
    r = iota((ROWS, n), 0)
    for j, out in enumerate(out_refs):
        first = j * box.capacity
        for g in range(box.groups):
            sel = jnp.where(line == first + g * ROWS + r, 1.0, 0.0).astype(BF)
            out[:, box.group(g)] = dot(sel, values).astype(BF)
        if box.extra:
            total = jnp.zeros((ROWS, box.wide), F32)
            for i in range(box.pieces):
                at, size = box.piece(i)
                hit = (line == first + box.groups * ROWS + r // box.cuts) & (r % box.cuts == i)
                hit &= r // box.cuts < box.extra
                got = dot(jnp.where(hit, 1.0, 0.0).astype(BF), values[:, at : at + size])
                if size < box.wide:
                    got = jnp.concatenate([got, jnp.zeros((ROWS, box.wide - size), F32)], axis=1)
                total = total + got
            out[:, box.tail()] = total.astype(BF)


def pick_rows(box, slots, boxes, n, picked):
    count = len(boxes)
    if box.groups:
        stack = jnp.concatenate(
            [b[:, g * box.width : (g + 1) * box.width] for b in boxes for g in range(box.groups)],
            axis=0,
        )
        tall = count * box.groups * ROWS
        c = iota((n, tall), 1)
        slot = c // (box.groups * ROWS) * box.capacity + c % (box.groups * ROWS)
        sel = jnp.where(slots.astype(jnp.int32) == slot, 1.0, 0.0).astype(BF)
        picked[...] = dot(sel, stack)
    else:
        picked[...] = jnp.zeros(picked.shape, F32)
    if box.extra:
        tails = jnp.concatenate([b[:, box.groups * box.width :] for b in boxes], axis=0)
        c = iota((n, count * ROWS), 1)
        r = c % ROWS
        slot = c // ROWS * box.capacity + box.groups * ROWS + r // box.cuts
        mine = (slots.astype(jnp.int32) == slot) & (r // box.cuts < box.extra)
        for i in range(box.pieces):
            at, size = box.piece(i)
            sel = jnp.where(mine & (r % box.cuts == i), 1.0, 0.0).astype(BF)
            picked[:, at : at + size] += dot(sel, tails[:, :size])


def heights(box, count):
    extra = -(-count * box.extra // ROWS) * ROWS
    return count * box.groups * ROWS, extra


def unpack(box, refs, stack, tails, at=0, part=(0, 1)):
    count = 0
    for ref in refs:
        for p in range(part[0], ref.shape[0] // ROWS, part[1]):
            for g in range(box.groups):
                stack[at : at + ROWS, :] = ref[p * ROWS : (p + 1) * ROWS, box.group(g)]
                at += ROWS
            if box.extra:
                tails[count * ROWS : (count + 1) * ROWS, :] = ref[
                    p * ROWS : (p + 1) * ROWS, box.tail()
                ]
            count += 1
    if box.extra:
        extra = heights(box, count)[1]
        r = iota((extra, count * ROWS), 0)
        c = iota((extra, count * ROWS), 1)
        mine = (r // box.extra == c // ROWS) & (r % box.extra == c % ROWS // box.cuts)
        for i in range(box.pieces):
            start, size = box.piece(i)
            sel = jnp.where(mine & (c % ROWS % box.cuts == i), 1.0, 0.0).astype(BF)
            stack[at : at + extra, start : start + size] = dot(sel, tails[:, :size]).astype(BF)


def repack(box, rows, refs):
    rows = rows.astype(BF)
    at = 0
    count = 0
    for ref in refs:
        for p in range(ref.shape[0] // ROWS):
            for g in range(box.groups):
                ref[p * ROWS : (p + 1) * ROWS, box.group(g)] = rows[at : at + ROWS]
                at += ROWS
            count += 1
    if box.extra:
        extra = heights(box, count)[1]
        r = iota((count * ROWS, extra), 0)
        c = iota((count * ROWS, extra), 1)
        mine = (c // box.extra == r // ROWS) & (c % box.extra == r % ROWS // box.cuts)
        total = jnp.zeros((count * ROWS, box.wide), F32)
        for i in range(box.pieces):
            start, size = box.piece(i)
            sel = jnp.where(mine & (r % ROWS % box.cuts == i), 1.0, 0.0).astype(BF)
            got = dot(sel, rows[at:, start : start + size])
            if size < box.wide:
                pad = jnp.zeros((count * ROWS, box.wide - size), F32)
                got = jnp.concatenate([got, pad], axis=1)
            total = total + got
        total = total.astype(BF)
        count = 0
        for ref in refs:
            tall = ref.shape[0]
            ref[:, box.tail()] = total[count : count + tall]
            count += tall


def inv_rms(wide):
    return lax.rsqrt(jnp.mean(wide * wide, axis=-1, keepdims=True) + EPSILON)


def total_of(refs):
    return sum(ref[...].astype(F32) for ref in refs).astype(BF)


def start_kernel(box, experts, tokens, cot, gain, ids, mix, meta0, meta1, *boxes):
    n = tokens.shape[0]
    lane = iota((n, LANES), 1)
    mine = lax.axis_index("expert") // SPLIT
    for k, meta in enumerate((meta0, meta1)):
        rel = ids[k : k + 1, :] - mine
        rel = jnp.where(rel < 0, rel + experts, rel).astype(F32)
        slots = slots_of(rel, experts, box.capacity)
        mixes = column_of(mix[k : k + 1, :])
        meta[:n] = jnp.where(lane == 0, slots, jnp.where(lane == 1, mixes, 0.0))
    for b in range(box.width // LANES):
        meta1[n + b : n + b + 1] = gain[:, b * LANES : (b + 1) * LANES]
    wide = tokens[...].astype(F32)
    normed = (wide * inv_rms(wide) * gain[...]).astype(BF)
    pack_rows(box, meta0[:n, 0:1], normed, [ref.at[:ROWS] for ref in boxes])
    pack_rows(box, meta1[:n, 0:1], cot[...], [ref.at[ROWS:] for ref in boxes])


def combine(box, meta, n, own, back, picked):
    sums = [total_of(own)] + [ref[...] for ref in back]
    pick_rows(box, meta[:n, 0:1], sums, n, picked)
    return meta[:n, 1:2] * picked[...]


def split_refs(refs, experts, outs):
    ins = refs[:-outs]
    return ins[: len(ins) + 1 - experts], ins[len(ins) + 1 - experts :], refs[-outs:]


def middle_kernel(box, experts, hidden, meta, meta_out, gain, *refs):
    boxes, picked = refs[-1 - experts : -1], refs[-1]
    own, back, (after,) = split_refs(refs[: -1 - experts], experts, 1)
    n = hidden.shape[0]
    later = (hidden[...].astype(F32) + combine(box, meta, n, own, back, picked)).astype(BF)
    after[...] = later
    wide = later.astype(F32)
    normed = (wide * inv_rms(wide) * gain[...]).astype(BF)
    pack_rows(box, meta_out[:n, 0:1], normed, boxes)


def final_kernel(box, experts, hidden, meta, *refs):
    picked = refs[-1]
    own, back, (out,) = split_refs(refs[:-1], experts, 1)
    n = hidden.shape[0]
    out[...] = (hidden[...].astype(F32) + combine(box, meta, n, own, back, picked)).astype(BF)


def norm_back(hidden, gain, grad):
    wide = hidden.astype(F32)
    inv = inv_rms(wide)
    scaled = grad * gain
    along = jnp.mean(scaled * wide, axis=-1, keepdims=True)
    return inv * scaled - wide * (inv * inv * inv * along)


def gradient_kernel(box, experts, packs, grad, hidden, meta, meta_out, gain, *refs):
    boxes, picked = (refs[-1 - experts : -1] if packs else ()), refs[-1]
    own, back, (out,) = split_refs(refs[: len(refs) - 1 - len(boxes)], experts, 1)
    n = hidden.shape[0]
    d_normed = combine(box, meta, n, own, back, picked)
    if packs:
        row = jnp.concatenate([meta[n + b : n + b + 1] for b in range(box.width // LANES)], axis=1)
    else:
        row = gain[...]
    now = (grad[...].astype(F32) + norm_back(hidden[...], row, d_normed)).astype(BF)
    out[...] = now
    if packs:
        pack_rows(box, meta_out[:n, 0:1], now, boxes)


def spans(tall):
    return pl.ds(0, 2 * tall), pl.ds(tall, 2 * tall)


def gate_up(rows, pack):
    return dot(rows, pack[0][...], NT)


def parts_of(both):
    units = both.shape[1] // 2
    return both[:, :units], both[:, units:]


def down_rows(both, pack):
    g, u = parts_of(both)
    return dot((jax.nn.silu(g) * u).astype(BF), pack[1][...])


def inner_of(rows, pack):
    return dot(rows, pack[1][...], NT)


def part_rows(d_inner, both, pack):
    g, u = parts_of(both)
    r = jax.nn.sigmoid(g)
    d_gate = d_inner * u * r * (1.0 + g * (1.0 - r))
    d_up = d_inner * g * r
    return dot(jnp.concatenate([d_gate, d_up], axis=1).astype(BF), pack[0][...])


def read_rows(box, rows, stack, tails, part):
    tall = stack.shape[0] // 3
    for at, ref in enumerate(rows):
        unpack(box, [ref], stack, tails, at * tall, part)
    return [stack[span, :] for span in spans(tall)]


def write_rows(box, top, bottom, outs):
    tall = top.shape[0] // 2
    for ref, value in zip(outs, (top[:tall], top[tall:] + bottom[:tall], bottom[tall:])):
        repack(box, value, [ref])


def forward_kernel(box, packs, saved, rows, outs, kept, stack, tails, part):
    sides = read_rows(box, rows, stack, tails, part)
    total = []
    for side, values in enumerate(sides):
        total.append(0.0)
        for at in (2 * side, 2 * side + 1):
            both = gate_up(values, packs[at])
            kept[at][...] = both
            total[side] = total[side] + down_rows(both, packs[at])
    write_rows(box, *total, outs)


def inner_kernel(box, packs, saved, rows, outs, kept, stack, tails, part):
    for side, values in enumerate(read_rows(box, rows, stack, tails, part)):
        for at in (2 * side, 2 * side + 1):
            kept[at][...] = inner_of(values, packs[at])


def gate_back_kernel(box, packs, saved, rows, outs, kept, stack, tails, part):
    sides = read_rows(box, rows, stack, tails, part)
    total = []
    for side, values in enumerate(sides):
        total.append(0.0)
        for at in (2 * side, 2 * side + 1):
            both = gate_up(values, packs[at])
            kept[at][...] = both
            total[side] = total[side] + part_rows(saved[at][...], both, packs[at])
    write_rows(box, *total, outs)


def back_kernel(box, packs, saved, rows, outs, kept, stack, tails, part):
    sides = read_rows(box, rows, stack, tails, part)
    total = []
    for side, values in enumerate(sides):
        total.append(0.0)
        for at in (2 * side, 2 * side + 1):
            d_inner = inner_of(values, packs[at])
            total[side] = total[side] + part_rows(d_inner, saved[at][...], packs[at])
    write_rows(box, *total, outs)


def down_kernel(box, packs, saved, rows, outs, kept, stack, tails, part):
    total = []
    for side in range(2):
        at = 2 * side
        total.append(sum(down_rows(saved[i][...], packs[i]) for i in (at, at + 1)))
    write_rows(box, *total, outs)


def expert_call(kernel, box, packs, rows, saved=(), outs=True, kept=0, reads=True, after=(), part=(0, 1)):
    width = packs[0][0].shape[1]
    count = rows[0].shape[0] // ROWS // part[1]
    tall = sum(heights(box, count))
    boxes = jax.ShapeDtypeStruct((count * ROWS, box.lanes), BF)
    results = [boxes] * len(rows) if outs else []
    if kept:
        results += [jax.ShapeDtypeStruct((2 * tall, kept * dn.shape[0]), F32) for _, dn in packs]
    inputs = [w for pack in packs for w in pack] + list(saved) + (list(rows) if reads else [])
    n_in, n_p, n_s, n_out = len(inputs), 2 * len(packs), len(saved), len(rows) if outs else 0

    def body(*refs):
        results_refs = refs[n_in:-2]
        kernel(
            box,
            [refs[at : at + 2] for at in range(0, n_p, 2)],
            refs[n_p : n_p + n_s],
            refs[n_p + n_s : n_in],
            results_refs[:n_out],
            results_refs[n_out:],
            refs[-2],
            refs[-1],
            part,
        )

    scratch = [
        pltpu.VMEM((3 * tall, width), BF),
        pltpu.VMEM((count * ROWS, max(box.wide, LANES)), BF),
    ]
    flops = sum(2 * 2 * tall * width * 3 * dn.shape[0] for _, dn in packs)
    results = call(body, results, *inputs, scratch=scratch, flops=flops, after=after)
    return results[:n_out], results[n_out:]


def local(tokens, norm_gain, w_gate, w_up, w_down, routes, mix_weights, cotangent):
    experts = lax.axis_size("expert") // SPLIT
    n, width = tokens.shape[1:]
    capacity = n // experts + max(1, n // (16 * experts))
    box = Box(capacity, width)
    gain = norm_gain
    gate_w, up_w, down_w = w_gate[0, 0].T, w_up[0, 0].T, w_down[0, 0]
    boxed = jax.ShapeDtypeStruct((ROWS, box.lanes), BF)
    rows_bf = jax.ShapeDtypeStruct((n, width), BF)
    picked = pltpu.VMEM((n, width), F32)
    bind = functools.partial

    def first_hop(boxes):
        crossed = [shift(boxes[j], experts=j) for j in range(1, experts)]
        cross = crossed[0] if experts == 2 else jnp.concatenate(crossed, axis=0)
        return cross, shift(boxes[0], flip=2), shift(boxes[0], flip=1)

    def second_hop(boxes, cross, own_z, own_x):
        return [own_z, boxes[0], own_x], [shift(cross, flip=2), cross, shift(cross, flip=1)]

    def dispatch(boxes):
        return second_hop(boxes, *lax.optimization_barrier(first_hop(boxes)))

    def add(*values):
        return sum(v.astype(F32) for v in values).astype(BF)

    def give_back(own, cross, sections, wait=None):
        total = add(cross[1], shift(cross[0], flip=2), shift(cross[2], flip=1))
        (total, own), wait = lax.optimization_barrier(((total, own), wait))
        back = [
            shift(total[(j - 1) * ROWS : j * ROWS], sections=sections, experts=-j)
            for j in range(1, experts)
        ]
        got = [
            shift(own[1], sections=sections),
            shift(own[0], sections=sections, flip=2),
            shift(own[2], sections=sections, flip=1),
        ] + back
        return got, wait

    meta_shape = jax.ShapeDtypeStruct((n, LANES), F32)
    meta_long = jax.ShapeDtypeStruct((n + -(-width // LANES // 8) * 8, LANES), F32)
    meta0, meta1, *boxes0 = call(
        bind(start_kernel, box, experts),
        [meta_shape, meta_long] + [jax.ShapeDtypeStruct((2 * ROWS, box.lanes), BF)] * experts,
        tokens[0],
        cotangent[0],
        gain,
        routes[0, :, :, 0],
        mix_weights[0, :, :, 0],
    )
    units = w_gate.shape[3]
    cut = -(-units * 7 // 12 // ROWS) * ROWS
    top_dn, bottom_dn = down_w[:cut], down_w[cut:]
    top_gu = jnp.concatenate([gate_w[:cut], up_w[:cut]], axis=0)
    bottom_gu = jnp.concatenate([gate_w[cut:], up_w[cut:]], axis=0)
    first, later = lax.optimization_barrier(
        (
            (
                first_hop(boxes0),
                shift(top_dn, flip=1),
                shift(bottom_dn, flip=2),
            ),
            (top_gu, bottom_gu, meta0, meta1, tokens[0], cotangent[0]),
        )
    )
    hop0, x_dn, z_dn = first
    top_gu, bottom_gu, meta0, meta1, tokens0, cot = later
    own0, cross0 = second_hop(boxes0, *hop0)
    packs = [
        (top_gu, top_dn),
        (shift(top_gu, flip=1), x_dn),
        (bottom_gu, bottom_dn),
        (shift(bottom_gu, flip=2), z_dn),
    ]
    meta0_prev = shift(meta0, sections=1)
    meta1_next = shift(meta1, sections=-1)
    tokens_prev = shift(tokens0, sections=1)
    cot_next = shift(cot, sections=-1)

    early = [meta0_prev, meta1_next, tokens_prev, cot_next]
    own_out, own_kept0 = expert_call(
        forward_kernel, box, packs, own0, kept=2, after=early, part=(0, 2)
    )
    cross_out, cross_kept0 = expert_call(
        forward_kernel, box, packs, cross0, kept=2, after=own_out[:1], part=(0, 2)
    )
    got, _ = give_back(own_out, cross_out, 1)
    inner = bind(expert_call, inner_kernel, box, packs, outs=False, kept=1, part=(1, 2))
    own_di, cross_di = inner(own0)[1], inner(cross0)[1]
    h1, *boxes1 = call(
        bind(middle_kernel, box, experts),
        [rows_bf] + [boxed] * experts,
        tokens_prev,
        meta0_prev,
        meta1,
        gain,
        *got,
        scratch=[picked],
        after=[own_di[0], cross_di[0]],
    )
    h1_home = shift(h1, sections=-1)
    own1, cross1 = dispatch(boxes1)

    gate_back = bind(expert_call, gate_back_kernel, box, packs, kept=2)
    own_grad, own_kept1 = gate_back(own1, own_di)
    cross_grad, cross_kept1 = gate_back(cross1, cross_di, after=own_grad[:1])
    got, _ = give_back(own_grad, cross_grad, -1)
    g1, *boxes_g = call(
        bind(gradient_kernel, box, experts, True),
        [rows_bf] + [boxed] * experts,
        cot_next,
        h1_home,
        meta1_next,
        meta0,
        gain,
        *got,
        scratch=[picked],
    )

    down = bind(expert_call, down_kernel, box, packs, reads=False)
    own_fin, cross_fin = down(own1, own_kept1)[0], down(cross1, cross_kept1)[0]
    hop_g = first_hop(boxes_g)
    fin, hop_g = give_back(own_fin, cross_fin, 0, wait=hop_g)
    own_g, cross_g = second_hop(boxes_g, *hop_g)
    (final,) = call(
        bind(final_kernel, box, experts), [rows_bf], h1, meta1, *fin, scratch=[picked]
    )
    back = bind(expert_call, back_kernel, box, packs)
    own_grad = back(own_g, own_kept0)[0]
    cross_grad = back(cross_g, cross_kept0, after=own_grad[:1])[0]
    got, final = give_back(own_grad, cross_grad, 0, wait=final)
    (g0,) = call(
        bind(gradient_kernel, box, experts, False),
        [rows_bf],
        g1,
        tokens[0],
        meta0,
        meta0,
        gain,
        *got,
        scratch=[picked],
    )
    return (final[None], g0[None])


def solution(mesh):
    in_specs = (
        P("section", "expert", None),
        P("section", None),
        P("section", "expert", None, None),
        P("section", "expert", None, None),
        P("section", "expert", None, None),
        P("section", None, "expert", None),
        P("section", None, "expert", None),
        P("section", "expert", None),
    )
    out_specs = (P("section", "expert", None), P("section", "expert", None))
    return jax.shard_map(local, mesh=mesh, in_specs=in_specs, out_specs=out_specs, check_vma=False)
```

```python
import functools

import jax
import jax.numpy as jnp
from jax import lax
from jax.experimental import pallas as pl
from jax.experimental.pallas import tpu as pltpu
from jax.sharding import PartitionSpec as P

SPLIT = 4
EPSILON = 1e-06
BF = jnp.bfloat16
F32 = jnp.float32
ROWS = 16
LANES = 128


def dot(left, right, dims=((1,), (0,))):
    return lax.dot_general(left, right, (dims, ((), ())), preferred_element_type=F32)


NT = ((1,), (1,))


def iota(shape, axis):
    return lax.broadcasted_iota(jnp.int32, shape, axis)


class Box:
    def __init__(self, capacity, width):
        self.capacity, self.width = capacity, width
        self.groups, self.extra = capacity // ROWS, capacity % ROWS
        self.cuts = ROWS // self.extra if self.extra else 1
        self.wide = -(-width // (LANES * self.cuts)) * LANES if self.extra else 0
        self.lanes = self.groups * width + self.wide
        self.pieces = -(-width // self.wide) if self.extra else 0

    def group(self, g):
        return pl.ds(g * self.width, self.width)

    def tail(self):
        return pl.ds(self.groups * self.width, self.wide)

    def piece(self, i):
        return i * self.wide, min(self.wide, self.width - i * self.wide)


def shift(value, sections=0, experts=0, flip=0):
    n_sec, n_own = lax.axis_size("section"), lax.axis_size("expert")
    n_exp = n_own // SPLIT
    if sections % n_sec == 0 and experts % n_exp == 0 and flip == 0:
        return value
    pairs = []
    for sec in range(n_sec):
        for own in range(n_own):
            exp, sl = own // SPLIT, own % SPLIT
            to = ((exp + experts) % n_exp) * SPLIT + (sl ^ flip)
            pairs.append((sec * n_own + own, ((sec + sections) % n_sec) * n_own + to))
    return lax.ppermute(value, ("section", "expert"), pairs)


def call(body, outs, *operands, scratch=(), flops=0, after=()):
    moved = sum(a.size * a.dtype.itemsize for a in operands)
    moved += sum(o.size * o.dtype.itemsize for o in outs)
    vmem = pl.BlockSpec(memory_space=pltpu.VMEM)
    read = len(operands)

    def reading(*refs):
        body(*refs[:read], *refs[read + len(after) :])

    return pl.pallas_call(
        reading,
        out_shape=list(outs),
        in_specs=[vmem] * read + [pl.BlockSpec(memory_space=pl.ANY)] * len(after),
        out_specs=[vmem] * len(outs),
        scratch_shapes=list(scratch),
        compiler_params=pltpu.CompilerParams(vmem_limit_bytes=40 * 2**20),
        cost_estimate=pl.CostEstimate(flops=flops, bytes_accessed=moved, transcendentals=0),
    )(*operands, *after)


def row_of(column):
    n = column.shape[0]
    eye = iota((n, n), 0) == iota((n, n), 1)
    return jnp.sum(jnp.where(eye, column, 0.0), axis=0, keepdims=True)


def column_of(row):
    n = row.shape[1]
    eye = iota((n, n), 0) == iota((n, n), 1)
    return jnp.sum(jnp.where(eye, row, 0.0), axis=1, keepdims=True)


def slots_of(rel, experts, capacity):
    n = rel.shape[1]
    column = column_of(rel)
    same = jnp.broadcast_to(column, (n, n)) == jnp.broadcast_to(rel, (n, n))
    before = iota((n, n), 1) < iota((n, n), 0)
    rank = jnp.sum(jnp.where(same & before, 1.0, 0.0), axis=1, keepdims=True)
    return column * capacity + rank


def pack_rows(box, slots, values, out_refs):
    n = values.shape[0]
    line = jnp.broadcast_to(row_of(slots).astype(jnp.int32), (ROWS, n))
    r = iota((ROWS, n), 0)
    for j, out in enumerate(out_refs):
        first = j * box.capacity
        for g in range(box.groups):
            sel = jnp.where(line == first + g * ROWS + r, 1.0, 0.0).astype(BF)
            out[:, box.group(g)] = dot(sel, values).astype(BF)
        if box.extra:
            total = jnp.zeros((ROWS, box.wide), F32)
            for i in range(box.pieces):
                at, size = box.piece(i)
                hit = (line == first + box.groups * ROWS + r // box.cuts) & (r % box.cuts == i)
                hit &= r // box.cuts < box.extra
                got = dot(jnp.where(hit, 1.0, 0.0).astype(BF), values[:, at : at + size])
                if size < box.wide:
                    got = jnp.concatenate([got, jnp.zeros((ROWS, box.wide - size), F32)], axis=1)
                total = total + got
            out[:, box.tail()] = total.astype(BF)


def pick_rows(box, slots, boxes, n, picked):
    count = len(boxes)
    if box.groups:
        stack = jnp.concatenate(
            [b[:, g * box.width : (g + 1) * box.width] for b in boxes for g in range(box.groups)],
            axis=0,
        )
        tall = count * box.groups * ROWS
        c = iota((n, tall), 1)
        slot = c // (box.groups * ROWS) * box.capacity + c % (box.groups * ROWS)
        sel = jnp.where(slots.astype(jnp.int32) == slot, 1.0, 0.0).astype(BF)
        picked[...] = dot(sel, stack)
    else:
        picked[...] = jnp.zeros(picked.shape, F32)
    if box.extra:
        tails = jnp.concatenate([b[:, box.groups * box.width :] for b in boxes], axis=0)
        c = iota((n, count * ROWS), 1)
        r = c % ROWS
        slot = c // ROWS * box.capacity + box.groups * ROWS + r // box.cuts
        mine = (slots.astype(jnp.int32) == slot) & (r // box.cuts < box.extra)
        for i in range(box.pieces):
            at, size = box.piece(i)
            sel = jnp.where(mine & (r % box.cuts == i), 1.0, 0.0).astype(BF)
            picked[:, at : at + size] += dot(sel, tails[:, :size])


def heights(box, count):
    extra = -(-count * box.extra // ROWS) * ROWS
    return count * box.groups * ROWS, extra


def unpack(box, refs, stack, tails, at=0):
    count = 0
    for ref in refs:
        for p in range(ref.shape[0] // ROWS):
            for g in range(box.groups):
                stack[at : at + ROWS, :] = ref[p * ROWS : (p + 1) * ROWS, box.group(g)]
                at += ROWS
            if box.extra:
                tails[count * ROWS : (count + 1) * ROWS, :] = ref[
                    p * ROWS : (p + 1) * ROWS, box.tail()
                ]
            count += 1
    if box.extra:
        extra = heights(box, count)[1]
        r = iota((extra, count * ROWS), 0)
        c = iota((extra, count * ROWS), 1)
        mine = (r // box.extra == c // ROWS) & (r % box.extra == c % ROWS // box.cuts)
        for i in range(box.pieces):
            start, size = box.piece(i)
            sel = jnp.where(mine & (c % ROWS % box.cuts == i), 1.0, 0.0).astype(BF)
            stack[at : at + extra, start : start + size] = dot(sel, tails[:, :size]).astype(BF)


def repack(box, rows, refs):
    rows = rows.astype(BF)
    at = 0
    count = 0
    for ref in refs:
        for p in range(ref.shape[0] // ROWS):
            for g in range(box.groups):
                ref[p * ROWS : (p + 1) * ROWS, box.group(g)] = rows[at : at + ROWS]
                at += ROWS
            count += 1
    if box.extra:
        extra = heights(box, count)[1]
        r = iota((count * ROWS, extra), 0)
        c = iota((count * ROWS, extra), 1)
        mine = (c // box.extra == r // ROWS) & (c % box.extra == r % ROWS // box.cuts)
        total = jnp.zeros((count * ROWS, box.wide), F32)
        for i in range(box.pieces):
            start, size = box.piece(i)
            sel = jnp.where(mine & (r % ROWS % box.cuts == i), 1.0, 0.0).astype(BF)
            got = dot(sel, rows[at:, start : start + size])
            if size < box.wide:
                pad = jnp.zeros((count * ROWS, box.wide - size), F32)
                got = jnp.concatenate([got, pad], axis=1)
            total = total + got
        total = total.astype(BF)
        count = 0
        for ref in refs:
            tall = ref.shape[0]
            ref[:, box.tail()] = total[count : count + tall]
            count += tall


def inv_rms(wide):
    return lax.rsqrt(jnp.mean(wide * wide, axis=-1, keepdims=True) + EPSILON)


def total_of(refs):
    return sum(ref[...].astype(F32) for ref in refs).astype(BF)


def start_kernel(box, experts, tokens, cot, gain, ids, mix, meta0, meta1, *boxes):
    n = tokens.shape[0]
    lane = iota((n, LANES), 1)
    mine = lax.axis_index("expert") // SPLIT
    for k, meta in enumerate((meta0, meta1)):
        rel = ids[k : k + 1, :] - mine
        rel = jnp.where(rel < 0, rel + experts, rel).astype(F32)
        slots = slots_of(rel, experts, box.capacity)
        mixes = column_of(mix[k : k + 1, :])
        meta[:n] = jnp.where(lane == 0, slots, jnp.where(lane == 1, mixes, 0.0))
    for b in range(box.width // LANES):
        meta1[n + b : n + b + 1] = gain[:, b * LANES : (b + 1) * LANES]
    wide = tokens[...].astype(F32)
    normed = (wide * inv_rms(wide) * gain[...]).astype(BF)
    crossing = boxes[2:]
    pack_rows(box, meta0[:n, 0:1], normed, [boxes[0]] + [ref.at[:ROWS] for ref in crossing])
    pack_rows(box, meta1[:n, 0:1], cot[...], [boxes[1]] + [ref.at[ROWS:] for ref in crossing])


def combine(box, meta, n, own, back, picked):
    sums = [total_of(own)] + [ref[...] for ref in back]
    pick_rows(box, meta[:n, 0:1], sums, n, picked)
    return meta[:n, 1:2] * picked[...]


def split_refs(refs, experts, outs):
    ins = refs[:-outs]
    return ins[experts - 1 :], ins[: experts - 1], refs[-outs:]


def middle_kernel(box, experts, hidden, meta, meta_out, gain, *refs):
    boxes, picked = refs[-1 - experts : -1], refs[-1]
    own, back, (after,) = split_refs(refs[: -1 - experts], experts, 1)
    n = hidden.shape[0]
    later = (hidden[...].astype(F32) + combine(box, meta, n, own, back, picked)).astype(BF)
    after[...] = later
    wide = later.astype(F32)
    normed = (wide * inv_rms(wide) * gain[...]).astype(BF)
    pack_rows(box, meta_out[:n, 0:1], normed, boxes)


def final_kernel(box, experts, hidden, meta, *refs):
    picked = refs[-1]
    own, back, (out,) = split_refs(refs[:-1], experts, 1)
    n = hidden.shape[0]
    out[...] = (hidden[...].astype(F32) + combine(box, meta, n, own, back, picked)).astype(BF)


def norm_back(hidden, gain, grad):
    wide = hidden.astype(F32)
    inv = inv_rms(wide)
    scaled = grad * gain
    along = jnp.mean(scaled * wide, axis=-1, keepdims=True)
    return inv * scaled - wide * (inv * inv * inv * along)


def gradient_kernel(box, experts, packs, grad, hidden, meta, meta_out, gain, *refs):
    boxes, picked = (refs[-1 - experts : -1] if packs else ()), refs[-1]
    own, back, (out,) = split_refs(refs[: len(refs) - 1 - len(boxes)], experts, 1)
    n = hidden.shape[0]
    d_normed = combine(box, meta, n, own, back, picked)
    if packs:
        row = jnp.concatenate([meta[n + b : n + b + 1] for b in range(box.width // LANES)], axis=1)
    else:
        row = gain[...]
    now = (grad[...].astype(F32) + norm_back(hidden[...], row, d_normed)).astype(BF)
    out[...] = now
    if packs:
        pack_rows(box, meta_out[:n, 0:1], now, boxes)


def spans(tall):
    return pl.ds(0, 2 * tall), pl.ds(tall, 2 * tall)


def gate_up(rows, pack):
    return dot(rows, pack[: 2 * (pack.shape[0] // 3)], NT)


def parts_of(both):
    units = both.shape[1] // 2
    return both[:, :units], both[:, units:]


def down_rows(both, pack):
    g, u = parts_of(both)
    return dot((jax.nn.silu(g) * u).astype(BF), pack[2 * g.shape[1] :])


def inner_of(rows, pack):
    return dot(rows, pack[2 * (pack.shape[0] // 3) :], NT)


def part_rows(d_inner, both, pack):
    g, u = parts_of(both)
    r = jax.nn.sigmoid(g)
    d_gate = d_inner * u * r * (1.0 + g * (1.0 - r))
    d_up = d_inner * g * r
    return dot(jnp.concatenate([d_gate, d_up], axis=1).astype(BF), pack[: both.shape[1]])


def read_rows(box, rows, stack, tails):
    tall = stack.shape[0] // 3
    for at, ref in enumerate(rows):
        unpack(box, [ref], stack, tails, at * tall)
    return [stack[span, :] for span in spans(tall)]


def write_rows(box, top, bottom, outs):
    tall = top.shape[0] // 2
    for ref, value in zip(outs, (top[:tall], top[tall:] + bottom[:tall], bottom[tall:])):
        repack(box, value, [ref])


def forward_kernel(box, packs, saved, rows, outs, kept, stack, tails):
    sides = read_rows(box, rows, stack, tails)
    total = []
    for side, values in enumerate(sides):
        total.append(0.0)
        for at in (2 * side, 2 * side + 1):
            both = gate_up(values, packs[at])
            kept[at][...] = both
            total[side] = total[side] + down_rows(both, packs[at])
    write_rows(box, *total, outs)


def inner_kernel(box, packs, saved, rows, outs, kept, stack, tails):
    for side, values in enumerate(read_rows(box, rows, stack, tails)):
        for at in (2 * side, 2 * side + 1):
            kept[at][...] = inner_of(values, packs[at])


def gate_back_kernel(box, packs, saved, rows, outs, kept, stack, tails):
    sides = read_rows(box, rows, stack, tails)
    total = []
    for side, values in enumerate(sides):
        total.append(0.0)
        for at in (2 * side, 2 * side + 1):
            both = gate_up(values, packs[at])
            kept[at][...] = both
            total[side] = total[side] + part_rows(saved[at][...], both, packs[at])
    write_rows(box, *total, outs)


def back_kernel(box, packs, saved, rows, outs, kept, stack, tails):
    sides = read_rows(box, rows, stack, tails)
    total = []
    for side, values in enumerate(sides):
        total.append(0.0)
        for at in (2 * side, 2 * side + 1):
            d_inner = inner_of(values, packs[at])
            total[side] = total[side] + part_rows(d_inner, saved[at][...], packs[at])
    write_rows(box, *total, outs)


def down_kernel(box, packs, saved, rows, outs, kept, stack, tails):
    total = []
    for side in range(2):
        at = 2 * side
        total.append(sum(down_rows(saved[i][...], packs[i]) for i in (at, at + 1)))
    write_rows(box, *total, outs)


def expert_call(kernel, box, packs, rows, saved=(), outs=True, kept=0, reads=True, after=()):
    width = packs[0].shape[1]
    count = rows[0].shape[0] // ROWS
    tall = sum(heights(box, count))
    boxes = jax.ShapeDtypeStruct((count * ROWS, box.lanes), BF)
    results = [boxes] * len(rows) if outs else []
    if kept:
        units = [pack.shape[0] // 3 for pack in packs]
        results += [jax.ShapeDtypeStruct((2 * tall, kept * u), F32) for u in units]
    inputs = list(packs) + list(saved) + (list(rows) if reads else [])
    n_in, n_p, n_s, n_out = len(inputs), len(packs), len(saved), len(rows) if outs else 0

    def body(*refs):
        results_refs = refs[n_in:-2]
        kernel(
            box,
            refs[:n_p],
            refs[n_p : n_p + n_s],
            refs[n_p + n_s : n_in],
            results_refs[:n_out],
            results_refs[n_out:],
            refs[-2],
            refs[-1],
        )

    scratch = [
        pltpu.VMEM((3 * tall, width), BF),
        pltpu.VMEM((count * ROWS, max(box.wide, LANES)), BF),
    ]
    flops = sum(2 * 2 * tall * pack.size for pack in packs)
    results = call(body, results, *inputs, scratch=scratch, flops=flops, after=after)
    return results[:n_out], results[n_out:]


def local(tokens, norm_gain, w_gate, w_up, w_down, routes, mix_weights, cotangent):
    experts = lax.axis_size("expert") // SPLIT
    n, width = tokens.shape[1:]
    capacity = n // experts + max(1, n // (16 * experts))
    box = Box(capacity, width)
    gain = norm_gain
    gate_w, up_w, down_w = w_gate[0, 0].T, w_up[0, 0].T, w_down[0, 0]
    boxed = jax.ShapeDtypeStruct((ROWS, box.lanes), BF)
    rows_bf = jax.ShapeDtypeStruct((n, width), BF)
    picked = pltpu.VMEM((n, width), F32)
    bind = functools.partial

    def joined(arrays):
        return arrays[0] if len(arrays) == 1 else jnp.concatenate(arrays, axis=0)

    def first_hop(boxes):
        crossed = [shift(boxes[j], experts=j) for j in range(1, experts)]
        return joined(crossed), shift(boxes[0], flip=2), shift(boxes[0], flip=1)

    def second_hop(boxes, cross, own_z, own_x):
        return [own_z, boxes[0], own_x], [shift(cross, flip=2), cross, shift(cross, flip=1)]

    def dispatch(boxes):
        return second_hop(boxes, *lax.optimization_barrier(first_hop(boxes)))

    def add(*values):
        return sum(v.astype(F32) for v in values).astype(BF)

    def give_back(own, cross, sections, wait=None):
        total = add(cross[1], shift(cross[0], flip=2), shift(cross[2], flip=1))
        (total, own), wait = lax.optimization_barrier(((total, own), wait))
        back = [
            shift(total[(j - 1) * ROWS : j * ROWS], sections=sections, experts=-j)
            for j in range(1, experts)
        ]
        got = back + [
            shift(own[0], sections=sections, flip=2),
            shift(own[2], sections=sections, flip=1),
            shift(own[1], sections=sections),
        ]
        return got, wait

    meta_shape = jax.ShapeDtypeStruct((n, LANES), F32)
    meta_long = jax.ShapeDtypeStruct((n + -(-width // LANES // 8) * 8, LANES), F32)
    units = w_gate.shape[3]
    cut = -(-units * 7 // 12 // ROWS) * ROWS
    top = jnp.concatenate([gate_w[:cut], up_w[:cut], down_w[:cut]], axis=0)
    bottom = jnp.concatenate([gate_w[cut:], up_w[cut:], down_w[cut:]], axis=0)
    packs = [top, shift(top, flip=1), bottom, shift(bottom, flip=2)]

    both = jax.ShapeDtypeStruct((2 * ROWS, box.lanes), BF)
    meta0, meta1, own_tok, own_cot, *crossing = call(
        bind(start_kernel, box, experts),
        [meta_shape, meta_long, boxed, boxed] + [both] * (experts - 1),
        tokens[0],
        cotangent[0],
        gain,
        routes[0, :, :, 0],
        mix_weights[0, :, :, 0],
    )
    crossed = [shift(crossing[j - 1], experts=j) for j in range(1, experts)]
    own_z, own_x = shift(own_tok, flip=2), shift(own_tok, flip=1)
    crossed, own_z, own_x = lax.optimization_barrier((crossed, own_z, own_x))
    cross_tok = joined([c[:ROWS] for c in crossed])
    cross_cot = joined([c[ROWS:] for c in crossed])
    own0, cross0 = second_hop([own_tok], cross_tok, own_z, own_x)
    cot_z, cot_x = shift(own_cot, flip=2), shift(own_cot, flip=1)
    cot_own, cot_cross = second_hop([own_cot], cross_cot, cot_z, cot_x)
    meta0_prev = shift(meta0, sections=1)
    meta1_next = shift(meta1, sections=-1)
    tokens_prev = shift(tokens[0], sections=1)
    cot_next = shift(cotangent[0], sections=-1)

    early = [meta0_prev, meta1_next, tokens_prev, cot_next]
    own_out, own_kept0 = expert_call(forward_kernel, box, packs, own0, kept=2, after=early)
    cross_out, cross_kept0 = expert_call(
        forward_kernel, box, packs, cross0, kept=2, after=own_out[:1]
    )
    got, _ = give_back(own_out, cross_out, 1)
    inner = bind(expert_call, inner_kernel, box, packs, outs=False, kept=1)
    own_di, cross_di = inner(cot_own)[1], inner(cot_cross)[1]
    h1, *boxes1 = call(
        bind(middle_kernel, box, experts),
        [rows_bf] + [boxed] * experts,
        tokens_prev,
        meta0_prev,
        meta1,
        gain,
        *got,
        scratch=[picked],
        after=[own_di[0], cross_di[0]],
    )
    h1_home = shift(h1, sections=-1)
    own1, cross1 = dispatch(boxes1)

    gate_back = bind(expert_call, gate_back_kernel, box, packs, kept=2)
    own_grad, own_kept1 = gate_back(own1, own_di)
    cross_grad, cross_kept1 = gate_back(cross1, cross_di, after=own_grad[:1])
    got, _ = give_back(own_grad, cross_grad, -1)
    g1, *boxes_g = call(
        bind(gradient_kernel, box, experts, True),
        [rows_bf] + [boxed] * experts,
        cot_next,
        h1_home,
        meta1_next,
        meta0,
        gain,
        *got,
        scratch=[picked],
    )

    down = bind(expert_call, down_kernel, box, packs, reads=False)
    own_fin, cross_fin = down(own1, own_kept1)[0], down(cross1, cross_kept1)[0]
    hop_g = lax.optimization_barrier(first_hop(boxes_g))
    fin, hop_g = give_back(own_fin, cross_fin, 0, wait=hop_g)
    own_g, cross_g = second_hop(boxes_g, *hop_g)
    (final,) = call(
        bind(final_kernel, box, experts), [rows_bf], h1, meta1, *fin, scratch=[picked]
    )
    back = bind(expert_call, back_kernel, box, packs)
    own_grad = back(own_g, own_kept0)[0]
    cross_grad = back(cross_g, cross_kept0, after=own_grad[:1])[0]
    got, final = give_back(own_grad, cross_grad, 0, wait=final)
    (g0,) = call(
        bind(gradient_kernel, box, experts, False),
        [rows_bf],
        g1,
        tokens[0],
        meta0,
        meta0,
        gain,
        *got,
        scratch=[picked],
    )
    return (final[None], g0[None])


def solution(mesh):
    in_specs = (
        P("section", "expert", None),
        P("section", None),
        P("section", "expert", None, None),
        P("section", "expert", None, None),
        P("section", "expert", None, None),
        P("section", None, "expert", None),
        P("section", None, "expert", None),
        P("section", "expert", None),
    )
    out_specs = (P("section", "expert", None), P("section", "expert", None))
    return jax.shard_map(local, mesh=mesh, in_specs=in_specs, out_specs=out_specs, check_vma=False)
```

```python
import functools

import jax
import jax.numpy as jnp
from jax import lax
from jax.experimental import pallas as pl
from jax.experimental.pallas import tpu as pltpu
from jax.sharding import PartitionSpec as P

SPLIT = 4
EPSILON = 1e-06
BF = jnp.bfloat16
F32 = jnp.float32
ROWS = 16
LANES = 128


def dot(left, right, dims=((1,), (0,))):
    return lax.dot_general(left, right, (dims, ((), ())), preferred_element_type=F32)


NT = ((1,), (1,))


def iota(shape, axis):
    return lax.broadcasted_iota(jnp.int32, shape, axis)


class Box:
    def __init__(self, capacity, width):
        self.capacity, self.width = capacity, width
        self.groups, self.extra = capacity // ROWS, capacity % ROWS
        self.cuts = ROWS // self.extra if self.extra else 1
        self.wide = -(-width // (LANES * self.cuts)) * LANES if self.extra else 0
        self.lanes = self.groups * width + self.wide
        self.pieces = -(-width // self.wide) if self.extra else 0

    def group(self, g):
        return pl.ds(g * self.width, self.width)

    def tail(self):
        return pl.ds(self.groups * self.width, self.wide)

    def piece(self, i):
        return i * self.wide, min(self.wide, self.width - i * self.wide)


def shift(value, sections=0, experts=0, flip=0):
    n_sec, n_own = lax.axis_size("section"), lax.axis_size("expert")
    n_exp = n_own // SPLIT
    if sections % n_sec == 0 and experts % n_exp == 0 and flip == 0:
        return value
    pairs = []
    for sec in range(n_sec):
        for own in range(n_own):
            exp, sl = own // SPLIT, own % SPLIT
            to = ((exp + experts) % n_exp) * SPLIT + (sl ^ flip)
            pairs.append((sec * n_own + own, ((sec + sections) % n_sec) * n_own + to))
    return lax.ppermute(value, ("section", "expert"), pairs)


def call(body, outs, *operands, scratch=(), flops=0, after=()):
    moved = sum(a.size * a.dtype.itemsize for a in operands)
    moved += sum(o.size * o.dtype.itemsize for o in outs)
    vmem = pl.BlockSpec(memory_space=pltpu.VMEM)
    read = len(operands)

    def reading(*refs):
        body(*refs[:read], *refs[read + len(after) :])

    return pl.pallas_call(
        reading,
        out_shape=list(outs),
        in_specs=[vmem] * read + [pl.BlockSpec(memory_space=pl.ANY)] * len(after),
        out_specs=[vmem] * len(outs),
        scratch_shapes=list(scratch),
        compiler_params=pltpu.CompilerParams(vmem_limit_bytes=40 * 2**20),
        cost_estimate=pl.CostEstimate(flops=flops, bytes_accessed=moved, transcendentals=0),
    )(*operands, *after)


def row_of(column):
    n = column.shape[0]
    eye = iota((n, n), 0) == iota((n, n), 1)
    return jnp.sum(jnp.where(eye, column, 0.0), axis=0, keepdims=True)


def column_of(row):
    n = row.shape[1]
    eye = iota((n, n), 0) == iota((n, n), 1)
    return jnp.sum(jnp.where(eye, row, 0.0), axis=1, keepdims=True)


def slots_of(rel, experts, capacity):
    n = rel.shape[1]
    column = column_of(rel)
    same = jnp.broadcast_to(column, (n, n)) == jnp.broadcast_to(rel, (n, n))
    before = iota((n, n), 1) < iota((n, n), 0)
    rank = jnp.sum(jnp.where(same & before, 1.0, 0.0), axis=1, keepdims=True)
    return column * capacity + rank


def pack_rows(box, slots, values, out_refs):
    n = values.shape[0]
    line = jnp.broadcast_to(row_of(slots).astype(jnp.int32), (ROWS, n))
    r = iota((ROWS, n), 0)
    for j, out in enumerate(out_refs):
        first = j * box.capacity
        for g in range(box.groups):
            sel = jnp.where(line == first + g * ROWS + r, 1.0, 0.0).astype(BF)
            out[:, box.group(g)] = dot(sel, values).astype(BF)
        if box.extra:
            total = jnp.zeros((ROWS, box.wide), F32)
            for i in range(box.pieces):
                at, size = box.piece(i)
                hit = (line == first + box.groups * ROWS + r // box.cuts) & (r % box.cuts == i)
                hit &= r // box.cuts < box.extra
                got = dot(jnp.where(hit, 1.0, 0.0).astype(BF), values[:, at : at + size])
                if size < box.wide:
                    got = jnp.concatenate([got, jnp.zeros((ROWS, box.wide - size), F32)], axis=1)
                total = total + got
            out[:, box.tail()] = total.astype(BF)


def pick_rows(box, slots, boxes, n, picked):
    count = len(boxes)
    if box.groups:
        stack = jnp.concatenate(
            [b[:, g * box.width : (g + 1) * box.width] for b in boxes for g in range(box.groups)],
            axis=0,
        )
        tall = count * box.groups * ROWS
        c = iota((n, tall), 1)
        slot = c // (box.groups * ROWS) * box.capacity + c % (box.groups * ROWS)
        sel = jnp.where(slots.astype(jnp.int32) == slot, 1.0, 0.0).astype(BF)
        picked[...] = dot(sel, stack)
    else:
        picked[...] = jnp.zeros(picked.shape, F32)
    if box.extra:
        tails = jnp.concatenate([b[:, box.groups * box.width :] for b in boxes], axis=0)
        c = iota((n, count * ROWS), 1)
        r = c % ROWS
        slot = c // ROWS * box.capacity + box.groups * ROWS + r // box.cuts
        mine = (slots.astype(jnp.int32) == slot) & (r // box.cuts < box.extra)
        for i in range(box.pieces):
            at, size = box.piece(i)
            sel = jnp.where(mine & (r % box.cuts == i), 1.0, 0.0).astype(BF)
            picked[:, at : at + size] += dot(sel, tails[:, :size])


def heights(box, count):
    extra = -(-count * box.extra // ROWS) * ROWS
    return count * box.groups * ROWS, extra


def unpack(box, refs, stack, tails, at=0):
    count = 0
    for ref in refs:
        for p in range(ref.shape[0] // ROWS):
            for g in range(box.groups):
                stack[at : at + ROWS, :] = ref[p * ROWS : (p + 1) * ROWS, box.group(g)]
                at += ROWS
            if box.extra:
                tails[count * ROWS : (count + 1) * ROWS, :] = ref[
                    p * ROWS : (p + 1) * ROWS, box.tail()
                ]
            count += 1
    if box.extra:
        extra = heights(box, count)[1]
        r = iota((extra, count * ROWS), 0)
        c = iota((extra, count * ROWS), 1)
        mine = (r // box.extra == c // ROWS) & (r % box.extra == c % ROWS // box.cuts)
        for i in range(box.pieces):
            start, size = box.piece(i)
            sel = jnp.where(mine & (c % ROWS % box.cuts == i), 1.0, 0.0).astype(BF)
            stack[at : at + extra, start : start + size] = dot(sel, tails[:, :size]).astype(BF)


def repack(box, rows, refs):
    rows = rows.astype(BF)
    at = 0
    count = 0
    for ref in refs:
        for p in range(ref.shape[0] // ROWS):
            for g in range(box.groups):
                ref[p * ROWS : (p + 1) * ROWS, box.group(g)] = rows[at : at + ROWS]
                at += ROWS
            count += 1
    if box.extra:
        extra = heights(box, count)[1]
        r = iota((count * ROWS, extra), 0)
        c = iota((count * ROWS, extra), 1)
        mine = (c // box.extra == r // ROWS) & (c % box.extra == r % ROWS // box.cuts)
        total = jnp.zeros((count * ROWS, box.wide), F32)
        for i in range(box.pieces):
            start, size = box.piece(i)
            sel = jnp.where(mine & (r % ROWS % box.cuts == i), 1.0, 0.0).astype(BF)
            got = dot(sel, rows[at:, start : start + size])
            if size < box.wide:
                pad = jnp.zeros((count * ROWS, box.wide - size), F32)
                got = jnp.concatenate([got, pad], axis=1)
            total = total + got
        total = total.astype(BF)
        count = 0
        for ref in refs:
            tall = ref.shape[0]
            ref[:, box.tail()] = total[count : count + tall]
            count += tall


def inv_rms(wide):
    return lax.rsqrt(jnp.mean(wide * wide, axis=-1, keepdims=True) + EPSILON)


def total_of(refs):
    return sum(ref[...].astype(F32) for ref in refs).astype(BF)


def start_kernel(box, experts, tokens, cot, gain, ids, mix, meta0, meta1, *boxes):
    n = tokens.shape[0]
    lane = iota((n, LANES), 1)
    mine = lax.axis_index("expert") // SPLIT
    for k, meta in enumerate((meta0, meta1)):
        rel = ids[k : k + 1, :] - mine
        rel = jnp.where(rel < 0, rel + experts, rel).astype(F32)
        slots = slots_of(rel, experts, box.capacity)
        mixes = column_of(mix[k : k + 1, :])
        meta[:n] = jnp.where(lane == 0, slots, jnp.where(lane == 1, mixes, 0.0))
    for b in range(box.width // LANES):
        meta1[n + b : n + b + 1] = gain[:, b * LANES : (b + 1) * LANES]
    wide = tokens[...].astype(F32)
    normed = (wide * inv_rms(wide) * gain[...]).astype(BF)
    crossing = boxes[2:]
    pack_rows(box, meta0[:n, 0:1], normed, [boxes[0]] + [ref.at[:ROWS] for ref in crossing])
    pack_rows(box, meta1[:n, 0:1], cot[...], [boxes[1]] + [ref.at[ROWS:] for ref in crossing])


def combine(box, meta, n, own, back, picked):
    sums = [total_of(own)] + [ref[...] for ref in back]
    pick_rows(box, meta[:n, 0:1], sums, n, picked)
    return meta[:n, 1:2] * picked[...]


def split_refs(refs, experts, outs):
    ins = refs[:-outs]
    return ins[experts - 1 :], ins[: experts - 1], refs[-outs:]


def middle_kernel(box, experts, hidden, meta, meta_out, gain, *refs):
    boxes, picked = refs[-1 - experts : -1], refs[-1]
    own, back, (after,) = split_refs(refs[: -1 - experts], experts, 1)
    n = hidden.shape[0]
    later = (hidden[...].astype(F32) + combine(box, meta, n, own, back, picked)).astype(BF)
    after[...] = later
    wide = later.astype(F32)
    normed = (wide * inv_rms(wide) * gain[...]).astype(BF)
    pack_rows(box, meta_out[:n, 0:1], normed, boxes)


def final_kernel(box, experts, hidden, meta, *refs):
    picked = refs[-1]
    own, back, (out,) = split_refs(refs[:-1], experts, 1)
    n = hidden.shape[0]
    out[...] = (hidden[...].astype(F32) + combine(box, meta, n, own, back, picked)).astype(BF)


def norm_back(hidden, gain, grad):
    wide = hidden.astype(F32)
    inv = inv_rms(wide)
    scaled = grad * gain
    along = jnp.mean(scaled * wide, axis=-1, keepdims=True)
    return inv * scaled - wide * (inv * inv * inv * along)


def gradient_kernel(box, experts, packs, grad, hidden, meta, meta_out, gain, *refs):
    boxes, picked = (refs[-1 - experts : -1] if packs else ()), refs[-1]
    own, back, (out,) = split_refs(refs[: len(refs) - 1 - len(boxes)], experts, 1)
    n = hidden.shape[0]
    d_normed = combine(box, meta, n, own, back, picked)
    if packs:
        row = jnp.concatenate([meta[n + b : n + b + 1] for b in range(box.width // LANES)], axis=1)
    else:
        row = gain[...]
    now = (grad[...].astype(F32) + norm_back(hidden[...], row, d_normed)).astype(BF)
    out[...] = now
    if packs:
        pack_rows(box, meta_out[:n, 0:1], now, boxes)


def spans(tall):
    return pl.ds(0, 2 * tall), pl.ds(tall, 2 * tall)


def gate_up(rows, pack):
    return dot(rows, pack[: 2 * (pack.shape[0] // 3)], NT)


def parts_of(both):
    units = both.shape[1] // 2
    return both[:, :units], both[:, units:]


def down_rows(both, pack):
    g, u = parts_of(both)
    return dot((jax.nn.silu(g) * u).astype(BF), pack[2 * g.shape[1] :])


def inner_of(rows, pack):
    return dot(rows, pack[2 * (pack.shape[0] // 3) :], NT)


def part_rows(d_inner, both, pack):
    g, u = parts_of(both)
    r = jax.nn.sigmoid(g)
    d_gate = d_inner * u * r * (1.0 + g * (1.0 - r))
    d_up = d_inner * g * r
    return dot(jnp.concatenate([d_gate, d_up], axis=1).astype(BF), pack[: both.shape[1]])


def read_rows(box, rows, stack, tails):
    tall = stack.shape[0] // 3
    for at, ref in enumerate(rows):
        unpack(box, [ref], stack, tails, at * tall)
    return [stack[span, :] for span in spans(tall)]


def write_rows(box, top, bottom, outs):
    tall = top.shape[0] // 2
    for ref, value in zip(outs, (top[:tall], top[tall:] + bottom[:tall], bottom[tall:])):
        repack(box, value, [ref])


def forward_kernel(box, packs, saved, rows, outs, kept, stack, tails):
    sides = read_rows(box, rows, stack, tails)
    total = []
    for side, values in enumerate(sides):
        total.append(0.0)
        for at in (2 * side, 2 * side + 1):
            both = gate_up(values, packs[at])
            kept[at][...] = both
            total[side] = total[side] + down_rows(both, packs[at])
    write_rows(box, *total, outs)


def inner_kernel(box, packs, saved, rows, outs, kept, stack, tails):
    for side, values in enumerate(read_rows(box, rows, stack, tails)):
        for at in (2 * side, 2 * side + 1):
            kept[at][...] = inner_of(values, packs[at])


def gate_back_kernel(box, packs, saved, rows, outs, kept, stack, tails):
    sides = read_rows(box, rows, stack, tails)
    total = []
    for side, values in enumerate(sides):
        total.append(0.0)
        for at in (2 * side, 2 * side + 1):
            both = gate_up(values, packs[at])
            kept[at][...] = both
            total[side] = total[side] + part_rows(saved[at][...], both, packs[at])
    write_rows(box, *total, outs)


def back_kernel(box, packs, saved, rows, outs, kept, stack, tails):
    sides = read_rows(box, rows, stack, tails)
    total = []
    for side, values in enumerate(sides):
        total.append(0.0)
        for at in (2 * side, 2 * side + 1):
            d_inner = inner_of(values, packs[at])
            total[side] = total[side] + part_rows(d_inner, saved[at][...], packs[at])
    write_rows(box, *total, outs)


def down_kernel(box, packs, saved, rows, outs, kept, stack, tails):
    total = []
    for side in range(2):
        at = 2 * side
        total.append(sum(down_rows(saved[i][...], packs[i]) for i in (at, at + 1)))
    write_rows(box, *total, outs)


def expert_call(kernel, box, packs, rows, saved=(), outs=True, kept=0, reads=True, after=()):
    width = packs[0].shape[1]
    count = rows[0].shape[0] // ROWS
    tall = sum(heights(box, count))
    boxes = jax.ShapeDtypeStruct((count * ROWS, box.lanes), BF)
    results = [boxes] * len(rows) if outs else []
    if kept:
        units = [pack.shape[0] // 3 for pack in packs]
        results += [jax.ShapeDtypeStruct((2 * tall, kept * u), F32) for u in units]
    inputs = list(packs) + list(saved) + (list(rows) if reads else [])
    n_in, n_p, n_s, n_out = len(inputs), len(packs), len(saved), len(rows) if outs else 0

    def body(*refs):
        results_refs = refs[n_in:-2]
        kernel(
            box,
            refs[:n_p],
            refs[n_p : n_p + n_s],
            refs[n_p + n_s : n_in],
            results_refs[:n_out],
            results_refs[n_out:],
            refs[-2],
            refs[-1],
        )

    scratch = [
        pltpu.VMEM((3 * tall, width), BF),
        pltpu.VMEM((count * ROWS, max(box.wide, LANES)), BF),
    ]
    flops = sum(2 * 2 * tall * pack.size for pack in packs)
    results = call(body, results, *inputs, scratch=scratch, flops=flops, after=after)
    return results[:n_out], results[n_out:]


def local(tokens, norm_gain, w_gate, w_up, w_down, routes, mix_weights, cotangent):
    experts = lax.axis_size("expert") // SPLIT
    n, width = tokens.shape[1:]
    capacity = n // experts + max(1, n // (16 * experts))
    box = Box(capacity, width)
    gain = norm_gain
    gate_w, up_w, down_w = w_gate[0, 0].T, w_up[0, 0].T, w_down[0, 0]
    boxed = jax.ShapeDtypeStruct((ROWS, box.lanes), BF)
    rows_bf = jax.ShapeDtypeStruct((n, width), BF)
    picked = pltpu.VMEM((n, width), F32)
    bind = functools.partial

    def joined(arrays):
        return arrays[0] if len(arrays) == 1 else jnp.concatenate(arrays, axis=0)

    fence = lax.optimization_barrier

    def crossing_of(boxes):
        return joined([shift(boxes[j - 1], experts=j) for j in range(1, experts)])

    def around(boxes):
        return [shift(boxes, flip=2), boxes, shift(boxes, flip=1)]

    def add(*values):
        return sum(v.astype(F32) for v in values).astype(BF)

    def sums(parts):
        return add(parts[1], shift(parts[0], flip=2), shift(parts[2], flip=1))

    def home(total, sections):
        return [
            shift(total[(j - 1) * ROWS : j * ROWS], sections=sections, experts=-j)
            for j in range(1, experts)
        ]

    def own_home(parts, sections):
        return [
            shift(parts[0], sections=sections, flip=2),
            shift(parts[2], sections=sections, flip=1),
            shift(parts[1], sections=sections),
        ]

    def give_back(cross, own, sections):
        total, own = fence((sums(cross), own))
        return home(total, sections) + own_home(own, sections)

    meta_shape = jax.ShapeDtypeStruct((n, LANES), F32)
    meta_long = jax.ShapeDtypeStruct((n + -(-width // LANES // 8) * 8, LANES), F32)
    units = w_gate.shape[3]
    cut = -(-units * 7 // 12 // ROWS) * ROWS
    top = jnp.concatenate([gate_w[:cut], up_w[:cut], down_w[:cut]], axis=0)
    bottom = jnp.concatenate([gate_w[cut:], up_w[cut:], down_w[cut:]], axis=0)
    packs = [top, shift(top, flip=1), bottom, shift(bottom, flip=2)]

    both = jax.ShapeDtypeStruct((2 * ROWS, box.lanes), BF)
    meta0, meta1, own_tok, own_cot, *crossing = call(
        bind(start_kernel, box, experts),
        [meta_shape, meta_long, boxed, boxed] + [both] * (experts - 1),
        tokens[0],
        cotangent[0],
        gain,
        routes[0, :, :, 0],
        mix_weights[0, :, :, 0],
        after=[top, bottom],
    )
    crossed = [shift(crossing[j - 1], experts=j) for j in range(1, experts)]
    own0 = around(own_tok)
    crossed, own0, packs[3] = fence((crossed, own0, packs[3]))
    cross0 = around(joined([c[:ROWS] for c in crossed]))
    cross_cot = joined([c[ROWS:] for c in crossed])
    meta0_prev = shift(meta0, sections=1)
    meta1_next = shift(meta1, sections=-1)
    tokens_prev = shift(tokens[0], sections=1)
    cot_next = shift(cotangent[0], sections=-1)

    early = [meta0_prev, meta1_next, tokens_prev, cot_next]
    own_out, own_kept0 = expert_call(forward_kernel, box, packs, own0, kept=2, after=early)
    cross_out, cross_kept0 = expert_call(
        forward_kernel, box, packs, cross0, kept=2, after=own_out[:1]
    )
    got = give_back(cross_out, own_out, 1)
    h1, own1, *boxes1 = call(
        bind(middle_kernel, box, experts),
        [rows_bf] + [boxed] * experts,
        tokens_prev,
        meta0_prev,
        meta1,
        gain,
        *got,
        scratch=[picked],
    )
    h1_home = shift(h1, sections=-1)
    boxes1, own_cot, cross_cot = fence((boxes1, own_cot, cross_cot))
    cross1, own1 = fence((crossing_of(boxes1), own1))
    cross1, own1 = around(cross1), around(own1)
    inner = bind(expert_call, inner_kernel, box, packs, outs=False, kept=1)
    own_di, cross_di = inner(around(own_cot))[1], inner(around(cross_cot))[1]

    gate_back = bind(expert_call, gate_back_kernel, box, packs, kept=2)
    cross_grad, cross_kept1 = gate_back(cross1, cross_di)
    own_grad, own_kept1 = gate_back(own1, own_di, after=cross_grad[:1])
    got = give_back(cross_grad, own_grad, -1)
    g1, own_g, *boxes_g = call(
        bind(gradient_kernel, box, experts, True),
        [rows_bf] + [boxed] * experts,
        cot_next,
        h1_home,
        meta1_next,
        meta0,
        gain,
        *got,
        scratch=[picked],
    )

    down = bind(expert_call, down_kernel, box, packs, reads=False)
    own_fin, cross_fin = down(own1, own_kept1)[0], down(cross1, cross_kept1)[0]
    boxes_g, own_fin, cross_fin = fence((boxes_g, own_fin, cross_fin))
    fin_own = own_home(own_fin, 0)
    fin_sums = sums(cross_fin)
    cross_g, own_g, fin_sums = fence((crossing_of(boxes_g), own_g, fin_sums))
    cross_g, own_g = around(cross_g), around(own_g)
    fin_back = home(fin_sums, 0)
    back = bind(expert_call, back_kernel, box, packs)
    cross_grad = back(cross_g, cross_kept0, after=fin_own)[0]
    own_grad = back(own_g, own_kept0, after=cross_grad[:1])[0]
    cross_grad, fin_back = fence((cross_grad, fin_back))
    (final,) = call(
        bind(final_kernel, box, experts),
        [rows_bf],
        h1,
        meta1,
        *fin_back,
        *fin_own,
        scratch=[picked],
    )
    got = give_back(cross_grad, own_grad, 0)
    (g0,) = call(
        bind(gradient_kernel, box, experts, False),
        [rows_bf],
        g1,
        tokens[0],
        meta0,
        meta0,
        gain,
        *got,
        scratch=[picked],
    )
    return (final[None], g0[None])


def solution(mesh):
    in_specs = (
        P("section", "expert", None),
        P("section", None),
        P("section", "expert", None, None),
        P("section", "expert", None, None),
        P("section", "expert", None, None),
        P("section", None, "expert", None),
        P("section", None, "expert", None),
        P("section", "expert", None),
    )
    out_specs = (P("section", "expert", None), P("section", "expert", None))
    return jax.shard_map(local, mesh=mesh, in_specs=in_specs, out_specs=out_specs, check_vma=False)
```

```python
import functools

import jax
import jax.numpy as jnp
from jax import lax
from jax.experimental import pallas as pl
from jax.experimental.pallas import tpu as pltpu
from jax.sharding import PartitionSpec as P

SPLIT = 4
EPSILON = 1e-06
BF = jnp.bfloat16
F32 = jnp.float32
ROWS = 16
LANES = 128


def dot(left, right, dims=((1,), (0,))):
    return lax.dot_general(left, right, (dims, ((), ())), preferred_element_type=F32)


NT = ((1,), (1,))


def iota(shape, axis):
    return lax.broadcasted_iota(jnp.int32, shape, axis)


class Box:
    def __init__(self, capacity, width):
        self.capacity, self.width = capacity, width
        self.groups, self.extra = capacity // ROWS, capacity % ROWS
        self.cuts = ROWS // self.extra if self.extra else 1
        self.wide = -(-width // (LANES * self.cuts)) * LANES if self.extra else 0
        self.lanes = self.groups * width + self.wide
        self.pieces = -(-width // self.wide) if self.extra else 0

    def group(self, g):
        return pl.ds(g * self.width, self.width)

    def tail(self):
        return pl.ds(self.groups * self.width, self.wide)

    def piece(self, i):
        return i * self.wide, min(self.wide, self.width - i * self.wide)


def shift(value, sections=0, experts=0, flip=0):
    n_sec, n_own = lax.axis_size("section"), lax.axis_size("expert")
    n_exp = n_own // SPLIT
    if sections % n_sec == 0 and experts % n_exp == 0 and flip == 0:
        return value
    pairs = []
    for sec in range(n_sec):
        for own in range(n_own):
            exp, sl = own // SPLIT, own % SPLIT
            to = ((exp + experts) % n_exp) * SPLIT + (sl ^ flip)
            pairs.append((sec * n_own + own, ((sec + sections) % n_sec) * n_own + to))
    return lax.ppermute(value, ("section", "expert"), pairs)


def call(body, outs, *operands, scratch=(), flops=0, after=()):
    moved = sum(a.size * a.dtype.itemsize for a in operands)
    moved += sum(o.size * o.dtype.itemsize for o in outs)
    vmem = pl.BlockSpec(memory_space=pltpu.VMEM)
    read = len(operands)

    def reading(*refs):
        body(*refs[:read], *refs[read + len(after) :])

    return pl.pallas_call(
        reading,
        out_shape=list(outs),
        in_specs=[vmem] * read + [pl.BlockSpec(memory_space=pl.ANY)] * len(after),
        out_specs=[vmem] * len(outs),
        scratch_shapes=list(scratch),
        compiler_params=pltpu.CompilerParams(vmem_limit_bytes=40 * 2**20),
        cost_estimate=pl.CostEstimate(flops=flops, bytes_accessed=moved, transcendentals=0),
    )(*operands, *after)


def row_of(column):
    n = column.shape[0]
    eye = iota((n, n), 0) == iota((n, n), 1)
    return jnp.sum(jnp.where(eye, column, 0.0), axis=0, keepdims=True)


def column_of(row):
    n = row.shape[1]
    eye = iota((n, n), 0) == iota((n, n), 1)
    return jnp.sum(jnp.where(eye, row, 0.0), axis=1, keepdims=True)


def slots_of(rel, experts, capacity):
    n = rel.shape[1]
    column = column_of(rel)
    same = jnp.broadcast_to(column, (n, n)) == jnp.broadcast_to(rel, (n, n))
    before = iota((n, n), 1) < iota((n, n), 0)
    rank = jnp.sum(jnp.where(same & before, 1.0, 0.0), axis=1, keepdims=True)
    return column * capacity + rank


def pack_rows(box, slots, values, out_refs):
    n = values.shape[0]
    line = jnp.broadcast_to(row_of(slots).astype(jnp.int32), (ROWS, n))
    r = iota((ROWS, n), 0)
    for j, out in enumerate(out_refs):
        first = j * box.capacity
        for g in range(box.groups):
            sel = jnp.where(line == first + g * ROWS + r, 1.0, 0.0).astype(BF)
            out[:, box.group(g)] = dot(sel, values).astype(BF)
        if box.extra:
            total = jnp.zeros((ROWS, box.wide), F32)
            for i in range(box.pieces):
                at, size = box.piece(i)
                hit = (line == first + box.groups * ROWS + r // box.cuts) & (r % box.cuts == i)
                hit &= r // box.cuts < box.extra
                got = dot(jnp.where(hit, 1.0, 0.0).astype(BF), values[:, at : at + size])
                if size < box.wide:
                    got = jnp.concatenate([got, jnp.zeros((ROWS, box.wide - size), F32)], axis=1)
                total = total + got
            out[:, box.tail()] = total.astype(BF)


def pick_rows(box, slots, boxes, n, picked):
    count = len(boxes)
    if box.groups:
        stack = jnp.concatenate(
            [b[:, g * box.width : (g + 1) * box.width] for b in boxes for g in range(box.groups)],
            axis=0,
        )
        tall = count * box.groups * ROWS
        c = iota((n, tall), 1)
        slot = c // (box.groups * ROWS) * box.capacity + c % (box.groups * ROWS)
        sel = jnp.where(slots.astype(jnp.int32) == slot, 1.0, 0.0).astype(BF)
        picked[...] = dot(sel, stack)
    else:
        picked[...] = jnp.zeros(picked.shape, F32)
    if box.extra:
        tails = jnp.concatenate([b[:, box.groups * box.width :] for b in boxes], axis=0)
        c = iota((n, count * ROWS), 1)
        r = c % ROWS
        slot = c // ROWS * box.capacity + box.groups * ROWS + r // box.cuts
        mine = (slots.astype(jnp.int32) == slot) & (r // box.cuts < box.extra)
        for i in range(box.pieces):
            at, size = box.piece(i)
            sel = jnp.where(mine & (r % box.cuts == i), 1.0, 0.0).astype(BF)
            picked[:, at : at + size] += dot(sel, tails[:, :size])


def heights(box, count):
    extra = -(-count * box.extra // ROWS) * ROWS
    return count * box.groups * ROWS, extra


def unpack(box, refs, stack, tails, at=0):
    count = 0
    for ref in refs:
        for p in range(ref.shape[0] // ROWS):
            for g in range(box.groups):
                stack[at : at + ROWS, :] = ref[p * ROWS : (p + 1) * ROWS, box.group(g)]
                at += ROWS
            if box.extra:
                tails[count * ROWS : (count + 1) * ROWS, :] = ref[
                    p * ROWS : (p + 1) * ROWS, box.tail()
                ]
            count += 1
    if box.extra:
        extra = heights(box, count)[1]
        r = iota((extra, count * ROWS), 0)
        c = iota((extra, count * ROWS), 1)
        mine = (r // box.extra == c // ROWS) & (r % box.extra == c % ROWS // box.cuts)
        for i in range(box.pieces):
            start, size = box.piece(i)
            sel = jnp.where(mine & (c % ROWS % box.cuts == i), 1.0, 0.0).astype(BF)
            stack[at : at + extra, start : start + size] = dot(sel, tails[:, :size]).astype(BF)


def repack(box, rows, refs):
    rows = rows.astype(BF)
    at = 0
    count = 0
    for ref in refs:
        for p in range(ref.shape[0] // ROWS):
            for g in range(box.groups):
                ref[p * ROWS : (p + 1) * ROWS, box.group(g)] = rows[at : at + ROWS]
                at += ROWS
            count += 1
    if box.extra:
        extra = heights(box, count)[1]
        r = iota((count * ROWS, extra), 0)
        c = iota((count * ROWS, extra), 1)
        mine = (c // box.extra == r // ROWS) & (c % box.extra == r % ROWS // box.cuts)
        total = jnp.zeros((count * ROWS, box.wide), F32)
        for i in range(box.pieces):
            start, size = box.piece(i)
            sel = jnp.where(mine & (r % ROWS % box.cuts == i), 1.0, 0.0).astype(BF)
            got = dot(sel, rows[at:, start : start + size])
            if size < box.wide:
                pad = jnp.zeros((count * ROWS, box.wide - size), F32)
                got = jnp.concatenate([got, pad], axis=1)
            total = total + got
        total = total.astype(BF)
        count = 0
        for ref in refs:
            tall = ref.shape[0]
            ref[:, box.tail()] = total[count : count + tall]
            count += tall


def inv_rms(wide):
    return lax.rsqrt(jnp.mean(wide * wide, axis=-1, keepdims=True) + EPSILON)


def total_of(refs):
    return sum(ref[...].astype(F32) for ref in refs).astype(BF)


def start_kernel(box, experts, tokens, cot, gain, ids, mix, meta0, meta1, *boxes):
    n = tokens.shape[0]
    lane = iota((n, LANES), 1)
    mine = lax.axis_index("expert") // SPLIT
    for k, meta in enumerate((meta0, meta1)):
        rel = ids[k : k + 1, :] - mine
        rel = jnp.where(rel < 0, rel + experts, rel).astype(F32)
        slots = slots_of(rel, experts, box.capacity)
        mixes = column_of(mix[k : k + 1, :])
        meta[:n] = jnp.where(lane == 0, slots, jnp.where(lane == 1, mixes, 0.0))
    for b in range(box.width // LANES):
        meta1[n + b : n + b + 1] = gain[:, b * LANES : (b + 1) * LANES]
    wide = tokens[...].astype(F32)
    normed = (wide * inv_rms(wide) * gain[...]).astype(BF)
    crossing = boxes[2:]
    pack_rows(box, meta0[:n, 0:1], normed, [boxes[0]] + [ref.at[:ROWS] for ref in crossing])
    pack_rows(box, meta1[:n, 0:1], cot[...], [boxes[1]] + [ref.at[ROWS:] for ref in crossing])


def combine(box, meta, n, own, back, picked):
    sums = [total_of(own)] + [ref[...] for ref in back]
    pick_rows(box, meta[:n, 0:1], sums, n, picked)
    return meta[:n, 1:2] * picked[...]


def split_refs(refs, experts, outs):
    ins = refs[:-outs]
    return ins[experts - 1 :], ins[: experts - 1], refs[-outs:]


def middle_kernel(box, experts, hidden, meta, meta_out, gain, *refs):
    boxes, picked = refs[-1 - experts : -1], refs[-1]
    own, back, (after,) = split_refs(refs[: -1 - experts], experts, 1)
    n = hidden.shape[0]
    later = (hidden[...].astype(F32) + combine(box, meta, n, own, back, picked)).astype(BF)
    after[...] = later
    wide = later.astype(F32)
    normed = (wide * inv_rms(wide) * gain[...]).astype(BF)
    pack_rows(box, meta_out[:n, 0:1], normed, boxes)


def final_kernel(box, experts, hidden, meta, *refs):
    picked = refs[-1]
    own, back, (out,) = split_refs(refs[:-1], experts, 1)
    n = hidden.shape[0]
    out[...] = (hidden[...].astype(F32) + combine(box, meta, n, own, back, picked)).astype(BF)


def norm_back(hidden, gain, grad):
    wide = hidden.astype(F32)
    inv = inv_rms(wide)
    scaled = grad * gain
    along = jnp.mean(scaled * wide, axis=-1, keepdims=True)
    return inv * scaled - wide * (inv * inv * inv * along)


def gradient_kernel(box, experts, packs, grad, hidden, meta, meta_out, gain, *refs):
    boxes, picked = (refs[-1 - experts : -1] if packs else ()), refs[-1]
    own, back, (out,) = split_refs(refs[: len(refs) - 1 - len(boxes)], experts, 1)
    n = hidden.shape[0]
    d_normed = combine(box, meta, n, own, back, picked)
    if packs:
        row = jnp.concatenate([meta[n + b : n + b + 1] for b in range(box.width // LANES)], axis=1)
    else:
        row = gain[...]
    now = (grad[...].astype(F32) + norm_back(hidden[...], row, d_normed)).astype(BF)
    out[...] = now
    if packs:
        pack_rows(box, meta_out[:n, 0:1], now, boxes)


def spans(tall):
    return pl.ds(0, 2 * tall), pl.ds(tall, 2 * tall)


def gate_up(rows, pack):
    return dot(rows, pack[: 2 * (pack.shape[0] // 3)], NT)


def parts_of(both):
    units = both.shape[1] // 2
    return both[:, :units], both[:, units:]


def down_rows(both, pack):
    g, u = parts_of(both)
    return dot((jax.nn.silu(g) * u).astype(BF), pack[2 * g.shape[1] :])


def inner_of(rows, pack):
    return dot(rows, pack[2 * (pack.shape[0] // 3) :], NT)


def part_rows(d_inner, both, pack):
    g, u = parts_of(both)
    r = jax.nn.sigmoid(g)
    d_gate = d_inner * u * r * (1.0 + g * (1.0 - r))
    d_up = d_inner * g * r
    return dot(jnp.concatenate([d_gate, d_up], axis=1).astype(BF), pack[: both.shape[1]])


def read_rows(box, rows, stack, tails):
    tall = stack.shape[0] // 3
    for at, ref in enumerate(rows):
        unpack(box, [ref], stack, tails, at * tall)
    return [stack[span, :] for span in spans(tall)]


def write_rows(box, top, bottom, outs):
    tall = top.shape[0] // 2
    for ref, value in zip(outs, (top[:tall], top[tall:] + bottom[:tall], bottom[tall:])):
        repack(box, value, [ref])


def forward_kernel(box, packs, saved, rows, outs, kept, stack, tails):
    sides = read_rows(box, rows, stack, tails)
    total = []
    for side, values in enumerate(sides):
        total.append(0.0)
        for at in (2 * side, 2 * side + 1):
            both = gate_up(values, packs[at])
            kept[at][...] = both
            total[side] = total[side] + down_rows(both, packs[at])
    write_rows(box, *total, outs)


def inner_kernel(box, packs, saved, rows, outs, kept, stack, tails):
    for side, values in enumerate(read_rows(box, rows, stack, tails)):
        for at in (2 * side, 2 * side + 1):
            kept[at][...] = inner_of(values, packs[at])


def gate_back_kernel(box, packs, saved, rows, outs, kept, stack, tails):
    sides = read_rows(box, rows, stack, tails)
    total = []
    for side, values in enumerate(sides):
        total.append(0.0)
        for at in (2 * side, 2 * side + 1):
            both = gate_up(values, packs[at])
            kept[at][...] = both
            total[side] = total[side] + part_rows(saved[at][...], both, packs[at])
    write_rows(box, *total, outs)


def back_kernel(box, packs, saved, rows, outs, kept, stack, tails):
    sides = read_rows(box, rows, stack, tails)
    total = []
    for side, values in enumerate(sides):
        total.append(0.0)
        for at in (2 * side, 2 * side + 1):
            d_inner = inner_of(values, packs[at])
            total[side] = total[side] + part_rows(d_inner, saved[at][...], packs[at])
    write_rows(box, *total, outs)


def down_kernel(box, packs, saved, rows, outs, kept, stack, tails):
    total = []
    for side in range(2):
        at = 2 * side
        total.append(sum(down_rows(saved[i][...], packs[i]) for i in (at, at + 1)))
    write_rows(box, *total, outs)


def expert_call(kernel, box, packs, rows, saved=(), outs=True, kept=0, reads=True, after=(), window=None):
    width = packs[0].shape[1]
    first, size = window or (0, rows[0].shape[0])
    count = size // ROWS
    tall = sum(heights(box, count))
    boxes = jax.ShapeDtypeStruct((count * ROWS, box.lanes), BF)
    results = [boxes] * len(rows) if outs else []
    if kept:
        units = [pack.shape[0] // 3 for pack in packs]
        results += [jax.ShapeDtypeStruct((2 * tall, kept * u), F32) for u in units]
    inputs = list(packs) + list(saved) + (list(rows) if reads else [])
    n_in, n_p, n_s, n_out = len(inputs), len(packs), len(saved), len(rows) if outs else 0

    def body(*refs):
        results_refs = refs[n_in:-2]
        kernel(
            box,
            refs[:n_p],
            refs[n_p : n_p + n_s],
            [ref.at[pl.ds(first, size)] for ref in refs[n_p + n_s : n_in]],
            results_refs[:n_out],
            results_refs[n_out:],
            refs[-2],
            refs[-1],
        )

    scratch = [
        pltpu.VMEM((3 * tall, width), BF),
        pltpu.VMEM((count * ROWS, max(box.wide, LANES)), BF),
    ]
    flops = sum(2 * 2 * tall * pack.size for pack in packs)
    results = call(body, results, *inputs, scratch=scratch, flops=flops, after=after)
    return results[:n_out], results[n_out:]


def local(tokens, norm_gain, w_gate, w_up, w_down, routes, mix_weights, cotangent):
    experts = lax.axis_size("expert") // SPLIT
    n, width = tokens.shape[1:]
    capacity = n // experts + max(1, n // (16 * experts))
    box = Box(capacity, width)
    gain = norm_gain
    gate_w, up_w, down_w = w_gate[0, 0].T, w_up[0, 0].T, w_down[0, 0]
    boxed = jax.ShapeDtypeStruct((ROWS, box.lanes), BF)
    rows_bf = jax.ShapeDtypeStruct((n, width), BF)
    picked = pltpu.VMEM((n, width), F32)
    bind = functools.partial

    def joined(arrays):
        return arrays[0] if len(arrays) == 1 else jnp.concatenate(arrays, axis=0)

    fence = lax.optimization_barrier

    def crossing_of(boxes):
        return joined([shift(boxes[j - 1], experts=j) for j in range(1, experts)])

    def around(boxes):
        return [shift(boxes, flip=2), boxes, shift(boxes, flip=1)]

    def add(*values):
        return sum(v.astype(F32) for v in values).astype(BF)

    def sums(parts):
        return add(parts[1], shift(parts[0], flip=2), shift(parts[2], flip=1))

    def home(total, sections):
        return [
            shift(total[(j - 1) * ROWS : j * ROWS], sections=sections, experts=-j)
            for j in range(1, experts)
        ]

    def own_home(parts, sections):
        return [
            shift(parts[0], sections=sections, flip=2),
            shift(parts[2], sections=sections, flip=1),
            shift(parts[1], sections=sections),
        ]

    def give_back(cross, own, sections):
        total, own = fence((sums(cross), own))
        return home(total, sections) + own_home(own, sections)

    meta_shape = jax.ShapeDtypeStruct((n, LANES), F32)
    meta_long = jax.ShapeDtypeStruct((n + -(-width // LANES // 8) * 8, LANES), F32)
    units = w_gate.shape[3]
    cut = -(-units * 7 // 12 // ROWS) * ROWS
    top = jnp.concatenate([gate_w[:cut], up_w[:cut], down_w[:cut]], axis=0)
    bottom = jnp.concatenate([gate_w[cut:], up_w[cut:], down_w[cut:]], axis=0)
    packs = [top, shift(top, flip=1), bottom, shift(bottom, flip=2)]

    both = jax.ShapeDtypeStruct((2 * ROWS, box.lanes), BF)
    meta0, meta1, own_tok, own_cot, *crossing = call(
        bind(start_kernel, box, experts),
        [meta_shape, meta_long, boxed, boxed] + [both] * (experts - 1),
        tokens[0],
        cotangent[0],
        gain,
        routes[0, :, :, 0],
        mix_weights[0, :, :, 0],
        after=[top, bottom],
    )
    crossed = [shift(crossing[j - 1], experts=j) for j in range(1, experts)]
    own0 = around(own_tok)
    hops = [
        shift(meta0, sections=1),
        shift(meta1, sections=-1),
        shift(tokens[0], sections=1),
        shift(cotangent[0], sections=-1),
    ]
    packs, crossed, own0, hops = fence((packs, crossed, own0, hops))
    meta0_prev, meta1_next, tokens_prev, cot_next = hops
    cross0 = around(joined([c[:ROWS] for c in crossed]))
    cots = around(joined([own_cot] + [c[ROWS:] for c in crossed]))

    own_out, own_kept0 = expert_call(forward_kernel, box, packs, own0, kept=2)
    cross_out, cross_kept0 = expert_call(
        forward_kernel, box, packs, cross0, kept=2, after=own_out[:1]
    )
    cross_out, cots = fence((cross_out, cots))
    got = give_back(cross_out, own_out, 1)
    h1, own1, *boxes1 = call(
        bind(middle_kernel, box, experts),
        [rows_bf] + [boxed] * experts,
        tokens_prev,
        meta0_prev,
        meta1,
        gain,
        *got,
        scratch=[picked],
    )
    h1_home = shift(h1, sections=-1)
    cross1, own_z, own_x = fence(
        (crossing_of(boxes1), shift(own1, flip=2), shift(own1, flip=1))
    )
    cross1, own1 = around(cross1), [own_z, own1, own_x]
    inner = bind(expert_call, inner_kernel, box, packs, cots, outs=False, kept=1)
    own_di = inner(window=(0, ROWS))[1]
    cross_di = inner(window=(ROWS, (experts - 1) * ROWS))[1]

    gate_back = bind(expert_call, gate_back_kernel, box, packs, kept=2)
    own_grad, own_kept1 = gate_back(own1, own_di)
    cross_grad, cross_kept1 = gate_back(cross1, cross_di, after=own_grad[:1])
    got = give_back(cross_grad, own_grad, -1)
    g1, own_g, *boxes_g = call(
        bind(gradient_kernel, box, experts, True),
        [rows_bf] + [boxed] * experts,
        cot_next,
        h1_home,
        meta1_next,
        meta0,
        gain,
        *got,
        scratch=[picked],
    )

    down = bind(expert_call, down_kernel, box, packs, reads=False)
    own_fin, cross_fin = down(own1, own_kept1)[0], down(cross1, cross_kept1)[0]
    fin_sums = sums(cross_fin)
    cross_g, own_g, fin_sums = fence((crossing_of(boxes_g), own_g, fin_sums))
    cross_g, own_g = around(cross_g), around(own_g)
    fin_back = home(fin_sums, 0)
    back = bind(expert_call, back_kernel, box, packs)
    cross_grad = back(cross_g, cross_kept0)[0]
    own_grad = back(own_g, own_kept0, after=cross_grad[:1])[0]
    cross_grad, fin_back = fence((cross_grad, fin_back))
    total, own_grad, own_fin = fence((sums(cross_grad), own_grad, own_fin))
    got = home(total, 0) + own_home(own_grad, 0)
    fin_own = own_home(own_fin, 0)
    (g0,) = call(
        bind(gradient_kernel, box, experts, False),
        [rows_bf],
        g1,
        tokens[0],
        meta0,
        meta0,
        gain,
        *got,
        scratch=[picked],
    )
    (final,) = call(
        bind(final_kernel, box, experts),
        [rows_bf],
        h1,
        meta1,
        *fin_back,
        *fin_own,
        scratch=[picked],
    )
    return (final[None], g0[None])


def solution(mesh):
    in_specs = (
        P("section", "expert", None),
        P("section", None),
        P("section", "expert", None, None),
        P("section", "expert", None, None),
        P("section", "expert", None, None),
        P("section", None, "expert", None),
        P("section", None, "expert", None),
        P("section", "expert", None),
    )
    out_specs = (P("section", "expert", None), P("section", "expert", None))
    return jax.shard_map(local, mesh=mesh, in_specs=in_specs, out_specs=out_specs, check_vma=False)
```

```python
import functools

import jax
import jax.numpy as jnp
from jax import lax
from jax.experimental import pallas as pl
from jax.experimental.pallas import tpu as pltpu
from jax.sharding import PartitionSpec as P

SPLIT = 4
EPSILON = 1e-06
BF = jnp.bfloat16
F32 = jnp.float32
ROWS = 16
LANES = 128


def dot(left, right, dims=((1,), (0,))):
    return lax.dot_general(left, right, (dims, ((), ())), preferred_element_type=F32)


NT = ((1,), (1,))


def iota(shape, axis):
    return lax.broadcasted_iota(jnp.int32, shape, axis)


class Box:
    def __init__(self, capacity, width):
        self.capacity, self.width = capacity, width
        self.groups, self.extra = capacity // ROWS, capacity % ROWS
        self.cuts = ROWS // self.extra if self.extra else 1
        self.wide = -(-width // (LANES * self.cuts)) * LANES if self.extra else 0
        self.lanes = self.groups * width + self.wide
        self.pieces = -(-width // self.wide) if self.extra else 0

    def group(self, g):
        return pl.ds(g * self.width, self.width)

    def tail(self):
        return pl.ds(self.groups * self.width, self.wide)

    def piece(self, i):
        return i * self.wide, min(self.wide, self.width - i * self.wide)


def shift(value, sections=0, experts=0, flip=0):
    n_sec, n_own = lax.axis_size("section"), lax.axis_size("expert")
    n_exp = n_own // SPLIT
    if sections % n_sec == 0 and experts % n_exp == 0 and flip == 0:
        return value
    pairs = []
    for sec in range(n_sec):
        for own in range(n_own):
            exp, sl = own // SPLIT, own % SPLIT
            to = ((exp + experts) % n_exp) * SPLIT + (sl ^ flip)
            pairs.append((sec * n_own + own, ((sec + sections) % n_sec) * n_own + to))
    return lax.ppermute(value, ("section", "expert"), pairs)


def call(body, outs, *operands, scratch=(), flops=0, after=()):
    moved = sum(a.size * a.dtype.itemsize for a in operands)
    moved += sum(o.size * o.dtype.itemsize for o in outs)
    vmem = pl.BlockSpec(memory_space=pltpu.VMEM)
    read = len(operands)

    def reading(*refs):
        body(*refs[:read], *refs[read + len(after) :])

    return pl.pallas_call(
        reading,
        out_shape=list(outs),
        in_specs=[vmem] * read + [pl.BlockSpec(memory_space=pl.ANY)] * len(after),
        out_specs=[vmem] * len(outs),
        scratch_shapes=list(scratch),
        compiler_params=pltpu.CompilerParams(vmem_limit_bytes=40 * 2**20),
        cost_estimate=pl.CostEstimate(flops=flops, bytes_accessed=moved, transcendentals=0),
    )(*operands, *after)


def column_of(row):
    n = row.shape[1]
    eye = iota((n, n), 0) == iota((n, n), 1)
    return jnp.sum(jnp.where(eye, row, 0.0), axis=1, keepdims=True)


def slots_of(rel, experts, capacity):
    n = rel.shape[1]
    same = jnp.broadcast_to(column_of(rel), (n, n)) == jnp.broadcast_to(rel, (n, n))
    before = iota((n, n), 0) < iota((n, n), 1)
    rank = jnp.sum(jnp.where(same & before, 1.0, 0.0), axis=0, keepdims=True)
    return rel * capacity + rank


def terms(value):
    high = value.astype(BF).astype(F32)
    middle = (value - high).astype(BF).astype(F32)
    return high, middle, value - high - middle


def notes_of(slots, mix, gain, n, width):
    r = iota((ROWS, n), 0)
    left = jnp.where(r == 0, slots, 0.0)
    for at, term in enumerate(terms(mix)):
        left = jnp.where(r == 1 + at, term, left)
    r = iota((ROWS, width), 0)
    wide = jnp.concatenate([left, jnp.zeros((ROWS, width - n), F32)], axis=1)
    for at, term in enumerate(terms(gain)):
        wide = jnp.where(r == 4 + at, term, wide)
    return wide.astype(BF)


def slots_in(notes, n):
    return notes[:, :n].astype(F32)[0:1]


def mix_in(notes, n):
    left = notes[:, :n].astype(F32)
    return column_of(left[1:2] + left[2:3] + left[3:4])


def gain_in(notes):
    wide = notes.astype(F32)
    return wide[4:5] + wide[5:6] + wide[6:7]


def pack_rows(box, slots, values, out_refs):
    n = values.shape[0]
    line = jnp.broadcast_to(slots.astype(jnp.int32), (ROWS, n))
    r = iota((ROWS, n), 0)
    for j, out in enumerate(out_refs):
        first = j * box.capacity
        for g in range(box.groups):
            sel = jnp.where(line == first + g * ROWS + r, 1.0, 0.0).astype(BF)
            out[:, box.group(g)] = dot(sel, values).astype(BF)
        if box.extra:
            total = jnp.zeros((ROWS, box.wide), F32)
            for i in range(box.pieces):
                at, size = box.piece(i)
                hit = (line == first + box.groups * ROWS + r // box.cuts) & (r % box.cuts == i)
                hit &= r // box.cuts < box.extra
                got = dot(jnp.where(hit, 1.0, 0.0).astype(BF), values[:, at : at + size])
                if size < box.wide:
                    got = jnp.concatenate([got, jnp.zeros((ROWS, box.wide - size), F32)], axis=1)
                total = total + got
            out[:, box.tail()] = total.astype(BF)


def pick_rows(box, slots, boxes, n, picked):
    count = len(boxes)
    slots = column_of(slots)
    if box.groups:
        stack = jnp.concatenate(
            [b[:, g * box.width : (g + 1) * box.width] for b in boxes for g in range(box.groups)],
            axis=0,
        )
        tall = count * box.groups * ROWS
        c = iota((n, tall), 1)
        slot = c // (box.groups * ROWS) * box.capacity + c % (box.groups * ROWS)
        sel = jnp.where(slots.astype(jnp.int32) == slot, 1.0, 0.0).astype(BF)
        picked[...] = dot(sel, stack)
    else:
        picked[...] = jnp.zeros(picked.shape, F32)
    if box.extra:
        tails = jnp.concatenate([b[:, box.groups * box.width :] for b in boxes], axis=0)
        c = iota((n, count * ROWS), 1)
        r = c % ROWS
        slot = c // ROWS * box.capacity + box.groups * ROWS + r // box.cuts
        mine = (slots.astype(jnp.int32) == slot) & (r // box.cuts < box.extra)
        for i in range(box.pieces):
            at, size = box.piece(i)
            sel = jnp.where(mine & (r % box.cuts == i), 1.0, 0.0).astype(BF)
            picked[:, at : at + size] += dot(sel, tails[:, :size])


def heights(box, count):
    extra = -(-count * box.extra // ROWS) * ROWS
    return count * box.groups * ROWS, extra


def unpack(box, refs, stack, tails, at=0):
    count = 0
    for ref in refs:
        for p in range(ref.shape[0] // ROWS):
            for g in range(box.groups):
                stack[at : at + ROWS, :] = ref[p * ROWS : (p + 1) * ROWS, box.group(g)]
                at += ROWS
            if box.extra:
                tails[count * ROWS : (count + 1) * ROWS, :] = ref[
                    p * ROWS : (p + 1) * ROWS, box.tail()
                ]
            count += 1
    if box.extra:
        extra = heights(box, count)[1]
        r = iota((extra, count * ROWS), 0)
        c = iota((extra, count * ROWS), 1)
        mine = (r // box.extra == c // ROWS) & (r % box.extra == c % ROWS // box.cuts)
        for i in range(box.pieces):
            start, size = box.piece(i)
            sel = jnp.where(mine & (c % ROWS % box.cuts == i), 1.0, 0.0).astype(BF)
            stack[at : at + extra, start : start + size] = dot(sel, tails[:, :size]).astype(BF)


def repack(box, rows, refs):
    rows = rows.astype(BF)
    at = 0
    count = 0
    for ref in refs:
        for p in range(ref.shape[0] // ROWS):
            for g in range(box.groups):
                ref[p * ROWS : (p + 1) * ROWS, box.group(g)] = rows[at : at + ROWS]
                at += ROWS
            count += 1
    if box.extra:
        extra = heights(box, count)[1]
        r = iota((count * ROWS, extra), 0)
        c = iota((count * ROWS, extra), 1)
        mine = (c // box.extra == r // ROWS) & (c % box.extra == r % ROWS // box.cuts)
        total = jnp.zeros((count * ROWS, box.wide), F32)
        for i in range(box.pieces):
            start, size = box.piece(i)
            sel = jnp.where(mine & (r % ROWS % box.cuts == i), 1.0, 0.0).astype(BF)
            got = dot(sel, rows[at:, start : start + size])
            if size < box.wide:
                pad = jnp.zeros((count * ROWS, box.wide - size), F32)
                got = jnp.concatenate([got, pad], axis=1)
            total = total + got
        total = total.astype(BF)
        count = 0
        for ref in refs:
            tall = ref.shape[0]
            ref[:, box.tail()] = total[count : count + tall]
            count += tall


def inv_rms(wide):
    return lax.rsqrt(jnp.mean(wide * wide, axis=-1, keepdims=True) + EPSILON)


def total_of(refs):
    return sum(ref[...].astype(F32) for ref in refs).astype(BF)


def start_kernel(box, experts, tokens, cot, gain, ids, mix, ahead, notes0, notes1, *boxes):
    n, width = tokens.shape
    mine = lax.axis_index("expert") // SPLIT
    for k, notes in enumerate((notes0, notes1)):
        rel = ids[k : k + 1, :] - mine
        rel = jnp.where(rel < 0, rel + experts, rel).astype(F32)
        slots = slots_of(rel, experts, box.capacity)
        notes[...] = notes_of(slots, mix[k : k + 1, :], gain[...], n, width)
    ahead[:n] = tokens[...]
    ahead[n:] = notes0[...]
    wide = tokens[...].astype(F32)
    normed = (wide * inv_rms(wide) * gain[...]).astype(BF)
    crossing = boxes[2:]
    firsts = [boxes[0]] + [ref.at[:ROWS] for ref in crossing]
    pack_rows(box, slots_in(notes0[...], n), normed, firsts)
    seconds = [boxes[1]] + [ref.at[ROWS:] for ref in crossing]
    pack_rows(box, slots_in(notes1[...], n), cot[...], seconds)


def combine(box, notes, n, own, back, picked):
    sums = [total_of(own)] + [ref[...] for ref in back]
    pick_rows(box, slots_in(notes, n), sums, n, picked)
    return mix_in(notes, n) * picked[...]


def split_refs(refs, experts, outs):
    ins = refs[:-outs]
    return ins[experts - 1 :], ins[: experts - 1], refs[-outs:]


def middle_kernel(box, experts, arrived, cot, notes1, gain, *refs):
    boxes, picked = refs[-1 - experts : -1], refs[-1]
    own, back, (after, behind) = split_refs(refs[: -1 - experts], experts, 2)
    n = cot.shape[0]
    update = combine(box, arrived[n:], n, own, back, picked)
    later = (arrived[:n].astype(F32) + update).astype(BF)
    after[...] = later
    behind[:n] = later
    behind[n : 2 * n] = cot[...]
    behind[2 * n :] = notes1[...]
    wide = later.astype(F32)
    normed = (wide * inv_rms(wide) * gain[...]).astype(BF)
    pack_rows(box, slots_in(notes1[...], n), normed, boxes)


def final_kernel(box, experts, hidden, notes, *refs):
    picked = refs[-1]
    own, back, (out,) = split_refs(refs[:-1], experts, 1)
    n = hidden.shape[0]
    update = combine(box, notes[...], n, own, back, picked)
    out[...] = (hidden[...].astype(F32) + update).astype(BF)


def norm_back(hidden, gain, grad):
    wide = hidden.astype(F32)
    inv = inv_rms(wide)
    scaled = grad * gain
    along = jnp.mean(scaled * wide, axis=-1, keepdims=True)
    return inv * scaled - wide * (inv * inv * inv * along)


def turn_kernel(box, experts, arrived, notes0, *refs):
    boxes, picked = refs[-1 - experts : -1], refs[-1]
    own, back, (out,) = split_refs(refs[: -1 - experts], experts, 1)
    n = out.shape[0]
    notes = arrived[2 * n :]
    d_normed = combine(box, notes, n, own, back, picked)
    change = norm_back(arrived[:n], gain_in(notes), d_normed)
    now = (arrived[n : 2 * n].astype(F32) + change).astype(BF)
    out[...] = now
    pack_rows(box, slots_in(notes0[...], n), now, boxes)


def last_kernel(box, experts, grad, hidden, notes0, gain, *refs):
    picked = refs[-1]
    own, back, (out,) = split_refs(refs[:-1], experts, 1)
    n = hidden.shape[0]
    d_normed = combine(box, notes0[...], n, own, back, picked)
    change = norm_back(hidden[...], gain[...], d_normed)
    out[...] = (grad[...].astype(F32) + change).astype(BF)


def spans(tall):
    return pl.ds(0, 2 * tall), pl.ds(tall, 2 * tall)


def gate_up(rows, pack):
    return dot(rows, pack[: 2 * (pack.shape[0] // 3)], NT)


def parts_of(both):
    units = both.shape[1] // 2
    return both[:, :units], both[:, units:]


def down_rows(both, pack):
    g, u = parts_of(both)
    return dot((jax.nn.silu(g) * u).astype(BF), pack[2 * g.shape[1] :])


def inner_of(rows, pack):
    return dot(rows, pack[2 * (pack.shape[0] // 3) :], NT)


def part_rows(d_inner, both, pack):
    g, u = parts_of(both)
    r = jax.nn.sigmoid(g)
    d_gate = d_inner * u * r * (1.0 + g * (1.0 - r))
    d_up = d_inner * g * r
    return dot(jnp.concatenate([d_gate, d_up], axis=1).astype(BF), pack[: both.shape[1]])


def read_rows(box, rows, stack, tails):
    tall = stack.shape[0] // 3
    for at, ref in enumerate(rows):
        unpack(box, [ref], stack, tails, at * tall)
    return [stack[span, :] for span in spans(tall)]


def write_rows(box, top, bottom, outs):
    tall = top.shape[0] // 2
    for ref, value in zip(outs, (top[:tall], top[tall:] + bottom[:tall], bottom[tall:])):
        repack(box, value, [ref])


def forward_kernel(box, packs, saved, rows, outs, kept, stack, tails):
    sides = read_rows(box, rows, stack, tails)
    total = []
    for side, values in enumerate(sides):
        total.append(0.0)
        for at in (2 * side, 2 * side + 1):
            both = gate_up(values, packs[at])
            kept[at][...] = both
            total[side] = total[side] + down_rows(both, packs[at])
    write_rows(box, *total, outs)


def inner_kernel(box, packs, saved, rows, outs, kept, stack, tails):
    for side, values in enumerate(read_rows(box, rows, stack, tails)):
        for at in (2 * side, 2 * side + 1):
            kept[at][...] = inner_of(values, packs[at])


def gate_back_kernel(box, packs, saved, rows, outs, kept, stack, tails):
    sides = read_rows(box, rows, stack, tails)
    total = []
    for side, values in enumerate(sides):
        total.append(0.0)
        for at in (2 * side, 2 * side + 1):
            both = gate_up(values, packs[at])
            kept[at][...] = both
            total[side] = total[side] + part_rows(saved[at][...], both, packs[at])
    write_rows(box, *total, outs)


def back_kernel(box, packs, saved, rows, outs, kept, stack, tails):
    sides = read_rows(box, rows, stack, tails)
    total = []
    for side, values in enumerate(sides):
        total.append(0.0)
        for at in (2 * side, 2 * side + 1):
            d_inner = inner_of(values, packs[at])
            total[side] = total[side] + part_rows(d_inner, saved[at][...], packs[at])
    write_rows(box, *total, outs)


def down_kernel(box, packs, saved, rows, outs, kept, stack, tails):
    total = []
    for side in range(2):
        at = 2 * side
        total.append(sum(down_rows(saved[i][...], packs[i]) for i in (at, at + 1)))
    write_rows(box, *total, outs)


def expert_call(kernel, box, packs, rows, saved=(), outs=True, kept=0, reads=True, after=(), window=None):
    width = packs[0].shape[1]
    first, size = window or (0, rows[0].shape[0])
    count = size // ROWS
    tall = sum(heights(box, count))
    boxes = jax.ShapeDtypeStruct((count * ROWS, box.lanes), BF)
    results = [boxes] * len(rows) if outs else []
    if kept:
        units = [pack.shape[0] // 3 for pack in packs]
        results += [jax.ShapeDtypeStruct((2 * tall, kept * u), F32) for u in units]
    inputs = list(packs) + list(saved) + (list(rows) if reads else [])
    n_in, n_p, n_s, n_out = len(inputs), len(packs), len(saved), len(rows) if outs else 0

    def body(*refs):
        results_refs = refs[n_in:-2]
        kernel(
            box,
            refs[:n_p],
            refs[n_p : n_p + n_s],
            [ref.at[pl.ds(first, size)] for ref in refs[n_p + n_s : n_in]],
            results_refs[:n_out],
            results_refs[n_out:],
            refs[-2],
            refs[-1],
        )

    scratch = [
        pltpu.VMEM((3 * tall, width), BF),
        pltpu.VMEM((count * ROWS, max(box.wide, LANES)), BF),
    ]
    flops = sum(2 * 2 * tall * pack.size for pack in packs)
    results = call(body, results, *inputs, scratch=scratch, flops=flops, after=after)
    return results[:n_out], results[n_out:]


def local(tokens, norm_gain, w_gate, w_up, w_down, routes, mix_weights, cotangent):
    experts = lax.axis_size("expert") // SPLIT
    n, width = tokens.shape[1:]
    capacity = n // experts + max(1, n // (16 * experts))
    box = Box(capacity, width)
    gain = norm_gain
    gate_w, up_w, down_w = w_gate[0, 0].T, w_up[0, 0].T, w_down[0, 0]
    boxed = jax.ShapeDtypeStruct((ROWS, box.lanes), BF)
    picked = pltpu.VMEM((n, width), F32)
    bind = functools.partial

    def joined(arrays):
        return arrays[0] if len(arrays) == 1 else jnp.concatenate(arrays, axis=0)

    fence = lax.optimization_barrier

    def crossing_of(boxes):
        return joined([shift(boxes[j - 1], experts=j) for j in range(1, experts)])

    def around(boxes):
        return [shift(boxes, flip=2), boxes, shift(boxes, flip=1)]

    def add(*values):
        return sum(v.astype(F32) for v in values).astype(BF)

    def sums(parts):
        return add(parts[1], shift(parts[0], flip=2), shift(parts[2], flip=1))

    def home(total, sections):
        return [
            shift(total[(j - 1) * ROWS : j * ROWS], sections=sections, experts=-j)
            for j in range(1, experts)
        ]

    def own_home(parts, sections):
        return [
            shift(parts[0], sections=sections, flip=2),
            shift(parts[2], sections=sections, flip=1),
            shift(parts[1], sections=sections),
        ]

    def give_back(cross, own, sections):
        total, own = fence((sums(cross), own))
        return home(total, sections) + own_home(own, sections)

    units = w_gate.shape[3]
    cut = -(-units * 7 // 12 // ROWS) * ROWS
    top = jnp.concatenate([gate_w[:cut], up_w[:cut], down_w[:cut]], axis=0)
    bottom = jnp.concatenate([gate_w[cut:], up_w[cut:], down_w[cut:]], axis=0)
    packs = [top, shift(top, flip=1), bottom, shift(bottom, flip=2)]

    def rows_of(count):
        return jax.ShapeDtypeStruct((count, width), BF)

    both = jax.ShapeDtypeStruct((2 * ROWS, box.lanes), BF)
    ahead, notes0, notes1, own_tok, own_cot, *crossing = call(
        bind(start_kernel, box, experts),
        [rows_of(n + ROWS), rows_of(ROWS), rows_of(ROWS), boxed, boxed] + [both] * (experts - 1),
        tokens[0],
        cotangent[0],
        gain,
        routes[0, :, :, 0],
        mix_weights[0, :, :, 0],
        after=[top, bottom],
    )
    crossed = [shift(crossing[j - 1], experts=j) for j in range(1, experts)]
    own0 = around(own_tok)
    packs, crossed, own0 = fence((packs, crossed, own0))
    cross0 = around(joined([c[:ROWS] for c in crossed]))
    cots = around(joined([own_cot] + [c[ROWS:] for c in crossed]))

    own_out, own_kept0 = expert_call(forward_kernel, box, packs, own0, kept=2)
    cross_out, cross_kept0 = expert_call(
        forward_kernel, box, packs, cross0, kept=2, after=own_out[:1]
    )
    cross_out, cots, ahead = fence((cross_out, cots, ahead))
    arrived0 = shift(ahead, sections=1)
    got = give_back(cross_out, own_out, 1)
    h1, behind, own1, *boxes1 = call(
        bind(middle_kernel, box, experts),
        [rows_of(n), rows_of(2 * n + ROWS)] + [boxed] * experts,
        arrived0,
        cotangent[0],
        notes1,
        gain,
        *got,
        scratch=[picked],
    )
    cross1, own_z, own_x = fence(
        (crossing_of(boxes1), shift(own1, flip=2), shift(own1, flip=1))
    )
    cross1, own1 = around(cross1), [own_z, own1, own_x]
    inner = bind(expert_call, inner_kernel, box, packs, cots, outs=False, kept=1)
    own_di = inner(window=(0, ROWS))[1]
    cross_di = inner(window=(ROWS, (experts - 1) * ROWS))[1]

    gate_back = bind(expert_call, gate_back_kernel, box, packs, kept=2)
    own_grad, own_kept1 = gate_back(own1, own_di)
    cross_grad, cross_kept1 = gate_back(cross1, cross_di, after=own_grad[:1])
    down = bind(expert_call, down_kernel, box, packs, reads=False)
    cross_fin = down(cross1, cross_kept1)[0]
    arrived1 = shift(behind, sections=-1)
    total = sums(cross_grad)
    back_grad = home(total, -1)
    own_grad, fin_sums = fence((own_grad, sums(cross_fin)))
    got = back_grad + own_home(own_grad, -1)
    fin_back = home(fin_sums, 0)
    own_fin = down(own1, own_kept1)[0]
    g1, own_g, *boxes_g = call(
        bind(turn_kernel, box, experts),
        [rows_of(n)] + [boxed] * experts,
        arrived1,
        notes0,
        *got,
        scratch=[picked],
    )

    cross_g, own_g, fin_back = fence((crossing_of(boxes_g), own_g, fin_back))
    cross_g, own_g = around(cross_g), around(own_g)
    back = bind(expert_call, back_kernel, box, packs)
    cross_grad = back(cross_g, cross_kept0)[0]
    own_grad = back(own_g, own_kept0, after=cross_grad[:1])[0]
    total, own_grad, own_fin = fence((sums(cross_grad), own_grad, own_fin))
    got = home(total, 0) + own_home(own_grad, 0)
    fin_own = own_home(own_fin, 0)
    (g0,) = call(
        bind(last_kernel, box, experts),
        [rows_of(n)],
        g1,
        tokens[0],
        notes0,
        gain,
        *got,
        scratch=[picked],
    )
    (final,) = call(
        bind(final_kernel, box, experts),
        [rows_of(n)],
        h1,
        notes1,
        *fin_back,
        *fin_own,
        scratch=[picked],
    )
    return (final[None], g0[None])


def solution(mesh):
    in_specs = (
        P("section", "expert", None),
        P("section", None),
        P("section", "expert", None, None),
        P("section", "expert", None, None),
        P("section", "expert", None, None),
        P("section", None, "expert", None),
        P("section", None, "expert", None),
        P("section", "expert", None),
    )
    out_specs = (P("section", "expert", None), P("section", "expert", None))
    return jax.shard_map(local, mesh=mesh, in_specs=in_specs, out_specs=out_specs, check_vma=False)
```

```python
import functools

import jax
import jax.numpy as jnp
from jax import lax
from jax.experimental import pallas as pl
from jax.experimental.pallas import tpu as pltpu
from jax.sharding import PartitionSpec as P

SPLIT = 4
EPSILON = 1e-06
BF = jnp.bfloat16
F32 = jnp.float32
ROWS = 16
LANES = 128


def dot(left, right, dims=((1,), (0,))):
    return lax.dot_general(left, right, (dims, ((), ())), preferred_element_type=F32)


NT = ((1,), (1,))


def iota(shape, axis):
    return lax.broadcasted_iota(jnp.int32, shape, axis)


class Box:
    def __init__(self, capacity, width):
        self.capacity, self.width = capacity, width
        self.groups, self.extra = capacity // ROWS, capacity % ROWS
        self.cuts = ROWS // self.extra if self.extra else 1
        self.wide = -(-width // (LANES * self.cuts)) * LANES if self.extra else 0
        self.lanes = self.groups * width + self.wide
        self.pieces = -(-width // self.wide) if self.extra else 0

    def group(self, g):
        return pl.ds(g * self.width, self.width)

    def tail(self):
        return pl.ds(self.groups * self.width, self.wide)

    def piece(self, i):
        return i * self.wide, min(self.wide, self.width - i * self.wide)


def shift(value, sections=0, experts=0, flip=0):
    n_sec, n_own = lax.axis_size("section"), lax.axis_size("expert")
    n_exp = n_own // SPLIT
    if sections % n_sec == 0 and experts % n_exp == 0 and flip == 0:
        return value
    pairs = []
    for sec in range(n_sec):
        for own in range(n_own):
            exp, sl = own // SPLIT, own % SPLIT
            to = ((exp + experts) % n_exp) * SPLIT + (sl ^ flip)
            pairs.append((sec * n_own + own, ((sec + sections) % n_sec) * n_own + to))
    return lax.ppermute(value, ("section", "expert"), pairs)


def call(body, outs, *operands, scratch=(), flops=0, after=()):
    moved = sum(a.size * a.dtype.itemsize for a in operands)
    moved += sum(o.size * o.dtype.itemsize for o in outs)
    vmem = pl.BlockSpec(memory_space=pltpu.VMEM)
    read = len(operands)

    def reading(*refs):
        body(*refs[:read], *refs[read + len(after) :])

    return pl.pallas_call(
        reading,
        out_shape=list(outs),
        in_specs=[vmem] * read + [pl.BlockSpec(memory_space=pl.ANY)] * len(after),
        out_specs=[vmem] * len(outs),
        scratch_shapes=list(scratch),
        compiler_params=pltpu.CompilerParams(vmem_limit_bytes=40 * 2**20),
        cost_estimate=pl.CostEstimate(flops=flops, bytes_accessed=moved, transcendentals=0),
    )(*operands, *after)


def column_of(row):
    n = row.shape[1]
    eye = iota((n, n), 0) == iota((n, n), 1)
    return jnp.sum(jnp.where(eye, row, 0.0), axis=1, keepdims=True)


def slots_of(rel, experts, capacity):
    n = rel.shape[1]
    same = jnp.broadcast_to(column_of(rel), (n, n)) == jnp.broadcast_to(rel, (n, n))
    before = iota((n, n), 0) < iota((n, n), 1)
    rank = jnp.sum(jnp.where(same & before, 1.0, 0.0), axis=0, keepdims=True)
    return rel * capacity + rank


def terms(value):
    high = value.astype(BF).astype(F32)
    middle = (value - high).astype(BF).astype(F32)
    return high, middle, value - high - middle


def notes_of(slots, mix, gain, n, width):
    r = iota((ROWS, n), 0)
    left = jnp.where(r == 0, slots, 0.0)
    for at, term in enumerate(terms(mix)):
        left = jnp.where(r == 1 + at, term, left)
    r = iota((ROWS, width), 0)
    wide = jnp.concatenate([left, jnp.zeros((ROWS, width - n), F32)], axis=1)
    for at, term in enumerate(terms(gain)):
        wide = jnp.where(r == 4 + at, term, wide)
    return wide.astype(BF)


def slots_in(notes, n):
    return notes[:, :n].astype(F32)[0:1]


def mix_in(notes, n):
    left = notes[:, :n].astype(F32)
    return column_of(left[1:2] + left[2:3] + left[3:4])


def gain_in(notes):
    wide = notes.astype(F32)
    return wide[4:5] + wide[5:6] + wide[6:7]


def pack_rows(box, slots, values, out_refs):
    n = values.shape[0]
    line = jnp.broadcast_to(slots.astype(jnp.int32), (ROWS, n))
    r = iota((ROWS, n), 0)
    for j, out in enumerate(out_refs):
        first = j * box.capacity
        for g in range(box.groups):
            sel = jnp.where(line == first + g * ROWS + r, 1.0, 0.0).astype(BF)
            out[:, box.group(g)] = dot(sel, values).astype(BF)
        if box.extra:
            total = jnp.zeros((ROWS, box.wide), F32)
            for i in range(box.pieces):
                at, size = box.piece(i)
                hit = (line == first + box.groups * ROWS + r // box.cuts) & (r % box.cuts == i)
                hit &= r // box.cuts < box.extra
                got = dot(jnp.where(hit, 1.0, 0.0).astype(BF), values[:, at : at + size])
                if size < box.wide:
                    got = jnp.concatenate([got, jnp.zeros((ROWS, box.wide - size), F32)], axis=1)
                total = total + got
            out[:, box.tail()] = total.astype(BF)


def pick_rows(box, slots, boxes, n, picked):
    count = len(boxes)
    slots = column_of(slots)
    if box.groups:
        stack = jnp.concatenate(
            [b[:, g * box.width : (g + 1) * box.width] for b in boxes for g in range(box.groups)],
            axis=0,
        )
        tall = count * box.groups * ROWS
        c = iota((n, tall), 1)
        slot = c // (box.groups * ROWS) * box.capacity + c % (box.groups * ROWS)
        sel = jnp.where(slots.astype(jnp.int32) == slot, 1.0, 0.0).astype(BF)
        picked[...] = dot(sel, stack)
    else:
        picked[...] = jnp.zeros(picked.shape, F32)
    if box.extra:
        tails = jnp.concatenate([b[:, box.groups * box.width :] for b in boxes], axis=0)
        c = iota((n, count * ROWS), 1)
        r = c % ROWS
        slot = c // ROWS * box.capacity + box.groups * ROWS + r // box.cuts
        mine = (slots.astype(jnp.int32) == slot) & (r // box.cuts < box.extra)
        for i in range(box.pieces):
            at, size = box.piece(i)
            sel = jnp.where(mine & (r % box.cuts == i), 1.0, 0.0).astype(BF)
            picked[:, at : at + size] += dot(sel, tails[:, :size])


def heights(box, count):
    extra = -(-count * box.extra // ROWS) * ROWS
    return count * box.groups * ROWS, extra


def unpack(box, refs, stack, tails, at=0):
    count = 0
    for ref in refs:
        for p in range(ref.shape[0] // ROWS):
            for g in range(box.groups):
                stack[at : at + ROWS, :] = ref[p * ROWS : (p + 1) * ROWS, box.group(g)]
                at += ROWS
            if box.extra:
                tails[count * ROWS : (count + 1) * ROWS, :] = ref[
                    p * ROWS : (p + 1) * ROWS, box.tail()
                ]
            count += 1
    if box.extra:
        extra = heights(box, count)[1]
        r = iota((extra, count * ROWS), 0)
        c = iota((extra, count * ROWS), 1)
        mine = (r // box.extra == c // ROWS) & (r % box.extra == c % ROWS // box.cuts)
        for i in range(box.pieces):
            start, size = box.piece(i)
            sel = jnp.where(mine & (c % ROWS % box.cuts == i), 1.0, 0.0).astype(BF)
            stack[at : at + extra, start : start + size] = dot(sel, tails[:, :size]).astype(BF)


def repack(box, rows, refs):
    rows = rows.astype(BF)
    at = 0
    count = 0
    for ref in refs:
        for p in range(ref.shape[0] // ROWS):
            for g in range(box.groups):
                ref[p * ROWS : (p + 1) * ROWS, box.group(g)] = rows[at : at + ROWS]
                at += ROWS
            count += 1
    if box.extra:
        extra = heights(box, count)[1]
        r = iota((count * ROWS, extra), 0)
        c = iota((count * ROWS, extra), 1)
        mine = (c // box.extra == r // ROWS) & (c % box.extra == r % ROWS // box.cuts)
        total = jnp.zeros((count * ROWS, box.wide), F32)
        for i in range(box.pieces):
            start, size = box.piece(i)
            sel = jnp.where(mine & (r % ROWS % box.cuts == i), 1.0, 0.0).astype(BF)
            got = dot(sel, rows[at:, start : start + size])
            if size < box.wide:
                pad = jnp.zeros((count * ROWS, box.wide - size), F32)
                got = jnp.concatenate([got, pad], axis=1)
            total = total + got
        total = total.astype(BF)
        count = 0
        for ref in refs:
            tall = ref.shape[0]
            ref[:, box.tail()] = total[count : count + tall]
            count += tall


def inv_rms(wide):
    return lax.rsqrt(jnp.mean(wide * wide, axis=-1, keepdims=True) + EPSILON)


def total_of(refs):
    return sum(ref[...].astype(F32) for ref in refs).astype(BF)


def start_kernel(box, experts, tokens, cot, gain, ids, mix, ahead, notes0, notes1, *boxes):
    n, width = tokens.shape
    mine = lax.axis_index("expert") // SPLIT
    for k, notes in enumerate((notes0, notes1)):
        rel = ids[k : k + 1, :] - mine
        rel = jnp.where(rel < 0, rel + experts, rel).astype(F32)
        slots = slots_of(rel, experts, box.capacity)
        notes[...] = notes_of(slots, mix[k : k + 1, :], gain[...], n, width)
    ahead[:n] = tokens[...]
    ahead[n:] = notes0[...]
    wide = tokens[...].astype(F32)
    normed = (wide * inv_rms(wide) * gain[...]).astype(BF)
    crossing = boxes[2:]
    firsts = [boxes[0]] + [ref.at[:ROWS] for ref in crossing]
    pack_rows(box, slots_in(notes0[...], n), normed, firsts)
    seconds = [boxes[1]] + [ref.at[ROWS:] for ref in crossing]
    pack_rows(box, slots_in(notes1[...], n), cot[...], seconds)


def combine(box, notes, n, own, back, picked):
    sums = [total_of(own)] + [ref[...] for ref in back]
    pick_rows(box, slots_in(notes, n), sums, n, picked)
    return mix_in(notes, n) * picked[...]


def split_refs(refs, experts, outs):
    ins = refs[:-outs]
    return ins[experts - 1 :], ins[: experts - 1], refs[-outs:]


def middle_kernel(box, experts, arrived, cot, notes1, gain, *refs):
    boxes, picked = refs[-1 - experts : -1], refs[-1]
    own, back, (after, behind) = split_refs(refs[: -1 - experts], experts, 2)
    n = cot.shape[0]
    update = combine(box, arrived[n:], n, own, back, picked)
    later = (arrived[:n].astype(F32) + update).astype(BF)
    after[...] = later
    behind[:n] = later
    behind[n : 2 * n] = cot[...]
    behind[2 * n :] = notes1[...]
    wide = later.astype(F32)
    normed = (wide * inv_rms(wide) * gain[...]).astype(BF)
    pack_rows(box, slots_in(notes1[...], n), normed, boxes)


def final_kernel(box, experts, hidden, notes, *refs):
    picked = refs[-1]
    own, back, (out,) = split_refs(refs[:-1], experts, 1)
    n = hidden.shape[0]
    update = combine(box, notes[...], n, own, back, picked)
    out[...] = (hidden[...].astype(F32) + update).astype(BF)


def norm_back(hidden, gain, grad):
    wide = hidden.astype(F32)
    inv = inv_rms(wide)
    scaled = grad * gain
    along = jnp.mean(scaled * wide, axis=-1, keepdims=True)
    return inv * scaled - wide * (inv * inv * inv * along)


def turn_kernel(box, experts, arrived, notes0, *refs):
    boxes, picked = refs[-1 - experts : -1], refs[-1]
    own, back, (out,) = split_refs(refs[: -1 - experts], experts, 1)
    n = out.shape[0]
    notes = arrived[2 * n :]
    d_normed = combine(box, notes, n, own, back, picked)
    change = norm_back(arrived[:n], gain_in(notes), d_normed)
    now = (arrived[n : 2 * n].astype(F32) + change).astype(BF)
    out[...] = now
    pack_rows(box, slots_in(notes0[...], n), now, boxes)


def last_kernel(box, experts, grad, hidden, notes0, gain, *refs):
    picked = refs[-1]
    own, back, (out,) = split_refs(refs[:-1], experts, 1)
    n = hidden.shape[0]
    d_normed = combine(box, notes0[...], n, own, back, picked)
    change = norm_back(hidden[...], gain[...], d_normed)
    out[...] = (grad[...].astype(F32) + change).astype(BF)


def spans(tall):
    return pl.ds(0, 2 * tall), pl.ds(tall, 2 * tall)


def gate_up(rows, pack):
    return dot(rows, pack[: 2 * (pack.shape[0] // 3)], NT)


def parts_of(both):
    units = both.shape[1] // 2
    return both[:, :units], both[:, units:]


def down_rows(both, pack):
    g, u = parts_of(both)
    return dot((jax.nn.silu(g) * u).astype(BF), pack[2 * g.shape[1] :])


def inner_of(rows, pack):
    return dot(rows, pack[2 * (pack.shape[0] // 3) :], NT)


def part_rows(d_inner, both, pack):
    g, u = parts_of(both)
    r = jax.nn.sigmoid(g)
    d_gate = d_inner * u * r * (1.0 + g * (1.0 - r))
    d_up = d_inner * g * r
    return dot(jnp.concatenate([d_gate, d_up], axis=1).astype(BF), pack[: both.shape[1]])


def read_rows(box, rows, stack, tails):
    tall = stack.shape[0] // 3
    for at, ref in enumerate(rows):
        unpack(box, [ref], stack, tails, at * tall)
    return [stack[span, :] for span in spans(tall)]


def write_rows(box, top, bottom, outs):
    tall = top.shape[0] // 2
    for ref, value in zip(outs, (top[:tall], top[tall:] + bottom[:tall], bottom[tall:])):
        repack(box, value, [ref])


def forward_kernel(box, packs, saved, rows, outs, kept, stack, tails):
    sides = read_rows(box, rows, stack, tails)
    total = []
    for side, values in enumerate(sides):
        total.append(0.0)
        for at in (2 * side, 2 * side + 1):
            both = gate_up(values, packs[at])
            kept[at][...] = both
            total[side] = total[side] + down_rows(both, packs[at])
    write_rows(box, *total, outs)


def inner_kernel(box, packs, saved, rows, outs, kept, stack, tails):
    for side, values in enumerate(read_rows(box, rows, stack, tails)):
        for at in (2 * side, 2 * side + 1):
            kept[at][...] = inner_of(values, packs[at])


def gate_back_kernel(box, packs, saved, rows, outs, kept, stack, tails):
    sides = read_rows(box, rows, stack, tails)
    total = []
    for side, values in enumerate(sides):
        total.append(0.0)
        for at in (2 * side, 2 * side + 1):
            both = gate_up(values, packs[at])
            kept[at][...] = both
            total[side] = total[side] + part_rows(saved[at][...], both, packs[at])
    write_rows(box, *total, outs)


def back_kernel(box, packs, saved, rows, outs, kept, stack, tails):
    sides = read_rows(box, rows, stack, tails)
    total = []
    for side, values in enumerate(sides):
        total.append(0.0)
        for at in (2 * side, 2 * side + 1):
            d_inner = inner_of(values, packs[at])
            total[side] = total[side] + part_rows(d_inner, saved[at][...], packs[at])
    write_rows(box, *total, outs)


def down_kernel(box, packs, saved, rows, outs, kept, stack, tails):
    total = []
    for side in range(2):
        at = 2 * side
        total.append(sum(down_rows(saved[i][...], packs[i]) for i in (at, at + 1)))
    write_rows(box, *total, outs)


def expert_call(kernel, box, packs, rows, saved=(), outs=True, kept=0, reads=True, after=(), window=None):
    width = packs[0].shape[1]
    first, size = window or (0, rows[0].shape[0])
    count = size // ROWS
    tall = sum(heights(box, count))
    boxes = jax.ShapeDtypeStruct((count * ROWS, box.lanes), BF)
    results = [boxes] * len(rows) if outs else []
    if kept:
        units = [pack.shape[0] // 3 for pack in packs]
        results += [jax.ShapeDtypeStruct((2 * tall, kept * u), F32) for u in units]
    inputs = list(packs) + list(saved) + (list(rows) if reads else [])
    n_in, n_p, n_s, n_out = len(inputs), len(packs), len(saved), len(rows) if outs else 0

    def body(*refs):
        results_refs = refs[n_in:-2]
        kernel(
            box,
            refs[:n_p],
            refs[n_p : n_p + n_s],
            [ref.at[pl.ds(first, size)] for ref in refs[n_p + n_s : n_in]],
            results_refs[:n_out],
            results_refs[n_out:],
            refs[-2],
            refs[-1],
        )

    scratch = [
        pltpu.VMEM((3 * tall, width), BF),
        pltpu.VMEM((count * ROWS, max(box.wide, LANES)), BF),
    ]
    flops = sum(2 * 2 * tall * pack.size for pack in packs)
    results = call(body, results, *inputs, scratch=scratch, flops=flops, after=after)
    return results[:n_out], results[n_out:]


def local(tokens, norm_gain, w_gate, w_up, w_down, routes, mix_weights, cotangent):
    experts = lax.axis_size("expert") // SPLIT
    n, width = tokens.shape[1:]
    capacity = n // experts + max(1, n // (16 * experts))
    box = Box(capacity, width)
    gain = norm_gain
    gate_w, up_w, down_w = w_gate[0, 0].T, w_up[0, 0].T, w_down[0, 0]
    boxed = jax.ShapeDtypeStruct((ROWS, box.lanes), BF)
    picked = pltpu.VMEM((n, width), F32)
    bind = functools.partial

    def joined(arrays):
        return arrays[0] if len(arrays) == 1 else jnp.concatenate(arrays, axis=0)

    fence = lax.optimization_barrier

    def crossing_of(boxes):
        return joined([shift(boxes[j - 1], experts=j) for j in range(1, experts)])

    def around(boxes):
        return [shift(boxes, flip=2), boxes, shift(boxes, flip=1)]

    def add(*values):
        return sum(v.astype(F32) for v in values).astype(BF)

    def sums(parts):
        return add(parts[1], shift(parts[0], flip=2), shift(parts[2], flip=1))

    def home(total, sections):
        return [
            shift(total[(j - 1) * ROWS : j * ROWS], sections=sections, experts=-j)
            for j in range(1, experts)
        ]

    def own_home(parts, sections):
        return [
            shift(parts[0], sections=sections, flip=2),
            shift(parts[2], sections=sections, flip=1),
            shift(parts[1], sections=sections),
        ]

    def give_back(cross, own, sections):
        total, own = fence((sums(cross), own))
        return home(total, sections) + own_home(own, sections)

    units = w_gate.shape[3]
    cut = -(-units * 7 // 12 // ROWS) * ROWS
    top = jnp.concatenate([gate_w[:cut], up_w[:cut], down_w[:cut]], axis=0)
    bottom = jnp.concatenate([gate_w[cut:], up_w[cut:], down_w[cut:]], axis=0)
    packs = [top, shift(top, flip=1), bottom, shift(bottom, flip=2)]

    def rows_of(count):
        return jax.ShapeDtypeStruct((count, width), BF)

    both = jax.ShapeDtypeStruct((2 * ROWS, box.lanes), BF)
    ahead, notes0, notes1, own_tok, own_cot, *crossing = call(
        bind(start_kernel, box, experts),
        [rows_of(n + ROWS), rows_of(ROWS), rows_of(ROWS), boxed, boxed] + [both] * (experts - 1),
        tokens[0],
        cotangent[0],
        gain,
        routes[0, :, :, 0],
        mix_weights[0, :, :, 0],
        after=[top, bottom],
    )
    crossed = [shift(crossing[j - 1], experts=j) for j in range(1, experts)]
    own0 = around(own_tok)
    packs, crossed, own0 = fence((packs, crossed, own0))
    cross0 = around(joined([c[:ROWS] for c in crossed]))
    cots = joined([own_cot] + [c[ROWS:] for c in crossed])
    cross0, cots = fence((cross0, cots))
    cots = around(cots)

    own_out, own_kept0 = expert_call(forward_kernel, box, packs, own0, kept=2)
    cross_out, cross_kept0 = expert_call(
        forward_kernel, box, packs, cross0, kept=2, after=own_out[:1]
    )
    cross_out, cots, ahead = fence((cross_out, cots, ahead))
    arrived0 = shift(ahead, sections=1)
    got = give_back(cross_out, own_out, 1)
    h1, behind, own1, *boxes1 = call(
        bind(middle_kernel, box, experts),
        [rows_of(n), rows_of(2 * n + ROWS)] + [boxed] * experts,
        arrived0,
        cotangent[0],
        notes1,
        gain,
        *got,
        scratch=[picked],
    )
    cross1, own_z, own_x = fence(
        (crossing_of(boxes1), shift(own1, flip=2), shift(own1, flip=1))
    )
    cross1, own1 = around(cross1), [own_z, own1, own_x]
    inner = bind(expert_call, inner_kernel, box, packs, cots, outs=False, kept=1)
    own_di = inner(window=(0, ROWS))[1]
    cross_di = inner(window=(ROWS, (experts - 1) * ROWS))[1]

    gate_back = bind(expert_call, gate_back_kernel, box, packs, kept=2)
    own_grad, own_kept1 = gate_back(own1, own_di)
    cross_grad, cross_kept1 = gate_back(cross1, cross_di, after=own_grad[:1])
    down = bind(expert_call, down_kernel, box, packs, reads=False)
    cross_fin = down(cross1, cross_kept1)[0]
    arrived1 = shift(behind, sections=-1)
    got = give_back(cross_grad, own_grad, -1)
    got[: experts - 1], fin_sums = fence((got[: experts - 1], sums(cross_fin)))
    own_fin = down(own1, own_kept1)[0]
    g1, own_g, *boxes_g = call(
        bind(turn_kernel, box, experts),
        [rows_of(n)] + [boxed] * experts,
        arrived1,
        notes0,
        *got,
        scratch=[picked],
    )

    cross_g, own_z, own_x = fence(
        (crossing_of(boxes_g), shift(own_g, flip=2), shift(own_g, flip=1))
    )
    cross_g, own_g = around(cross_g), [own_z, own_g, own_x]
    cross_g, fin_sums = fence((cross_g, fin_sums))
    fin_back = home(fin_sums, 0)
    back = bind(expert_call, back_kernel, box, packs)
    own_grad = back(own_g, own_kept0)[0]
    cross_grad = back(cross_g, cross_kept0, after=own_grad[:1])[0]
    total, own_grad, own_fin, fin_back = fence((sums(cross_grad), own_grad, own_fin, fin_back))
    got = home(total, 0) + own_home(own_grad, 0)
    fin_own = own_home(own_fin, 0)
    (g0,) = call(
        bind(last_kernel, box, experts),
        [rows_of(n)],
        g1,
        tokens[0],
        notes0,
        gain,
        *got,
        scratch=[picked],
    )
    (final,) = call(
        bind(final_kernel, box, experts),
        [rows_of(n)],
        h1,
        notes1,
        *fin_back,
        *fin_own,
        scratch=[picked],
    )
    return (final[None], g0[None])


def solution(mesh):
    in_specs = (
        P("section", "expert", None),
        P("section", None),
        P("section", "expert", None, None),
        P("section", "expert", None, None),
        P("section", "expert", None, None),
        P("section", None, "expert", None),
        P("section", None, "expert", None),
        P("section", "expert", None),
    )
    out_specs = (P("section", "expert", None), P("section", "expert", None))
    return jax.shard_map(local, mesh=mesh, in_specs=in_specs, out_specs=out_specs, check_vma=False)
```

```python
import functools

import jax
import jax.numpy as jnp
from jax import lax
from jax.experimental import pallas as pl
from jax.experimental.pallas import tpu as pltpu
from jax.sharding import PartitionSpec as P

SPLIT = 4
EPSILON = 1e-06
BF = jnp.bfloat16
F32 = jnp.float32
ROWS = 16
LANES = 128


def dot(left, right, dims=((1,), (0,))):
    return lax.dot_general(left, right, (dims, ((), ())), preferred_element_type=F32)


NT = ((1,), (1,))


def iota(shape, axis):
    return lax.broadcasted_iota(jnp.int32, shape, axis)


class Box:
    def __init__(self, capacity, width):
        self.capacity, self.width = capacity, width
        self.groups, self.extra = capacity // ROWS, capacity % ROWS
        self.cuts = ROWS // self.extra if self.extra else 1
        self.wide = -(-width // (LANES * self.cuts)) * LANES if self.extra else 0
        self.lanes = self.groups * width + self.wide
        self.pieces = -(-width // self.wide) if self.extra else 0

    def group(self, g):
        return pl.ds(g * self.width, self.width)

    def tail(self):
        return pl.ds(self.groups * self.width, self.wide)

    def piece(self, i):
        return i * self.wide, min(self.wide, self.width - i * self.wide)


def shift(value, sections=0, experts=0, flip=0):
    n_sec, n_own = lax.axis_size("section"), lax.axis_size("expert")
    n_exp = n_own // SPLIT
    if sections % n_sec == 0 and experts % n_exp == 0 and flip == 0:
        return value
    pairs = []
    for sec in range(n_sec):
        for own in range(n_own):
            exp, sl = own // SPLIT, own % SPLIT
            to = ((exp + experts) % n_exp) * SPLIT + (sl ^ flip)
            pairs.append((sec * n_own + own, ((sec + sections) % n_sec) * n_own + to))
    return lax.ppermute(value, ("section", "expert"), pairs)


def call(body, outs, *operands, scratch=(), flops=0, after=()):
    moved = sum(a.size * a.dtype.itemsize for a in operands)
    moved += sum(o.size * o.dtype.itemsize for o in outs)
    vmem = pl.BlockSpec(memory_space=pltpu.VMEM)
    read = len(operands)

    def reading(*refs):
        body(*refs[:read], *refs[read + len(after) :])

    return pl.pallas_call(
        reading,
        out_shape=list(outs),
        in_specs=[vmem] * read + [pl.BlockSpec(memory_space=pl.ANY)] * len(after),
        out_specs=[vmem] * len(outs),
        scratch_shapes=list(scratch),
        compiler_params=pltpu.CompilerParams(vmem_limit_bytes=40 * 2**20),
        cost_estimate=pl.CostEstimate(flops=flops, bytes_accessed=moved, transcendentals=0),
    )(*operands, *after)


def column_of(row):
    n = row.shape[1]
    eye = iota((n, n), 0) == iota((n, n), 1)
    return jnp.sum(jnp.where(eye, row, 0.0), axis=1, keepdims=True)


def slots_of(rel, experts, capacity):
    n = rel.shape[1]
    same = jnp.broadcast_to(column_of(rel), (n, n)) == jnp.broadcast_to(rel, (n, n))
    before = iota((n, n), 0) < iota((n, n), 1)
    rank = jnp.sum(jnp.where(same & before, 1.0, 0.0), axis=0, keepdims=True)
    return rel * capacity + rank


def terms(value):
    high = value.astype(BF).astype(F32)
    middle = (value - high).astype(BF).astype(F32)
    return high, middle, value - high - middle


def notes_of(slots, mix, gain, n, width):
    r = iota((ROWS, n), 0)
    left = jnp.where(r == 0, slots, 0.0)
    for at, term in enumerate(terms(mix)):
        left = jnp.where(r == 1 + at, term, left)
    r = iota((ROWS, width), 0)
    wide = jnp.concatenate([left, jnp.zeros((ROWS, width - n), F32)], axis=1)
    for at, term in enumerate(terms(gain)):
        wide = jnp.where(r == 4 + at, term, wide)
    return wide.astype(BF)


def slots_in(notes, n):
    return notes[:, :n].astype(F32)[0:1]


def mix_in(notes, n):
    left = notes[:, :n].astype(F32)
    return column_of(left[1:2] + left[2:3] + left[3:4])


def gain_in(notes):
    wide = notes.astype(F32)
    return wide[4:5] + wide[5:6] + wide[6:7]


def pack_rows(box, slots, values, out_refs):
    n = values.shape[0]
    line = jnp.broadcast_to(slots.astype(jnp.int32), (ROWS, n))
    r = iota((ROWS, n), 0)
    for j, out in enumerate(out_refs):
        first = j * box.capacity
        for g in range(box.groups):
            sel = jnp.where(line == first + g * ROWS + r, 1.0, 0.0).astype(BF)
            out[:, box.group(g)] = dot(sel, values).astype(BF)
        if box.extra:
            total = jnp.zeros((ROWS, box.wide), F32)
            for i in range(box.pieces):
                at, size = box.piece(i)
                hit = (line == first + box.groups * ROWS + r // box.cuts) & (r % box.cuts == i)
                hit &= r // box.cuts < box.extra
                got = dot(jnp.where(hit, 1.0, 0.0).astype(BF), values[:, at : at + size])
                if size < box.wide:
                    got = jnp.concatenate([got, jnp.zeros((ROWS, box.wide - size), F32)], axis=1)
                total = total + got
            out[:, box.tail()] = total.astype(BF)


def pick_rows(box, slots, boxes, n, picked):
    count = len(boxes)
    slots = column_of(slots)
    if box.groups:
        stack = jnp.concatenate(
            [b[:, g * box.width : (g + 1) * box.width] for b in boxes for g in range(box.groups)],
            axis=0,
        )
        tall = count * box.groups * ROWS
        c = iota((n, tall), 1)
        slot = c // (box.groups * ROWS) * box.capacity + c % (box.groups * ROWS)
        sel = jnp.where(slots.astype(jnp.int32) == slot, 1.0, 0.0).astype(BF)
        picked[...] = dot(sel, stack)
    else:
        picked[...] = jnp.zeros(picked.shape, F32)
    if box.extra:
        tails = jnp.concatenate([b[:, box.groups * box.width :] for b in boxes], axis=0)
        c = iota((n, count * ROWS), 1)
        r = c % ROWS
        slot = c // ROWS * box.capacity + box.groups * ROWS + r // box.cuts
        mine = (slots.astype(jnp.int32) == slot) & (r // box.cuts < box.extra)
        for i in range(box.pieces):
            at, size = box.piece(i)
            sel = jnp.where(mine & (r % box.cuts == i), 1.0, 0.0).astype(BF)
            picked[:, at : at + size] += dot(sel, tails[:, :size])


def heights(box, count):
    extra = -(-count * box.extra // ROWS) * ROWS
    return count * box.groups * ROWS, extra


def unpack(box, refs, stack, tails, at=0):
    count = 0
    for ref in refs:
        for p in range(ref.shape[0] // ROWS):
            for g in range(box.groups):
                stack[at : at + ROWS, :] = ref[p * ROWS : (p + 1) * ROWS, box.group(g)]
                at += ROWS
            if box.extra:
                tails[count * ROWS : (count + 1) * ROWS, :] = ref[
                    p * ROWS : (p + 1) * ROWS, box.tail()
                ]
            count += 1
    if box.extra:
        extra = heights(box, count)[1]
        r = iota((extra, count * ROWS), 0)
        c = iota((extra, count * ROWS), 1)
        mine = (r // box.extra == c // ROWS) & (r % box.extra == c % ROWS // box.cuts)
        for i in range(box.pieces):
            start, size = box.piece(i)
            sel = jnp.where(mine & (c % ROWS % box.cuts == i), 1.0, 0.0).astype(BF)
            stack[at : at + extra, start : start + size] = dot(sel, tails[:, :size]).astype(BF)


def repack(box, rows, refs):
    rows = rows.astype(BF)
    at = 0
    count = 0
    for ref in refs:
        for p in range(ref.shape[0] // ROWS):
            for g in range(box.groups):
                ref[p * ROWS : (p + 1) * ROWS, box.group(g)] = rows[at : at + ROWS]
                at += ROWS
            count += 1
    if box.extra:
        extra = heights(box, count)[1]
        r = iota((count * ROWS, extra), 0)
        c = iota((count * ROWS, extra), 1)
        mine = (c // box.extra == r // ROWS) & (c % box.extra == r % ROWS // box.cuts)
        total = jnp.zeros((count * ROWS, box.wide), F32)
        for i in range(box.pieces):
            start, size = box.piece(i)
            sel = jnp.where(mine & (r % ROWS % box.cuts == i), 1.0, 0.0).astype(BF)
            got = dot(sel, rows[at:, start : start + size])
            if size < box.wide:
                pad = jnp.zeros((count * ROWS, box.wide - size), F32)
                got = jnp.concatenate([got, pad], axis=1)
            total = total + got
        total = total.astype(BF)
        count = 0
        for ref in refs:
            tall = ref.shape[0]
            ref[:, box.tail()] = total[count : count + tall]
            count += tall


def inv_rms(wide):
    return lax.rsqrt(jnp.mean(wide * wide, axis=-1, keepdims=True) + EPSILON)


def total_of(refs):
    return sum(ref[...].astype(F32) for ref in refs).astype(BF)


def start_kernel(box, experts, tokens, cot, gain, ids, mix, ahead, notes0, notes1, *boxes):
    n, width = tokens.shape
    mine = lax.axis_index("expert") // SPLIT
    for k, notes in enumerate((notes0, notes1)):
        rel = ids[k : k + 1, :] - mine
        rel = jnp.where(rel < 0, rel + experts, rel).astype(F32)
        slots = slots_of(rel, experts, box.capacity)
        notes[...] = notes_of(slots, mix[k : k + 1, :], gain[...], n, width)
    ahead[:n] = tokens[...]
    ahead[n:] = notes0[...]
    wide = tokens[...].astype(F32)
    normed = (wide * inv_rms(wide) * gain[...]).astype(BF)
    crossing = boxes[2:]
    firsts = [boxes[0]] + [ref.at[:ROWS] for ref in crossing]
    pack_rows(box, slots_in(notes0[...], n), normed, firsts)
    seconds = [boxes[1]] + [ref.at[ROWS:] for ref in crossing]
    pack_rows(box, slots_in(notes1[...], n), cot[...], seconds)


def combine(box, notes, n, own, back, picked):
    sums = [total_of(own)] + [ref[...] for ref in back]
    pick_rows(box, slots_in(notes, n), sums, n, picked)
    return mix_in(notes, n) * picked[...]


def split_refs(refs, experts, outs):
    ins = refs[:-outs]
    return ins[experts - 1 :], ins[: experts - 1], refs[-outs:]


def middle_kernel(box, experts, arrived, cot, notes1, gain, *refs):
    boxes, picked = refs[-1 - experts : -1], refs[-1]
    own, back, (after, behind) = split_refs(refs[: -1 - experts], experts, 2)
    n = cot.shape[0]
    update = combine(box, arrived[n:], n, own, back, picked)
    later = (arrived[:n].astype(F32) + update).astype(BF)
    after[...] = later
    behind[:n] = later
    behind[n : 2 * n] = cot[...]
    behind[2 * n :] = notes1[...]
    wide = later.astype(F32)
    normed = (wide * inv_rms(wide) * gain[...]).astype(BF)
    pack_rows(box, slots_in(notes1[...], n), normed, boxes)


def final_kernel(box, experts, hidden, notes, *refs):
    picked = refs[-1]
    own, back, (out,) = split_refs(refs[:-1], experts, 1)
    n = hidden.shape[0]
    update = combine(box, notes[...], n, own, back, picked)
    out[...] = (hidden[...].astype(F32) + update).astype(BF)


def norm_back(hidden, gain, grad):
    wide = hidden.astype(F32)
    inv = inv_rms(wide)
    scaled = grad * gain
    along = jnp.mean(scaled * wide, axis=-1, keepdims=True)
    return inv * scaled - wide * (inv * inv * inv * along)


def turn_kernel(box, experts, arrived, notes0, *refs):
    boxes, picked = refs[-1 - experts : -1], refs[-1]
    own, back, (out,) = split_refs(refs[: -1 - experts], experts, 1)
    n = out.shape[0]
    notes = arrived[2 * n :]
    d_normed = combine(box, notes, n, own, back, picked)
    change = norm_back(arrived[:n], gain_in(notes), d_normed)
    now = (arrived[n : 2 * n].astype(F32) + change).astype(BF)
    out[...] = now
    pack_rows(box, slots_in(notes0[...], n), now, boxes)


def last_kernel(box, experts, grad, hidden, notes0, gain, *refs):
    picked = refs[-1]
    own, back, (out,) = split_refs(refs[:-1], experts, 1)
    n = hidden.shape[0]
    d_normed = combine(box, notes0[...], n, own, back, picked)
    change = norm_back(hidden[...], gain[...], d_normed)
    out[...] = (grad[...].astype(F32) + change).astype(BF)


def spans(tall):
    return pl.ds(0, 2 * tall), pl.ds(tall, 2 * tall)


def gate_up(rows, pack):
    return dot(rows, pack[: 2 * (pack.shape[0] // 3)], NT)


def parts_of(both):
    units = both.shape[1] // 2
    return both[:, :units], both[:, units:]


def down_rows(both, pack):
    g, u = parts_of(both)
    return dot((jax.nn.silu(g) * u).astype(BF), pack[2 * g.shape[1] :])


def inner_of(rows, pack):
    return dot(rows, pack[2 * (pack.shape[0] // 3) :], NT)


def part_rows(d_inner, both, pack):
    g, u = parts_of(both)
    r = jax.nn.sigmoid(g)
    d_gate = d_inner * u * r * (1.0 + g * (1.0 - r))
    d_up = d_inner * g * r
    return dot(jnp.concatenate([d_gate, d_up], axis=1).astype(BF), pack[: both.shape[1]])


def read_rows(box, rows, stack, tails):
    tall = stack.shape[0] // 3
    for at, ref in enumerate(rows):
        unpack(box, [ref], stack, tails, at * tall)
    return [stack[span, :] for span in spans(tall)]


def write_rows(box, top, bottom, outs):
    tall = top.shape[0] // 2
    for ref, value in zip(outs, (top[:tall], top[tall:] + bottom[:tall], bottom[tall:])):
        repack(box, value, [ref])


def forward_kernel(box, packs, saved, rows, outs, kept, stack, tails):
    sides = read_rows(box, rows, stack, tails)
    total = []
    for side, values in enumerate(sides):
        total.append(0.0)
        for at in (2 * side, 2 * side + 1):
            both = gate_up(values, packs[at])
            kept[at][...] = both
            total[side] = total[side] + down_rows(both, packs[at])
    write_rows(box, *total, outs)


def inner_kernel(box, packs, saved, rows, outs, kept, stack, tails):
    for side, values in enumerate(read_rows(box, rows, stack, tails)):
        for at in (2 * side, 2 * side + 1):
            kept[at][...] = inner_of(values, packs[at])


def gate_back_kernel(box, packs, saved, rows, outs, kept, stack, tails):
    sides = read_rows(box, rows, stack, tails)
    total = []
    for side, values in enumerate(sides):
        total.append(0.0)
        for at in (2 * side, 2 * side + 1):
            both = gate_up(values, packs[at])
            kept[at][...] = both
            total[side] = total[side] + part_rows(saved[at][...], both, packs[at])
    write_rows(box, *total, outs)


def back_kernel(box, packs, saved, rows, outs, kept, stack, tails):
    sides = read_rows(box, rows, stack, tails)
    total = []
    for side, values in enumerate(sides):
        total.append(0.0)
        for at in (2 * side, 2 * side + 1):
            d_inner = inner_of(values, packs[at])
            total[side] = total[side] + part_rows(d_inner, saved[at][...], packs[at])
    write_rows(box, *total, outs)


def down_kernel(box, packs, saved, rows, outs, kept, stack, tails):
    total = []
    for side in range(2):
        at = 2 * side
        total.append(sum(down_rows(saved[i][...], packs[i]) for i in (at, at + 1)))
    write_rows(box, *total, outs)


def expert_call(kernel, box, packs, rows, saved=(), outs=True, kept=0, reads=True, after=(), window=None):
    width = packs[0].shape[1]
    first, size = window or (0, rows[0].shape[0])
    count = size // ROWS
    tall = sum(heights(box, count))
    boxes = jax.ShapeDtypeStruct((count * ROWS, box.lanes), BF)
    results = [boxes] * len(rows) if outs else []
    if kept:
        units = [pack.shape[0] // 3 for pack in packs]
        results += [jax.ShapeDtypeStruct((2 * tall, kept * u), F32) for u in units]
    inputs = list(packs) + list(saved) + (list(rows) if reads else [])
    n_in, n_p, n_s, n_out = len(inputs), len(packs), len(saved), len(rows) if outs else 0

    def body(*refs):
        results_refs = refs[n_in:-2]
        kernel(
            box,
            refs[:n_p],
            refs[n_p : n_p + n_s],
            [ref.at[pl.ds(first, size)] for ref in refs[n_p + n_s : n_in]],
            results_refs[:n_out],
            results_refs[n_out:],
            refs[-2],
            refs[-1],
        )

    scratch = [
        pltpu.VMEM((3 * tall, width), BF),
        pltpu.VMEM((count * ROWS, max(box.wide, LANES)), BF),
    ]
    flops = sum(2 * 2 * tall * pack.size for pack in packs)
    results = call(body, results, *inputs, scratch=scratch, flops=flops, after=after)
    return results[:n_out], results[n_out:]


def local(tokens, norm_gain, w_gate, w_up, w_down, routes, mix_weights, cotangent):
    experts = lax.axis_size("expert") // SPLIT
    n, width = tokens.shape[1:]
    capacity = n // experts + max(1, n // (16 * experts))
    box = Box(capacity, width)
    gain = norm_gain
    gate_w, up_w, down_w = w_gate[0, 0].T, w_up[0, 0].T, w_down[0, 0]
    boxed = jax.ShapeDtypeStruct((ROWS, box.lanes), BF)
    picked = pltpu.VMEM((n, width), F32)
    bind = functools.partial

    def joined(arrays):
        return arrays[0] if len(arrays) == 1 else jnp.concatenate(arrays, axis=0)

    fence = lax.optimization_barrier

    def crossing_of(boxes):
        return joined([shift(boxes[j - 1], experts=j) for j in range(1, experts)])

    def around(boxes):
        return [shift(boxes, flip=2), boxes, shift(boxes, flip=1)]

    def add(*values):
        return sum(v.astype(F32) for v in values).astype(BF)

    def sums(parts):
        return add(parts[1], shift(parts[0], flip=2), shift(parts[2], flip=1))

    def home(total, sections):
        return [
            shift(total[(j - 1) * ROWS : j * ROWS], sections=sections, experts=-j)
            for j in range(1, experts)
        ]

    def own_home(parts, sections):
        return [
            shift(parts[0], sections=sections, flip=2),
            shift(parts[2], sections=sections, flip=1),
            shift(parts[1], sections=sections),
        ]

    def give_back(cross, own, sections):
        total = sums(cross)
        back = home(total, sections)
        own, _ = fence((own, total))
        return back + own_home(own, sections)

    units = w_gate.shape[3]
    cut = -(-units * 7 // 12 // ROWS) * ROWS
    top = jnp.concatenate([gate_w[:cut], up_w[:cut], down_w[:cut]], axis=0)
    bottom = jnp.concatenate([gate_w[cut:], up_w[cut:], down_w[cut:]], axis=0)
    packs = [top, shift(top, flip=1), bottom, shift(bottom, flip=2)]

    def rows_of(count):
        return jax.ShapeDtypeStruct((count, width), BF)

    both = jax.ShapeDtypeStruct((2 * ROWS, box.lanes), BF)
    ahead, notes0, notes1, own_tok, own_cot, *crossing = call(
        bind(start_kernel, box, experts),
        [rows_of(n + ROWS), rows_of(ROWS), rows_of(ROWS), boxed, boxed] + [both] * (experts - 1),
        tokens[0],
        cotangent[0],
        gain,
        routes[0, :, :, 0],
        mix_weights[0, :, :, 0],
        after=[top, bottom],
    )
    crossed = [shift(crossing[j - 1], experts=j) for j in range(1, experts)]
    own0 = around(own_tok)
    packs, crossed, own0 = fence((packs, crossed, own0))
    cross0 = around(joined([c[:ROWS] for c in crossed]))
    cots = joined([own_cot] + [c[ROWS:] for c in crossed])
    cross0, cots = fence((cross0, cots))
    cots = around(cots)

    cross_out, cross_kept0 = expert_call(forward_kernel, box, packs, cross0, kept=2)
    own_out, own_kept0 = expert_call(
        forward_kernel, box, packs, own0, kept=2, after=list(cross_out[:1]) + list(cots)
    )
    cross_out, ahead = fence((cross_out, ahead))
    arrived0 = shift(ahead, sections=1)
    got = give_back(cross_out, own_out, 1)
    h1, behind, own1, *boxes1 = call(
        bind(middle_kernel, box, experts),
        [rows_of(n), rows_of(2 * n + ROWS)] + [boxed] * experts,
        arrived0,
        cotangent[0],
        notes1,
        gain,
        *got,
        scratch=[picked],
    )
    cross1, own_z, own_x = fence(
        (crossing_of(boxes1), shift(own1, flip=2), shift(own1, flip=1))
    )
    cross1, own1 = around(cross1), [own_z, own1, own_x]
    inner = bind(expert_call, inner_kernel, box, packs, cots, outs=False, kept=1)
    own_di = inner(window=(0, ROWS))[1]
    cross_di = inner(window=(ROWS, (experts - 1) * ROWS))[1]

    gate_back = bind(expert_call, gate_back_kernel, box, packs, kept=2)
    own_grad, own_kept1 = gate_back(own1, own_di)
    cross_grad, cross_kept1 = gate_back(cross1, cross_di, after=own_grad[:1])
    down = bind(expert_call, down_kernel, box, packs, reads=False)
    cross_fin = down(cross1, cross_kept1)[0]
    arrived1 = shift(behind, sections=-1)
    got = give_back(cross_grad, own_grad, -1)
    got[: experts - 1], fin_sums = fence((got[: experts - 1], sums(cross_fin)))
    fin_back = home(fin_sums, 0)
    own_fin = down(own1, own_kept1)[0]
    g1, own_g, *boxes_g = call(
        bind(turn_kernel, box, experts),
        [rows_of(n)] + [boxed] * experts,
        arrived1,
        notes0,
        *got,
        scratch=[picked],
    )

    cross_g, own_z, own_x, fin_back = fence(
        (crossing_of(boxes_g), shift(own_g, flip=2), shift(own_g, flip=1), fin_back)
    )
    cross_g, own_g = around(cross_g), [own_z, own_g, own_x]
    back = bind(expert_call, back_kernel, box, packs)
    own_grad = back(own_g, own_kept0)[0]
    cross_grad = back(cross_g, cross_kept0, after=own_grad[:1])[0]
    total = sums(cross_grad)
    own_grad, own_fin, _ = fence((own_grad, own_fin, total))
    got = home(total, 0) + own_home(own_grad, 0)
    fin_own = own_home(own_fin, 0)
    (g0,) = call(
        bind(last_kernel, box, experts),
        [rows_of(n)],
        g1,
        tokens[0],
        notes0,
        gain,
        *got,
        scratch=[picked],
    )
    (final,) = call(
        bind(final_kernel, box, experts),
        [rows_of(n)],
        h1,
        notes1,
        *fin_back,
        *fin_own,
        scratch=[picked],
    )
    return (final[None], g0[None])


def solution(mesh):
    in_specs = (
        P("section", "expert", None),
        P("section", None),
        P("section", "expert", None, None),
        P("section", "expert", None, None),
        P("section", "expert", None, None),
        P("section", None, "expert", None),
        P("section", None, "expert", None),
        P("section", "expert", None),
    )
    out_specs = (P("section", "expert", None), P("section", "expert", None))
    return jax.shard_map(local, mesh=mesh, in_specs=in_specs, out_specs=out_specs, check_vma=False)
```

```python
import functools

import jax
import jax.numpy as jnp
from jax import lax
from jax.experimental import pallas as pl
from jax.experimental.pallas import tpu as pltpu
from jax.sharding import PartitionSpec as P

SPLIT = 4
EPSILON = 1e-06
BF = jnp.bfloat16
F32 = jnp.float32
ROWS = 16
LANES = 128


def dot(left, right, dims=((1,), (0,))):
    return lax.dot_general(left, right, (dims, ((), ())), preferred_element_type=F32)


NT = ((1,), (1,))


def iota(shape, axis):
    return lax.broadcasted_iota(jnp.int32, shape, axis)


class Box:
    def __init__(self, capacity, width):
        self.capacity, self.width = capacity, width
        self.groups, self.extra = capacity // ROWS, capacity % ROWS
        self.cuts = ROWS // self.extra if self.extra else 1
        self.wide = -(-width // (LANES * self.cuts)) * LANES if self.extra else 0
        self.lanes = self.groups * width + self.wide
        self.pieces = -(-width // self.wide) if self.extra else 0

    def group(self, g):
        return pl.ds(g * self.width, self.width)

    def tail(self):
        return pl.ds(self.groups * self.width, self.wide)

    def piece(self, i):
        return i * self.wide, min(self.wide, self.width - i * self.wide)


def shift(value, sections=0, experts=0, flip=0):
    n_sec, n_own = lax.axis_size("section"), lax.axis_size("expert")
    n_exp = n_own // SPLIT
    if sections % n_sec == 0 and experts % n_exp == 0 and flip == 0:
        return value
    pairs = []
    for sec in range(n_sec):
        for own in range(n_own):
            exp, sl = own // SPLIT, own % SPLIT
            to = ((exp + experts) % n_exp) * SPLIT + (sl ^ flip)
            pairs.append((sec * n_own + own, ((sec + sections) % n_sec) * n_own + to))
    return lax.ppermute(value, ("section", "expert"), pairs)


def call(body, outs, *operands, scratch=(), flops=0, after=()):
    moved = sum(a.size * a.dtype.itemsize for a in operands)
    moved += sum(o.size * o.dtype.itemsize for o in outs)
    vmem = pl.BlockSpec(memory_space=pltpu.VMEM)
    read = len(operands)

    def reading(*refs):
        body(*refs[:read], *refs[read + len(after) :])

    return pl.pallas_call(
        reading,
        out_shape=list(outs),
        in_specs=[vmem] * read + [pl.BlockSpec(memory_space=pl.ANY)] * len(after),
        out_specs=[vmem] * len(outs),
        scratch_shapes=list(scratch),
        compiler_params=pltpu.CompilerParams(vmem_limit_bytes=40 * 2**20),
        cost_estimate=pl.CostEstimate(flops=flops, bytes_accessed=moved, transcendentals=0),
    )(*operands, *after)


def column_of(row):
    n = row.shape[1]
    eye = iota((n, n), 0) == iota((n, n), 1)
    return jnp.sum(jnp.where(eye, row, 0.0), axis=1, keepdims=True)


def slots_of(rel, experts, capacity):
    n = rel.shape[1]
    same = jnp.broadcast_to(column_of(rel), (n, n)) == jnp.broadcast_to(rel, (n, n))
    before = iota((n, n), 0) < iota((n, n), 1)
    rank = jnp.sum(jnp.where(same & before, 1.0, 0.0), axis=0, keepdims=True)
    return rel * capacity + rank


def terms(value):
    high = value.astype(BF).astype(F32)
    middle = (value - high).astype(BF).astype(F32)
    return high, middle, value - high - middle


def notes_of(slots, mix, gain, n, width):
    r = iota((ROWS, n), 0)
    left = jnp.where(r == 0, slots, 0.0)
    for at, term in enumerate(terms(mix)):
        left = jnp.where(r == 1 + at, term, left)
    r = iota((ROWS, width), 0)
    wide = jnp.concatenate([left, jnp.zeros((ROWS, width - n), F32)], axis=1)
    for at, term in enumerate(terms(gain)):
        wide = jnp.where(r == 4 + at, term, wide)
    return wide.astype(BF)


def slots_in(notes, n):
    return notes[:, :n].astype(F32)[0:1]


def mix_in(notes, n):
    left = notes[:, :n].astype(F32)
    return column_of(left[1:2] + left[2:3] + left[3:4])


def gain_in(notes):
    wide = notes.astype(F32)
    return wide[4:5] + wide[5:6] + wide[6:7]


def pack_rows(box, slots, values, out_refs):
    n = values.shape[0]
    line = jnp.broadcast_to(slots.astype(jnp.int32), (ROWS, n))
    r = iota((ROWS, n), 0)
    for j, out in enumerate(out_refs):
        first = j * box.capacity
        for g in range(box.groups):
            sel = jnp.where(line == first + g * ROWS + r, 1.0, 0.0).astype(BF)
            out[:, box.group(g)] = dot(sel, values).astype(BF)
        if box.extra:
            total = jnp.zeros((ROWS, box.wide), F32)
            for i in range(box.pieces):
                at, size = box.piece(i)
                hit = (line == first + box.groups * ROWS + r // box.cuts) & (r % box.cuts == i)
                hit &= r // box.cuts < box.extra
                got = dot(jnp.where(hit, 1.0, 0.0).astype(BF), values[:, at : at + size])
                if size < box.wide:
                    got = jnp.concatenate([got, jnp.zeros((ROWS, box.wide - size), F32)], axis=1)
                total = total + got
            out[:, box.tail()] = total.astype(BF)


def pick_rows(box, slots, boxes, n, picked):
    count = len(boxes)
    slots = column_of(slots)
    if box.groups:
        stack = jnp.concatenate(
            [b[:, g * box.width : (g + 1) * box.width] for b in boxes for g in range(box.groups)],
            axis=0,
        )
        tall = count * box.groups * ROWS
        c = iota((n, tall), 1)
        slot = c // (box.groups * ROWS) * box.capacity + c % (box.groups * ROWS)
        sel = jnp.where(slots.astype(jnp.int32) == slot, 1.0, 0.0).astype(BF)
        picked[...] = dot(sel, stack)
    else:
        picked[...] = jnp.zeros(picked.shape, F32)
    if box.extra:
        tails = jnp.concatenate([b[:, box.groups * box.width :] for b in boxes], axis=0)
        c = iota((n, count * ROWS), 1)
        r = c % ROWS
        slot = c // ROWS * box.capacity + box.groups * ROWS + r // box.cuts
        mine = (slots.astype(jnp.int32) == slot) & (r // box.cuts < box.extra)
        for i in range(box.pieces):
            at, size = box.piece(i)
            sel = jnp.where(mine & (r % box.cuts == i), 1.0, 0.0).astype(BF)
            picked[:, at : at + size] += dot(sel, tails[:, :size])


def heights(box, count):
    extra = -(-count * box.extra // ROWS) * ROWS
    return count * box.groups * ROWS, extra


def unpack(box, refs, stack, tails, at=0):
    count = 0
    for ref in refs:
        for p in range(ref.shape[0] // ROWS):
            for g in range(box.groups):
                stack[at : at + ROWS, :] = ref[p * ROWS : (p + 1) * ROWS, box.group(g)]
                at += ROWS
            if box.extra:
                tails[count * ROWS : (count + 1) * ROWS, :] = ref[
                    p * ROWS : (p + 1) * ROWS, box.tail()
                ]
            count += 1
    if box.extra:
        extra = heights(box, count)[1]
        r = iota((extra, count * ROWS), 0)
        c = iota((extra, count * ROWS), 1)
        mine = (r // box.extra == c // ROWS) & (r % box.extra == c % ROWS // box.cuts)
        for i in range(box.pieces):
            start, size = box.piece(i)
            sel = jnp.where(mine & (c % ROWS % box.cuts == i), 1.0, 0.0).astype(BF)
            stack[at : at + extra, start : start + size] = dot(sel, tails[:, :size]).astype(BF)


def repack(box, rows, refs):
    rows = rows.astype(BF)
    at = 0
    count = 0
    for ref in refs:
        for p in range(ref.shape[0] // ROWS):
            for g in range(box.groups):
                ref[p * ROWS : (p + 1) * ROWS, box.group(g)] = rows[at : at + ROWS]
                at += ROWS
            count += 1
    if box.extra:
        extra = heights(box, count)[1]
        r = iota((count * ROWS, extra), 0)
        c = iota((count * ROWS, extra), 1)
        mine = (c // box.extra == r // ROWS) & (c % box.extra == r % ROWS // box.cuts)
        total = jnp.zeros((count * ROWS, box.wide), F32)
        for i in range(box.pieces):
            start, size = box.piece(i)
            sel = jnp.where(mine & (r % ROWS % box.cuts == i), 1.0, 0.0).astype(BF)
            got = dot(sel, rows[at:, start : start + size])
            if size < box.wide:
                pad = jnp.zeros((count * ROWS, box.wide - size), F32)
                got = jnp.concatenate([got, pad], axis=1)
            total = total + got
        total = total.astype(BF)
        count = 0
        for ref in refs:
            tall = ref.shape[0]
            ref[:, box.tail()] = total[count : count + tall]
            count += tall


def inv_rms(wide):
    return lax.rsqrt(jnp.mean(wide * wide, axis=-1, keepdims=True) + EPSILON)


def total_of(refs):
    return sum(ref[...].astype(F32) for ref in refs).astype(BF)


def start_kernel(box, experts, tokens, cot, gain, ids, mix, ahead, notes0, notes1, *boxes):
    n, width = tokens.shape
    mine = lax.axis_index("expert") // SPLIT
    for k, notes in enumerate((notes0, notes1)):
        rel = ids[k : k + 1, :] - mine
        rel = jnp.where(rel < 0, rel + experts, rel).astype(F32)
        slots = slots_of(rel, experts, box.capacity)
        notes[...] = notes_of(slots, mix[k : k + 1, :], gain[...], n, width)
    ahead[:n] = tokens[...]
    ahead[n:] = notes0[...]
    wide = tokens[...].astype(F32)
    normed = (wide * inv_rms(wide) * gain[...]).astype(BF)
    crossing = boxes[2:]
    firsts = [boxes[0]] + [ref.at[:ROWS] for ref in crossing]
    pack_rows(box, slots_in(notes0[...], n), normed, firsts)
    seconds = [boxes[1]] + [ref.at[ROWS:] for ref in crossing]
    pack_rows(box, slots_in(notes1[...], n), cot[...], seconds)


def combine(box, notes, n, own, back, picked):
    sums = [total_of(own)] + [ref[...] for ref in back]
    pick_rows(box, slots_in(notes, n), sums, n, picked)
    return mix_in(notes, n) * picked[...]


def split_refs(refs, experts, outs):
    ins = refs[:-outs]
    return ins[experts - 1 :], ins[: experts - 1], refs[-outs:]


def middle_kernel(box, experts, arrived, cot, notes1, gain, *refs):
    boxes, picked = refs[-1 - experts : -1], refs[-1]
    own, back, (after, behind) = split_refs(refs[: -1 - experts], experts, 2)
    n = cot.shape[0]
    update = combine(box, arrived[n:], n, own, back, picked)
    later = (arrived[:n].astype(F32) + update).astype(BF)
    after[...] = later
    behind[:n] = later
    behind[n : 2 * n] = cot[...]
    behind[2 * n :] = notes1[...]
    wide = later.astype(F32)
    normed = (wide * inv_rms(wide) * gain[...]).astype(BF)
    pack_rows(box, slots_in(notes1[...], n), normed, boxes)


def final_kernel(box, experts, hidden, notes, *refs):
    picked = refs[-1]
    own, back, (out,) = split_refs(refs[:-1], experts, 1)
    n = hidden.shape[0]
    update = combine(box, notes[...], n, own, back, picked)
    out[...] = (hidden[...].astype(F32) + update).astype(BF)


def norm_back(hidden, gain, grad):
    wide = hidden.astype(F32)
    inv = inv_rms(wide)
    scaled = grad * gain
    along = jnp.mean(scaled * wide, axis=-1, keepdims=True)
    return inv * scaled - wide * (inv * inv * inv * along)


def turn_kernel(box, experts, arrived, notes0, *refs):
    boxes, picked = refs[-1 - experts : -1], refs[-1]
    own, back, (out,) = split_refs(refs[: -1 - experts], experts, 1)
    n = out.shape[0]
    notes = arrived[2 * n :]
    d_normed = combine(box, notes, n, own, back, picked)
    change = norm_back(arrived[:n], gain_in(notes), d_normed)
    now = (arrived[n : 2 * n].astype(F32) + change).astype(BF)
    out[...] = now
    pack_rows(box, slots_in(notes0[...], n), now, boxes)


def last_kernel(box, experts, grad, hidden, notes0, gain, *refs):
    picked = refs[-1]
    own, back, (out,) = split_refs(refs[:-1], experts, 1)
    n = hidden.shape[0]
    d_normed = combine(box, notes0[...], n, own, back, picked)
    change = norm_back(hidden[...], gain[...], d_normed)
    out[...] = (grad[...].astype(F32) + change).astype(BF)


def spans(tall):
    return pl.ds(0, 2 * tall), pl.ds(tall, 2 * tall)


def gate_up(rows, pack):
    return dot(rows, pack[: 2 * (pack.shape[0] // 3)], NT)


def parts_of(both):
    units = both.shape[1] // 2
    return both[:, :units], both[:, units:]


def down_rows(both, pack):
    g, u = parts_of(both)
    return dot((jax.nn.silu(g) * u).astype(BF), pack[2 * g.shape[1] :])


def inner_of(rows, pack):
    return dot(rows, pack[2 * (pack.shape[0] // 3) :], NT)


def part_rows(d_inner, both, pack):
    g, u = parts_of(both)
    r = jax.nn.sigmoid(g)
    d_gate = d_inner * u * r * (1.0 + g * (1.0 - r))
    d_up = d_inner * g * r
    return dot(jnp.concatenate([d_gate, d_up], axis=1).astype(BF), pack[: both.shape[1]])


def read_rows(box, rows, stack, tails):
    tall = stack.shape[0] // 3
    for at, ref in enumerate(rows):
        unpack(box, [ref], stack, tails, at * tall)
    return [stack[span, :] for span in spans(tall)]


def write_rows(box, top, bottom, outs):
    tall = top.shape[0] // 2
    for ref, value in zip(outs, (top[:tall], top[tall:] + bottom[:tall], bottom[tall:])):
        repack(box, value, [ref])


def forward_kernel(box, packs, saved, rows, outs, kept, stack, tails):
    sides = read_rows(box, rows, stack, tails)
    total = []
    for side, values in enumerate(sides):
        total.append(0.0)
        for at in (2 * side, 2 * side + 1):
            both = gate_up(values, packs[at])
            kept[at][...] = both
            total[side] = total[side] + down_rows(both, packs[at])
    write_rows(box, *total, outs)


def inner_kernel(box, packs, saved, rows, outs, kept, stack, tails):
    for side, values in enumerate(read_rows(box, rows, stack, tails)):
        for at in (2 * side, 2 * side + 1):
            kept[at][...] = inner_of(values, packs[at])


def gate_back_kernel(box, packs, saved, rows, outs, kept, stack, tails):
    sides = read_rows(box, rows, stack, tails)
    total = []
    for side, values in enumerate(sides):
        total.append(0.0)
        for at in (2 * side, 2 * side + 1):
            both = gate_up(values, packs[at])
            kept[at][...] = both
            total[side] = total[side] + part_rows(saved[at][...], both, packs[at])
    write_rows(box, *total, outs)


def back_kernel(box, packs, saved, rows, outs, kept, stack, tails):
    sides = read_rows(box, rows, stack, tails)
    total = []
    for side, values in enumerate(sides):
        total.append(0.0)
        for at in (2 * side, 2 * side + 1):
            d_inner = inner_of(values, packs[at])
            total[side] = total[side] + part_rows(d_inner, saved[at][...], packs[at])
    write_rows(box, *total, outs)


def down_kernel(box, packs, saved, rows, outs, kept, stack, tails):
    total = []
    for side in range(2):
        at = 2 * side
        total.append(sum(down_rows(saved[i][...], packs[i]) for i in (at, at + 1)))
    write_rows(box, *total, outs)


def expert_call(kernel, box, packs, rows, saved=(), outs=True, kept=0, reads=True, after=(), window=None):
    width = packs[0].shape[1]
    first, size = window or (0, rows[0].shape[0])
    count = size // ROWS
    tall = sum(heights(box, count))
    boxes = jax.ShapeDtypeStruct((count * ROWS, box.lanes), BF)
    results = [boxes] * len(rows) if outs else []
    if kept:
        units = [pack.shape[0] // 3 for pack in packs]
        results += [jax.ShapeDtypeStruct((2 * tall, kept * u), F32) for u in units]
    inputs = list(packs) + list(saved) + (list(rows) if reads else [])
    n_in, n_p, n_s, n_out = len(inputs), len(packs), len(saved), len(rows) if outs else 0

    def body(*refs):
        results_refs = refs[n_in:-2]
        kernel(
            box,
            refs[:n_p],
            refs[n_p : n_p + n_s],
            [ref.at[pl.ds(first, size)] for ref in refs[n_p + n_s : n_in]],
            results_refs[:n_out],
            results_refs[n_out:],
            refs[-2],
            refs[-1],
        )

    scratch = [
        pltpu.VMEM((3 * tall, width), BF),
        pltpu.VMEM((count * ROWS, max(box.wide, LANES)), BF),
    ]
    flops = sum(2 * 2 * tall * pack.size for pack in packs)
    results = call(body, results, *inputs, scratch=scratch, flops=flops, after=after)
    return results[:n_out], results[n_out:]


def local(tokens, norm_gain, w_gate, w_up, w_down, routes, mix_weights, cotangent):
    experts = lax.axis_size("expert") // SPLIT
    n, width = tokens.shape[1:]
    capacity = n // experts + max(1, n // (16 * experts))
    box = Box(capacity, width)
    gain = norm_gain
    gate_w, up_w, down_w = w_gate[0, 0].T, w_up[0, 0].T, w_down[0, 0]
    boxed = jax.ShapeDtypeStruct((ROWS, box.lanes), BF)
    picked = pltpu.VMEM((n, width), F32)
    bind = functools.partial

    def joined(arrays):
        return arrays[0] if len(arrays) == 1 else jnp.concatenate(arrays, axis=0)

    fence = lax.optimization_barrier

    def crossing_of(boxes):
        return joined([shift(boxes[j - 1], experts=j) for j in range(1, experts)])

    def around(boxes):
        return [shift(boxes, flip=2), boxes, shift(boxes, flip=1)]

    def add(*values):
        return sum(v.astype(F32) for v in values).astype(BF)

    def sums(parts):
        return add(parts[1], shift(parts[0], flip=2), shift(parts[2], flip=1))

    def home(total, sections):
        return [
            shift(total[(j - 1) * ROWS : j * ROWS], sections=sections, experts=-j)
            for j in range(1, experts)
        ]

    def own_home(parts, sections):
        return [
            shift(parts[0], sections=sections, flip=2),
            shift(parts[2], sections=sections, flip=1),
            shift(parts[1], sections=sections),
        ]

    def give_back(cross, own, sections, others=()):
        total = sums(cross)
        back = home(total, sections)
        own, _, others = fence((own, total, others))
        return back + own_home(own, sections), others

    units = w_gate.shape[3]
    cut = -(-units * 7 // 12 // ROWS) * ROWS
    top = jnp.concatenate([gate_w[:cut], up_w[:cut], down_w[:cut]], axis=0)
    bottom = jnp.concatenate([gate_w[cut:], up_w[cut:], down_w[cut:]], axis=0)
    packs = [top, shift(top, flip=1), bottom, shift(bottom, flip=2)]

    def rows_of(count):
        return jax.ShapeDtypeStruct((count, width), BF)

    both = jax.ShapeDtypeStruct((2 * ROWS, box.lanes), BF)
    ahead, notes0, notes1, own_tok, own_cot, *crossing = call(
        bind(start_kernel, box, experts),
        [rows_of(n + ROWS), rows_of(ROWS), rows_of(ROWS), boxed, boxed] + [both] * (experts - 1),
        tokens[0],
        cotangent[0],
        gain,
        routes[0, :, :, 0],
        mix_weights[0, :, :, 0],
        after=[top, bottom],
    )
    crossed = [shift(crossing[j - 1], experts=j) for j in range(1, experts)]
    own0 = around(own_tok)
    packs, crossed, own0 = fence((packs, crossed, own0))
    cross0 = around(joined([c[:ROWS] for c in crossed]))
    cots = joined([own_cot] + [c[ROWS:] for c in crossed])
    cross0, cots = fence((cross0, cots))
    cots = around(cots)

    cross_out, cross_kept0 = expert_call(forward_kernel, box, packs, cross0, kept=2)
    own_out, own_kept0 = expert_call(
        forward_kernel, box, packs, own0, kept=2, after=cross_out[:1]
    )
    cross_out, ahead = fence((cross_out, ahead))
    arrived0 = shift(ahead, sections=1)
    got, cots = give_back(cross_out, own_out, 1, cots)
    h1, behind, own1, *boxes1 = call(
        bind(middle_kernel, box, experts),
        [rows_of(n), rows_of(2 * n + ROWS)] + [boxed] * experts,
        arrived0,
        cotangent[0],
        notes1,
        gain,
        *got,
        scratch=[picked],
    )
    cross1, own_z, own_x = fence(
        (crossing_of(boxes1), shift(own1, flip=2), shift(own1, flip=1))
    )
    cross1, own1 = around(cross1), [own_z, own1, own_x]
    inner = bind(expert_call, inner_kernel, box, packs, cots, outs=False, kept=1)
    own_di = inner(window=(0, ROWS))[1]
    cross_di = inner(window=(ROWS, (experts - 1) * ROWS))[1]

    gate_back = bind(expert_call, gate_back_kernel, box, packs, kept=2)
    own_grad, own_kept1 = gate_back(own1, own_di)
    cross_grad, cross_kept1 = gate_back(cross1, cross_di, after=own_grad[:1])
    down = bind(expert_call, down_kernel, box, packs, reads=False)
    cross_fin = down(cross1, cross_kept1)[0]
    arrived1 = shift(behind, sections=-1)
    got, _ = give_back(cross_grad, own_grad, -1)
    fin_back = home(sums(cross_fin), 0)
    own_fin = down(own1, own_kept1)[0]
    g1, own_g, *boxes_g = call(
        bind(turn_kernel, box, experts),
        [rows_of(n)] + [boxed] * experts,
        arrived1,
        notes0,
        *got,
        scratch=[picked],
        after=fin_back,
    )

    cross_g, own_z, own_x = fence(
        (crossing_of(boxes_g), shift(own_g, flip=2), shift(own_g, flip=1))
    )
    cross_g, own_g = around(cross_g), [own_z, own_g, own_x]
    back = bind(expert_call, back_kernel, box, packs)
    own_grad = back(own_g, own_kept0)[0]
    cross_grad = back(cross_g, cross_kept0, after=own_grad[:1])[0]
    total = sums(cross_grad)
    own_grad, own_fin, _ = fence((own_grad, own_fin, total))
    got = home(total, 0) + own_home(own_grad, 0)
    fin_own = own_home(own_fin, 0)
    (g0,) = call(
        bind(last_kernel, box, experts),
        [rows_of(n)],
        g1,
        tokens[0],
        notes0,
        gain,
        *got,
        scratch=[picked],
    )
    (final,) = call(
        bind(final_kernel, box, experts),
        [rows_of(n)],
        h1,
        notes1,
        *fin_back,
        *fin_own,
        scratch=[picked],
        after=[g0],
    )
    return (final[None], g0[None])


def solution(mesh):
    in_specs = (
        P("section", "expert", None),
        P("section", None),
        P("section", "expert", None, None),
        P("section", "expert", None, None),
        P("section", "expert", None, None),
        P("section", None, "expert", None),
        P("section", None, "expert", None),
        P("section", "expert", None),
    )
    out_specs = (P("section", "expert", None), P("section", "expert", None))
    return jax.shard_map(local, mesh=mesh, in_specs=in_specs, out_specs=out_specs, check_vma=False)
```

```python
import functools

import jax
import jax.numpy as jnp
from jax import lax
from jax.experimental import pallas as pl
from jax.experimental.pallas import tpu as pltpu
from jax.sharding import PartitionSpec as P

SPLIT = 4
EPSILON = 1e-06
BF = jnp.bfloat16
F32 = jnp.float32
ROWS = 16
LANES = 128


def dot(left, right, dims=((1,), (0,))):
    return lax.dot_general(left, right, (dims, ((), ())), preferred_element_type=F32)


NT = ((1,), (1,))


def iota(shape, axis):
    return lax.broadcasted_iota(jnp.int32, shape, axis)


class Box:
    def __init__(self, capacity, width):
        self.capacity, self.width = capacity, width
        self.groups, self.extra = capacity // ROWS, capacity % ROWS
        self.cuts = ROWS // self.extra if self.extra else 1
        self.wide = -(-width // (LANES * self.cuts)) * LANES if self.extra else 0
        self.lanes = self.groups * width + self.wide
        self.pieces = -(-width // self.wide) if self.extra else 0

    def group(self, g):
        return pl.ds(g * self.width, self.width)

    def tail(self):
        return pl.ds(self.groups * self.width, self.wide)

    def piece(self, i):
        return i * self.wide, min(self.wide, self.width - i * self.wide)


def shift(value, sections=0, experts=0, flip=0):
    n_sec, n_own = lax.axis_size("section"), lax.axis_size("expert")
    n_exp = n_own // SPLIT
    if sections % n_sec == 0 and experts % n_exp == 0 and flip == 0:
        return value
    pairs = []
    for sec in range(n_sec):
        for own in range(n_own):
            exp, sl = own // SPLIT, own % SPLIT
            to = ((exp + experts) % n_exp) * SPLIT + (sl ^ flip)
            pairs.append((sec * n_own + own, ((sec + sections) % n_sec) * n_own + to))
    return lax.ppermute(value, ("section", "expert"), pairs)


def call(body, outs, *operands, scratch=(), flops=0, after=()):
    moved = sum(a.size * a.dtype.itemsize for a in operands)
    moved += sum(o.size * o.dtype.itemsize for o in outs)
    vmem = pl.BlockSpec(memory_space=pltpu.VMEM)
    read = len(operands)

    def reading(*refs):
        body(*refs[:read], *refs[read + len(after) :])

    return pl.pallas_call(
        reading,
        out_shape=list(outs),
        in_specs=[vmem] * read + [pl.BlockSpec(memory_space=pl.ANY)] * len(after),
        out_specs=[vmem] * len(outs),
        scratch_shapes=list(scratch),
        compiler_params=pltpu.CompilerParams(vmem_limit_bytes=40 * 2**20),
        cost_estimate=pl.CostEstimate(flops=flops, bytes_accessed=moved, transcendentals=0),
    )(*operands, *after)


def column_of(row):
    n = row.shape[1]
    eye = iota((n, n), 0) == iota((n, n), 1)
    return jnp.sum(jnp.where(eye, row, 0.0), axis=1, keepdims=True)


def slots_of(rel, experts, capacity):
    n = rel.shape[1]
    same = jnp.broadcast_to(column_of(rel), (n, n)) == jnp.broadcast_to(rel, (n, n))
    before = iota((n, n), 0) < iota((n, n), 1)
    rank = jnp.sum(jnp.where(same & before, 1.0, 0.0), axis=0, keepdims=True)
    return rel * capacity + rank


def terms(value):
    high = value.astype(BF).astype(F32)
    middle = (value - high).astype(BF).astype(F32)
    return high, middle, value - high - middle


def notes_of(slots, mix, gain, n, width):
    r = iota((ROWS, n), 0)
    left = jnp.where(r == 0, slots, 0.0)
    for at, term in enumerate(terms(mix)):
        left = jnp.where(r == 1 + at, term, left)
    r = iota((ROWS, width), 0)
    wide = jnp.concatenate([left, jnp.zeros((ROWS, width - n), F32)], axis=1)
    for at, term in enumerate(terms(gain)):
        wide = jnp.where(r == 4 + at, term, wide)
    return wide.astype(BF)


def slots_in(notes, n):
    return notes[:, :n].astype(F32)[0:1]


def mix_in(notes, n):
    left = notes[:, :n].astype(F32)
    return column_of(left[1:2] + left[2:3] + left[3:4])


def gain_in(notes):
    wide = notes.astype(F32)
    return wide[4:5] + wide[5:6] + wide[6:7]


def pack_rows(box, slots, values, out_refs):
    n = values.shape[0]
    line = jnp.broadcast_to(slots.astype(jnp.int32), (ROWS, n))
    r = iota((ROWS, n), 0)
    for j, out in enumerate(out_refs):
        first = j * box.capacity
        for g in range(box.groups):
            sel = jnp.where(line == first + g * ROWS + r, 1.0, 0.0).astype(BF)
            out[:, box.group(g)] = dot(sel, values).astype(BF)
        if box.extra:
            total = jnp.zeros((ROWS, box.wide), F32)
            for i in range(box.pieces):
                at, size = box.piece(i)
                hit = (line == first + box.groups * ROWS + r // box.cuts) & (r % box.cuts == i)
                hit &= r // box.cuts < box.extra
                got = dot(jnp.where(hit, 1.0, 0.0).astype(BF), values[:, at : at + size])
                if size < box.wide:
                    got = jnp.concatenate([got, jnp.zeros((ROWS, box.wide - size), F32)], axis=1)
                total = total + got
            out[:, box.tail()] = total.astype(BF)


def pick_rows(box, slots, boxes, n, picked):
    count = len(boxes)
    slots = column_of(slots)
    if box.groups:
        stack = jnp.concatenate(
            [b[:, g * box.width : (g + 1) * box.width] for b in boxes for g in range(box.groups)],
            axis=0,
        )
        tall = count * box.groups * ROWS
        c = iota((n, tall), 1)
        slot = c // (box.groups * ROWS) * box.capacity + c % (box.groups * ROWS)
        sel = jnp.where(slots.astype(jnp.int32) == slot, 1.0, 0.0).astype(BF)
        picked[...] = dot(sel, stack)
    else:
        picked[...] = jnp.zeros(picked.shape, F32)
    if box.extra:
        tails = jnp.concatenate([b[:, box.groups * box.width :] for b in boxes], axis=0)
        c = iota((n, count * ROWS), 1)
        r = c % ROWS
        slot = c // ROWS * box.capacity + box.groups * ROWS + r // box.cuts
        mine = (slots.astype(jnp.int32) == slot) & (r // box.cuts < box.extra)
        for i in range(box.pieces):
            at, size = box.piece(i)
            sel = jnp.where(mine & (r % box.cuts == i), 1.0, 0.0).astype(BF)
            picked[:, at : at + size] += dot(sel, tails[:, :size])


def heights(box, count):
    extra = -(-count * box.extra // ROWS) * ROWS
    return count * box.groups * ROWS, extra


def unpack(box, refs, stack, tails, at=0):
    count = 0
    for ref in refs:
        for p in range(ref.shape[0] // ROWS):
            for g in range(box.groups):
                stack[at : at + ROWS, :] = ref[p * ROWS : (p + 1) * ROWS, box.group(g)]
                at += ROWS
            if box.extra:
                tails[count * ROWS : (count + 1) * ROWS, :] = ref[
                    p * ROWS : (p + 1) * ROWS, box.tail()
                ]
            count += 1
    if box.extra:
        extra = heights(box, count)[1]
        r = iota((extra, count * ROWS), 0)
        c = iota((extra, count * ROWS), 1)
        mine = (r // box.extra == c // ROWS) & (r % box.extra == c % ROWS // box.cuts)
        for i in range(box.pieces):
            start, size = box.piece(i)
            sel = jnp.where(mine & (c % ROWS % box.cuts == i), 1.0, 0.0).astype(BF)
            stack[at : at + extra, start : start + size] = dot(sel, tails[:, :size]).astype(BF)


def repack(box, rows, refs):
    rows = rows.astype(BF)
    at = 0
    count = 0
    for ref in refs:
        for p in range(ref.shape[0] // ROWS):
            for g in range(box.groups):
                ref[p * ROWS : (p + 1) * ROWS, box.group(g)] = rows[at : at + ROWS]
                at += ROWS
            count += 1
    if box.extra:
        extra = heights(box, count)[1]
        r = iota((count * ROWS, extra), 0)
        c = iota((count * ROWS, extra), 1)
        mine = (c // box.extra == r // ROWS) & (c % box.extra == r % ROWS // box.cuts)
        total = jnp.zeros((count * ROWS, box.wide), F32)
        for i in range(box.pieces):
            start, size = box.piece(i)
            sel = jnp.where(mine & (r % ROWS % box.cuts == i), 1.0, 0.0).astype(BF)
            got = dot(sel, rows[at:, start : start + size])
            if size < box.wide:
                pad = jnp.zeros((count * ROWS, box.wide - size), F32)
                got = jnp.concatenate([got, pad], axis=1)
            total = total + got
        total = total.astype(BF)
        count = 0
        for ref in refs:
            tall = ref.shape[0]
            ref[:, box.tail()] = total[count : count + tall]
            count += tall


def inv_rms(wide):
    return lax.rsqrt(jnp.mean(wide * wide, axis=-1, keepdims=True) + EPSILON)


def total_of(refs):
    return sum(ref[...].astype(F32) for ref in refs).astype(BF)


def start_kernel(box, experts, tokens, cot, gain, ids, mix, ahead, notes0, notes1, *boxes):
    n, width = tokens.shape
    mine = lax.axis_index("expert") // SPLIT
    for k, notes in enumerate((notes0, notes1)):
        rel = ids[k : k + 1, :] - mine
        rel = jnp.where(rel < 0, rel + experts, rel).astype(F32)
        slots = slots_of(rel, experts, box.capacity)
        notes[...] = notes_of(slots, mix[k : k + 1, :], gain[...], n, width)
    ahead[:n] = tokens[...]
    ahead[n:] = notes0[...]
    wide = tokens[...].astype(F32)
    normed = (wide * inv_rms(wide) * gain[...]).astype(BF)
    crossing = boxes[2:]
    firsts = [boxes[0]] + [ref.at[:ROWS] for ref in crossing]
    pack_rows(box, slots_in(notes0[...], n), normed, firsts)
    seconds = [boxes[1]] + [ref.at[ROWS:] for ref in crossing]
    pack_rows(box, slots_in(notes1[...], n), cot[...], seconds)


def combine(box, notes, n, own, back, picked):
    sums = [total_of(own)] + [ref[...] for ref in back]
    pick_rows(box, slots_in(notes, n), sums, n, picked)
    return mix_in(notes, n) * picked[...]


def split_refs(refs, experts, outs):
    ins = refs[:-outs]
    return ins[experts - 1 :], ins[: experts - 1], refs[-outs:]


def middle_kernel(box, experts, arrived, cot, notes1, gain, *refs):
    boxes, picked = refs[-1 - experts : -1], refs[-1]
    own, back, (after, behind) = split_refs(refs[: -1 - experts], experts, 2)
    n = cot.shape[0]
    update = combine(box, arrived[n:], n, own, back, picked)
    later = (arrived[:n].astype(F32) + update).astype(BF)
    after[...] = later
    behind[:n] = later
    behind[n : 2 * n] = cot[...]
    behind[2 * n :] = notes1[...]
    wide = later.astype(F32)
    normed = (wide * inv_rms(wide) * gain[...]).astype(BF)
    pack_rows(box, slots_in(notes1[...], n), normed, boxes)


def final_kernel(box, experts, hidden, notes, *refs):
    picked = refs[-1]
    own, back, (out,) = split_refs(refs[:-1], experts, 1)
    n = hidden.shape[0]
    update = combine(box, notes[...], n, own, back, picked)
    out[...] = (hidden[...].astype(F32) + update).astype(BF)


def norm_back(hidden, gain, grad):
    wide = hidden.astype(F32)
    inv = inv_rms(wide)
    scaled = grad * gain
    along = jnp.mean(scaled * wide, axis=-1, keepdims=True)
    return inv * scaled - wide * (inv * inv * inv * along)


def turn_kernel(box, experts, arrived, notes0, *refs):
    boxes, picked = refs[-1 - experts : -1], refs[-1]
    own, back, (out,) = split_refs(refs[: -1 - experts], experts, 1)
    n = out.shape[0]
    notes = arrived[2 * n :]
    d_normed = combine(box, notes, n, own, back, picked)
    change = norm_back(arrived[:n], gain_in(notes), d_normed)
    now = (arrived[n : 2 * n].astype(F32) + change).astype(BF)
    out[...] = now
    pack_rows(box, slots_in(notes0[...], n), now, boxes)


def last_kernel(box, experts, grad, hidden, notes0, gain, *refs):
    picked = refs[-1]
    own, back, (out,) = split_refs(refs[:-1], experts, 1)
    n = hidden.shape[0]
    d_normed = combine(box, notes0[...], n, own, back, picked)
    change = norm_back(hidden[...], gain[...], d_normed)
    out[...] = (grad[...].astype(F32) + change).astype(BF)


def spans(tall):
    return pl.ds(0, 2 * tall), pl.ds(tall, 2 * tall)


def gate_up(rows, pack):
    return dot(rows, pack[: 2 * (pack.shape[0] // 3)], NT)


def parts_of(both):
    units = both.shape[1] // 2
    return both[:, :units], both[:, units:]


def down_rows(both, pack):
    g, u = parts_of(both)
    return dot((jax.nn.silu(g) * u).astype(BF), pack[2 * g.shape[1] :])


def inner_of(rows, pack):
    return dot(rows, pack[2 * (pack.shape[0] // 3) :], NT)


def part_rows(d_inner, both, pack):
    g, u = parts_of(both)
    r = jax.nn.sigmoid(g)
    d_gate = d_inner * u * r * (1.0 + g * (1.0 - r))
    d_up = d_inner * g * r
    return dot(jnp.concatenate([d_gate, d_up], axis=1).astype(BF), pack[: both.shape[1]])


def read_rows(box, rows, stack, tails):
    tall = stack.shape[0] // 3
    for at, ref in enumerate(rows):
        unpack(box, [ref], stack, tails, at * tall)
    return [stack[span, :] for span in spans(tall)]


def write_rows(box, top, bottom, outs):
    tall = top.shape[0] // 2
    for ref, value in zip(outs, (top[:tall], top[tall:] + bottom[:tall], bottom[tall:])):
        repack(box, value, [ref])


def forward_kernel(box, packs, saved, rows, outs, kept, stack, tails):
    sides = read_rows(box, rows, stack, tails)
    total = []
    for side, values in enumerate(sides):
        total.append(0.0)
        for at in (2 * side, 2 * side + 1):
            both = gate_up(values, packs[at])
            kept[at][...] = both
            total[side] = total[side] + down_rows(both, packs[at])
    write_rows(box, *total, outs)


def inner_kernel(box, packs, saved, rows, outs, kept, stack, tails):
    for side, values in enumerate(read_rows(box, rows, stack, tails)):
        for at in (2 * side, 2 * side + 1):
            kept[at][...] = inner_of(values, packs[at])


def gate_back_kernel(box, packs, saved, rows, outs, kept, stack, tails):
    sides = read_rows(box, rows, stack, tails)
    total = []
    for side, values in enumerate(sides):
        total.append(0.0)
        for at in (2 * side, 2 * side + 1):
            both = gate_up(values, packs[at])
            kept[at][...] = both
            total[side] = total[side] + part_rows(saved[at][...], both, packs[at])
    write_rows(box, *total, outs)


def back_kernel(box, packs, saved, rows, outs, kept, stack, tails):
    sides = read_rows(box, rows, stack, tails)
    total = []
    for side, values in enumerate(sides):
        total.append(0.0)
        for at in (2 * side, 2 * side + 1):
            d_inner = inner_of(values, packs[at])
            total[side] = total[side] + part_rows(d_inner, saved[at][...], packs[at])
    write_rows(box, *total, outs)


def down_kernel(box, packs, saved, rows, outs, kept, stack, tails):
    total = []
    for side in range(2):
        at = 2 * side
        total.append(sum(down_rows(saved[i][...], packs[i]) for i in (at, at + 1)))
    write_rows(box, *total, outs)


def expert_call(kernel, box, packs, rows, saved=(), outs=True, kept=0, reads=True, after=(), window=None):
    width = packs[0].shape[1]
    first, size = window or (0, rows[0].shape[0])
    count = size // ROWS
    tall = sum(heights(box, count))
    boxes = jax.ShapeDtypeStruct((count * ROWS, box.lanes), BF)
    results = [boxes] * len(rows) if outs else []
    if kept:
        units = [pack.shape[0] // 3 for pack in packs]
        results += [jax.ShapeDtypeStruct((2 * tall, kept * u), F32) for u in units]
    inputs = list(packs) + list(saved) + (list(rows) if reads else [])
    n_in, n_p, n_s, n_out = len(inputs), len(packs), len(saved), len(rows) if outs else 0

    def body(*refs):
        results_refs = refs[n_in:-2]
        kernel(
            box,
            refs[:n_p],
            refs[n_p : n_p + n_s],
            [ref.at[pl.ds(first, size)] for ref in refs[n_p + n_s : n_in]],
            results_refs[:n_out],
            results_refs[n_out:],
            refs[-2],
            refs[-1],
        )

    scratch = [
        pltpu.VMEM((3 * tall, width), BF),
        pltpu.VMEM((count * ROWS, max(box.wide, LANES)), BF),
    ]
    flops = sum(2 * 2 * tall * pack.size for pack in packs)
    results = call(body, results, *inputs, scratch=scratch, flops=flops, after=after)
    return results[:n_out], results[n_out:]


def local(tokens, norm_gain, w_gate, w_up, w_down, routes, mix_weights, cotangent):
    experts = lax.axis_size("expert") // SPLIT
    n, width = tokens.shape[1:]
    capacity = n // experts + max(1, n // (16 * experts))
    box = Box(capacity, width)
    gain = norm_gain
    gate_w, up_w, down_w = w_gate[0, 0].T, w_up[0, 0].T, w_down[0, 0]
    boxed = jax.ShapeDtypeStruct((ROWS, box.lanes), BF)
    picked = pltpu.VMEM((n, width), F32)
    bind = functools.partial

    def joined(arrays):
        return arrays[0] if len(arrays) == 1 else jnp.concatenate(arrays, axis=0)

    fence = lax.optimization_barrier

    def crossing_of(boxes):
        return joined([shift(boxes[j - 1], experts=j) for j in range(1, experts)])

    def around(boxes):
        return [shift(boxes, flip=2), boxes, shift(boxes, flip=1)]

    def add(*values):
        return sum(v.astype(F32) for v in values).astype(BF)

    def sums(parts):
        return add(parts[1], shift(parts[0], flip=2), shift(parts[2], flip=1))

    def home(total, sections):
        return [
            shift(total[(j - 1) * ROWS : j * ROWS], sections=sections, experts=-j)
            for j in range(1, experts)
        ]

    def own_home(parts, sections):
        return [
            shift(parts[0], sections=sections, flip=2),
            shift(parts[2], sections=sections, flip=1),
            shift(parts[1], sections=sections),
        ]

    def give_back(cross, own, sections, others=()):
        total = sums(cross)
        back = home(total, sections)
        own, _, others = fence((own, total, others))
        return back + own_home(own, sections), others

    units = w_gate.shape[3]
    cut = -(-units * 7 // 12 // ROWS) * ROWS
    top = jnp.concatenate([gate_w[:cut], up_w[:cut], down_w[:cut]], axis=0)
    bottom = jnp.concatenate([gate_w[cut:], up_w[cut:], down_w[cut:]], axis=0)
    packs = [top, shift(top, flip=1), bottom, shift(bottom, flip=2)]

    def rows_of(count):
        return jax.ShapeDtypeStruct((count, width), BF)

    both = jax.ShapeDtypeStruct((2 * ROWS, box.lanes), BF)
    ahead, notes0, notes1, own_tok, own_cot, *crossing = call(
        bind(start_kernel, box, experts),
        [rows_of(n + ROWS), rows_of(ROWS), rows_of(ROWS), boxed, boxed] + [both] * (experts - 1),
        tokens[0],
        cotangent[0],
        gain,
        routes[0, :, :, 0],
        mix_weights[0, :, :, 0],
        after=[top, bottom],
    )
    crossed = [shift(crossing[j - 1], experts=j) for j in range(1, experts)]
    own0 = around(own_tok)
    packs, crossed, own0 = fence((packs, crossed, own0))
    cross0 = around(joined([c[:ROWS] for c in crossed]))
    cots = joined([own_cot] + [c[ROWS:] for c in crossed])
    cross0, cots = fence((cross0, cots))
    cots = around(cots)

    cross_out, cross_kept0 = expert_call(forward_kernel, box, packs, cross0, kept=2)
    own_out, own_kept0 = expert_call(
        forward_kernel, box, packs, own0, kept=2, after=cross_out[:1]
    )
    cross_out, ahead = fence((cross_out, ahead))
    arrived0 = shift(ahead, sections=1)
    got, cots = give_back(cross_out, own_out, 1, cots)
    h1, behind, own1, *boxes1 = call(
        bind(middle_kernel, box, experts),
        [rows_of(n), rows_of(2 * n + ROWS)] + [boxed] * experts,
        arrived0,
        cotangent[0],
        notes1,
        gain,
        *got,
        scratch=[picked],
    )
    cross1, own_z, own_x = fence(
        (crossing_of(boxes1), shift(own1, flip=2), shift(own1, flip=1))
    )
    cross1, own1 = around(cross1), [own_z, own1, own_x]
    inner = bind(expert_call, inner_kernel, box, packs, cots, outs=False, kept=1)
    own_di = inner(window=(0, ROWS))[1]
    cross_di = inner(window=(ROWS, (experts - 1) * ROWS))[1]

    gate_back = bind(expert_call, gate_back_kernel, box, packs, kept=2)
    cross_grad, cross_kept1 = gate_back(cross1, cross_di)
    total = sums(cross_grad)
    own_grad, own_kept1 = gate_back(own1, own_di, after=[total])
    down = bind(expert_call, down_kernel, box, packs, reads=False)
    cross_kept1, _ = fence((cross_kept1, total))
    cross_fin = down(cross1, cross_kept1)[0]
    arrived1 = shift(behind, sections=-1)
    got = home(total, -1) + own_home(own_grad, -1)
    fin_back = home(sums(cross_fin), 0)
    own_fin = down(own1, own_kept1)[0]
    g1, own_g, *boxes_g = call(
        bind(turn_kernel, box, experts),
        [rows_of(n)] + [boxed] * experts,
        arrived1,
        notes0,
        *got,
        scratch=[picked],
    )

    cross_g, own_z, own_x, fin_back = fence(
        (crossing_of(boxes_g), shift(own_g, flip=2), shift(own_g, flip=1), fin_back)
    )
    cross_g, own_g = around(cross_g), [own_z, own_g, own_x]
    back = bind(expert_call, back_kernel, box, packs)
    cross_grad = back(cross_g, cross_kept0)[0]
    total = sums(cross_grad)
    own_grad = back(own_g, own_kept0, after=[total])[0]
    own_grad, own_fin = fence((own_grad, own_fin))
    got = home(total, 0) + own_home(own_grad, 0)
    fin_own = own_home(own_fin, 0)
    (g0,) = call(
        bind(last_kernel, box, experts),
        [rows_of(n)],
        g1,
        tokens[0],
        notes0,
        gain,
        *got,
        scratch=[picked],
    )
    (final,) = call(
        bind(final_kernel, box, experts),
        [rows_of(n)],
        h1,
        notes1,
        *fin_back,
        *fin_own,
        scratch=[picked],
        after=[g0],
    )
    return (final[None], g0[None])


def solution(mesh):
    in_specs = (
        P("section", "expert", None),
        P("section", None),
        P("section", "expert", None, None),
        P("section", "expert", None, None),
        P("section", "expert", None, None),
        P("section", None, "expert", None),
        P("section", None, "expert", None),
        P("section", "expert", None),
    )
    out_specs = (P("section", "expert", None), P("section", "expert", None))
    return jax.shard_map(local, mesh=mesh, in_specs=in_specs, out_specs=out_specs, check_vma=False)
```

```python
import functools

import jax
import jax.numpy as jnp
from jax import lax
from jax.experimental import pallas as pl
from jax.experimental.pallas import tpu as pltpu
from jax.sharding import PartitionSpec as P

SPLIT = 4
EPSILON = 1e-06
BF = jnp.bfloat16
F32 = jnp.float32
ROWS = 16
LANES = 128


def dot(left, right, dims=((1,), (0,))):
    return lax.dot_general(left, right, (dims, ((), ())), preferred_element_type=F32)


NT = ((1,), (1,))


def iota(shape, axis):
    return lax.broadcasted_iota(jnp.int32, shape, axis)


class Box:
    def __init__(self, capacity, width):
        self.capacity, self.width = capacity, width
        self.groups, self.extra = capacity // ROWS, capacity % ROWS
        self.cuts = ROWS // self.extra if self.extra else 1
        self.wide = -(-width // (LANES * self.cuts)) * LANES if self.extra else 0
        self.lanes = self.groups * width + self.wide
        self.pieces = -(-width // self.wide) if self.extra else 0

    def group(self, g):
        return pl.ds(g * self.width, self.width)

    def tail(self):
        return pl.ds(self.groups * self.width, self.wide)

    def piece(self, i):
        return i * self.wide, min(self.wide, self.width - i * self.wide)


def shift(value, sections=0, experts=0, flip=0):
    n_sec, n_own = lax.axis_size("section"), lax.axis_size("expert")
    n_exp = n_own // SPLIT
    if sections % n_sec == 0 and experts % n_exp == 0 and flip == 0:
        return value
    pairs = []
    for sec in range(n_sec):
        for own in range(n_own):
            exp, sl = own // SPLIT, own % SPLIT
            to = ((exp + experts) % n_exp) * SPLIT + (sl ^ flip)
            pairs.append((sec * n_own + own, ((sec + sections) % n_sec) * n_own + to))
    return lax.ppermute(value, ("section", "expert"), pairs)


def call(body, outs, *operands, scratch=(), after=()):
    vmem = pl.BlockSpec(memory_space=pltpu.VMEM)
    read = len(operands)

    def reading(*refs):
        body(*refs[:read], *refs[read + len(after) :])

    return pl.pallas_call(
        reading,
        out_shape=list(outs),
        in_specs=[vmem] * read + [pl.BlockSpec(memory_space=pl.ANY)] * len(after),
        out_specs=[vmem] * len(outs),
        scratch_shapes=list(scratch),
        compiler_params=pltpu.CompilerParams(vmem_limit_bytes=40 * 2**20),
        cost_estimate=pl.CostEstimate(flops=0, bytes_accessed=0, transcendentals=0),
    )(*operands, *after)


def column_of(row):
    n = row.shape[1]
    eye = iota((n, n), 0) == iota((n, n), 1)
    return jnp.sum(jnp.where(eye, row, 0.0), axis=1, keepdims=True)


def slots_of(rel, experts, capacity):
    n = rel.shape[1]
    same = jnp.broadcast_to(column_of(rel), (n, n)) == jnp.broadcast_to(rel, (n, n))
    before = iota((n, n), 0) < iota((n, n), 1)
    rank = jnp.sum(jnp.where(same & before, 1.0, 0.0), axis=0, keepdims=True)
    return rel * capacity + rank


def terms(value):
    high = value.astype(BF).astype(F32)
    middle = (value - high).astype(BF).astype(F32)
    return high, middle, value - high - middle


def notes_of(slots, mix, gain, n, width):
    r = iota((ROWS, n), 0)
    left = jnp.where(r == 0, slots, 0.0)
    for at, term in enumerate(terms(mix)):
        left = jnp.where(r == 1 + at, term, left)
    r = iota((ROWS, width), 0)
    wide = jnp.concatenate([left, jnp.zeros((ROWS, width - n), F32)], axis=1)
    for at, term in enumerate(terms(gain)):
        wide = jnp.where(r == 4 + at, term, wide)
    return wide.astype(BF)


def slots_in(notes, n):
    return notes[:, :n].astype(F32)[0:1]


def mix_in(notes, n):
    left = notes[:, :n].astype(F32)
    return column_of(left[1:2] + left[2:3] + left[3:4])


def gain_in(notes):
    wide = notes.astype(F32)
    return wide[4:5] + wide[5:6] + wide[6:7]


def pack_rows(box, slots, values, out_refs):
    n = values.shape[0]
    line = jnp.broadcast_to(slots.astype(jnp.int32), (ROWS, n))
    r = iota((ROWS, n), 0)
    for j, out in enumerate(out_refs):
        first = j * box.capacity
        for g in range(box.groups):
            sel = jnp.where(line == first + g * ROWS + r, 1.0, 0.0).astype(BF)
            out[:, box.group(g)] = dot(sel, values).astype(BF)
        if box.extra:
            total = jnp.zeros((ROWS, box.wide), F32)
            for i in range(box.pieces):
                at, size = box.piece(i)
                hit = (line == first + box.groups * ROWS + r // box.cuts) & (r % box.cuts == i)
                hit &= r // box.cuts < box.extra
                got = dot(jnp.where(hit, 1.0, 0.0).astype(BF), values[:, at : at + size])
                if size < box.wide:
                    got = jnp.concatenate([got, jnp.zeros((ROWS, box.wide - size), F32)], axis=1)
                total = total + got
            out[:, box.tail()] = total.astype(BF)


def pick_rows(box, slots, boxes, n, picked):
    count = len(boxes)
    slots = column_of(slots)
    if box.groups:
        stack = jnp.concatenate(
            [b[:, g * box.width : (g + 1) * box.width] for b in boxes for g in range(box.groups)],
            axis=0,
        )
        tall = count * box.groups * ROWS
        c = iota((n, tall), 1)
        slot = c // (box.groups * ROWS) * box.capacity + c % (box.groups * ROWS)
        sel = jnp.where(slots.astype(jnp.int32) == slot, 1.0, 0.0).astype(BF)
        picked[...] = dot(sel, stack)
    else:
        picked[...] = jnp.zeros(picked.shape, F32)
    if box.extra:
        tails = jnp.concatenate([b[:, box.groups * box.width :] for b in boxes], axis=0)
        c = iota((n, count * ROWS), 1)
        r = c % ROWS
        slot = c // ROWS * box.capacity + box.groups * ROWS + r // box.cuts
        mine = (slots.astype(jnp.int32) == slot) & (r // box.cuts < box.extra)
        for i in range(box.pieces):
            at, size = box.piece(i)
            sel = jnp.where(mine & (r % box.cuts == i), 1.0, 0.0).astype(BF)
            picked[:, at : at + size] += dot(sel, tails[:, :size])


def heights(box, count):
    extra = -(-count * box.extra // ROWS) * ROWS
    return count * box.groups * ROWS, extra


def unpack(box, refs, stack, tails, at=0):
    count = 0
    for ref in refs:
        for p in range(ref.shape[0] // ROWS):
            for g in range(box.groups):
                stack[at : at + ROWS, :] = ref[p * ROWS : (p + 1) * ROWS, box.group(g)]
                at += ROWS
            if box.extra:
                tails[count * ROWS : (count + 1) * ROWS, :] = ref[
                    p * ROWS : (p + 1) * ROWS, box.tail()
                ]
            count += 1
    if box.extra:
        extra = heights(box, count)[1]
        r = iota((extra, count * ROWS), 0)
        c = iota((extra, count * ROWS), 1)
        mine = (r // box.extra == c // ROWS) & (r % box.extra == c % ROWS // box.cuts)
        for i in range(box.pieces):
            start, size = box.piece(i)
            sel = jnp.where(mine & (c % ROWS % box.cuts == i), 1.0, 0.0).astype(BF)
            stack[at : at + extra, start : start + size] = dot(sel, tails[:, :size]).astype(BF)


def repack(box, rows, refs):
    rows = rows.astype(BF)
    at = 0
    count = 0
    for ref in refs:
        for p in range(ref.shape[0] // ROWS):
            for g in range(box.groups):
                ref[p * ROWS : (p + 1) * ROWS, box.group(g)] = rows[at : at + ROWS]
                at += ROWS
            count += 1
    if box.extra:
        extra = heights(box, count)[1]
        r = iota((count * ROWS, extra), 0)
        c = iota((count * ROWS, extra), 1)
        mine = (c // box.extra == r // ROWS) & (c % box.extra == r % ROWS // box.cuts)
        total = jnp.zeros((count * ROWS, box.wide), F32)
        for i in range(box.pieces):
            start, size = box.piece(i)
            sel = jnp.where(mine & (r % ROWS % box.cuts == i), 1.0, 0.0).astype(BF)
            got = dot(sel, rows[at:, start : start + size])
            if size < box.wide:
                pad = jnp.zeros((count * ROWS, box.wide - size), F32)
                got = jnp.concatenate([got, pad], axis=1)
            total = total + got
        total = total.astype(BF)
        count = 0
        for ref in refs:
            tall = ref.shape[0]
            ref[:, box.tail()] = total[count : count + tall]
            count += tall


def inv_rms(wide):
    return lax.rsqrt(jnp.mean(wide * wide, axis=-1, keepdims=True) + EPSILON)


def total_of(refs):
    return sum(ref[...].astype(F32) for ref in refs).astype(BF)


def start_kernel(box, experts, tokens, cot, gain, ids, mix, ahead, notes0, notes1, *boxes):
    n, width = tokens.shape
    mine = lax.axis_index("expert") // SPLIT
    for k, notes in enumerate((notes0, notes1)):
        rel = ids[k : k + 1, :] - mine
        rel = jnp.where(rel < 0, rel + experts, rel).astype(F32)
        slots = slots_of(rel, experts, box.capacity)
        notes[...] = notes_of(slots, mix[k : k + 1, :], gain[...], n, width)
    ahead[:n] = tokens[...]
    ahead[n:] = notes0[...]
    wide = tokens[...].astype(F32)
    normed = (wide * inv_rms(wide) * gain[...]).astype(BF)
    crossing = boxes[2:]
    firsts = [boxes[0]] + [ref.at[:ROWS] for ref in crossing]
    pack_rows(box, slots_in(notes0[...], n), normed, firsts)
    seconds = [boxes[1]] + [ref.at[ROWS:] for ref in crossing]
    pack_rows(box, slots_in(notes1[...], n), cot[...], seconds)


def combine(box, notes, n, own, back, picked):
    sums = [total_of(own)] + [ref[...] for ref in back]
    pick_rows(box, slots_in(notes, n), sums, n, picked)
    return mix_in(notes, n) * picked[...]


def split_refs(refs, experts, outs):
    ins = refs[:-outs]
    return ins[experts - 1 :], ins[: experts - 1], refs[-outs:]


def middle_kernel(box, experts, arrived, cot, notes1, gain, *refs):
    boxes, picked = refs[-1 - experts : -1], refs[-1]
    own, back, (after, behind) = split_refs(refs[: -1 - experts], experts, 2)
    n = cot.shape[0]
    update = combine(box, arrived[n:], n, own, back, picked)
    later = (arrived[:n].astype(F32) + update).astype(BF)
    after[...] = later
    behind[:n] = later
    behind[n : 2 * n] = cot[...]
    behind[2 * n :] = notes1[...]
    wide = later.astype(F32)
    normed = (wide * inv_rms(wide) * gain[...]).astype(BF)
    pack_rows(box, slots_in(notes1[...], n), normed, boxes)


def final_kernel(box, experts, hidden, notes, *refs):
    picked = refs[-1]
    own, back, (out,) = split_refs(refs[:-1], experts, 1)
    n = hidden.shape[0]
    update = combine(box, notes[...], n, own, back, picked)
    out[...] = (hidden[...].astype(F32) + update).astype(BF)


def norm_back(hidden, gain, grad):
    wide = hidden.astype(F32)
    inv = inv_rms(wide)
    scaled = grad * gain
    along = jnp.mean(scaled * wide, axis=-1, keepdims=True)
    return inv * scaled - wide * (inv * inv * inv * along)


def turn_kernel(box, experts, arrived, notes0, *refs):
    boxes, picked = refs[-1 - experts : -1], refs[-1]
    own, back, (out,) = split_refs(refs[: -1 - experts], experts, 1)
    n = out.shape[0]
    notes = arrived[2 * n :]
    d_normed = combine(box, notes, n, own, back, picked)
    change = norm_back(arrived[:n], gain_in(notes), d_normed)
    now = (arrived[n : 2 * n].astype(F32) + change).astype(BF)
    out[...] = now
    pack_rows(box, slots_in(notes0[...], n), now, boxes)


def last_kernel(box, experts, grad, hidden, notes0, gain, *refs):
    picked = refs[-1]
    own, back, (out,) = split_refs(refs[:-1], experts, 1)
    n = hidden.shape[0]
    d_normed = combine(box, notes0[...], n, own, back, picked)
    change = norm_back(hidden[...], gain[...], d_normed)
    out[...] = (grad[...].astype(F32) + change).astype(BF)


def spans(tall):
    return pl.ds(0, 2 * tall), pl.ds(tall, 2 * tall)


def gate_up(rows, pack):
    return dot(rows, pack[: 2 * (pack.shape[0] // 3)], NT)


def parts_of(both):
    units = both.shape[1] // 2
    return both[:, :units], both[:, units:]


def down_rows(both, pack):
    g, u = parts_of(both)
    return dot((jax.nn.silu(g) * u).astype(BF), pack[2 * g.shape[1] :])


def inner_of(rows, pack):
    return dot(rows, pack[2 * (pack.shape[0] // 3) :], NT)


def part_rows(d_inner, both, pack):
    g, u = parts_of(both)
    r = jax.nn.sigmoid(g)
    d_gate = d_inner * u * r * (1.0 + g * (1.0 - r))
    d_up = d_inner * g * r
    return dot(jnp.concatenate([d_gate, d_up], axis=1).astype(BF), pack[: both.shape[1]])


def read_rows(box, rows, stack, tails):
    tall = stack.shape[0] // 3
    for at, ref in enumerate(rows):
        unpack(box, [ref], stack, tails, at * tall)
    return [stack[span, :] for span in spans(tall)]


def write_rows(box, top, bottom, outs):
    tall = top.shape[0] // 2
    for ref, value in zip(outs, (top[:tall], top[tall:] + bottom[:tall], bottom[tall:])):
        repack(box, value, [ref])


def forward_kernel(box, packs, saved, rows, outs, kept, stack, tails):
    sides = read_rows(box, rows, stack, tails)
    total = []
    for side, values in enumerate(sides):
        total.append(0.0)
        for at in (2 * side, 2 * side + 1):
            both = gate_up(values, packs[at])
            kept[at][...] = both
            total[side] = total[side] + down_rows(both, packs[at])
    write_rows(box, *total, outs)


def inner_kernel(box, packs, saved, rows, outs, kept, stack, tails):
    for side, values in enumerate(read_rows(box, rows, stack, tails)):
        for at in (2 * side, 2 * side + 1):
            kept[at][...] = inner_of(values, packs[at])


def gate_back_kernel(box, packs, saved, rows, outs, kept, stack, tails):
    sides = read_rows(box, rows, stack, tails)
    total = []
    for side, values in enumerate(sides):
        total.append(0.0)
        for at in (2 * side, 2 * side + 1):
            both = gate_up(values, packs[at])
            kept[at][...] = both
            total[side] = total[side] + part_rows(saved[at][...], both, packs[at])
    write_rows(box, *total, outs)


def back_kernel(box, packs, saved, rows, outs, kept, stack, tails):
    sides = read_rows(box, rows, stack, tails)
    total = []
    for side, values in enumerate(sides):
        total.append(0.0)
        for at in (2 * side, 2 * side + 1):
            d_inner = inner_of(values, packs[at])
            total[side] = total[side] + part_rows(d_inner, saved[at][...], packs[at])
    write_rows(box, *total, outs)


def down_kernel(box, packs, saved, rows, outs, kept, stack, tails):
    total = []
    for side in range(2):
        at = 2 * side
        total.append(sum(down_rows(saved[i][...], packs[i]) for i in (at, at + 1)))
    write_rows(box, *total, outs)


def expert_call(kernel, box, packs, rows, saved=(), outs=True, kept=0, reads=True, after=(), window=None):
    width = packs[0].shape[1]
    first, size = window or (0, rows[0].shape[0])
    count = size // ROWS
    tall = sum(heights(box, count))
    boxes = jax.ShapeDtypeStruct((count * ROWS, box.lanes), BF)
    results = [boxes] * len(rows) if outs else []
    if kept:
        units = [pack.shape[0] // 3 for pack in packs]
        results += [jax.ShapeDtypeStruct((2 * tall, kept * u), F32) for u in units]
    inputs = list(packs) + list(saved) + (list(rows) if reads else [])
    n_in, n_p, n_s, n_out = len(inputs), len(packs), len(saved), len(rows) if outs else 0

    def body(*refs):
        results_refs = refs[n_in:-2]
        kernel(
            box,
            refs[:n_p],
            refs[n_p : n_p + n_s],
            [ref.at[pl.ds(first, size)] for ref in refs[n_p + n_s : n_in]],
            results_refs[:n_out],
            results_refs[n_out:],
            refs[-2],
            refs[-1],
        )

    scratch = [
        pltpu.VMEM((3 * tall, width), BF),
        pltpu.VMEM((count * ROWS, max(box.wide, LANES)), BF),
    ]
    results = call(body, results, *inputs, scratch=scratch, after=after)
    return results[:n_out], results[n_out:]


def local(tokens, norm_gain, w_gate, w_up, w_down, routes, mix_weights, cotangent):
    experts = lax.axis_size("expert") // SPLIT
    n, width = tokens.shape[1:]
    capacity = n // experts + max(1, n // (16 * experts))
    box = Box(capacity, width)
    gain = norm_gain
    gate_w, up_w, down_w = w_gate[0, 0].T, w_up[0, 0].T, w_down[0, 0]
    boxed = jax.ShapeDtypeStruct((ROWS, box.lanes), BF)
    picked = pltpu.VMEM((n, width), F32)
    bind = functools.partial

    def joined(arrays):
        return arrays[0] if len(arrays) == 1 else jnp.concatenate(arrays, axis=0)

    fence = lax.optimization_barrier

    def crossing_of(boxes):
        return joined([shift(boxes[j - 1], experts=j) for j in range(1, experts)])

    def around(boxes):
        return [shift(boxes, flip=2), boxes, shift(boxes, flip=1)]

    def add(*values):
        return sum(v.astype(F32) for v in values).astype(BF)

    def sums(parts):
        return add(parts[1], shift(parts[0], flip=2), shift(parts[2], flip=1))

    def home(total, sections):
        return [
            shift(total[(j - 1) * ROWS : j * ROWS], sections=sections, experts=-j)
            for j in range(1, experts)
        ]

    def own_home(parts, sections):
        return [
            shift(parts[0], sections=sections, flip=2),
            shift(parts[2], sections=sections, flip=1),
            shift(parts[1], sections=sections),
        ]

    def give_back(cross, own, sections, others=()):
        total = sums(cross)
        back = home(total, sections)
        own, _, others = fence((own, total, others))
        return back + own_home(own, sections), others

    units = w_gate.shape[3]
    cut = -(-units * 7 // 12 // ROWS) * ROWS
    top = jnp.concatenate([gate_w[:cut], up_w[:cut], down_w[:cut]], axis=0)
    bottom = jnp.concatenate([gate_w[cut:], up_w[cut:], down_w[cut:]], axis=0)
    packs = [top, shift(top, flip=1), bottom, shift(bottom, flip=2)]

    def rows_of(count):
        return jax.ShapeDtypeStruct((count, width), BF)

    both = jax.ShapeDtypeStruct((2 * ROWS, box.lanes), BF)
    ahead, notes0, notes1, own_tok, own_cot, *crossing = call(
        bind(start_kernel, box, experts),
        [rows_of(n + ROWS), rows_of(ROWS), rows_of(ROWS), boxed, boxed] + [both] * (experts - 1),
        tokens[0],
        cotangent[0],
        gain,
        routes[0, :, :, 0],
        mix_weights[0, :, :, 0],
        after=[top, bottom],
    )
    crossed = [shift(crossing[j - 1], experts=j) for j in range(1, experts)]
    own0 = around(own_tok)
    packs, crossed, own0 = fence((packs, crossed, own0))
    cross0 = around(joined([c[:ROWS] for c in crossed]))
    cots = joined([own_cot] + [c[ROWS:] for c in crossed])
    cross0, cots = fence((cross0, cots))
    cots = around(cots)

    cross_out, cross_kept0 = expert_call(forward_kernel, box, packs, cross0, kept=2)
    own_out, own_kept0 = expert_call(
        forward_kernel, box, packs, own0, kept=2, after=cross_out[:1]
    )
    cross_out, ahead = fence((cross_out, ahead))
    arrived0 = shift(ahead, sections=1)
    got, cots = give_back(cross_out, own_out, 1, cots)
    h1, behind, own1, *boxes1 = call(
        bind(middle_kernel, box, experts),
        [rows_of(n), rows_of(2 * n + ROWS)] + [boxed] * experts,
        arrived0,
        cotangent[0],
        notes1,
        gain,
        *got,
        scratch=[picked],
    )
    cross1, own_z, own_x = fence(
        (crossing_of(boxes1), shift(own1, flip=2), shift(own1, flip=1))
    )
    cross1, own1 = around(cross1), [own_z, own1, own_x]
    inner = bind(expert_call, inner_kernel, box, packs, cots, outs=False, kept=1)
    own_di = inner(window=(0, ROWS))[1]
    cross_di = inner(window=(ROWS, (experts - 1) * ROWS))[1]

    gate_back = bind(expert_call, gate_back_kernel, box, packs, kept=2)
    cross_grad, cross_kept1 = gate_back(cross1, cross_di)
    total = sums(cross_grad)
    own_grad, own_kept1 = gate_back(own1, own_di, after=[total])
    down = bind(expert_call, down_kernel, box, packs, reads=False)
    cross_kept1, _ = fence((cross_kept1, total))
    cross_fin = down(cross1, cross_kept1)[0]
    arrived1 = shift(behind, sections=-1)
    got = home(total, -1) + own_home(own_grad, -1)
    fin_back = home(sums(cross_fin), 0)
    own_fin = down(own1, own_kept1)[0]
    g1, own_g, *boxes_g = call(
        bind(turn_kernel, box, experts),
        [rows_of(n)] + [boxed] * experts,
        arrived1,
        notes0,
        *got,
        scratch=[picked],
    )

    cross_g, own_z, own_x, fin_back = fence(
        (crossing_of(boxes_g), shift(own_g, flip=2), shift(own_g, flip=1), fin_back)
    )
    cross_g, own_g = around(cross_g), [own_z, own_g, own_x]
    back = bind(expert_call, back_kernel, box, packs)
    cross_grad = back(cross_g, cross_kept0)[0]
    total = sums(cross_grad)
    own_grad = back(own_g, own_kept0, after=[total])[0]
    own_grad, own_fin = fence((own_grad, own_fin))
    got = home(total, 0) + own_home(own_grad, 0)
    fin_own = own_home(own_fin, 0)
    (g0,) = call(
        bind(last_kernel, box, experts),
        [rows_of(n)],
        g1,
        tokens[0],
        notes0,
        gain,
        *got,
        scratch=[picked],
    )
    (final,) = call(
        bind(final_kernel, box, experts),
        [rows_of(n)],
        h1,
        notes1,
        *fin_back,
        *fin_own,
        scratch=[picked],
        after=[g0],
    )
    return (final[None], g0[None])


def solution(mesh):
    in_specs = (
        P("section", "expert", None),
        P("section", None),
        P("section", "expert", None, None),
        P("section", "expert", None, None),
        P("section", "expert", None, None),
        P("section", None, "expert", None),
        P("section", None, "expert", None),
        P("section", "expert", None),
    )
    out_specs = (P("section", "expert", None), P("section", "expert", None))
    return jax.shard_map(local, mesh=mesh, in_specs=in_specs, out_specs=out_specs, check_vma=False)
```

```python
import functools

import jax
import jax.numpy as jnp
from jax import lax
from jax.experimental import pallas as pl
from jax.experimental.pallas import tpu as pltpu
from jax.sharding import PartitionSpec as P

SPLIT = 4
EPSILON = 1e-06
BF = jnp.bfloat16
F32 = jnp.float32
ROWS = 16
LANES = 128


def dot(left, right, dims=((1,), (0,))):
    return lax.dot_general(left, right, (dims, ((), ())), preferred_element_type=F32)


NT = ((1,), (1,))


def iota(shape, axis):
    return lax.broadcasted_iota(jnp.int32, shape, axis)


class Box:
    def __init__(self, capacity, width):
        self.capacity, self.width = capacity, width
        self.groups, self.extra = capacity // ROWS, capacity % ROWS
        self.cuts = ROWS // self.extra if self.extra else 1
        self.wide = -(-width // (LANES * self.cuts)) * LANES if self.extra else 0
        self.lanes = self.groups * width + self.wide
        self.pieces = -(-width // self.wide) if self.extra else 0

    def group(self, g):
        return pl.ds(g * self.width, self.width)

    def tail(self):
        return pl.ds(self.groups * self.width, self.wide)

    def piece(self, i):
        return i * self.wide, min(self.wide, self.width - i * self.wide)


def shift(value, sections=0, experts=0, flip=0):
    n_sec, n_own = lax.axis_size("section"), lax.axis_size("expert")
    n_exp = n_own // SPLIT
    if sections % n_sec == 0 and experts % n_exp == 0 and flip == 0:
        return value
    pairs = []
    for sec in range(n_sec):
        for own in range(n_own):
            exp, sl = own // SPLIT, own % SPLIT
            to = ((exp + experts) % n_exp) * SPLIT + (sl ^ flip)
            pairs.append((sec * n_own + own, ((sec + sections) % n_sec) * n_own + to))
    return lax.ppermute(value, ("section", "expert"), pairs)


def call(body, outs, *operands, scratch=(), flops=0, after=()):
    moved = sum(a.size * a.dtype.itemsize for a in operands)
    moved += sum(o.size * o.dtype.itemsize for o in outs)
    vmem = pl.BlockSpec(memory_space=pltpu.VMEM)
    read = len(operands)

    def reading(*refs):
        body(*refs[:read], *refs[read + len(after) :])

    return pl.pallas_call(
        reading,
        out_shape=list(outs),
        in_specs=[vmem] * read + [pl.BlockSpec(memory_space=pl.ANY)] * len(after),
        out_specs=[vmem] * len(outs),
        scratch_shapes=list(scratch),
        compiler_params=pltpu.CompilerParams(vmem_limit_bytes=40 * 2**20),
        cost_estimate=pl.CostEstimate(flops=flops, bytes_accessed=moved, transcendentals=0),
    )(*operands, *after)


def column_of(row):
    n = row.shape[1]
    eye = iota((n, n), 0) == iota((n, n), 1)
    return jnp.sum(jnp.where(eye, row, 0.0), axis=1, keepdims=True)


def slots_of(rel, experts, capacity):
    n = rel.shape[1]
    same = jnp.broadcast_to(column_of(rel), (n, n)) == jnp.broadcast_to(rel, (n, n))
    before = iota((n, n), 0) < iota((n, n), 1)
    rank = jnp.sum(jnp.where(same & before, 1.0, 0.0), axis=0, keepdims=True)
    return rel * capacity + rank


def terms(value):
    high = value.astype(BF).astype(F32)
    middle = (value - high).astype(BF).astype(F32)
    return high, middle, value - high - middle


def notes_of(slots, mix, gain, n, width):
    r = iota((ROWS, n), 0)
    left = jnp.where(r == 0, slots, 0.0)
    for at, term in enumerate(terms(mix)):
        left = jnp.where(r == 1 + at, term, left)
    r = iota((ROWS, width), 0)
    wide = jnp.concatenate([left, jnp.zeros((ROWS, width - n), F32)], axis=1)
    for at, term in enumerate(terms(gain)):
        wide = jnp.where(r == 4 + at, term, wide)
    return wide.astype(BF)


def slots_in(notes, n):
    return notes[:, :n].astype(F32)[0:1]


def mix_in(notes, n):
    left = notes[:, :n].astype(F32)
    return column_of(left[1:2] + left[2:3] + left[3:4])


def gain_in(notes):
    wide = notes.astype(F32)
    return wide[4:5] + wide[5:6] + wide[6:7]


def pack_rows(box, slots, values, out_refs):
    n = values.shape[0]
    line = jnp.broadcast_to(slots.astype(jnp.int32), (ROWS, n))
    r = iota((ROWS, n), 0)
    for j, out in enumerate(out_refs):
        first = j * box.capacity
        for g in range(box.groups):
            sel = jnp.where(line == first + g * ROWS + r, 1.0, 0.0).astype(BF)
            out[:, box.group(g)] = dot(sel, values).astype(BF)
        if box.extra:
            total = jnp.zeros((ROWS, box.wide), F32)
            for i in range(box.pieces):
                at, size = box.piece(i)
                hit = (line == first + box.groups * ROWS + r // box.cuts) & (r % box.cuts == i)
                hit &= r // box.cuts < box.extra
                got = dot(jnp.where(hit, 1.0, 0.0).astype(BF), values[:, at : at + size])
                if size < box.wide:
                    got = jnp.concatenate([got, jnp.zeros((ROWS, box.wide - size), F32)], axis=1)
                total = total + got
            out[:, box.tail()] = total.astype(BF)


def pick_rows(box, slots, boxes, n, picked):
    count = len(boxes)
    slots = column_of(slots)
    if box.groups:
        stack = jnp.concatenate(
            [b[:, g * box.width : (g + 1) * box.width] for b in boxes for g in range(box.groups)],
            axis=0,
        )
        tall = count * box.groups * ROWS
        c = iota((n, tall), 1)
        slot = c // (box.groups * ROWS) * box.capacity + c % (box.groups * ROWS)
        sel = jnp.where(slots.astype(jnp.int32) == slot, 1.0, 0.0).astype(BF)
        picked[...] = dot(sel, stack)
    else:
        picked[...] = jnp.zeros(picked.shape, F32)
    if box.extra:
        tails = jnp.concatenate([b[:, box.groups * box.width :] for b in boxes], axis=0)
        c = iota((n, count * ROWS), 1)
        r = c % ROWS
        slot = c // ROWS * box.capacity + box.groups * ROWS + r // box.cuts
        mine = (slots.astype(jnp.int32) == slot) & (r // box.cuts < box.extra)
        for i in range(box.pieces):
            at, size = box.piece(i)
            sel = jnp.where(mine & (r % box.cuts == i), 1.0, 0.0).astype(BF)
            picked[:, at : at + size] += dot(sel, tails[:, :size])


def heights(box, count):
    extra = -(-count * box.extra // ROWS) * ROWS
    return count * box.groups * ROWS, extra


def unpack(box, refs, stack, tails, at=0):
    count = 0
    for ref in refs:
        for p in range(ref.shape[0] // ROWS):
            for g in range(box.groups):
                stack[at : at + ROWS, :] = ref[p * ROWS : (p + 1) * ROWS, box.group(g)]
                at += ROWS
            if box.extra:
                tails[count * ROWS : (count + 1) * ROWS, :] = ref[
                    p * ROWS : (p + 1) * ROWS, box.tail()
                ]
            count += 1
    if box.extra:
        extra = heights(box, count)[1]
        r = iota((extra, count * ROWS), 0)
        c = iota((extra, count * ROWS), 1)
        mine = (r // box.extra == c // ROWS) & (r % box.extra == c % ROWS // box.cuts)
        for i in range(box.pieces):
            start, size = box.piece(i)
            sel = jnp.where(mine & (c % ROWS % box.cuts == i), 1.0, 0.0).astype(BF)
            stack[at : at + extra, start : start + size] = dot(sel, tails[:, :size]).astype(BF)


def repack(box, rows, refs):
    rows = rows.astype(BF)
    at = 0
    count = 0
    for ref in refs:
        for p in range(ref.shape[0] // ROWS):
            for g in range(box.groups):
                ref[p * ROWS : (p + 1) * ROWS, box.group(g)] = rows[at : at + ROWS]
                at += ROWS
            count += 1
    if box.extra:
        extra = heights(box, count)[1]
        r = iota((count * ROWS, extra), 0)
        c = iota((count * ROWS, extra), 1)
        mine = (c // box.extra == r // ROWS) & (c % box.extra == r % ROWS // box.cuts)
        total = jnp.zeros((count * ROWS, box.wide), F32)
        for i in range(box.pieces):
            start, size = box.piece(i)
            sel = jnp.where(mine & (r % ROWS % box.cuts == i), 1.0, 0.0).astype(BF)
            got = dot(sel, rows[at:, start : start + size])
            if size < box.wide:
                pad = jnp.zeros((count * ROWS, box.wide - size), F32)
                got = jnp.concatenate([got, pad], axis=1)
            total = total + got
        total = total.astype(BF)
        count = 0
        for ref in refs:
            tall = ref.shape[0]
            ref[:, box.tail()] = total[count : count + tall]
            count += tall


def inv_rms(wide):
    return lax.rsqrt(jnp.mean(wide * wide, axis=-1, keepdims=True) + EPSILON)


def total_of(refs):
    return sum(ref[...].astype(F32) for ref in refs).astype(BF)


def start_kernel(box, experts, tokens, cot, gain, ids, mix, ahead, notes0, notes1, *boxes):
    n, width = tokens.shape
    mine = lax.axis_index("expert") // SPLIT
    for k, notes in enumerate((notes0, notes1)):
        rel = ids[k : k + 1, :] - mine
        rel = jnp.where(rel < 0, rel + experts, rel).astype(F32)
        slots = slots_of(rel, experts, box.capacity)
        notes[...] = notes_of(slots, mix[k : k + 1, :], gain[...], n, width)
    ahead[:n] = tokens[...]
    ahead[n:] = notes0[...]
    wide = tokens[...].astype(F32)
    normed = (wide * inv_rms(wide) * gain[...]).astype(BF)
    crossing = boxes[2:]
    firsts = [boxes[0]] + [ref.at[:ROWS] for ref in crossing]
    pack_rows(box, slots_in(notes0[...], n), normed, firsts)
    seconds = [boxes[1]] + [ref.at[ROWS:] for ref in crossing]
    pack_rows(box, slots_in(notes1[...], n), cot[...], seconds)


def combine(box, notes, n, own, back, picked):
    sums = [total_of(own)] + [ref[...] for ref in back]
    pick_rows(box, slots_in(notes, n), sums, n, picked)
    return mix_in(notes, n) * picked[...]


def split_refs(refs, experts, outs):
    ins = refs[:-outs]
    return ins[experts - 1 :], ins[: experts - 1], refs[-outs:]


def middle_kernel(box, experts, arrived, cot, notes1, gain, *refs):
    boxes, picked = refs[-1 - experts : -1], refs[-1]
    own, back, (after, behind) = split_refs(refs[: -1 - experts], experts, 2)
    n = cot.shape[0]
    update = combine(box, arrived[n:], n, own, back, picked)
    later = (arrived[:n].astype(F32) + update).astype(BF)
    after[...] = later
    behind[:n] = later
    behind[n : 2 * n] = cot[...]
    behind[2 * n :] = notes1[...]
    wide = later.astype(F32)
    normed = (wide * inv_rms(wide) * gain[...]).astype(BF)
    pack_rows(box, slots_in(notes1[...], n), normed, boxes)


def final_kernel(box, experts, hidden, notes, *refs):
    picked = refs[-1]
    own, back, (out,) = split_refs(refs[:-1], experts, 1)
    n = hidden.shape[0]
    own = [ref.at[ROWS:] for ref in own]
    update = combine(box, notes[...], n, own, back, picked)
    out[...] = (hidden[...].astype(F32) + update).astype(BF)


def norm_back(hidden, gain, grad):
    wide = hidden.astype(F32)
    inv = inv_rms(wide)
    scaled = grad * gain
    along = jnp.mean(scaled * wide, axis=-1, keepdims=True)
    return inv * scaled - wide * (inv * inv * inv * along)


def turn_kernel(box, experts, arrived, notes0, *refs):
    boxes, picked = refs[-1 - experts : -1], refs[-1]
    own, back, (out,) = split_refs(refs[: -1 - experts], experts, 1)
    n = out.shape[0]
    notes = arrived[2 * n :]
    d_normed = combine(box, notes, n, own, back, picked)
    change = norm_back(arrived[:n], gain_in(notes), d_normed)
    now = (arrived[n : 2 * n].astype(F32) + change).astype(BF)
    out[...] = now
    pack_rows(box, slots_in(notes0[...], n), now, boxes)


def last_kernel(box, experts, grad, hidden, notes0, gain, *refs):
    picked = refs[-1]
    own, back, (out,) = split_refs(refs[:-1], experts, 1)
    n = hidden.shape[0]
    own = [ref.at[:ROWS] for ref in own]
    d_normed = combine(box, notes0[...], n, own, back, picked)
    change = norm_back(hidden[...], gain[...], d_normed)
    out[...] = (grad[...].astype(F32) + change).astype(BF)


def spans(tall):
    return pl.ds(0, 2 * tall), pl.ds(tall, 2 * tall)


def gate_up(rows, pack):
    return dot(rows, pack[: 2 * (pack.shape[0] // 3)], NT)


def parts_of(both):
    units = both.shape[1] // 2
    return both[:, :units], both[:, units:]


def down_rows(both, pack):
    g, u = parts_of(both)
    return dot((jax.nn.silu(g) * u).astype(BF), pack[2 * g.shape[1] :])


def inner_of(rows, pack):
    return dot(rows, pack[2 * (pack.shape[0] // 3) :], NT)


def part_rows(d_inner, both, pack):
    g, u = parts_of(both)
    r = jax.nn.sigmoid(g)
    d_gate = d_inner * u * r * (1.0 + g * (1.0 - r))
    d_up = d_inner * g * r
    return dot(jnp.concatenate([d_gate, d_up], axis=1).astype(BF), pack[: both.shape[1]])


def read_rows(box, rows, stack, tails):
    tall = stack.shape[0] // 3
    for at, ref in enumerate(rows):
        unpack(box, [ref], stack, tails, at * tall)
    return [stack[span, :] for span in spans(tall)]


def write_rows(box, top, bottom, outs):
    tall = top.shape[0] // 2
    for ref, value in zip(outs, (top[:tall], top[tall:] + bottom[:tall], bottom[tall:])):
        repack(box, value, [ref])


def forward_kernel(box, packs, saved, rows, outs, kept, stack, tails):
    sides = read_rows(box, rows, stack, tails)
    total = []
    for side, values in enumerate(sides):
        total.append(0.0)
        for at in (2 * side, 2 * side + 1):
            both = gate_up(values, packs[at])
            kept[at][...] = both
            total[side] = total[side] + down_rows(both, packs[at])
    write_rows(box, *total, outs)


def inner_kernel(box, packs, saved, rows, outs, kept, stack, tails):
    for side, values in enumerate(read_rows(box, rows, stack, tails)):
        for at in (2 * side, 2 * side + 1):
            kept[at][...] = inner_of(values, packs[at])


def gate_back_kernel(box, packs, saved, rows, outs, kept, stack, tails):
    sides = read_rows(box, rows, stack, tails)
    total = []
    for side, values in enumerate(sides):
        total.append(0.0)
        for at in (2 * side, 2 * side + 1):
            both = gate_up(values, packs[at])
            kept[at][...] = both
            total[side] = total[side] + part_rows(saved[at][...], both, packs[at])
    write_rows(box, *total, outs)


def back_kernel(box, packs, saved, rows, outs, kept, stack, tails):
    sides = read_rows(box, rows, stack, tails)
    total = []
    for side, values in enumerate(sides):
        total.append(0.0)
        for at in (2 * side, 2 * side + 1):
            d_inner = inner_of(values, packs[at])
            total[side] = total[side] + part_rows(d_inner, saved[at][...], packs[at])
    write_rows(box, *total, outs)


def down_kernel(box, packs, saved, rows, outs, kept, stack, tails):
    total = []
    for side in range(2):
        at = 2 * side
        total.append(sum(down_rows(saved[i][...], packs[i]) for i in (at, at + 1)))
    write_rows(box, *total, outs)


def expert_call(kernel, box, packs, rows, saved=(), outs=True, kept=0, reads=True, after=(), window=None):
    width = packs[0].shape[1]
    first, size = window or (0, rows[0].shape[0])
    count = size // ROWS
    tall = sum(heights(box, count))
    boxes = jax.ShapeDtypeStruct((count * ROWS, box.lanes), BF)
    results = [boxes] * len(rows) if outs else []
    if kept:
        units = [pack.shape[0] // 3 for pack in packs]
        results += [jax.ShapeDtypeStruct((2 * tall, kept * u), F32) for u in units]
    inputs = list(packs) + list(saved) + (list(rows) if reads else [])
    n_in, n_p, n_s, n_out = len(inputs), len(packs), len(saved), len(rows) if outs else 0

    def body(*refs):
        results_refs = refs[n_in:-2]
        kernel(
            box,
            refs[:n_p],
            refs[n_p : n_p + n_s],
            [ref.at[pl.ds(first, size)] for ref in refs[n_p + n_s : n_in]],
            results_refs[:n_out],
            results_refs[n_out:],
            refs[-2],
            refs[-1],
        )

    scratch = [
        pltpu.VMEM((3 * tall, width), BF),
        pltpu.VMEM((count * ROWS, max(box.wide, LANES)), BF),
    ]
    flops = sum(2 * 2 * tall * pack.size for pack in packs)
    results = call(body, results, *inputs, scratch=scratch, flops=flops, after=after)
    return results[:n_out], results[n_out:]


def local(tokens, norm_gain, w_gate, w_up, w_down, routes, mix_weights, cotangent):
    experts = lax.axis_size("expert") // SPLIT
    n, width = tokens.shape[1:]
    capacity = n // experts + max(1, n // (16 * experts))
    box = Box(capacity, width)
    gain = norm_gain
    gate_w, up_w, down_w = w_gate[0, 0].T, w_up[0, 0].T, w_down[0, 0]
    boxed = jax.ShapeDtypeStruct((ROWS, box.lanes), BF)
    picked = pltpu.VMEM((n, width), F32)
    bind = functools.partial

    def joined(arrays):
        return arrays[0] if len(arrays) == 1 else jnp.concatenate(arrays, axis=0)

    fence = lax.optimization_barrier

    def crossing_of(boxes):
        return joined([shift(boxes[j - 1], experts=j) for j in range(1, experts)])

    def around(boxes):
        return [shift(boxes, flip=2), boxes, shift(boxes, flip=1)]

    def add(*values):
        return sum(v.astype(F32) for v in values).astype(BF)

    def sums(parts):
        return add(parts[1], shift(parts[0], flip=2), shift(parts[2], flip=1))

    def home(total, sections):
        return [
            shift(total[(j - 1) * ROWS : j * ROWS], sections=sections, experts=-j)
            for j in range(1, experts)
        ]

    def own_home(parts, sections):
        return [
            shift(parts[0], sections=sections, flip=2),
            shift(parts[2], sections=sections, flip=1),
            shift(parts[1], sections=sections),
        ]

    def give_back(cross, own, sections, others=()):
        total = sums(cross)
        back = home(total, sections)
        own, _, others = fence((own, total, others))
        return back + own_home(own, sections), others

    units = w_gate.shape[3]
    cut = -(-units * 7 // 12 // ROWS) * ROWS
    top = jnp.concatenate([gate_w[:cut], up_w[:cut], down_w[:cut]], axis=0)
    bottom = jnp.concatenate([gate_w[cut:], up_w[cut:], down_w[cut:]], axis=0)
    packs = [top, shift(top, flip=1), bottom, shift(bottom, flip=2)]

    def rows_of(count):
        return jax.ShapeDtypeStruct((count, width), BF)

    both = jax.ShapeDtypeStruct((2 * ROWS, box.lanes), BF)
    ahead, notes0, notes1, own_tok, own_cot, *crossing = call(
        bind(start_kernel, box, experts),
        [rows_of(n + ROWS), rows_of(ROWS), rows_of(ROWS), boxed, boxed] + [both] * (experts - 1),
        tokens[0],
        cotangent[0],
        gain,
        routes[0, :, :, 0],
        mix_weights[0, :, :, 0],
        after=[top, bottom],
    )
    crossed = [shift(crossing[j - 1], experts=j) for j in range(1, experts)]
    own0 = around(own_tok)
    packs, crossed, own0 = fence((packs, crossed, own0))
    cross0 = around(joined([c[:ROWS] for c in crossed]))
    cots = joined([own_cot] + [c[ROWS:] for c in crossed])
    cross0, cots = fence((cross0, cots))
    cots = around(cots)

    cross_out, cross_kept0 = expert_call(forward_kernel, box, packs, cross0, kept=2)
    own_out, own_kept0 = expert_call(
        forward_kernel, box, packs, own0, kept=2, after=cross_out[:1]
    )
    cross_out, ahead = fence((cross_out, ahead))
    arrived0 = shift(ahead, sections=1)
    got, cots = give_back(cross_out, own_out, 1, cots)
    h1, behind, own1, *boxes1 = call(
        bind(middle_kernel, box, experts),
        [rows_of(n), rows_of(2 * n + ROWS)] + [boxed] * experts,
        arrived0,
        cotangent[0],
        notes1,
        gain,
        *got,
        scratch=[picked],
    )
    arrived1 = shift(behind, sections=-1)
    cross1, own_z, own_x, arrived1 = fence(
        (crossing_of(boxes1), shift(own1, flip=2), shift(own1, flip=1), arrived1)
    )
    cross1, own1 = around(cross1), [own_z, own1, own_x]
    inner = bind(expert_call, inner_kernel, box, packs, cots, outs=False, kept=1)
    own_di = inner(window=(0, ROWS))[1]
    cross_di = inner(window=(ROWS, (experts - 1) * ROWS))[1]

    gate_back = bind(expert_call, gate_back_kernel, box, packs, kept=2)
    own_grad, own_kept1 = gate_back(own1, own_di)
    cross_grad, cross_kept1 = gate_back(cross1, cross_di, after=own_grad[:1])
    down = bind(expert_call, down_kernel, box, packs, reads=False)
    cross_fin = down(cross1, cross_kept1)[0]
    got, _ = give_back(cross_grad, own_grad, -1)
    got[: experts - 1], fin_sums = fence((got[: experts - 1], sums(cross_fin)))
    fin_back = home(fin_sums, 0)
    own_fin = down(own1, own_kept1)[0]
    g1, own_g, *boxes_g = call(
        bind(turn_kernel, box, experts),
        [rows_of(n)] + [boxed] * experts,
        arrived1,
        notes0,
        *got,
        scratch=[picked],
    )

    cross_g, own_z, own_x, fin_back = fence(
        (crossing_of(boxes_g), shift(own_g, flip=2), shift(own_g, flip=1), fin_back)
    )
    cross_g, own_g = around(cross_g), [own_z, own_g, own_x]
    back = bind(expert_call, back_kernel, box, packs)
    own_grad = back(own_g, own_kept0)[0]
    cross_grad = back(cross_g, cross_kept0, after=own_grad[:1])[0]
    got = home(sums(cross_grad), 0)
    pairs = own_home([joined(list(both)) for both in zip(own_grad, own_fin)], 0)
    (g0,) = call(
        bind(last_kernel, box, experts),
        [rows_of(n)],
        g1,
        tokens[0],
        notes0,
        gain,
        *got,
        *pairs,
        scratch=[picked],
    )
    (final,) = call(
        bind(final_kernel, box, experts),
        [rows_of(n)],
        h1,
        notes1,
        *fin_back,
        *pairs,
        scratch=[picked],
    )
    return (final[None], g0[None])


def solution(mesh):
    in_specs = (
        P("section", "expert", None),
        P("section", None),
        P("section", "expert", None, None),
        P("section", "expert", None, None),
        P("section", "expert", None, None),
        P("section", None, "expert", None),
        P("section", None, "expert", None),
        P("section", "expert", None),
    )
    out_specs = (P("section", "expert", None), P("section", "expert", None))
    return jax.shard_map(local, mesh=mesh, in_specs=in_specs, out_specs=out_specs, check_vma=False)
```

```python
import functools

import jax
import jax.numpy as jnp
from jax import lax
from jax.experimental import pallas as pl
from jax.experimental.pallas import tpu as pltpu
from jax.sharding import PartitionSpec as P

SPLIT = 4
EPSILON = 1e-06
BF = jnp.bfloat16
F32 = jnp.float32
ROWS = 16
LANES = 128


def dot(left, right, dims=((1,), (0,))):
    return lax.dot_general(left, right, (dims, ((), ())), preferred_element_type=F32)


NT = ((1,), (1,))


def iota(shape, axis):
    return lax.broadcasted_iota(jnp.int32, shape, axis)


class Box:
    def __init__(self, capacity, width):
        self.capacity, self.width = capacity, width
        self.groups, self.extra = capacity // ROWS, capacity % ROWS
        self.cuts = ROWS // self.extra if self.extra else 1
        self.wide = -(-width // (LANES * self.cuts)) * LANES if self.extra else 0
        self.lanes = self.groups * width + self.wide
        self.pieces = -(-width // self.wide) if self.extra else 0

    def group(self, g):
        return pl.ds(g * self.width, self.width)

    def tail(self):
        return pl.ds(self.groups * self.width, self.wide)

    def piece(self, i):
        return i * self.wide, min(self.wide, self.width - i * self.wide)


def shift(value, sections=0, experts=0, flip=0):
    n_sec, n_own = lax.axis_size("section"), lax.axis_size("expert")
    n_exp = n_own // SPLIT
    if sections % n_sec == 0 and experts % n_exp == 0 and flip == 0:
        return value
    pairs = []
    for sec in range(n_sec):
        for own in range(n_own):
            exp, sl = own // SPLIT, own % SPLIT
            to = ((exp + experts) % n_exp) * SPLIT + (sl ^ flip)
            pairs.append((sec * n_own + own, ((sec + sections) % n_sec) * n_own + to))
    return lax.ppermute(value, ("section", "expert"), pairs)


def call(body, outs, *operands, scratch=(), flops=0, after=()):
    moved = sum(a.size * a.dtype.itemsize for a in operands)
    moved += sum(o.size * o.dtype.itemsize for o in outs)
    vmem = pl.BlockSpec(memory_space=pltpu.VMEM)
    read = len(operands)

    def reading(*refs):
        body(*refs[:read], *refs[read + len(after) :])

    return pl.pallas_call(
        reading,
        out_shape=list(outs),
        in_specs=[vmem] * read + [pl.BlockSpec(memory_space=pl.ANY)] * len(after),
        out_specs=[vmem] * len(outs),
        scratch_shapes=list(scratch),
        compiler_params=pltpu.CompilerParams(vmem_limit_bytes=40 * 2**20),
        cost_estimate=pl.CostEstimate(flops=flops, bytes_accessed=moved, transcendentals=0),
    )(*operands, *after)


def column_of(row):
    n = row.shape[1]
    eye = iota((n, n), 0) == iota((n, n), 1)
    return jnp.sum(jnp.where(eye, row, 0.0), axis=1, keepdims=True)


def slots_of(rel, experts, capacity):
    n = rel.shape[1]
    same = jnp.broadcast_to(column_of(rel), (n, n)) == jnp.broadcast_to(rel, (n, n))
    before = iota((n, n), 0) < iota((n, n), 1)
    rank = jnp.sum(jnp.where(same & before, 1.0, 0.0), axis=0, keepdims=True)
    return rel * capacity + rank


def terms(value):
    high = value.astype(BF).astype(F32)
    middle = (value - high).astype(BF).astype(F32)
    return high, middle, value - high - middle


def notes_of(slots, mix, gain, n, width):
    r = iota((ROWS, n), 0)
    left = jnp.where(r == 0, slots, 0.0)
    for at, term in enumerate(terms(mix)):
        left = jnp.where(r == 1 + at, term, left)
    r = iota((ROWS, width), 0)
    wide = jnp.concatenate([left, jnp.zeros((ROWS, width - n), F32)], axis=1)
    for at, term in enumerate(terms(gain)):
        wide = jnp.where(r == 4 + at, term, wide)
    return wide.astype(BF)


def slots_in(notes, n):
    return notes[:, :n].astype(F32)[0:1]


def mix_in(notes, n):
    left = notes[:, :n].astype(F32)
    return column_of(left[1:2] + left[2:3] + left[3:4])


def gain_in(notes):
    wide = notes.astype(F32)
    return wide[4:5] + wide[5:6] + wide[6:7]


def pack_rows(box, slots, values, out_refs):
    n = values.shape[0]
    line = jnp.broadcast_to(slots.astype(jnp.int32), (ROWS, n))
    r = iota((ROWS, n), 0)
    for j, out in enumerate(out_refs):
        first = j * box.capacity
        for g in range(box.groups):
            sel = jnp.where(line == first + g * ROWS + r, 1.0, 0.0).astype(BF)
            out[:, box.group(g)] = dot(sel, values).astype(BF)
        if box.extra:
            total = jnp.zeros((ROWS, box.wide), F32)
            for i in range(box.pieces):
                at, size = box.piece(i)
                hit = (line == first + box.groups * ROWS + r // box.cuts) & (r % box.cuts == i)
                hit &= r // box.cuts < box.extra
                got = dot(jnp.where(hit, 1.0, 0.0).astype(BF), values[:, at : at + size])
                if size < box.wide:
                    got = jnp.concatenate([got, jnp.zeros((ROWS, box.wide - size), F32)], axis=1)
                total = total + got
            out[:, box.tail()] = total.astype(BF)


def pick_rows(box, slots, boxes, n, picked):
    count = len(boxes)
    slots = column_of(slots)
    if box.groups:
        stack = jnp.concatenate(
            [b[:, g * box.width : (g + 1) * box.width] for b in boxes for g in range(box.groups)],
            axis=0,
        )
        tall = count * box.groups * ROWS
        c = iota((n, tall), 1)
        slot = c // (box.groups * ROWS) * box.capacity + c % (box.groups * ROWS)
        sel = jnp.where(slots.astype(jnp.int32) == slot, 1.0, 0.0).astype(BF)
        picked[...] = dot(sel, stack)
    else:
        picked[...] = jnp.zeros(picked.shape, F32)
    if box.extra:
        tails = jnp.concatenate([b[:, box.groups * box.width :] for b in boxes], axis=0)
        c = iota((n, count * ROWS), 1)
        r = c % ROWS
        slot = c // ROWS * box.capacity + box.groups * ROWS + r // box.cuts
        mine = (slots.astype(jnp.int32) == slot) & (r // box.cuts < box.extra)
        for i in range(box.pieces):
            at, size = box.piece(i)
            sel = jnp.where(mine & (r % box.cuts == i), 1.0, 0.0).astype(BF)
            picked[:, at : at + size] += dot(sel, tails[:, :size])


def heights(box, count):
    extra = -(-count * box.extra // ROWS) * ROWS
    return count * box.groups * ROWS, extra


def unpack(box, refs, stack, tails, at=0):
    count = 0
    for ref in refs:
        for p in range(ref.shape[0] // ROWS):
            for g in range(box.groups):
                stack[at : at + ROWS, :] = ref[p * ROWS : (p + 1) * ROWS, box.group(g)]
                at += ROWS
            if box.extra:
                tails[count * ROWS : (count + 1) * ROWS, :] = ref[
                    p * ROWS : (p + 1) * ROWS, box.tail()
                ]
            count += 1
    if box.extra:
        extra = heights(box, count)[1]
        r = iota((extra, count * ROWS), 0)
        c = iota((extra, count * ROWS), 1)
        mine = (r // box.extra == c // ROWS) & (r % box.extra == c % ROWS // box.cuts)
        for i in range(box.pieces):
            start, size = box.piece(i)
            sel = jnp.where(mine & (c % ROWS % box.cuts == i), 1.0, 0.0).astype(BF)
            stack[at : at + extra, start : start + size] = dot(sel, tails[:, :size]).astype(BF)


def repack(box, rows, refs):
    rows = rows.astype(BF)
    at = 0
    count = 0
    for ref in refs:
        for p in range(ref.shape[0] // ROWS):
            for g in range(box.groups):
                ref[p * ROWS : (p + 1) * ROWS, box.group(g)] = rows[at : at + ROWS]
                at += ROWS
            count += 1
    if box.extra:
        extra = heights(box, count)[1]
        r = iota((count * ROWS, extra), 0)
        c = iota((count * ROWS, extra), 1)
        mine = (c // box.extra == r // ROWS) & (c % box.extra == r % ROWS // box.cuts)
        total = jnp.zeros((count * ROWS, box.wide), F32)
        for i in range(box.pieces):
            start, size = box.piece(i)
            sel = jnp.where(mine & (r % ROWS % box.cuts == i), 1.0, 0.0).astype(BF)
            got = dot(sel, rows[at:, start : start + size])
            if size < box.wide:
                pad = jnp.zeros((count * ROWS, box.wide - size), F32)
                got = jnp.concatenate([got, pad], axis=1)
            total = total + got
        total = total.astype(BF)
        count = 0
        for ref in refs:
            tall = ref.shape[0]
            ref[:, box.tail()] = total[count : count + tall]
            count += tall


def inv_rms(wide):
    return lax.rsqrt(jnp.mean(wide * wide, axis=-1, keepdims=True) + EPSILON)


def total_of(refs):
    return sum(ref[...].astype(F32) for ref in refs).astype(BF)


def start_kernel(box, experts, tokens, cot, gain, ids, mix, ahead, notes0, notes1, *boxes):
    n, width = tokens.shape
    mine = lax.axis_index("expert") // SPLIT
    for k, notes in enumerate((notes0, notes1)):
        rel = ids[k : k + 1, :] - mine
        rel = jnp.where(rel < 0, rel + experts, rel).astype(F32)
        slots = slots_of(rel, experts, box.capacity)
        notes[...] = notes_of(slots, mix[k : k + 1, :], gain[...], n, width)
    ahead[:n] = tokens[...]
    ahead[n:] = notes0[...]
    wide = tokens[...].astype(F32)
    normed = (wide * inv_rms(wide) * gain[...]).astype(BF)
    crossing = boxes[2:]
    firsts = [boxes[0]] + [ref.at[:ROWS] for ref in crossing]
    pack_rows(box, slots_in(notes0[...], n), normed, firsts)
    seconds = [boxes[1]] + [ref.at[ROWS:] for ref in crossing]
    pack_rows(box, slots_in(notes1[...], n), cot[...], seconds)


def combine(box, notes, n, own, back, picked):
    sums = [total_of(own)] + [ref[...] for ref in back]
    pick_rows(box, slots_in(notes, n), sums, n, picked)
    return mix_in(notes, n) * picked[...]


def split_refs(refs, experts, outs):
    ins = refs[:-outs]
    return ins[experts - 1 :], ins[: experts - 1], refs[-outs:]


def middle_kernel(box, experts, arrived, cot, notes1, gain, *refs):
    boxes, picked = refs[-1 - experts : -1], refs[-1]
    own, back, (after, behind) = split_refs(refs[: -1 - experts], experts, 2)
    n = cot.shape[0]
    update = combine(box, arrived[n:], n, own, back, picked)
    later = (arrived[:n].astype(F32) + update).astype(BF)
    after[...] = later
    behind[:n] = later
    behind[n : 2 * n] = cot[...]
    behind[2 * n :] = notes1[...]
    wide = later.astype(F32)
    normed = (wide * inv_rms(wide) * gain[...]).astype(BF)
    pack_rows(box, slots_in(notes1[...], n), normed, boxes)


def final_kernel(box, experts, hidden, notes, *refs):
    picked = refs[-1]
    own, back, (out,) = split_refs(refs[:-1], experts, 1)
    n = hidden.shape[0]
    update = combine(box, notes[...], n, own, back, picked)
    out[...] = (hidden[...].astype(F32) + update).astype(BF)


def norm_back(hidden, gain, grad):
    wide = hidden.astype(F32)
    inv = inv_rms(wide)
    scaled = grad * gain
    along = jnp.mean(scaled * wide, axis=-1, keepdims=True)
    return inv * scaled - wide * (inv * inv * inv * along)


def turn_kernel(box, experts, arrived, notes0, *refs):
    boxes, picked = refs[-1 - experts : -1], refs[-1]
    own, back, (out,) = split_refs(refs[: -1 - experts], experts, 1)
    n = out.shape[0]
    notes = arrived[2 * n :]
    d_normed = combine(box, notes, n, own, back, picked)
    change = norm_back(arrived[:n], gain_in(notes), d_normed)
    now = (arrived[n : 2 * n].astype(F32) + change).astype(BF)
    out[...] = now
    pack_rows(box, slots_in(notes0[...], n), now, boxes)


def last_kernel(box, experts, grad, hidden, notes0, gain, *refs):
    picked = refs[-1]
    own, back, (out,) = split_refs(refs[:-1], experts, 1)
    n = hidden.shape[0]
    d_normed = combine(box, notes0[...], n, own, back, picked)
    change = norm_back(hidden[...], gain[...], d_normed)
    out[...] = (grad[...].astype(F32) + change).astype(BF)


def spans(tall):
    return pl.ds(0, 2 * tall), pl.ds(tall, 2 * tall)


def gate_up(rows, pack):
    return dot(rows, pack[: 2 * (pack.shape[0] // 3)], NT)


def parts_of(both):
    units = both.shape[1] // 2
    return both[:, :units], both[:, units:]


def down_rows(both, pack):
    g, u = parts_of(both)
    return dot((jax.nn.silu(g) * u).astype(BF), pack[2 * g.shape[1] :])


def inner_of(rows, pack):
    return dot(rows, pack[2 * (pack.shape[0] // 3) :], NT)


def part_rows(d_inner, both, pack):
    g, u = parts_of(both)
    r = jax.nn.sigmoid(g)
    d_gate = d_inner * u * r * (1.0 + g * (1.0 - r))
    d_up = d_inner * g * r
    return dot(jnp.concatenate([d_gate, d_up], axis=1).astype(BF), pack[: both.shape[1]])


def read_rows(box, rows, stack, tails):
    tall = stack.shape[0] // 3
    for at, ref in enumerate(rows):
        unpack(box, [ref], stack, tails, at * tall)
    return [stack[span, :] for span in spans(tall)]


def write_rows(box, top, bottom, outs):
    tall = top.shape[0] // 2
    for ref, value in zip(outs, (top[:tall], top[tall:] + bottom[:tall], bottom[tall:])):
        repack(box, value, [ref])


def forward_kernel(box, packs, saved, rows, outs, kept, stack, tails):
    sides = read_rows(box, rows, stack, tails)
    total = []
    for side, values in enumerate(sides):
        total.append(0.0)
        for at in (2 * side, 2 * side + 1):
            both = gate_up(values, packs[at])
            kept[at][...] = both
            total[side] = total[side] + down_rows(both, packs[at])
    write_rows(box, *total, outs)


def inner_kernel(box, packs, saved, rows, outs, kept, stack, tails):
    for side, values in enumerate(read_rows(box, rows, stack, tails)):
        for at in (2 * side, 2 * side + 1):
            kept[at][...] = inner_of(values, packs[at])


def gate_back_kernel(box, packs, saved, rows, outs, kept, stack, tails):
    sides = read_rows(box, rows, stack, tails)
    total = []
    for side, values in enumerate(sides):
        total.append(0.0)
        for at in (2 * side, 2 * side + 1):
            both = gate_up(values, packs[at])
            kept[at][...] = both
            total[side] = total[side] + part_rows(saved[at][...], both, packs[at])
    write_rows(box, *total, outs)


def back_kernel(box, packs, saved, rows, outs, kept, stack, tails):
    sides = read_rows(box, rows, stack, tails)
    total = []
    for side, values in enumerate(sides):
        total.append(0.0)
        for at in (2 * side, 2 * side + 1):
            d_inner = inner_of(values, packs[at])
            total[side] = total[side] + part_rows(d_inner, saved[at][...], packs[at])
    write_rows(box, *total, outs)


def down_kernel(box, packs, saved, rows, outs, kept, stack, tails):
    total = []
    for side in range(2):
        at = 2 * side
        total.append(sum(down_rows(saved[i][...], packs[i]) for i in (at, at + 1)))
    write_rows(box, *total, outs)


def expert_call(kernel, box, packs, rows, saved=(), outs=True, kept=0, reads=True, after=(), window=None):
    width = packs[0].shape[1]
    first, size = window or (0, rows[0].shape[0])
    count = size // ROWS
    tall = sum(heights(box, count))
    boxes = jax.ShapeDtypeStruct((count * ROWS, box.lanes), BF)
    results = [boxes] * len(rows) if outs else []
    if kept:
        units = [pack.shape[0] // 3 for pack in packs]
        results += [jax.ShapeDtypeStruct((2 * tall, kept * u), F32) for u in units]
    inputs = list(packs) + list(saved) + (list(rows) if reads else [])
    n_in, n_p, n_s, n_out = len(inputs), len(packs), len(saved), len(rows) if outs else 0

    def body(*refs):
        results_refs = refs[n_in:-2]
        kernel(
            box,
            refs[:n_p],
            refs[n_p : n_p + n_s],
            [ref.at[pl.ds(first, size)] for ref in refs[n_p + n_s : n_in]],
            results_refs[:n_out],
            results_refs[n_out:],
            refs[-2],
            refs[-1],
        )

    scratch = [
        pltpu.VMEM((3 * tall, width), BF),
        pltpu.VMEM((count * ROWS, max(box.wide, LANES)), BF),
    ]
    flops = sum(2 * 2 * tall * pack.size for pack in packs)
    results = call(body, results, *inputs, scratch=scratch, flops=flops, after=after)
    return results[:n_out], results[n_out:]


def local(tokens, norm_gain, w_gate, w_up, w_down, routes, mix_weights, cotangent):
    experts = lax.axis_size("expert") // SPLIT
    n, width = tokens.shape[1:]
    capacity = n // experts + max(1, n // (16 * experts))
    box = Box(capacity, width)
    gain = norm_gain
    gate_w, up_w, down_w = w_gate[0, 0].T, w_up[0, 0].T, w_down[0, 0]
    boxed = jax.ShapeDtypeStruct((ROWS, box.lanes), BF)
    picked = pltpu.VMEM((n, width), F32)
    bind = functools.partial

    def joined(arrays):
        return arrays[0] if len(arrays) == 1 else jnp.concatenate(arrays, axis=0)

    fence = lax.optimization_barrier

    def crossing_of(boxes):
        return joined([shift(boxes[j - 1], experts=j) for j in range(1, experts)])

    def around(boxes):
        return [shift(boxes, flip=2), boxes, shift(boxes, flip=1)]

    def add(*values):
        return sum(v.astype(F32) for v in values).astype(BF)

    def sums(parts):
        return add(parts[1], shift(parts[0], flip=2), shift(parts[2], flip=1))

    def home(total, sections):
        return [
            shift(total[(j - 1) * ROWS : j * ROWS], sections=sections, experts=-j)
            for j in range(1, experts)
        ]

    def own_home(parts, sections):
        return [
            shift(parts[0], sections=sections, flip=2),
            shift(parts[2], sections=sections, flip=1),
            shift(parts[1], sections=sections),
        ]

    def give_back(cross, own, sections, others=()):
        total = sums(cross)
        back = home(total, sections)
        own, _, others = fence((own, total, others))
        return back + own_home(own, sections), others

    units = w_gate.shape[3]
    cut = -(-units * 7 // 12 // ROWS) * ROWS
    top = jnp.concatenate([gate_w[:cut], up_w[:cut], down_w[:cut]], axis=0)
    bottom = jnp.concatenate([gate_w[cut:], up_w[cut:], down_w[cut:]], axis=0)
    packs = [top, shift(top, flip=1), bottom, shift(bottom, flip=2)]

    def rows_of(count):
        return jax.ShapeDtypeStruct((count, width), BF)

    both = jax.ShapeDtypeStruct((2 * ROWS, box.lanes), BF)
    ahead, notes0, notes1, own_tok, own_cot, *crossing = call(
        bind(start_kernel, box, experts),
        [rows_of(n + ROWS), rows_of(ROWS), rows_of(ROWS), boxed, boxed] + [both] * (experts - 1),
        tokens[0],
        cotangent[0],
        gain,
        routes[0, :, :, 0],
        mix_weights[0, :, :, 0],
        after=[top, bottom],
    )
    crossed = [shift(crossing[j - 1], experts=j) for j in range(1, experts)]
    own0 = around(own_tok)
    packs, crossed, own0 = fence((packs, crossed, own0))
    cross0 = around(joined([c[:ROWS] for c in crossed]))
    cots = joined([own_cot] + [c[ROWS:] for c in crossed])
    cross0, cots = fence((cross0, cots))
    cots = around(cots)

    cross_out, cross_kept0 = expert_call(forward_kernel, box, packs, cross0, kept=2)
    own_out, own_kept0 = expert_call(
        forward_kernel, box, packs, own0, kept=2, after=cross_out[:1]
    )
    cross_out, ahead = fence((cross_out, ahead))
    arrived0 = shift(ahead, sections=1)
    got, cots = give_back(cross_out, own_out, 1, cots)
    h1, behind, own1, *boxes1 = call(
        bind(middle_kernel, box, experts),
        [rows_of(n), rows_of(2 * n + ROWS)] + [boxed] * experts,
        arrived0,
        cotangent[0],
        notes1,
        gain,
        *got,
        scratch=[picked],
    )
    arrived1 = shift(behind, sections=-1)
    cross1, own_z, own_x, arrived1 = fence(
        (crossing_of(boxes1), shift(own1, flip=2), shift(own1, flip=1), arrived1)
    )
    cross1, own1 = around(cross1), [own_z, own1, own_x]
    inner = bind(expert_call, inner_kernel, box, packs, cots, outs=False, kept=1)
    own_di = inner(window=(0, ROWS))[1]
    cross_di = inner(window=(ROWS, (experts - 1) * ROWS))[1]

    gate_back = bind(expert_call, gate_back_kernel, box, packs, kept=2)
    own_grad, own_kept1 = gate_back(own1, own_di)
    cross_grad, cross_kept1 = gate_back(cross1, cross_di, after=own_grad[:1])
    down = bind(expert_call, down_kernel, box, packs, reads=False)
    cross_fin = down(cross1, cross_kept1)[0]
    got, _ = give_back(cross_grad, own_grad, -1)
    got[: experts - 1], fin_sums = fence((got[: experts - 1], sums(cross_fin)))
    fin_back = home(fin_sums, 0)
    own_fin = down(own1, own_kept1)[0]
    g1, own_g, *boxes_g = call(
        bind(turn_kernel, box, experts),
        [rows_of(n)] + [boxed] * experts,
        arrived1,
        notes0,
        *got,
        scratch=[picked],
    )

    cross_g, own_z, own_x = fence(
        (crossing_of(boxes_g), shift(own_g, flip=2), shift(own_g, flip=1))
    )
    cross_g, own_g = around(cross_g), [own_z, own_g, own_x]
    back = bind(expert_call, back_kernel, box, packs)
    fin = fin_back + own_home(own_fin, 0)
    own_grad = back(own_g, own_kept0, after=fin)[0]
    cross_grad = back(cross_g, cross_kept0, after=own_grad[:1])[0]
    got = home(sums(cross_grad), 0) + own_home(own_grad, 0)
    (g0,) = call(
        bind(last_kernel, box, experts),
        [rows_of(n)],
        g1,
        tokens[0],
        notes0,
        gain,
        *got,
        scratch=[picked],
    )
    (final,) = call(
        bind(final_kernel, box, experts),
        [rows_of(n)],
        h1,
        notes1,
        *fin,
        scratch=[picked],
    )
    return (final[None], g0[None])


def solution(mesh):
    in_specs = (
        P("section", "expert", None),
        P("section", None),
        P("section", "expert", None, None),
        P("section", "expert", None, None),
        P("section", "expert", None, None),
        P("section", None, "expert", None),
        P("section", None, "expert", None),
        P("section", "expert", None),
    )
    out_specs = (P("section", "expert", None), P("section", "expert", None))
    return jax.shard_map(local, mesh=mesh, in_specs=in_specs, out_specs=out_specs, check_vma=False)
```

```python
import functools

import jax
import jax.numpy as jnp
from jax import lax
from jax.experimental import pallas as pl
from jax.experimental.pallas import tpu as pltpu
from jax.sharding import PartitionSpec as P

SPLIT = 4
EPSILON = 1e-06
BF = jnp.bfloat16
F32 = jnp.float32
ROWS = 16
LANES = 128


def dot(left, right, dims=((1,), (0,))):
    return lax.dot_general(left, right, (dims, ((), ())), preferred_element_type=F32)


NT = ((1,), (1,))


def iota(shape, axis):
    return lax.broadcasted_iota(jnp.int32, shape, axis)


class Box:
    def __init__(self, capacity, width):
        self.capacity, self.width = capacity, width
        self.groups, self.extra = capacity // ROWS, capacity % ROWS
        self.cuts = ROWS // self.extra if self.extra else 1
        self.wide = -(-width // (LANES * self.cuts)) * LANES if self.extra else 0
        self.lanes = self.groups * width + self.wide
        self.pieces = -(-width // self.wide) if self.extra else 0

    def group(self, g):
        return pl.ds(g * self.width, self.width)

    def tail(self):
        return pl.ds(self.groups * self.width, self.wide)

    def piece(self, i):
        return i * self.wide, min(self.wide, self.width - i * self.wide)


def shift(value, sections=0, experts=0, flip=0):
    n_sec, n_own = lax.axis_size("section"), lax.axis_size("expert")
    n_exp = n_own // SPLIT
    if sections % n_sec == 0 and experts % n_exp == 0 and flip == 0:
        return value
    pairs = []
    for sec in range(n_sec):
        for own in range(n_own):
            exp, sl = own // SPLIT, own % SPLIT
            to = ((exp + experts) % n_exp) * SPLIT + (sl ^ flip)
            pairs.append((sec * n_own + own, ((sec + sections) % n_sec) * n_own + to))
    return lax.ppermute(value, ("section", "expert"), pairs)


def call(body, outs, *operands, scratch=(), flops=0, after=()):
    moved = sum(a.size * a.dtype.itemsize for a in operands)
    moved += sum(o.size * o.dtype.itemsize for o in outs)
    vmem = pl.BlockSpec(memory_space=pltpu.VMEM)
    read = len(operands)

    def reading(*refs):
        body(*refs[:read], *refs[read + len(after) :])

    return pl.pallas_call(
        reading,
        out_shape=list(outs),
        in_specs=[vmem] * read + [pl.BlockSpec(memory_space=pl.ANY)] * len(after),
        out_specs=[vmem] * len(outs),
        scratch_shapes=list(scratch),
        compiler_params=pltpu.CompilerParams(vmem_limit_bytes=40 * 2**20),
        cost_estimate=pl.CostEstimate(flops=flops, bytes_accessed=moved, transcendentals=0),
    )(*operands, *after)


def column_of(row):
    n = row.shape[1]
    eye = iota((n, n), 0) == iota((n, n), 1)
    return jnp.sum(jnp.where(eye, row, 0.0), axis=1, keepdims=True)


def slots_of(rel, experts, capacity):
    n = rel.shape[1]
    same = jnp.broadcast_to(column_of(rel), (n, n)) == jnp.broadcast_to(rel, (n, n))
    before = iota((n, n), 0) < iota((n, n), 1)
    rank = jnp.sum(jnp.where(same & before, 1.0, 0.0), axis=0, keepdims=True)
    return rel * capacity + rank


def terms(value):
    high = value.astype(BF).astype(F32)
    middle = (value - high).astype(BF).astype(F32)
    return high, middle, value - high - middle


def notes_of(slots, mix, gain, n, width):
    r = iota((ROWS, n), 0)
    left = jnp.where(r == 0, slots, 0.0)
    for at, term in enumerate(terms(mix)):
        left = jnp.where(r == 1 + at, term, left)
    r = iota((ROWS, width), 0)
    wide = jnp.concatenate([left, jnp.zeros((ROWS, width - n), F32)], axis=1)
    for at, term in enumerate(terms(gain)):
        wide = jnp.where(r == 4 + at, term, wide)
    return wide.astype(BF)


def slots_in(notes, n):
    return notes[:, :n].astype(F32)[0:1]


def mix_in(notes, n):
    left = notes[:, :n].astype(F32)
    return column_of(left[1:2] + left[2:3] + left[3:4])


def gain_in(notes):
    wide = notes.astype(F32)
    return wide[4:5] + wide[5:6] + wide[6:7]


def pack_rows(box, slots, values, out_refs):
    n = values.shape[0]
    line = jnp.broadcast_to(slots.astype(jnp.int32), (ROWS, n))
    r = iota((ROWS, n), 0)
    for j, out in enumerate(out_refs):
        first = j * box.capacity
        for g in range(box.groups):
            sel = jnp.where(line == first + g * ROWS + r, 1.0, 0.0).astype(BF)
            out[:, box.group(g)] = dot(sel, values).astype(BF)
        if box.extra:
            total = jnp.zeros((ROWS, box.wide), F32)
            for i in range(box.pieces):
                at, size = box.piece(i)
                hit = (line == first + box.groups * ROWS + r // box.cuts) & (r % box.cuts == i)
                hit &= r // box.cuts < box.extra
                got = dot(jnp.where(hit, 1.0, 0.0).astype(BF), values[:, at : at + size])
                if size < box.wide:
                    got = jnp.concatenate([got, jnp.zeros((ROWS, box.wide - size), F32)], axis=1)
                total = total + got
            out[:, box.tail()] = total.astype(BF)


def pick_rows(box, slots, boxes, n, picked):
    count = len(boxes)
    slots = column_of(slots)
    if box.groups:
        stack = jnp.concatenate(
            [b[:, g * box.width : (g + 1) * box.width] for b in boxes for g in range(box.groups)],
            axis=0,
        )
        tall = count * box.groups * ROWS
        c = iota((n, tall), 1)
        slot = c // (box.groups * ROWS) * box.capacity + c % (box.groups * ROWS)
        sel = jnp.where(slots.astype(jnp.int32) == slot, 1.0, 0.0).astype(BF)
        picked[...] = dot(sel, stack)
    else:
        picked[...] = jnp.zeros(picked.shape, F32)
    if box.extra:
        tails = jnp.concatenate([b[:, box.groups * box.width :] for b in boxes], axis=0)
        c = iota((n, count * ROWS), 1)
        r = c % ROWS
        slot = c // ROWS * box.capacity + box.groups * ROWS + r // box.cuts
        mine = (slots.astype(jnp.int32) == slot) & (r // box.cuts < box.extra)
        for i in range(box.pieces):
            at, size = box.piece(i)
            sel = jnp.where(mine & (r % box.cuts == i), 1.0, 0.0).astype(BF)
            picked[:, at : at + size] += dot(sel, tails[:, :size])


def heights(box, count):
    extra = -(-count * box.extra // ROWS) * ROWS
    return count * box.groups * ROWS, extra


def unpack(box, refs, stack, tails, at=0):
    count = 0
    for ref in refs:
        for p in range(ref.shape[0] // ROWS):
            for g in range(box.groups):
                stack[at : at + ROWS, :] = ref[p * ROWS : (p + 1) * ROWS, box.group(g)]
                at += ROWS
            if box.extra:
                tails[count * ROWS : (count + 1) * ROWS, :] = ref[
                    p * ROWS : (p + 1) * ROWS, box.tail()
                ]
            count += 1
    if box.extra:
        extra = heights(box, count)[1]
        r = iota((extra, count * ROWS), 0)
        c = iota((extra, count * ROWS), 1)
        mine = (r // box.extra == c // ROWS) & (r % box.extra == c % ROWS // box.cuts)
        for i in range(box.pieces):
            start, size = box.piece(i)
            sel = jnp.where(mine & (c % ROWS % box.cuts == i), 1.0, 0.0).astype(BF)
            stack[at : at + extra, start : start + size] = dot(sel, tails[:, :size]).astype(BF)


def repack(box, rows, refs):
    rows = rows.astype(BF)
    at = 0
    count = 0
    for ref in refs:
        for p in range(ref.shape[0] // ROWS):
            for g in range(box.groups):
                ref[p * ROWS : (p + 1) * ROWS, box.group(g)] = rows[at : at + ROWS]
                at += ROWS
            count += 1
    if box.extra:
        extra = heights(box, count)[1]
        r = iota((count * ROWS, extra), 0)
        c = iota((count * ROWS, extra), 1)
        mine = (c // box.extra == r // ROWS) & (c % box.extra == r % ROWS // box.cuts)
        total = jnp.zeros((count * ROWS, box.wide), F32)
        for i in range(box.pieces):
            start, size = box.piece(i)
            sel = jnp.where(mine & (r % ROWS % box.cuts == i), 1.0, 0.0).astype(BF)
            got = dot(sel, rows[at:, start : start + size])
            if size < box.wide:
                pad = jnp.zeros((count * ROWS, box.wide - size), F32)
                got = jnp.concatenate([got, pad], axis=1)
            total = total + got
        total = total.astype(BF)
        count = 0
        for ref in refs:
            tall = ref.shape[0]
            ref[:, box.tail()] = total[count : count + tall]
            count += tall


def inv_rms(wide):
    return lax.rsqrt(jnp.mean(wide * wide, axis=-1, keepdims=True) + EPSILON)


def total_of(refs):
    return sum(ref[...].astype(F32) for ref in refs).astype(BF)


def start_kernel(box, experts, tokens, cot, gain, ids, mix, ahead, notes0, notes1, *boxes):
    n, width = tokens.shape
    mine = lax.axis_index("expert") // SPLIT
    for k, notes in enumerate((notes0, notes1)):
        rel = ids[k : k + 1, :] - mine
        rel = jnp.where(rel < 0, rel + experts, rel).astype(F32)
        slots = slots_of(rel, experts, box.capacity)
        notes[...] = notes_of(slots, mix[k : k + 1, :], gain[...], n, width)
    ahead[:n] = tokens[...]
    ahead[n:] = notes0[...]
    wide = tokens[...].astype(F32)
    normed = (wide * inv_rms(wide) * gain[...]).astype(BF)
    crossing = boxes[2:]
    firsts = [boxes[0]] + [ref.at[:ROWS] for ref in crossing]
    pack_rows(box, slots_in(notes0[...], n), normed, firsts)
    seconds = [boxes[1]] + [ref.at[ROWS:] for ref in crossing]
    pack_rows(box, slots_in(notes1[...], n), cot[...], seconds)


def combine(box, notes, n, own, back, picked):
    sums = [total_of(own)] + [ref[...] for ref in back]
    pick_rows(box, slots_in(notes, n), sums, n, picked)
    return mix_in(notes, n) * picked[...]


def split_refs(refs, experts, outs):
    ins = refs[:-outs]
    return ins[experts - 1 :], ins[: experts - 1], refs[-outs:]


def middle_kernel(box, experts, arrived, cot, notes1, gain, *refs):
    boxes, picked = refs[-1 - experts : -1], refs[-1]
    own, back, (after, behind) = split_refs(refs[: -1 - experts], experts, 2)
    n = cot.shape[0]
    update = combine(box, arrived[n:], n, own, back, picked)
    later = (arrived[:n].astype(F32) + update).astype(BF)
    after[...] = later
    behind[:n] = later
    behind[n : 2 * n] = cot[...]
    behind[2 * n :] = notes1[...]
    wide = later.astype(F32)
    normed = (wide * inv_rms(wide) * gain[...]).astype(BF)
    pack_rows(box, slots_in(notes1[...], n), normed, boxes)


def final_kernel(box, experts, hidden, notes, *refs):
    picked = refs[-1]
    own, back, (out,) = split_refs(refs[:-1], experts, 1)
    n = hidden.shape[0]
    update = combine(box, notes[...], n, own, back, picked)
    out[...] = (hidden[...].astype(F32) + update).astype(BF)


def norm_back(hidden, gain, grad):
    wide = hidden.astype(F32)
    inv = inv_rms(wide)
    scaled = grad * gain
    along = jnp.mean(scaled * wide, axis=-1, keepdims=True)
    return inv * scaled - wide * (inv * inv * inv * along)


def turn_kernel(box, experts, arrived, notes0, *refs):
    boxes, picked = refs[-1 - experts : -1], refs[-1]
    own, back, (out,) = split_refs(refs[: -1 - experts], experts, 1)
    n = out.shape[0]
    notes = arrived[2 * n :]
    d_normed = combine(box, notes, n, own, back, picked)
    change = norm_back(arrived[:n], gain_in(notes), d_normed)
    now = (arrived[n : 2 * n].astype(F32) + change).astype(BF)
    out[...] = now
    pack_rows(box, slots_in(notes0[...], n), now, boxes)


def last_kernel(box, experts, grad, hidden, notes0, gain, *refs):
    picked = refs[-1]
    own, back, (out,) = split_refs(refs[:-1], experts, 1)
    n = hidden.shape[0]
    d_normed = combine(box, notes0[...], n, own, back, picked)
    change = norm_back(hidden[...], gain[...], d_normed)
    out[...] = (grad[...].astype(F32) + change).astype(BF)


def spans(tall):
    return pl.ds(0, 2 * tall), pl.ds(tall, 2 * tall)


def gate_up(rows, pack):
    return dot(rows, pack[: 2 * (pack.shape[0] // 3)], NT)


def parts_of(both):
    units = both.shape[1] // 2
    return both[:, :units], both[:, units:]


def down_rows(both, pack):
    g, u = parts_of(both)
    return dot((jax.nn.silu(g) * u).astype(BF), pack[2 * g.shape[1] :])


def inner_of(rows, pack):
    return dot(rows, pack[2 * (pack.shape[0] // 3) :], NT)


def part_rows(d_inner, both, pack):
    g, u = parts_of(both)
    r = jax.nn.sigmoid(g)
    d_gate = d_inner * u * r * (1.0 + g * (1.0 - r))
    d_up = d_inner * g * r
    return dot(jnp.concatenate([d_gate, d_up], axis=1).astype(BF), pack[: both.shape[1]])


def read_rows(box, rows, stack, tails):
    tall = stack.shape[0] // 3
    for at, ref in enumerate(rows):
        unpack(box, [ref], stack, tails, at * tall)
    return [stack[span, :] for span in spans(tall)]


def write_rows(box, top, bottom, outs):
    tall = top.shape[0] // 2
    for ref, value in zip(outs, (top[:tall], top[tall:] + bottom[:tall], bottom[tall:])):
        repack(box, value, [ref])


def forward_kernel(box, packs, saved, rows, outs, kept, stack, tails):
    sides = read_rows(box, rows, stack, tails)
    total = []
    for side, values in enumerate(sides):
        total.append(0.0)
        for at in (2 * side, 2 * side + 1):
            both = gate_up(values, packs[at])
            kept[at][...] = both
            total[side] = total[side] + down_rows(both, packs[at])
    write_rows(box, *total, outs)


def inner_kernel(box, packs, saved, rows, outs, kept, stack, tails):
    for side, values in enumerate(read_rows(box, rows, stack, tails)):
        for at in (2 * side, 2 * side + 1):
            kept[at][...] = inner_of(values, packs[at])


def gate_back_kernel(box, packs, saved, rows, outs, kept, stack, tails):
    sides = read_rows(box, rows, stack, tails)
    total = []
    for side, values in enumerate(sides):
        total.append(0.0)
        for at in (2 * side, 2 * side + 1):
            both = gate_up(values, packs[at])
            kept[at][...] = both
            total[side] = total[side] + part_rows(saved[at][...], both, packs[at])
    write_rows(box, *total, outs)


def back_kernel(box, packs, saved, rows, outs, kept, stack, tails):
    sides = read_rows(box, rows, stack, tails)
    total = []
    for side, values in enumerate(sides):
        total.append(0.0)
        for at in (2 * side, 2 * side + 1):
            d_inner = inner_of(values, packs[at])
            total[side] = total[side] + part_rows(d_inner, saved[at][...], packs[at])
    write_rows(box, *total, outs)


def down_kernel(box, packs, saved, rows, outs, kept, stack, tails):
    total = []
    for side in range(2):
        at = 2 * side
        total.append(sum(down_rows(saved[i][...], packs[i]) for i in (at, at + 1)))
    write_rows(box, *total, outs)


def expert_call(kernel, box, packs, rows, saved=(), outs=True, kept=0, reads=True, after=(), window=None):
    width = packs[0].shape[1]
    first, size = window or (0, rows[0].shape[0])
    count = size // ROWS
    tall = sum(heights(box, count))
    boxes = jax.ShapeDtypeStruct((count * ROWS, box.lanes), BF)
    results = [boxes] * len(rows) if outs else []
    if kept:
        units = [pack.shape[0] // 3 for pack in packs]
        results += [jax.ShapeDtypeStruct((2 * tall, kept * u), F32) for u in units]
    inputs = list(packs) + list(saved) + (list(rows) if reads else [])
    n_in, n_p, n_s, n_out = len(inputs), len(packs), len(saved), len(rows) if outs else 0

    def body(*refs):
        results_refs = refs[n_in:-2]
        kernel(
            box,
            refs[:n_p],
            refs[n_p : n_p + n_s],
            [ref.at[pl.ds(first, size)] for ref in refs[n_p + n_s : n_in]],
            results_refs[:n_out],
            results_refs[n_out:],
            refs[-2],
            refs[-1],
        )

    scratch = [
        pltpu.VMEM((3 * tall, width), BF),
        pltpu.VMEM((count * ROWS, max(box.wide, LANES)), BF),
    ]
    flops = sum(2 * 2 * tall * pack.size for pack in packs)
    results = call(body, results, *inputs, scratch=scratch, flops=flops, after=after)
    return results[:n_out], results[n_out:]


def local(tokens, norm_gain, w_gate, w_up, w_down, routes, mix_weights, cotangent):
    experts = lax.axis_size("expert") // SPLIT
    n, width = tokens.shape[1:]
    capacity = n // experts + max(1, n // (16 * experts))
    box = Box(capacity, width)
    gain = norm_gain
    gate_w, up_w, down_w = w_gate[0, 0].T, w_up[0, 0].T, w_down[0, 0]
    boxed = jax.ShapeDtypeStruct((ROWS, box.lanes), BF)
    picked = pltpu.VMEM((n, width), F32)
    bind = functools.partial

    def joined(arrays):
        return arrays[0] if len(arrays) == 1 else jnp.concatenate(arrays, axis=0)

    fence = lax.optimization_barrier

    def crossing_of(boxes):
        return joined([shift(boxes[j - 1], experts=j) for j in range(1, experts)])

    def around(boxes):
        return [shift(boxes, flip=2), boxes, shift(boxes, flip=1)]

    def add(*values):
        return sum(v.astype(F32) for v in values).astype(BF)

    def sums(parts):
        return add(parts[1], shift(parts[0], flip=2), shift(parts[2], flip=1))

    def home(total, sections):
        return [
            shift(total[(j - 1) * ROWS : j * ROWS], sections=sections, experts=-j)
            for j in range(1, experts)
        ]

    def own_home(parts, sections):
        return [
            shift(parts[0], sections=sections, flip=2),
            shift(parts[2], sections=sections, flip=1),
            shift(parts[1], sections=sections),
        ]

    def give_back(cross, own, sections, others=()):
        total = sums(cross)
        back = home(total, sections)
        own, _, others = fence((own, total, others))
        return back + own_home(own, sections), others

    units = w_gate.shape[3]
    cut = -(-units * 7 // 12 // ROWS) * ROWS
    top = jnp.concatenate([gate_w[:cut], up_w[:cut], down_w[:cut]], axis=0)
    bottom = jnp.concatenate([gate_w[cut:], up_w[cut:], down_w[cut:]], axis=0)
    packs = [top, shift(top, flip=1), bottom, shift(bottom, flip=2)]

    def rows_of(count):
        return jax.ShapeDtypeStruct((count, width), BF)

    both = jax.ShapeDtypeStruct((2 * ROWS, box.lanes), BF)
    ahead, notes0, notes1, own_tok, own_cot, *crossing = call(
        bind(start_kernel, box, experts),
        [rows_of(n + ROWS), rows_of(ROWS), rows_of(ROWS), boxed, boxed] + [both] * (experts - 1),
        tokens[0],
        cotangent[0],
        gain,
        routes[0, :, :, 0],
        mix_weights[0, :, :, 0],
        after=[top, bottom],
    )
    crossed = [shift(crossing[j - 1], experts=j) for j in range(1, experts)]
    own0 = around(own_tok)
    packs, crossed, own0 = fence((packs, crossed, own0))
    cross0 = around(joined([c[:ROWS] for c in crossed]))
    cots = joined([own_cot] + [c[ROWS:] for c in crossed])
    cross0, cots = fence((cross0, cots))
    cots = around(cots)

    cross_out, cross_kept0 = expert_call(forward_kernel, box, packs, cross0, kept=2)
    own_out, own_kept0 = expert_call(
        forward_kernel, box, packs, own0, kept=2, after=cross_out[:1]
    )
    cross_out, ahead = fence((cross_out, ahead))
    arrived0 = shift(ahead, sections=1)
    got, cots = give_back(cross_out, own_out, 1, cots)
    h1, behind, own1, *boxes1 = call(
        bind(middle_kernel, box, experts),
        [rows_of(n), rows_of(2 * n + ROWS)] + [boxed] * experts,
        arrived0,
        cotangent[0],
        notes1,
        gain,
        *got,
        scratch=[picked],
    )
    arrived1 = shift(behind, sections=-1)
    cross1, own_z, own_x, arrived1 = fence(
        (crossing_of(boxes1), shift(own1, flip=2), shift(own1, flip=1), arrived1)
    )
    cross1, own1 = around(cross1), [own_z, own1, own_x]
    inner = bind(expert_call, inner_kernel, box, packs, cots, outs=False, kept=1)
    own_di = inner(window=(0, ROWS))[1]
    cross_di = inner(window=(ROWS, (experts - 1) * ROWS))[1]

    gate_back = bind(expert_call, gate_back_kernel, box, packs, kept=2)
    own_grad, own_kept1 = gate_back(own1, own_di)
    cross_grad, cross_kept1 = gate_back(cross1, cross_di, after=own_grad[:1])
    down = bind(expert_call, down_kernel, box, packs, reads=False)
    cross_fin = down(cross1, cross_kept1)[0]
    got, _ = give_back(cross_grad, own_grad, -1)
    got[: experts - 1], fin_sums = fence((got[: experts - 1], sums(cross_fin)))
    fin_back = home(fin_sums, 0)
    own_fin = down(own1, own_kept1)[0]
    g1, own_g, *boxes_g = call(
        bind(turn_kernel, box, experts),
        [rows_of(n)] + [boxed] * experts,
        arrived1,
        notes0,
        *got,
        scratch=[picked],
    )

    cross_g, own_z, own_x = fence(
        (crossing_of(boxes_g), shift(own_g, flip=2), shift(own_g, flip=1))
    )
    cross_g, own_g = around(cross_g), [own_z, own_g, own_x]
    back = bind(expert_call, back_kernel, box, packs)
    fin = fin_back + own_home(own_fin, 0)
    cross_grad = back(cross_g, cross_kept0)[0]
    own_grad = back(own_g, own_kept0, after=cross_grad[:1] + tuple(fin))[0]
    got = home(sums(cross_grad), 0) + own_home(own_grad, 0)
    (g0,) = call(
        bind(last_kernel, box, experts),
        [rows_of(n)],
        g1,
        tokens[0],
        notes0,
        gain,
        *got,
        scratch=[picked],
    )
    (final,) = call(
        bind(final_kernel, box, experts),
        [rows_of(n)],
        h1,
        notes1,
        *fin,
        scratch=[picked],
    )
    return (final[None], g0[None])


def solution(mesh):
    in_specs = (
        P("section", "expert", None),
        P("section", None),
        P("section", "expert", None, None),
        P("section", "expert", None, None),
        P("section", "expert", None, None),
        P("section", None, "expert", None),
        P("section", None, "expert", None),
        P("section", "expert", None),
    )
    out_specs = (P("section", "expert", None), P("section", "expert", None))
    return jax.shard_map(local, mesh=mesh, in_specs=in_specs, out_specs=out_specs, check_vma=False)
```

```python
import functools

import jax
import jax.numpy as jnp
from jax import lax
from jax.experimental import pallas as pl
from jax.experimental.pallas import tpu as pltpu
from jax.sharding import PartitionSpec as P

SPLIT = 4
EPSILON = 1e-06
BF = jnp.bfloat16
F32 = jnp.float32
ROWS = 16
LANES = 128


def dot(left, right, dims=((1,), (0,))):
    return lax.dot_general(left, right, (dims, ((), ())), preferred_element_type=F32)


NT = ((1,), (1,))


def iota(shape, axis):
    return lax.broadcasted_iota(jnp.int32, shape, axis)


class Box:
    def __init__(self, capacity, width):
        self.capacity, self.width = capacity, width
        self.groups, self.extra = capacity // ROWS, capacity % ROWS
        self.cuts = ROWS // self.extra if self.extra else 1
        self.wide = -(-width // (LANES * self.cuts)) * LANES if self.extra else 0
        self.lanes = self.groups * width + self.wide
        self.pieces = -(-width // self.wide) if self.extra else 0

    def group(self, g):
        return pl.ds(g * self.width, self.width)

    def tail(self):
        return pl.ds(self.groups * self.width, self.wide)

    def piece(self, i):
        return i * self.wide, min(self.wide, self.width - i * self.wide)


def shift(value, sections=0, experts=0, flip=0):
    n_sec, n_own = lax.axis_size("section"), lax.axis_size("expert")
    n_exp = n_own // SPLIT
    if sections % n_sec == 0 and experts % n_exp == 0 and flip == 0:
        return value
    pairs = []
    for sec in range(n_sec):
        for own in range(n_own):
            exp, sl = own // SPLIT, own % SPLIT
            to = ((exp + experts) % n_exp) * SPLIT + (sl ^ flip)
            pairs.append((sec * n_own + own, ((sec + sections) % n_sec) * n_own + to))
    return lax.ppermute(value, ("section", "expert"), pairs)


def call(body, outs, *operands, scratch=(), flops=0, after=()):
    moved = sum(a.size * a.dtype.itemsize for a in operands)
    moved += sum(o.size * o.dtype.itemsize for o in outs)
    vmem = pl.BlockSpec(memory_space=pltpu.VMEM)
    read = len(operands)

    def reading(*refs):
        body(*refs[:read], *refs[read + len(after) :])

    return pl.pallas_call(
        reading,
        out_shape=list(outs),
        in_specs=[vmem] * read + [pl.BlockSpec(memory_space=pl.ANY)] * len(after),
        out_specs=[vmem] * len(outs),
        scratch_shapes=list(scratch),
        compiler_params=pltpu.CompilerParams(vmem_limit_bytes=40 * 2**20),
        cost_estimate=pl.CostEstimate(flops=flops, bytes_accessed=moved, transcendentals=0),
    )(*operands, *after)


def column_of(row):
    n = row.shape[1]
    eye = iota((n, n), 0) == iota((n, n), 1)
    return jnp.sum(jnp.where(eye, row, 0.0), axis=1, keepdims=True)


def slots_of(rel, experts, capacity):
    n = rel.shape[1]
    same = jnp.broadcast_to(column_of(rel), (n, n)) == jnp.broadcast_to(rel, (n, n))
    before = iota((n, n), 0) < iota((n, n), 1)
    rank = jnp.sum(jnp.where(same & before, 1.0, 0.0), axis=0, keepdims=True)
    return rel * capacity + rank


def terms(value):
    high = value.astype(BF).astype(F32)
    middle = (value - high).astype(BF).astype(F32)
    return high, middle, value - high - middle


def notes_of(slots, mix, gain, n, width):
    r = iota((ROWS, n), 0)
    left = jnp.where(r == 0, slots, 0.0)
    for at, term in enumerate(terms(mix)):
        left = jnp.where(r == 1 + at, term, left)
    r = iota((ROWS, width), 0)
    wide = jnp.concatenate([left, jnp.zeros((ROWS, width - n), F32)], axis=1)
    for at, term in enumerate(terms(gain)):
        wide = jnp.where(r == 4 + at, term, wide)
    return wide.astype(BF)


def slots_in(notes, n):
    return notes[:, :n].astype(F32)[0:1]


def mix_in(notes, n):
    left = notes[:, :n].astype(F32)
    return column_of(left[1:2] + left[2:3] + left[3:4])


def gain_in(notes):
    wide = notes.astype(F32)
    return wide[4:5] + wide[5:6] + wide[6:7]


def pack_rows(box, slots, values, out_refs):
    n = values.shape[0]
    line = jnp.broadcast_to(slots.astype(jnp.int32), (ROWS, n))
    r = iota((ROWS, n), 0)
    for j, out in enumerate(out_refs):
        first = j * box.capacity
        for g in range(box.groups):
            sel = jnp.where(line == first + g * ROWS + r, 1.0, 0.0).astype(BF)
            out[:, box.group(g)] = dot(sel, values).astype(BF)
        if box.extra:
            total = jnp.zeros((ROWS, box.wide), F32)
            for i in range(box.pieces):
                at, size = box.piece(i)
                hit = (line == first + box.groups * ROWS + r // box.cuts) & (r % box.cuts == i)
                hit &= r // box.cuts < box.extra
                got = dot(jnp.where(hit, 1.0, 0.0).astype(BF), values[:, at : at + size])
                if size < box.wide:
                    got = jnp.concatenate([got, jnp.zeros((ROWS, box.wide - size), F32)], axis=1)
                total = total + got
            out[:, box.tail()] = total.astype(BF)


def pick_rows(box, slots, boxes, n, picked):
    count = len(boxes)
    slots = column_of(slots)
    if box.groups:
        stack = jnp.concatenate(
            [b[:, g * box.width : (g + 1) * box.width] for b in boxes for g in range(box.groups)],
            axis=0,
        )
        tall = count * box.groups * ROWS
        c = iota((n, tall), 1)
        slot = c // (box.groups * ROWS) * box.capacity + c % (box.groups * ROWS)
        sel = jnp.where(slots.astype(jnp.int32) == slot, 1.0, 0.0).astype(BF)
        picked[...] = dot(sel, stack)
    else:
        picked[...] = jnp.zeros(picked.shape, F32)
    if box.extra:
        tails = jnp.concatenate([b[:, box.groups * box.width :] for b in boxes], axis=0)
        c = iota((n, count * ROWS), 1)
        r = c % ROWS
        slot = c // ROWS * box.capacity + box.groups * ROWS + r // box.cuts
        mine = (slots.astype(jnp.int32) == slot) & (r // box.cuts < box.extra)
        for i in range(box.pieces):
            at, size = box.piece(i)
            sel = jnp.where(mine & (r % box.cuts == i), 1.0, 0.0).astype(BF)
            picked[:, at : at + size] += dot(sel, tails[:, :size])


def heights(box, count):
    extra = -(-count * box.extra // ROWS) * ROWS
    return count * box.groups * ROWS, extra


def unpack(box, refs, stack, tails):
    count = refs[0].shape[0] // ROWS
    tall = stack.shape[0] // len(refs)
    whole, extra = heights(box, count)
    for which, ref in enumerate(refs):
        for p in range(count):
            for g in range(box.groups):
                at = which * tall + (p * box.groups + g) * ROWS
                stack[at : at + ROWS, :] = ref[p * ROWS : (p + 1) * ROWS, box.group(g)]
        if box.extra:
            tails[which * count * ROWS : (which + 1) * count * ROWS, :] = ref[:, box.tail()]
    if box.extra:
        r = iota((len(refs) * extra, tails.shape[0]), 0)
        c = iota((len(refs) * extra, tails.shape[0]), 1)
        mine, cut = place_of(box, count, r, c)
        for i in range(box.pieces):
            start, size = box.piece(i)
            sel = jnp.where(mine & (cut == i), 1.0, 0.0).astype(BF)
            got = dot(sel, tails[:, :size]).astype(BF)
            for which in range(len(refs)):
                at = which * tall + whole
                stack[at : at + extra, start : start + size] = got[
                    which * extra : (which + 1) * extra
                ]


def place_of(box, count, row, tail):
    extra = heights(box, count)[1]
    inside, within = row % extra, tail % (count * ROWS)
    mine = row // extra == tail // (count * ROWS)
    mine &= (inside // box.extra == within // ROWS) & (inside < count * box.extra)
    mine &= inside % box.extra == within % ROWS // box.cuts
    return mine, within % ROWS % box.cuts


def repack(box, values, refs):
    count = refs[0].shape[0] // ROWS
    whole, extra = heights(box, count)
    values = [value.astype(BF) for value in values]
    for value, ref in zip(values, refs):
        for p in range(count):
            for g in range(box.groups):
                at = (p * box.groups + g) * ROWS
                ref[p * ROWS : (p + 1) * ROWS, box.group(g)] = value[at : at + ROWS]
    if box.extra:
        lot = len(refs) * count * ROWS
        rest = jnp.concatenate([value[whole:] for value in values], axis=0)
        r = iota((lot, len(refs) * extra), 0)
        c = iota((lot, len(refs) * extra), 1)
        mine, cut = place_of(box, count, c, r)
        total = jnp.zeros((lot, box.wide), F32)
        for i in range(box.pieces):
            start, size = box.piece(i)
            sel = jnp.where(mine & (cut == i), 1.0, 0.0).astype(BF)
            got = dot(sel, rest[:, start : start + size])
            if size < box.wide:
                got = jnp.concatenate([got, jnp.zeros((lot, box.wide - size), F32)], axis=1)
            total = total + got
        total = total.astype(BF)
        for which, ref in enumerate(refs):
            ref[:, box.tail()] = total[which * count * ROWS : (which + 1) * count * ROWS]


def inv_rms(wide):
    return lax.rsqrt(jnp.mean(wide * wide, axis=-1, keepdims=True) + EPSILON)


def total_of(refs):
    return sum(ref[...].astype(F32) for ref in refs).astype(BF)


def gather_kernel(rows, *refs):
    arrays, (out, sems) = refs[:-2], refs[-2:]
    copies = [
        pltpu.make_async_copy(
            ref.at[pl.ds(*rows)], out.at[pl.ds(at * rows[1], rows[1])], sems.at[at]
        )
        for at, ref in enumerate(arrays)
    ]
    for copy in copies:
        copy.start()
    for copy in copies:
        copy.wait()


def gather(rows, *arrays):
    shape = (len(arrays) * rows[1], arrays[0].shape[1])
    return pl.pallas_call(
        functools.partial(gather_kernel, rows),
        out_shape=jax.ShapeDtypeStruct(shape, arrays[0].dtype),
        in_specs=[pl.BlockSpec(memory_space=pl.ANY)] * len(arrays),
        out_specs=pl.BlockSpec(memory_space=pltpu.VMEM),
        scratch_shapes=[pltpu.SemaphoreType.DMA((len(arrays),))],
    )(*arrays)


def start_kernel(box, experts, tokens, cot, gain, ids, mix, ahead, notes0, notes1, *boxes):
    n, width = tokens.shape
    mine = lax.axis_index("expert") // SPLIT
    for k, notes in enumerate((notes0, notes1)):
        rel = ids[k : k + 1, :] - mine
        rel = jnp.where(rel < 0, rel + experts, rel).astype(F32)
        slots = slots_of(rel, experts, box.capacity)
        notes[...] = notes_of(slots, mix[k : k + 1, :], gain[...], n, width)
    ahead[:n] = tokens[...]
    ahead[n:] = notes0[...]
    wide = tokens[...].astype(F32)
    normed = (wide * inv_rms(wide) * gain[...]).astype(BF)
    crossing = boxes[2:]
    firsts = [boxes[0]] + [ref.at[:ROWS] for ref in crossing]
    pack_rows(box, slots_in(notes0[...], n), normed, firsts)
    seconds = [boxes[1]] + [ref.at[ROWS:] for ref in crossing]
    pack_rows(box, slots_in(notes1[...], n), cot[...], seconds)


def combine(box, notes, n, own, back, picked):
    sums = [total_of(own)] + [ref[...] for ref in back]
    pick_rows(box, slots_in(notes, n), sums, n, picked)
    return mix_in(notes, n) * picked[...]


def split_refs(refs, experts, outs):
    ins = refs[:-outs]
    return ins[experts - 1 :], ins[: experts - 1], refs[-outs:]


def middle_kernel(box, experts, arrived, cot, notes1, gain, *refs):
    boxes, picked = refs[-1 - experts : -1], refs[-1]
    own, back, (after, behind) = split_refs(refs[: -1 - experts], experts, 2)
    n = cot.shape[0]
    update = combine(box, arrived[n:], n, own, back, picked)
    later = (arrived[:n].astype(F32) + update).astype(BF)
    after[...] = later
    behind[:n] = later
    behind[n : 2 * n] = cot[...]
    behind[2 * n :] = notes1[...]
    wide = later.astype(F32)
    normed = (wide * inv_rms(wide) * gain[...]).astype(BF)
    pack_rows(box, slots_in(notes1[...], n), normed, boxes)


def final_kernel(box, experts, hidden, notes, *refs):
    picked = refs[-1]
    own, back, (out,) = split_refs(refs[:-1], experts, 1)
    n = hidden.shape[0]
    update = combine(box, notes[...], n, own, back, picked)
    out[...] = (hidden[...].astype(F32) + update).astype(BF)


def norm_back(hidden, gain, grad):
    wide = hidden.astype(F32)
    inv = inv_rms(wide)
    scaled = grad * gain
    along = jnp.mean(scaled * wide, axis=-1, keepdims=True)
    return inv * scaled - wide * (inv * inv * inv * along)


def turn_kernel(box, experts, arrived, notes0, *refs):
    boxes, picked = refs[-1 - experts : -1], refs[-1]
    own, back, (out,) = split_refs(refs[: -1 - experts], experts, 1)
    n = out.shape[0]
    notes = arrived[2 * n :]
    d_normed = combine(box, notes, n, own, back, picked)
    change = norm_back(arrived[:n], gain_in(notes), d_normed)
    now = (arrived[n : 2 * n].astype(F32) + change).astype(BF)
    out[...] = now
    pack_rows(box, slots_in(notes0[...], n), now, boxes)


def last_kernel(box, experts, grad, hidden, notes0, gain, *refs):
    picked = refs[-1]
    own, back, (out,) = split_refs(refs[:-1], experts, 1)
    n = hidden.shape[0]
    d_normed = combine(box, notes0[...], n, own, back, picked)
    change = norm_back(hidden[...], gain[...], d_normed)
    out[...] = (grad[...].astype(F32) + change).astype(BF)


def spans(tall):
    return pl.ds(0, 2 * tall), pl.ds(tall, 2 * tall)


def gate_up(rows, pack):
    return dot(rows, pack[: 2 * (pack.shape[0] // 3)], NT)


def parts_of(both):
    units = both.shape[1] // 2
    return both[:, :units], both[:, units:]


def down_rows(both, pack):
    g, u = parts_of(both)
    return dot((jax.nn.silu(g) * u).astype(BF), pack[2 * g.shape[1] :])


def inner_of(rows, pack):
    return dot(rows, pack[2 * (pack.shape[0] // 3) :], NT)


def part_rows(d_inner, both, pack):
    g, u = parts_of(both)
    r = jax.nn.sigmoid(g)
    d_gate = d_inner * u * r * (1.0 + g * (1.0 - r))
    d_up = d_inner * g * r
    return dot(jnp.concatenate([d_gate, d_up], axis=1).astype(BF), pack[: both.shape[1]])


def read_rows(box, rows, stack, tails):
    tall = stack.shape[0] // 3
    unpack(box, rows, stack, tails)
    return [stack[span, :] for span in spans(tall)]


def write_rows(box, top, bottom, outs):
    tall = top.shape[0] // 2
    repack(box, (top[:tall], top[tall:] + bottom[:tall], bottom[tall:]), outs)


def forward_kernel(box, packs, saved, rows, outs, kept, stack, tails):
    sides = read_rows(box, rows, stack, tails)
    total = []
    for side, values in enumerate(sides):
        total.append(0.0)
        for at in (2 * side, 2 * side + 1):
            both = gate_up(values, packs[at])
            kept[at][...] = both
            total[side] = total[side] + down_rows(both, packs[at])
    write_rows(box, *total, outs)


def inner_kernel(box, packs, saved, rows, outs, kept, stack, tails):
    for side, values in enumerate(read_rows(box, rows, stack, tails)):
        for at in (2 * side, 2 * side + 1):
            kept[at][...] = inner_of(values, packs[at])


def gate_back_kernel(box, packs, saved, rows, outs, kept, stack, tails):
    sides = read_rows(box, rows, stack, tails)
    total = []
    for side, values in enumerate(sides):
        total.append(0.0)
        for at in (2 * side, 2 * side + 1):
            both = gate_up(values, packs[at])
            kept[at][...] = both
            total[side] = total[side] + part_rows(saved[at][...], both, packs[at])
    write_rows(box, *total, outs)


def back_kernel(box, packs, saved, rows, outs, kept, stack, tails):
    sides = read_rows(box, rows, stack, tails)
    total = []
    for side, values in enumerate(sides):
        total.append(0.0)
        for at in (2 * side, 2 * side + 1):
            d_inner = inner_of(values, packs[at])
            total[side] = total[side] + part_rows(d_inner, saved[at][...], packs[at])
    write_rows(box, *total, outs)


def down_kernel(box, packs, saved, rows, outs, kept, stack, tails):
    total = []
    for side in range(2):
        at = 2 * side
        total.append(sum(down_rows(saved[i][...], packs[i]) for i in (at, at + 1)))
    write_rows(box, *total, outs)


def expert_call(kernel, box, packs, rows, saved=(), outs=True, kept=0, reads=True, after=(), window=None):
    width = packs[0].shape[1]
    first, size = window or (0, rows[0].shape[0])
    count = size // ROWS
    tall = sum(heights(box, count))
    boxes = jax.ShapeDtypeStruct((count * ROWS, box.lanes), BF)
    results = [boxes] * len(rows) if outs else []
    if kept:
        units = [pack.shape[0] // 3 for pack in packs]
        results += [jax.ShapeDtypeStruct((2 * tall, kept * u), F32) for u in units]
    inputs = list(packs) + list(saved) + (list(rows) if reads else [])
    n_in, n_p, n_s, n_out = len(inputs), len(packs), len(saved), len(rows) if outs else 0

    def body(*refs):
        results_refs = refs[n_in:-2]
        kernel(
            box,
            refs[:n_p],
            refs[n_p : n_p + n_s],
            [ref.at[pl.ds(first, size)] for ref in refs[n_p + n_s : n_in]],
            results_refs[:n_out],
            results_refs[n_out:],
            refs[-2],
            refs[-1],
        )

    scratch = [
        pltpu.VMEM((3 * tall, width), BF),
        pltpu.VMEM((3 * count * ROWS, max(box.wide, LANES)), BF),
    ]
    flops = sum(2 * 2 * tall * pack.size for pack in packs)
    results = call(body, results, *inputs, scratch=scratch, flops=flops, after=after)
    return results[:n_out], results[n_out:]


def local(tokens, norm_gain, w_gate, w_up, w_down, routes, mix_weights, cotangent):
    experts = lax.axis_size("expert") // SPLIT
    n, width = tokens.shape[1:]
    capacity = n // experts + max(1, n // (16 * experts))
    box = Box(capacity, width)
    gain = norm_gain
    gate_w, up_w, down_w = w_gate[0, 0].T, w_up[0, 0].T, w_down[0, 0]
    boxed = jax.ShapeDtypeStruct((ROWS, box.lanes), BF)
    picked = pltpu.VMEM((n, width), F32)
    bind = functools.partial

    def joined(arrays):
        return arrays[0] if len(arrays) == 1 else jnp.concatenate(arrays, axis=0)

    fence = lax.optimization_barrier

    def crossing_of(boxes):
        return joined([shift(boxes[j - 1], experts=j) for j in range(1, experts)])

    def around(boxes):
        return [shift(boxes, flip=2), boxes, shift(boxes, flip=1)]

    def add(*values):
        return sum(v.astype(F32) for v in values).astype(BF)

    def sums(parts):
        return add(parts[1], shift(parts[0], flip=2), shift(parts[2], flip=1))

    def home(total, sections):
        return [
            shift(total[(j - 1) * ROWS : j * ROWS], sections=sections, experts=-j)
            for j in range(1, experts)
        ]

    def own_home(parts, sections):
        return [
            shift(parts[0], sections=sections, flip=2),
            shift(parts[2], sections=sections, flip=1),
            shift(parts[1], sections=sections),
        ]

    def give_back(cross, own, sections, others=()):
        total = sums(cross)
        back = home(total, sections)
        own, _, others = fence((own, total, others))
        return back + own_home(own, sections), others

    units = w_gate.shape[3]
    cut = -(-units * 7 // 12 // ROWS) * ROWS
    top = gather((0, cut), gate_w, up_w, down_w)
    bottom = gather((cut, units - cut), gate_w, up_w, down_w)
    packs = [top, shift(top, flip=1), bottom, shift(bottom, flip=2)]

    def rows_of(count):
        return jax.ShapeDtypeStruct((count, width), BF)

    both = jax.ShapeDtypeStruct((2 * ROWS, box.lanes), BF)
    ahead, notes0, notes1, own_tok, own_cot, *crossing = call(
        bind(start_kernel, box, experts),
        [rows_of(n + ROWS), rows_of(ROWS), rows_of(ROWS), boxed, boxed] + [both] * (experts - 1),
        tokens[0],
        cotangent[0],
        gain,
        routes[0, :, :, 0],
        mix_weights[0, :, :, 0],
        after=[top, bottom],
    )
    crossed = [shift(crossing[j - 1], experts=j) for j in range(1, experts)]
    own0 = around(own_tok)
    packs, crossed, own0 = fence((packs, crossed, own0))
    cross0 = around(joined([c[:ROWS] for c in crossed]))
    cots = joined([own_cot] + [c[ROWS:] for c in crossed])
    cross0, cots = fence((cross0, cots))
    cots = around(cots)

    cross_out, cross_kept0 = expert_call(forward_kernel, box, packs, cross0, kept=2)
    own_out, own_kept0 = expert_call(
        forward_kernel, box, packs, own0, kept=2, after=cross_out[:1]
    )
    cross_out, ahead = fence((cross_out, ahead))
    arrived0 = shift(ahead, sections=1)
    got, cots = give_back(cross_out, own_out, 1, cots)
    h1, behind, own1, *boxes1 = call(
        bind(middle_kernel, box, experts),
        [rows_of(n), rows_of(2 * n + ROWS)] + [boxed] * experts,
        arrived0,
        cotangent[0],
        notes1,
        gain,
        *got,
        scratch=[picked],
    )
    arrived1 = shift(behind, sections=-1)
    cross1, own_z, own_x, arrived1 = fence(
        (crossing_of(boxes1), shift(own1, flip=2), shift(own1, flip=1), arrived1)
    )
    cross1, own1 = around(cross1), [own_z, own1, own_x]
    inner = bind(expert_call, inner_kernel, box, packs, cots, outs=False, kept=1)
    own_di = inner(window=(0, ROWS))[1]
    cross_di = inner(window=(ROWS, (experts - 1) * ROWS))[1]

    gate_back = bind(expert_call, gate_back_kernel, box, packs, kept=2)
    own_grad, own_kept1 = gate_back(own1, own_di)
    cross_grad, cross_kept1 = gate_back(cross1, cross_di, after=own_grad[:1])
    down = bind(expert_call, down_kernel, box, packs, reads=False)
    cross_fin = down(cross1, cross_kept1)[0]
    got, _ = give_back(cross_grad, own_grad, -1)
    got[: experts - 1], fin_sums = fence((got[: experts - 1], sums(cross_fin)))
    fin_back = home(fin_sums, 0)
    own_fin = down(own1, own_kept1)[0]
    g1, own_g, *boxes_g = call(
        bind(turn_kernel, box, experts),
        [rows_of(n)] + [boxed] * experts,
        arrived1,
        notes0,
        *got,
        scratch=[picked],
    )

    cross_g, own_z, own_x, fin_own = fence(
        (crossing_of(boxes_g), shift(own_g, flip=2), shift(own_g, flip=1), own_home(own_fin, 0))
    )
    cross_g, own_g = around(cross_g), [own_z, own_g, own_x]
    back = bind(expert_call, back_kernel, box, packs)
    fin = fin_back + fin_own
    cross_grad = back(cross_g, cross_kept0)[0]
    own_grad = back(own_g, own_kept0, after=cross_grad[:1] + tuple(fin))[0]
    got = home(sums(cross_grad), 0) + own_home(own_grad, 0)
    (g0,) = call(
        bind(last_kernel, box, experts),
        [rows_of(n)],
        g1,
        tokens[0],
        notes0,
        gain,
        *got,
        scratch=[picked],
    )
    (final,) = call(
        bind(final_kernel, box, experts),
        [rows_of(n)],
        h1,
        notes1,
        *fin,
        scratch=[picked],
    )
    return (final[None], g0[None])


def solution(mesh):
    in_specs = (
        P("section", "expert", None),
        P("section", None),
        P("section", "expert", None, None),
        P("section", "expert", None, None),
        P("section", "expert", None, None),
        P("section", None, "expert", None),
        P("section", None, "expert", None),
        P("section", "expert", None),
    )
    out_specs = (P("section", "expert", None), P("section", "expert", None))
    return jax.shard_map(local, mesh=mesh, in_specs=in_specs, out_specs=out_specs, check_vma=False)
```

```python
import functools

import jax
import jax.numpy as jnp
from jax import lax
from jax.experimental import pallas as pl
from jax.experimental.pallas import tpu as pltpu
from jax.sharding import PartitionSpec as P

SPLIT = 4
EPSILON = 1e-06
BF = jnp.bfloat16
F32 = jnp.float32
ROWS = 16
LANES = 128


def dot(left, right, dims=((1,), (0,))):
    return lax.dot_general(left, right, (dims, ((), ())), preferred_element_type=F32)


NT = ((1,), (1,))


def iota(shape, axis):
    return lax.broadcasted_iota(jnp.int32, shape, axis)


class Box:
    def __init__(self, capacity, width):
        self.capacity, self.width = capacity, width
        self.groups, self.extra = capacity // ROWS, capacity % ROWS
        self.cuts = ROWS // self.extra if self.extra else 1
        self.wide = -(-width // (LANES * self.cuts)) * LANES if self.extra else 0
        self.lanes = self.groups * width + self.wide
        self.pieces = -(-width // self.wide) if self.extra else 0

    def group(self, g):
        return pl.ds(g * self.width, self.width)

    def tail(self):
        return pl.ds(self.groups * self.width, self.wide)

    def piece(self, i):
        return i * self.wide, min(self.wide, self.width - i * self.wide)


def shift(value, sections=0, experts=0, flip=0):
    n_sec, n_own = lax.axis_size("section"), lax.axis_size("expert")
    n_exp = n_own // SPLIT
    if sections % n_sec == 0 and experts % n_exp == 0 and flip == 0:
        return value
    pairs = []
    for sec in range(n_sec):
        for own in range(n_own):
            exp, sl = own // SPLIT, own % SPLIT
            to = ((exp + experts) % n_exp) * SPLIT + (sl ^ flip)
            pairs.append((sec * n_own + own, ((sec + sections) % n_sec) * n_own + to))
    return lax.ppermute(value, ("section", "expert"), pairs)


def call(body, outs, *operands, scratch=(), flops=0, after=()):
    moved = sum(a.size * a.dtype.itemsize for a in operands)
    moved += sum(o.size * o.dtype.itemsize for o in outs)
    vmem = pl.BlockSpec(memory_space=pltpu.VMEM)
    read = len(operands)

    def reading(*refs):
        body(*refs[:read], *refs[read + len(after) :])

    return pl.pallas_call(
        reading,
        out_shape=list(outs),
        in_specs=[vmem] * read + [pl.BlockSpec(memory_space=pl.ANY)] * len(after),
        out_specs=[vmem] * len(outs),
        scratch_shapes=list(scratch),
        compiler_params=pltpu.CompilerParams(vmem_limit_bytes=40 * 2**20),
        cost_estimate=pl.CostEstimate(flops=flops, bytes_accessed=moved, transcendentals=0),
    )(*operands, *after)


def column_of(row):
    n = row.shape[1]
    eye = iota((n, n), 0) == iota((n, n), 1)
    return jnp.sum(jnp.where(eye, row, 0.0), axis=1, keepdims=True)


def slots_of(rel, experts, capacity):
    n = rel.shape[1]
    same = jnp.broadcast_to(column_of(rel), (n, n)) == jnp.broadcast_to(rel, (n, n))
    before = iota((n, n), 0) < iota((n, n), 1)
    rank = jnp.sum(jnp.where(same & before, 1.0, 0.0), axis=0, keepdims=True)
    return rel * capacity + rank


def terms(value):
    high = value.astype(BF).astype(F32)
    middle = (value - high).astype(BF).astype(F32)
    return high, middle, value - high - middle


def notes_of(slots, mix, gain, n, width):
    r = iota((ROWS, n), 0)
    left = jnp.where(r == 0, slots, 0.0)
    for at, term in enumerate(terms(mix)):
        left = jnp.where(r == 1 + at, term, left)
    r = iota((ROWS, width), 0)
    wide = jnp.concatenate([left, jnp.zeros((ROWS, width - n), F32)], axis=1)
    for at, term in enumerate(terms(gain)):
        wide = jnp.where(r == 4 + at, term, wide)
    return wide.astype(BF)


def slots_in(notes, n):
    return notes[:, :n].astype(F32)[0:1]


def mix_in(notes, n):
    left = notes[:, :n].astype(F32)
    return column_of(left[1:2] + left[2:3] + left[3:4])


def gain_in(notes):
    wide = notes.astype(F32)
    return wide[4:5] + wide[5:6] + wide[6:7]


def pack_rows(box, slots, values, out_refs):
    n = values.shape[0]
    line = jnp.broadcast_to(slots.astype(jnp.int32), (ROWS, n))
    r = iota((ROWS, n), 0)
    for j, out in enumerate(out_refs):
        first = j * box.capacity
        for g in range(box.groups):
            sel = jnp.where(line == first + g * ROWS + r, 1.0, 0.0).astype(BF)
            out[:, box.group(g)] = dot(sel, values).astype(BF)
        if box.extra:
            total = jnp.zeros((ROWS, box.wide), F32)
            for i in range(box.pieces):
                at, size = box.piece(i)
                hit = (line == first + box.groups * ROWS + r // box.cuts) & (r % box.cuts == i)
                hit &= r // box.cuts < box.extra
                got = dot(jnp.where(hit, 1.0, 0.0).astype(BF), values[:, at : at + size])
                if size < box.wide:
                    got = jnp.concatenate([got, jnp.zeros((ROWS, box.wide - size), F32)], axis=1)
                total = total + got
            out[:, box.tail()] = total.astype(BF)


def pick_rows(box, slots, boxes, n, picked):
    count = len(boxes)
    slots = column_of(slots)
    if box.groups:
        stack = jnp.concatenate(
            [b[:, g * box.width : (g + 1) * box.width] for b in boxes for g in range(box.groups)],
            axis=0,
        )
        tall = count * box.groups * ROWS
        c = iota((n, tall), 1)
        slot = c // (box.groups * ROWS) * box.capacity + c % (box.groups * ROWS)
        sel = jnp.where(slots.astype(jnp.int32) == slot, 1.0, 0.0).astype(BF)
        picked[...] = dot(sel, stack)
    else:
        picked[...] = jnp.zeros(picked.shape, F32)
    if box.extra:
        tails = jnp.concatenate([b[:, box.groups * box.width :] for b in boxes], axis=0)
        c = iota((n, count * ROWS), 1)
        r = c % ROWS
        slot = c // ROWS * box.capacity + box.groups * ROWS + r // box.cuts
        mine = (slots.astype(jnp.int32) == slot) & (r // box.cuts < box.extra)
        for i in range(box.pieces):
            at, size = box.piece(i)
            sel = jnp.where(mine & (r % box.cuts == i), 1.0, 0.0).astype(BF)
            picked[:, at : at + size] += dot(sel, tails[:, :size])


def heights(box, count):
    extra = -(-count * box.extra // ROWS) * ROWS
    return count * box.groups * ROWS, extra


def unpack(box, refs, stack, tails, at=0):
    count = 0
    for ref in refs:
        for p in range(ref.shape[0] // ROWS):
            for g in range(box.groups):
                stack[at : at + ROWS, :] = ref[p * ROWS : (p + 1) * ROWS, box.group(g)]
                at += ROWS
            if box.extra:
                tails[count * ROWS : (count + 1) * ROWS, :] = ref[
                    p * ROWS : (p + 1) * ROWS, box.tail()
                ]
            count += 1
    if box.extra:
        extra = heights(box, count)[1]
        r = iota((extra, count * ROWS), 0)
        c = iota((extra, count * ROWS), 1)
        mine = (r // box.extra == c // ROWS) & (r % box.extra == c % ROWS // box.cuts)
        for i in range(box.pieces):
            start, size = box.piece(i)
            sel = jnp.where(mine & (c % ROWS % box.cuts == i), 1.0, 0.0).astype(BF)
            stack[at : at + extra, start : start + size] = dot(sel, tails[:, :size]).astype(BF)


def repack(box, rows, refs):
    rows = rows.astype(BF)
    at = 0
    count = 0
    for ref in refs:
        for p in range(ref.shape[0] // ROWS):
            for g in range(box.groups):
                ref[p * ROWS : (p + 1) * ROWS, box.group(g)] = rows[at : at + ROWS]
                at += ROWS
            count += 1
    if box.extra:
        extra = heights(box, count)[1]
        r = iota((count * ROWS, extra), 0)
        c = iota((count * ROWS, extra), 1)
        mine = (c // box.extra == r // ROWS) & (c % box.extra == r % ROWS // box.cuts)
        total = jnp.zeros((count * ROWS, box.wide), F32)
        for i in range(box.pieces):
            start, size = box.piece(i)
            sel = jnp.where(mine & (r % ROWS % box.cuts == i), 1.0, 0.0).astype(BF)
            got = dot(sel, rows[at:, start : start + size])
            if size < box.wide:
                pad = jnp.zeros((count * ROWS, box.wide - size), F32)
                got = jnp.concatenate([got, pad], axis=1)
            total = total + got
        total = total.astype(BF)
        count = 0
        for ref in refs:
            tall = ref.shape[0]
            ref[:, box.tail()] = total[count : count + tall]
            count += tall


def inv_rms(wide):
    return lax.rsqrt(jnp.mean(wide * wide, axis=-1, keepdims=True) + EPSILON)


def total_of(refs):
    return sum(ref[...].astype(F32) for ref in refs).astype(BF)


def start_kernel(box, experts, tokens, cot, gain, ids, mix, ahead, notes0, notes1, *boxes):
    n, width = tokens.shape
    mine = lax.axis_index("expert") // SPLIT
    for k, notes in enumerate((notes0, notes1)):
        rel = ids[k : k + 1, :] - mine
        rel = jnp.where(rel < 0, rel + experts, rel).astype(F32)
        slots = slots_of(rel, experts, box.capacity)
        notes[...] = notes_of(slots, mix[k : k + 1, :], gain[...], n, width)
    ahead[:n] = tokens[...]
    ahead[n:] = notes0[...]
    wide = tokens[...].astype(F32)
    normed = (wide * inv_rms(wide) * gain[...]).astype(BF)
    crossing = boxes[2:]
    firsts = [boxes[0]] + [ref.at[:ROWS] for ref in crossing]
    pack_rows(box, slots_in(notes0[...], n), normed, firsts)
    seconds = [boxes[1]] + [ref.at[ROWS:] for ref in crossing]
    pack_rows(box, slots_in(notes1[...], n), cot[...], seconds)


def combine(box, notes, n, own, back, picked):
    sums = [total_of(own)] + [ref[...].astype(BF) for ref in back]
    pick_rows(box, slots_in(notes, n), sums, n, picked)
    return mix_in(notes, n) * picked[...]


def split_refs(refs, experts, outs):
    ins = refs[:-outs]
    return ins[experts - 1 :], ins[: experts - 1], refs[-outs:]


def middle_kernel(box, experts, arrived, cot, notes1, gain, *refs):
    boxes, picked = refs[-1 - experts : -1], refs[-1]
    own, back, (after, behind) = split_refs(refs[: -1 - experts], experts, 2)
    n = cot.shape[0]
    update = combine(box, arrived[n:], n, own, back, picked)
    later = (arrived[:n].astype(F32) + update).astype(BF)
    after[...] = later
    behind[:n] = later
    behind[n : 2 * n] = cot[...]
    behind[2 * n :] = notes1[...]
    wide = later.astype(F32)
    normed = (wide * inv_rms(wide) * gain[...]).astype(BF)
    pack_rows(box, slots_in(notes1[...], n), normed, boxes)


def final_kernel(box, experts, hidden, notes, *refs):
    picked = refs[-1]
    own, back, (out,) = split_refs(refs[:-1], experts, 1)
    n = hidden.shape[0]
    update = combine(box, notes[...], n, own, back, picked)
    out[...] = (hidden[...].astype(F32) + update).astype(BF)


def norm_back(hidden, gain, grad):
    wide = hidden.astype(F32)
    inv = inv_rms(wide)
    scaled = grad * gain
    along = jnp.mean(scaled * wide, axis=-1, keepdims=True)
    return inv * scaled - wide * (inv * inv * inv * along)


def turn_kernel(box, experts, arrived, notes0, *refs):
    boxes, picked = refs[-1 - experts : -1], refs[-1]
    own, back, (out,) = split_refs(refs[: -1 - experts], experts, 1)
    n = out.shape[0]
    notes = arrived[2 * n :]
    d_normed = combine(box, notes, n, own, back, picked)
    change = norm_back(arrived[:n], gain_in(notes), d_normed)
    now = (arrived[n : 2 * n].astype(F32) + change).astype(BF)
    out[...] = now
    pack_rows(box, slots_in(notes0[...], n), now, boxes)


def last_kernel(box, experts, grad, hidden, notes0, gain, *refs):
    picked = refs[-1]
    own, back, (out,) = split_refs(refs[:-1], experts, 1)
    n = hidden.shape[0]
    d_normed = combine(box, notes0[...], n, own, back, picked)
    change = norm_back(hidden[...], gain[...], d_normed)
    out[...] = (grad[...].astype(F32) + change).astype(BF)


def spans(tall):
    return pl.ds(0, 2 * tall), pl.ds(tall, 2 * tall)


def gate_up(rows, pack):
    return dot(rows, pack[: 2 * (pack.shape[0] // 3)], NT)


def parts_of(both):
    units = both.shape[1] // 2
    return both[:, :units], both[:, units:]


def down_rows(both, pack):
    g, u = parts_of(both)
    return dot((jax.nn.silu(g) * u).astype(BF), pack[2 * g.shape[1] :])


def inner_of(rows, pack):
    return dot(rows, pack[2 * (pack.shape[0] // 3) :], NT)


def part_rows(d_inner, both, pack):
    g, u = parts_of(both)
    r = jax.nn.sigmoid(g)
    d_gate = d_inner * u * r * (1.0 + g * (1.0 - r))
    d_up = d_inner * g * r
    return dot(jnp.concatenate([d_gate, d_up], axis=1).astype(BF), pack[: both.shape[1]])


def read_rows(box, rows, stack, tails):
    tall = stack.shape[0] // 3
    for at, ref in enumerate(rows):
        unpack(box, [ref], stack, tails, at * tall)
    return [stack[span, :] for span in spans(tall)]


def write_rows(box, top, bottom, outs):
    tall = top.shape[0] // 2
    for ref, value in zip(outs, (top[:tall], top[tall:] + bottom[:tall], bottom[tall:])):
        repack(box, value, [ref])


def forward_kernel(box, packs, saved, rows, outs, kept, stack, tails):
    sides = read_rows(box, rows, stack, tails)
    total = []
    for side, values in enumerate(sides):
        total.append(0.0)
        for at in (2 * side, 2 * side + 1):
            both = gate_up(values, packs[at])
            kept[at][...] = both
            total[side] = total[side] + down_rows(both, packs[at])
    write_rows(box, *total, outs)


def inner_kernel(box, packs, saved, rows, outs, kept, stack, tails):
    for side, values in enumerate(read_rows(box, rows, stack, tails)):
        for at in (2 * side, 2 * side + 1):
            kept[at][...] = inner_of(values, packs[at])


def gate_back_kernel(box, packs, saved, rows, outs, kept, stack, tails):
    sides = read_rows(box, rows, stack, tails)
    total = []
    for side, values in enumerate(sides):
        total.append(0.0)
        for at in (2 * side, 2 * side + 1):
            both = gate_up(values, packs[at])
            kept[at][...] = both
            total[side] = total[side] + part_rows(saved[at][...], both, packs[at])
    write_rows(box, *total, outs)


def back_kernel(box, packs, saved, rows, outs, kept, stack, tails):
    sides = read_rows(box, rows, stack, tails)
    total = []
    for side, values in enumerate(sides):
        total.append(0.0)
        for at in (2 * side, 2 * side + 1):
            d_inner = inner_of(values, packs[at])
            total[side] = total[side] + part_rows(d_inner, saved[at][...], packs[at])
    write_rows(box, *total, outs)


def down_kernel(box, packs, saved, rows, outs, kept, stack, tails):
    total = []
    for side in range(2):
        at = 2 * side
        total.append(sum(down_rows(saved[i][...], packs[i]) for i in (at, at + 1)))
    write_rows(box, *total, outs)


def expert_call(kernel, box, packs, rows, saved=(), outs=True, kept=0, reads=True, after=(), window=None):
    width = packs[0].shape[1]
    first, size = window or (0, rows[0].shape[0])
    count = size // ROWS
    tall = sum(heights(box, count))
    boxes = jax.ShapeDtypeStruct((count * ROWS, box.lanes), BF)
    results = [boxes] * len(rows) if outs else []
    if kept:
        units = [pack.shape[0] // 3 for pack in packs]
        results += [jax.ShapeDtypeStruct((2 * tall, kept * u), F32) for u in units]
    inputs = list(packs) + list(saved) + (list(rows) if reads else [])
    n_in, n_p, n_s, n_out = len(inputs), len(packs), len(saved), len(rows) if outs else 0

    def body(*refs):
        results_refs = refs[n_in:-2]
        kernel(
            box,
            refs[:n_p],
            refs[n_p : n_p + n_s],
            [ref.at[pl.ds(first, size)] for ref in refs[n_p + n_s : n_in]],
            results_refs[:n_out],
            results_refs[n_out:],
            refs[-2],
            refs[-1],
        )

    scratch = [
        pltpu.VMEM((3 * tall, width), BF),
        pltpu.VMEM((count * ROWS, max(box.wide, LANES)), BF),
    ]
    flops = sum(2 * 2 * tall * pack.size for pack in packs)
    results = call(body, results, *inputs, scratch=scratch, flops=flops, after=after)
    return results[:n_out], results[n_out:]


def local(tokens, norm_gain, w_gate, w_up, w_down, routes, mix_weights, cotangent):
    experts = lax.axis_size("expert") // SPLIT
    n, width = tokens.shape[1:]
    capacity = n // experts + max(1, n // (16 * experts))
    box = Box(capacity, width)
    gain = norm_gain
    gate_w, up_w, down_w = w_gate[0, 0].T, w_up[0, 0].T, w_down[0, 0]
    boxed = jax.ShapeDtypeStruct((ROWS, box.lanes), BF)
    picked = pltpu.VMEM((n, width), F32)
    bind = functools.partial

    def joined(arrays):
        return arrays[0] if len(arrays) == 1 else jnp.concatenate(arrays, axis=0)

    fence = lax.optimization_barrier

    def crossing_of(boxes):
        return joined([shift(boxes[j - 1], experts=j) for j in range(1, experts)])

    def around(boxes):
        return [shift(boxes, flip=2), boxes, shift(boxes, flip=1)]

    def add(*values):
        return sum(v.astype(F32) for v in values).astype(BF)

    def sums(parts):
        return add(parts[1], shift(parts[0], flip=2), shift(parts[2], flip=1))

    def home(total, sections):
        return [
            shift(total[(j - 1) * ROWS : j * ROWS], sections=sections, experts=-j)
            for j in range(1, experts)
        ]

    def own_home(parts, sections):
        return [
            shift(parts[0], sections=sections, flip=2),
            shift(parts[2], sections=sections, flip=1),
            shift(parts[1], sections=sections),
        ]

    def give_back(cross, own, sections, others=()):
        total = sums(cross)
        back = home(total, sections)
        own, _, others = fence((own, total, others))
        return back + own_home(own, sections), others

    units = w_gate.shape[3]
    cut = -(-units * 7 // 12 // ROWS) * ROWS
    top = jnp.concatenate([gate_w[:cut], up_w[:cut], down_w[:cut]], axis=0)
    bottom = jnp.concatenate([gate_w[cut:], up_w[cut:], down_w[cut:]], axis=0)
    packs = [top, shift(top, flip=1), bottom, shift(bottom, flip=2)]

    def rows_of(count):
        return jax.ShapeDtypeStruct((count, width), BF)

    both = jax.ShapeDtypeStruct((2 * ROWS, box.lanes), BF)
    ahead, notes0, notes1, own_tok, own_cot, *crossing = call(
        bind(start_kernel, box, experts),
        [rows_of(n + ROWS), rows_of(ROWS), rows_of(ROWS), boxed, boxed] + [both] * (experts - 1),
        tokens[0],
        cotangent[0],
        gain,
        routes[0, :, :, 0],
        mix_weights[0, :, :, 0],
        after=[top, bottom],
    )
    crossed = [shift(crossing[j - 1], experts=j) for j in range(1, experts)]
    own0 = around(own_tok)
    packs, crossed, own0 = fence((packs, crossed, own0))
    cross0 = around(joined([c[:ROWS] for c in crossed]))
    cots = joined([own_cot] + [c[ROWS:] for c in crossed])
    cross0, cots = fence((cross0, cots))
    cots = around(cots)

    cross_out, cross_kept0 = expert_call(forward_kernel, box, packs, cross0, kept=2)
    own_out, own_kept0 = expert_call(
        forward_kernel, box, packs, own0, kept=2, after=cross_out[:1]
    )
    cross_out, ahead = fence((cross_out, ahead))
    arrived0 = shift(ahead, sections=1)
    got, cots = give_back(cross_out, own_out, 1, cots)
    h1, behind, own1, *boxes1 = call(
        bind(middle_kernel, box, experts),
        [rows_of(n), rows_of(2 * n + ROWS)] + [boxed] * experts,
        arrived0,
        cotangent[0],
        notes1,
        gain,
        *got,
        scratch=[picked],
    )
    arrived1 = shift(behind, sections=-1)
    cross1, own_z, own_x, arrived1 = fence(
        (crossing_of(boxes1), shift(own1, flip=2), shift(own1, flip=1), arrived1)
    )
    cross1, own1 = around(cross1), [own_z, own1, own_x]
    inner = bind(expert_call, inner_kernel, box, packs, cots, outs=False, kept=1)
    own_di = inner(window=(0, ROWS))[1]
    cross_di = inner(window=(ROWS, (experts - 1) * ROWS))[1]

    gate_back = bind(expert_call, gate_back_kernel, box, packs, kept=2)
    own_grad, own_kept1 = gate_back(own1, own_di)
    cross_grad, cross_kept1 = gate_back(cross1, cross_di, after=own_grad[:1])
    down = bind(expert_call, down_kernel, box, packs, reads=False)
    cross_fin = down(cross1, cross_kept1)[0]
    got, _ = give_back(cross_grad, own_grad, -1)
    got[: experts - 1], fin_sums = fence((got[: experts - 1], sums(cross_fin)))
    fin_back = home(fin_sums, 0)
    own_fin = down(own1, own_kept1)[0]
    g1, own_g, *boxes_g = call(
        bind(turn_kernel, box, experts),
        [rows_of(n)] + [boxed] * experts,
        arrived1,
        notes0,
        *got,
        scratch=[picked],
    )

    cross_g, own_z, own_x = fence(
        (crossing_of(boxes_g), shift(own_g, flip=2), shift(own_g, flip=1))
    )
    cross_g, own_g = around(cross_g), [own_z, own_g, own_x]
    back = bind(expert_call, back_kernel, box, packs)
    fin = fin_back + own_home(own_fin, 0)
    cross_grad = back(cross_g, cross_kept0)[0]
    own_grad = back(own_g, own_kept0, after=cross_grad[:1] + tuple(fin))[0]
    got, _ = give_back(cross_grad, own_grad, 0)
    got[: experts - 1] = [sums_home.astype(F32) for sums_home in got[: experts - 1]]
    (g0,) = call(
        bind(last_kernel, box, experts),
        [rows_of(n)],
        g1,
        tokens[0],
        notes0,
        gain,
        *got,
        scratch=[picked],
    )
    (final,) = call(
        bind(final_kernel, box, experts),
        [rows_of(n)],
        h1,
        notes1,
        *fin,
        scratch=[picked],
    )
    return (final[None], g0[None])


def solution(mesh):
    in_specs = (
        P("section", "expert", None),
        P("section", None),
        P("section", "expert", None, None),
        P("section", "expert", None, None),
        P("section", "expert", None, None),
        P("section", None, "expert", None),
        P("section", None, "expert", None),
        P("section", "expert", None),
    )
    out_specs = (P("section", "expert", None), P("section", "expert", None))
    return jax.shard_map(local, mesh=mesh, in_specs=in_specs, out_specs=out_specs, check_vma=False)
```

```python
import functools

import jax
import jax.numpy as jnp
from jax import lax
from jax.experimental import pallas as pl
from jax.experimental.pallas import tpu as pltpu
from jax.sharding import PartitionSpec as P

SPLIT = 4
EPSILON = 1e-06
BF = jnp.bfloat16
F32 = jnp.float32
ROWS = 16
LANES = 128


def dot(left, right, dims=((1,), (0,))):
    return lax.dot_general(left, right, (dims, ((), ())), preferred_element_type=F32)


NT = ((1,), (1,))


def iota(shape, axis):
    return lax.broadcasted_iota(jnp.int32, shape, axis)


class Box:
    def __init__(self, capacity, width):
        self.capacity, self.width = capacity, width
        self.groups, self.extra = capacity // ROWS, capacity % ROWS
        self.cuts = ROWS // self.extra if self.extra else 1
        self.wide = -(-width // (LANES * self.cuts)) * LANES if self.extra else 0
        self.lanes = self.groups * width + self.wide
        self.pieces = -(-width // self.wide) if self.extra else 0

    def group(self, g):
        return pl.ds(g * self.width, self.width)

    def tail(self):
        return pl.ds(self.groups * self.width, self.wide)

    def piece(self, i):
        return i * self.wide, min(self.wide, self.width - i * self.wide)


def shift(value, sections=0, experts=0, flip=0):
    n_sec, n_own = lax.axis_size("section"), lax.axis_size("expert")
    n_exp = n_own // SPLIT
    if sections % n_sec == 0 and experts % n_exp == 0 and flip == 0:
        return value
    pairs = []
    for sec in range(n_sec):
        for own in range(n_own):
            exp, sl = own // SPLIT, own % SPLIT
            to = ((exp + experts) % n_exp) * SPLIT + (sl ^ flip)
            pairs.append((sec * n_own + own, ((sec + sections) % n_sec) * n_own + to))
    return lax.ppermute(value, ("section", "expert"), pairs)


def call(body, outs, *operands, scratch=(), flops=0, after=()):
    moved = sum(a.size * a.dtype.itemsize for a in operands)
    moved += sum(o.size * o.dtype.itemsize for o in outs)
    vmem = pl.BlockSpec(memory_space=pltpu.VMEM)
    read = len(operands)

    def reading(*refs):
        body(*refs[:read], *refs[read + len(after) :])

    return pl.pallas_call(
        reading,
        out_shape=list(outs),
        in_specs=[vmem] * read + [pl.BlockSpec(memory_space=pl.ANY)] * len(after),
        out_specs=[vmem] * len(outs),
        scratch_shapes=list(scratch),
        compiler_params=pltpu.CompilerParams(vmem_limit_bytes=40 * 2**20),
        cost_estimate=pl.CostEstimate(flops=flops, bytes_accessed=moved, transcendentals=0),
    )(*operands, *after)


def column_of(row):
    n = row.shape[1]
    eye = iota((n, n), 0) == iota((n, n), 1)
    return jnp.sum(jnp.where(eye, row, 0.0), axis=1, keepdims=True)


def slots_of(rel, experts, capacity):
    n = rel.shape[1]
    same = jnp.broadcast_to(column_of(rel), (n, n)) == jnp.broadcast_to(rel, (n, n))
    before = iota((n, n), 0) < iota((n, n), 1)
    rank = jnp.sum(jnp.where(same & before, 1.0, 0.0), axis=0, keepdims=True)
    return rel * capacity + rank


def terms(value):
    high = value.astype(BF).astype(F32)
    middle = (value - high).astype(BF).astype(F32)
    return high, middle, value - high - middle


def notes_of(slots, mix, gain, n, width):
    r = iota((ROWS, n), 0)
    left = jnp.where(r == 0, slots, 0.0)
    for at, term in enumerate(terms(mix)):
        left = jnp.where(r == 1 + at, term, left)
    r = iota((ROWS, width), 0)
    wide = jnp.concatenate([left, jnp.zeros((ROWS, width - n), F32)], axis=1)
    for at, term in enumerate(terms(gain)):
        wide = jnp.where(r == 4 + at, term, wide)
    return wide.astype(BF)


def slots_in(notes, n):
    return notes[:, :n].astype(F32)[0:1]


def mix_in(notes, n):
    left = notes[:, :n].astype(F32)
    return column_of(left[1:2] + left[2:3] + left[3:4])


def gain_in(notes):
    wide = notes.astype(F32)
    return wide[4:5] + wide[5:6] + wide[6:7]


def pack_rows(box, slots, values, out_refs):
    n = values.shape[0]
    line = jnp.broadcast_to(slots.astype(jnp.int32), (ROWS, n))
    r = iota((ROWS, n), 0)
    for j, out in enumerate(out_refs):
        first = j * box.capacity
        for g in range(box.groups):
            sel = jnp.where(line == first + g * ROWS + r, 1.0, 0.0).astype(BF)
            out[:, box.group(g)] = dot(sel, values).astype(BF)
        if box.extra:
            total = jnp.zeros((ROWS, box.wide), F32)
            for i in range(box.pieces):
                at, size = box.piece(i)
                hit = (line == first + box.groups * ROWS + r // box.cuts) & (r % box.cuts == i)
                hit &= r // box.cuts < box.extra
                got = dot(jnp.where(hit, 1.0, 0.0).astype(BF), values[:, at : at + size])
                if size < box.wide:
                    got = jnp.concatenate([got, jnp.zeros((ROWS, box.wide - size), F32)], axis=1)
                total = total + got
            out[:, box.tail()] = total.astype(BF)


def pick_rows(box, slots, boxes, n, picked):
    count = len(boxes)
    slots = column_of(slots)
    if box.groups:
        stack = jnp.concatenate(
            [b[:, g * box.width : (g + 1) * box.width] for b in boxes for g in range(box.groups)],
            axis=0,
        )
        tall = count * box.groups * ROWS
        c = iota((n, tall), 1)
        slot = c // (box.groups * ROWS) * box.capacity + c % (box.groups * ROWS)
        sel = jnp.where(slots.astype(jnp.int32) == slot, 1.0, 0.0).astype(BF)
        picked[...] = dot(sel, stack)
    else:
        picked[...] = jnp.zeros(picked.shape, F32)
    if box.extra:
        tails = jnp.concatenate([b[:, box.groups * box.width :] for b in boxes], axis=0)
        c = iota((n, count * ROWS), 1)
        r = c % ROWS
        slot = c // ROWS * box.capacity + box.groups * ROWS + r // box.cuts
        mine = (slots.astype(jnp.int32) == slot) & (r // box.cuts < box.extra)
        for i in range(box.pieces):
            at, size = box.piece(i)
            sel = jnp.where(mine & (r % box.cuts == i), 1.0, 0.0).astype(BF)
            picked[:, at : at + size] += dot(sel, tails[:, :size])


def heights(box, count):
    extra = -(-count * box.extra // ROWS) * ROWS
    return count * box.groups * ROWS, extra


def unpack(box, refs, stack, tails, at=0):
    count = 0
    for ref in refs:
        for p in range(ref.shape[0] // ROWS):
            for g in range(box.groups):
                stack[at : at + ROWS, :] = ref[p * ROWS : (p + 1) * ROWS, box.group(g)]
                at += ROWS
            if box.extra:
                tails[count * ROWS : (count + 1) * ROWS, :] = ref[
                    p * ROWS : (p + 1) * ROWS, box.tail()
                ]
            count += 1
    if box.extra:
        extra = heights(box, count)[1]
        r = iota((extra, count * ROWS), 0)
        c = iota((extra, count * ROWS), 1)
        mine = (r // box.extra == c // ROWS) & (r % box.extra == c % ROWS // box.cuts)
        for i in range(box.pieces):
            start, size = box.piece(i)
            sel = jnp.where(mine & (c % ROWS % box.cuts == i), 1.0, 0.0).astype(BF)
            stack[at : at + extra, start : start + size] = dot(sel, tails[:, :size]).astype(BF)


def repack(box, rows, refs):
    rows = rows.astype(BF)
    at = 0
    count = 0
    for ref in refs:
        for p in range(ref.shape[0] // ROWS):
            for g in range(box.groups):
                ref[p * ROWS : (p + 1) * ROWS, box.group(g)] = rows[at : at + ROWS]
                at += ROWS
            count += 1
    if box.extra:
        extra = heights(box, count)[1]
        r = iota((count * ROWS, extra), 0)
        c = iota((count * ROWS, extra), 1)
        mine = (c // box.extra == r // ROWS) & (c % box.extra == r % ROWS // box.cuts)
        total = jnp.zeros((count * ROWS, box.wide), F32)
        for i in range(box.pieces):
            start, size = box.piece(i)
            sel = jnp.where(mine & (r % ROWS % box.cuts == i), 1.0, 0.0).astype(BF)
            got = dot(sel, rows[at:, start : start + size])
            if size < box.wide:
                pad = jnp.zeros((count * ROWS, box.wide - size), F32)
                got = jnp.concatenate([got, pad], axis=1)
            total = total + got
        total = total.astype(BF)
        count = 0
        for ref in refs:
            tall = ref.shape[0]
            ref[:, box.tail()] = total[count : count + tall]
            count += tall


def inv_rms(wide):
    return lax.rsqrt(jnp.mean(wide * wide, axis=-1, keepdims=True) + EPSILON)


def total_of(refs):
    return sum(ref[...].astype(F32) for ref in refs).astype(BF)


def start_kernel(box, experts, tokens, cot, gain, ids, mix, ahead, notes0, notes1, *boxes):
    n, width = tokens.shape
    mine = lax.axis_index("expert") // SPLIT
    for k, notes in enumerate((notes0, notes1)):
        rel = ids[k : k + 1, :] - mine
        rel = jnp.where(rel < 0, rel + experts, rel).astype(F32)
        slots = slots_of(rel, experts, box.capacity)
        notes[...] = notes_of(slots, mix[k : k + 1, :], gain[...], n, width)
    ahead[:n] = tokens[...]
    ahead[n:] = notes0[...]
    wide = tokens[...].astype(F32)
    normed = (wide * inv_rms(wide) * gain[...]).astype(BF)
    crossing = boxes[2:]
    firsts = [boxes[0]] + [ref.at[:ROWS] for ref in crossing]
    pack_rows(box, slots_in(notes0[...], n), normed, firsts)
    seconds = [boxes[1]] + [ref.at[ROWS:] for ref in crossing]
    pack_rows(box, slots_in(notes1[...], n), cot[...], seconds)


def combine(box, notes, n, own, back, picked):
    sums = [total_of(own)] + [ref[...].astype(BF) for ref in back]
    pick_rows(box, slots_in(notes, n), sums, n, picked)
    return mix_in(notes, n) * picked[...]


def split_refs(refs, experts, outs):
    ins = refs[:-outs]
    return ins[experts - 1 :], ins[: experts - 1], refs[-outs:]


def middle_kernel(box, experts, arrived, cot, notes1, gain, *refs):
    boxes, picked = refs[-1 - experts : -1], refs[-1]
    own, back, (after, behind) = split_refs(refs[: -1 - experts], experts, 2)
    n = cot.shape[0]
    update = combine(box, arrived[n:], n, own, back, picked)
    later = (arrived[:n].astype(F32) + update).astype(BF)
    after[...] = later
    behind[:n] = later
    behind[n : 2 * n] = cot[...]
    behind[2 * n :] = notes1[...]
    wide = later.astype(F32)
    normed = (wide * inv_rms(wide) * gain[...]).astype(BF)
    pack_rows(box, slots_in(notes1[...], n), normed, boxes)


def final_kernel(box, experts, hidden, notes, *refs):
    picked = refs[-1]
    own, back, (out,) = split_refs(refs[:-1], experts, 1)
    n = hidden.shape[0]
    update = combine(box, notes[...], n, own, back, picked)
    out[...] = (hidden[...].astype(F32) + update).astype(BF)


def norm_back(hidden, gain, grad):
    wide = hidden.astype(F32)
    inv = inv_rms(wide)
    scaled = grad * gain
    along = jnp.mean(scaled * wide, axis=-1, keepdims=True)
    return inv * scaled - wide * (inv * inv * inv * along)


def turn_kernel(box, experts, arrived, notes0, *refs):
    boxes, picked = refs[-1 - experts : -1], refs[-1]
    own, back, (out,) = split_refs(refs[: -1 - experts], experts, 1)
    n = out.shape[0]
    notes = arrived[2 * n :]
    d_normed = combine(box, notes, n, own, back, picked)
    change = norm_back(arrived[:n], gain_in(notes), d_normed)
    now = (arrived[n : 2 * n].astype(F32) + change).astype(BF)
    out[...] = now
    pack_rows(box, slots_in(notes0[...], n), now, boxes)


def last_kernel(box, experts, grad, hidden, notes0, gain, *refs):
    picked = refs[-1]
    own, back, (out,) = split_refs(refs[:-1], experts, 1)
    n = hidden.shape[0]
    d_normed = combine(box, notes0[...], n, own, back, picked)
    change = norm_back(hidden[...], gain[...], d_normed)
    out[...] = (grad[...].astype(F32) + change).astype(BF)


def spans(tall):
    return pl.ds(0, 2 * tall), pl.ds(tall, 2 * tall)


def gate_up(rows, pack):
    return dot(rows, pack[: 2 * (pack.shape[0] // 3)], NT)


def parts_of(both):
    units = both.shape[1] // 2
    return both[:, :units], both[:, units:]


def down_rows(both, pack):
    g, u = parts_of(both)
    return dot((jax.nn.silu(g) * u).astype(BF), pack[2 * g.shape[1] :])


def inner_of(rows, pack):
    return dot(rows, pack[2 * (pack.shape[0] // 3) :], NT)


def part_rows(d_inner, both, pack):
    g, u = parts_of(both)
    r = jax.nn.sigmoid(g)
    d_gate = d_inner * u * r * (1.0 + g * (1.0 - r))
    d_up = d_inner * g * r
    return dot(jnp.concatenate([d_gate, d_up], axis=1).astype(BF), pack[: both.shape[1]])


def read_rows(box, rows, stack, tails):
    tall = stack.shape[0] // 3
    for at, ref in enumerate(rows):
        unpack(box, [ref], stack, tails, at * tall)
    return [stack[span, :] for span in spans(tall)]


def write_rows(box, top, bottom, outs):
    tall = top.shape[0] // 2
    for ref, value in zip(outs, (top[:tall], top[tall:] + bottom[:tall], bottom[tall:])):
        repack(box, value, [ref])


def forward_kernel(box, packs, saved, rows, outs, kept, stack, tails):
    sides = read_rows(box, rows, stack, tails)
    total = []
    for side, values in enumerate(sides):
        total.append(0.0)
        for at in (2 * side, 2 * side + 1):
            both = gate_up(values, packs[at])
            kept[at][...] = both
            total[side] = total[side] + down_rows(both, packs[at])
    write_rows(box, *total, outs)


def inner_kernel(box, packs, saved, rows, outs, kept, stack, tails):
    for side, values in enumerate(read_rows(box, rows, stack, tails)):
        for at in (2 * side, 2 * side + 1):
            kept[at][...] = inner_of(values, packs[at])


def gate_back_kernel(box, packs, saved, rows, outs, kept, stack, tails):
    sides = read_rows(box, rows, stack, tails)
    total = []
    for side, values in enumerate(sides):
        total.append(0.0)
        for at in (2 * side, 2 * side + 1):
            both = gate_up(values, packs[at])
            kept[at][...] = both
            total[side] = total[side] + part_rows(saved[at][...], both, packs[at])
    write_rows(box, *total, outs)


def back_kernel(box, packs, saved, rows, outs, kept, stack, tails):
    sides = read_rows(box, rows, stack, tails)
    total = []
    for side, values in enumerate(sides):
        total.append(0.0)
        for at in (2 * side, 2 * side + 1):
            d_inner = inner_of(values, packs[at])
            total[side] = total[side] + part_rows(d_inner, saved[at][...], packs[at])
    write_rows(box, *total, outs)


def down_kernel(box, packs, saved, rows, outs, kept, stack, tails):
    total = []
    for side in range(2):
        at = 2 * side
        total.append(sum(down_rows(saved[i][...], packs[i]) for i in (at, at + 1)))
    write_rows(box, *total, outs)


def expert_call(kernel, box, packs, rows, saved=(), outs=True, kept=0, reads=True, after=(), window=None):
    width = packs[0].shape[1]
    first, size = window or (0, rows[0].shape[0])
    count = size // ROWS
    tall = sum(heights(box, count))
    boxes = jax.ShapeDtypeStruct((count * ROWS, box.lanes), BF)
    results = [boxes] * len(rows) if outs else []
    if kept:
        units = [pack.shape[0] // 3 for pack in packs]
        results += [jax.ShapeDtypeStruct((2 * tall, kept * u), F32) for u in units]
    inputs = list(packs) + list(saved) + (list(rows) if reads else [])
    n_in, n_p, n_s, n_out = len(inputs), len(packs), len(saved), len(rows) if outs else 0

    def body(*refs):
        results_refs = refs[n_in:-2]
        kernel(
            box,
            refs[:n_p],
            refs[n_p : n_p + n_s],
            [ref.at[pl.ds(first, size)] for ref in refs[n_p + n_s : n_in]],
            results_refs[:n_out],
            results_refs[n_out:],
            refs[-2],
            refs[-1],
        )

    scratch = [
        pltpu.VMEM((3 * tall, width), BF),
        pltpu.VMEM((count * ROWS, max(box.wide, LANES)), BF),
    ]
    flops = sum(2 * 2 * tall * pack.size for pack in packs)
    results = call(body, results, *inputs, scratch=scratch, flops=flops, after=after)
    return results[:n_out], results[n_out:]


def local(tokens, norm_gain, w_gate, w_up, w_down, routes, mix_weights, cotangent):
    experts = lax.axis_size("expert") // SPLIT
    n, width = tokens.shape[1:]
    capacity = n // experts + max(1, n // (16 * experts))
    box = Box(capacity, width)
    gain = norm_gain
    gate_w, up_w, down_w = w_gate[0, 0].T, w_up[0, 0].T, w_down[0, 0]
    boxed = jax.ShapeDtypeStruct((ROWS, box.lanes), BF)
    picked = pltpu.VMEM((n, width), F32)
    bind = functools.partial

    def joined(arrays):
        return arrays[0] if len(arrays) == 1 else jnp.concatenate(arrays, axis=0)

    fence = lax.optimization_barrier

    def crossing_of(boxes):
        return joined([shift(boxes[j - 1], experts=j) for j in range(1, experts)])

    def around(boxes):
        return [shift(boxes, flip=2), boxes, shift(boxes, flip=1)]

    def add(*values):
        return sum(v.astype(F32) for v in values).astype(BF)

    def sums(parts):
        return add(parts[1], shift(parts[0], flip=2), shift(parts[2], flip=1))

    def home(total, sections):
        return [
            shift(total[(j - 1) * ROWS : j * ROWS], sections=sections, experts=-j)
            for j in range(1, experts)
        ]

    def own_home(parts, sections):
        return [
            shift(parts[0], sections=sections, flip=2),
            shift(parts[2], sections=sections, flip=1),
            shift(parts[1], sections=sections),
        ]

    def give_back(cross, own, sections, others=()):
        total = sums(cross)
        back = home(total, sections)
        own, _, others = fence((own, total, others))
        return back + own_home(own, sections), others

    units = w_gate.shape[3]
    cut = -(-units * 7 // 12 // ROWS) * ROWS
    top = jnp.concatenate([gate_w[:cut], up_w[:cut], down_w[:cut]], axis=0)
    bottom = jnp.concatenate([gate_w[cut:], up_w[cut:], down_w[cut:]], axis=0)
    packs = [top, shift(top, flip=1), bottom, shift(bottom, flip=2)]

    def rows_of(count):
        return jax.ShapeDtypeStruct((count, width), BF)

    both = jax.ShapeDtypeStruct((2 * ROWS, box.lanes), BF)
    ahead, notes0, notes1, own_tok, own_cot, *crossing = call(
        bind(start_kernel, box, experts),
        [rows_of(n + ROWS), rows_of(ROWS), rows_of(ROWS), boxed, boxed] + [both] * (experts - 1),
        tokens[0],
        cotangent[0],
        gain,
        routes[0, :, :, 0],
        mix_weights[0, :, :, 0],
        after=[top, bottom],
    )
    crossed = [shift(crossing[j - 1], experts=j) for j in range(1, experts)]
    own0 = around(own_tok)
    packs, crossed, own0 = fence((packs, crossed, own0))
    cross0 = around(joined([c[:ROWS] for c in crossed]))
    cots = joined([own_cot] + [c[ROWS:] for c in crossed])
    cross0, cots = fence((cross0, cots))
    cots = around(cots)

    cross_out, cross_kept0 = expert_call(forward_kernel, box, packs, cross0, kept=2)
    own_out, own_kept0 = expert_call(
        forward_kernel, box, packs, own0, kept=2, after=cross_out[:1]
    )
    cross_out, ahead = fence((cross_out, ahead))
    arrived0 = shift(ahead, sections=1)
    got, cots = give_back(cross_out, own_out, 1, cots)
    h1, behind, own1, *boxes1 = call(
        bind(middle_kernel, box, experts),
        [rows_of(n), rows_of(2 * n + ROWS)] + [boxed] * experts,
        arrived0,
        cotangent[0],
        notes1,
        gain,
        *got,
        scratch=[picked],
    )
    arrived1 = shift(behind, sections=-1)
    cross1, own_z, own_x, arrived1 = fence(
        (crossing_of(boxes1), shift(own1, flip=2), shift(own1, flip=1), arrived1)
    )
    cross1, own1 = around(cross1), [own_z, own1, own_x]
    inner = bind(expert_call, inner_kernel, box, packs, cots, outs=False, kept=1)
    own_di = inner(window=(0, ROWS))[1]
    cross_di = inner(window=(ROWS, (experts - 1) * ROWS))[1]

    gate_back = bind(expert_call, gate_back_kernel, box, packs, kept=2)
    own_grad, own_kept1 = gate_back(own1, own_di)
    cross_grad, cross_kept1 = gate_back(cross1, cross_di, after=own_grad[:1])
    down = bind(expert_call, down_kernel, box, packs, reads=False)
    cross_fin = down(cross1, cross_kept1)[0]
    got, _ = give_back(cross_grad, own_grad, -1)
    got[: experts - 1], fin_sums = fence((got[: experts - 1], sums(cross_fin)))
    fin_back = home(fin_sums, 0)
    own_fin = down(own1, own_kept1)[0]
    g1, own_g, *boxes_g = call(
        bind(turn_kernel, box, experts),
        [rows_of(n)] + [boxed] * experts,
        arrived1,
        notes0,
        *got,
        scratch=[picked],
    )

    cross_g, own_z, own_x, fin_back = fence(
        (crossing_of(boxes_g), shift(own_g, flip=2), shift(own_g, flip=1), fin_back)
    )
    cross_g, own_g = around(cross_g), [own_z, own_g, own_x]
    back = bind(expert_call, back_kernel, box, packs)
    fin_own = own_home(own_fin, 0)
    fin = fin_back + fin_own
    own_grad = back(own_g, own_kept0, after=fin_own)[0]
    cross_grad = back(cross_g, cross_kept0, after=own_grad[:1])[0]
    got, _ = give_back(cross_grad, own_grad, 0)
    got[: experts - 1] = [sums_home.astype(F32) for sums_home in got[: experts - 1]]
    (g0,) = call(
        bind(last_kernel, box, experts),
        [rows_of(n)],
        g1,
        tokens[0],
        notes0,
        gain,
        *got,
        scratch=[picked],
    )
    (final,) = call(
        bind(final_kernel, box, experts),
        [rows_of(n)],
        h1,
        notes1,
        *fin,
        scratch=[picked],
    )
    return (final[None], g0[None])


def solution(mesh):
    in_specs = (
        P("section", "expert", None),
        P("section", None),
        P("section", "expert", None, None),
        P("section", "expert", None, None),
        P("section", "expert", None, None),
        P("section", None, "expert", None),
        P("section", None, "expert", None),
        P("section", "expert", None),
    )
    out_specs = (P("section", "expert", None), P("section", "expert", None))
    return jax.shard_map(local, mesh=mesh, in_specs=in_specs, out_specs=out_specs, check_vma=False)
```

```python
import functools

import jax
import jax.numpy as jnp
from jax import lax
from jax.experimental import pallas as pl
from jax.experimental.pallas import tpu as pltpu
from jax.sharding import PartitionSpec as P

SPLIT = 4
EPSILON = 1e-06
BF = jnp.bfloat16
F32 = jnp.float32
ROWS = 16
LANES = 128


def dot(left, right, dims=((1,), (0,))):
    return lax.dot_general(left, right, (dims, ((), ())), preferred_element_type=F32)


NT = ((1,), (1,))


def iota(shape, axis):
    return lax.broadcasted_iota(jnp.int32, shape, axis)


class Box:
    def __init__(self, capacity, width):
        self.capacity, self.width = capacity, width
        self.groups, self.extra = capacity // ROWS, capacity % ROWS
        self.cuts = ROWS // self.extra if self.extra else 1
        self.wide = -(-width // (LANES * self.cuts)) * LANES if self.extra else 0
        self.lanes = self.groups * width + self.wide
        self.pieces = -(-width // self.wide) if self.extra else 0

    def group(self, g):
        return pl.ds(g * self.width, self.width)

    def tail(self):
        return pl.ds(self.groups * self.width, self.wide)

    def piece(self, i):
        return i * self.wide, min(self.wide, self.width - i * self.wide)


def shift(value, sections=0, experts=0, flip=0):
    n_sec, n_own = lax.axis_size("section"), lax.axis_size("expert")
    n_exp = n_own // SPLIT
    if sections % n_sec == 0 and experts % n_exp == 0 and flip == 0:
        return value
    pairs = []
    for sec in range(n_sec):
        for own in range(n_own):
            exp, sl = own // SPLIT, own % SPLIT
            to = ((exp + experts) % n_exp) * SPLIT + (sl ^ flip)
            pairs.append((sec * n_own + own, ((sec + sections) % n_sec) * n_own + to))
    return lax.ppermute(value, ("section", "expert"), pairs)


def call(body, outs, *operands, scratch=(), flops=0, after=()):
    moved = sum(a.size * a.dtype.itemsize for a in operands)
    moved += sum(o.size * o.dtype.itemsize for o in outs)
    vmem = pl.BlockSpec(memory_space=pltpu.VMEM)
    read = len(operands)

    def reading(*refs):
        body(*refs[:read], *refs[read + len(after) :])

    return pl.pallas_call(
        reading,
        out_shape=list(outs),
        in_specs=[vmem] * read + [pl.BlockSpec(memory_space=pl.ANY)] * len(after),
        out_specs=[vmem] * len(outs),
        scratch_shapes=list(scratch),
        compiler_params=pltpu.CompilerParams(vmem_limit_bytes=40 * 2**20),
        cost_estimate=pl.CostEstimate(flops=flops, bytes_accessed=moved, transcendentals=0),
    )(*operands, *after)


def column_of(row):
    n = row.shape[1]
    eye = iota((n, n), 0) == iota((n, n), 1)
    return jnp.sum(jnp.where(eye, row, 0.0), axis=1, keepdims=True)


def slots_of(rel, experts, capacity):
    n = rel.shape[1]
    same = jnp.broadcast_to(column_of(rel), (n, n)) == jnp.broadcast_to(rel, (n, n))
    before = iota((n, n), 0) < iota((n, n), 1)
    rank = jnp.sum(jnp.where(same & before, 1.0, 0.0), axis=0, keepdims=True)
    return rel * capacity + rank


def terms(value):
    high = value.astype(BF).astype(F32)
    middle = (value - high).astype(BF).astype(F32)
    return high, middle, value - high - middle


def notes_of(slots, mix, gain, n, width):
    r = iota((ROWS, n), 0)
    left = jnp.where(r == 0, slots, 0.0)
    for at, term in enumerate(terms(mix)):
        left = jnp.where(r == 1 + at, term, left)
    r = iota((ROWS, width), 0)
    wide = jnp.concatenate([left, jnp.zeros((ROWS, width - n), F32)], axis=1)
    for at, term in enumerate(terms(gain)):
        wide = jnp.where(r == 4 + at, term, wide)
    return wide.astype(BF)


def slots_in(notes, n):
    return notes[:, :n].astype(F32)[0:1]


def mix_in(notes, n):
    left = notes[:, :n].astype(F32)
    return column_of(left[1:2] + left[2:3] + left[3:4])


def gain_in(notes):
    wide = notes.astype(F32)
    return wide[4:5] + wide[5:6] + wide[6:7]


def pack_rows(box, slots, values, out_refs):
    n = values.shape[0]
    line = jnp.broadcast_to(slots.astype(jnp.int32), (ROWS, n))
    r = iota((ROWS, n), 0)
    for j, out in enumerate(out_refs):
        first = j * box.capacity
        for g in range(box.groups):
            sel = jnp.where(line == first + g * ROWS + r, 1.0, 0.0).astype(BF)
            out[:, box.group(g)] = dot(sel, values).astype(BF)
        if box.extra:
            total = jnp.zeros((ROWS, box.wide), F32)
            for i in range(box.pieces):
                at, size = box.piece(i)
                hit = (line == first + box.groups * ROWS + r // box.cuts) & (r % box.cuts == i)
                hit &= r // box.cuts < box.extra
                got = dot(jnp.where(hit, 1.0, 0.0).astype(BF), values[:, at : at + size])
                if size < box.wide:
                    got = jnp.concatenate([got, jnp.zeros((ROWS, box.wide - size), F32)], axis=1)
                total = total + got
            out[:, box.tail()] = total.astype(BF)


def pick_rows(box, slots, boxes, n, picked):
    count = len(boxes)
    slots = column_of(slots)
    if box.groups:
        stack = jnp.concatenate(
            [b[:, g * box.width : (g + 1) * box.width] for b in boxes for g in range(box.groups)],
            axis=0,
        )
        tall = count * box.groups * ROWS
        c = iota((n, tall), 1)
        slot = c // (box.groups * ROWS) * box.capacity + c % (box.groups * ROWS)
        sel = jnp.where(slots.astype(jnp.int32) == slot, 1.0, 0.0).astype(BF)
        picked[...] = dot(sel, stack)
    else:
        picked[...] = jnp.zeros(picked.shape, F32)
    if box.extra:
        tails = jnp.concatenate([b[:, box.groups * box.width :] for b in boxes], axis=0)
        c = iota((n, count * ROWS), 1)
        r = c % ROWS
        slot = c // ROWS * box.capacity + box.groups * ROWS + r // box.cuts
        mine = (slots.astype(jnp.int32) == slot) & (r // box.cuts < box.extra)
        for i in range(box.pieces):
            at, size = box.piece(i)
            sel = jnp.where(mine & (r % box.cuts == i), 1.0, 0.0).astype(BF)
            picked[:, at : at + size] += dot(sel, tails[:, :size])


def heights(box, count):
    extra = -(-count * box.extra // ROWS) * ROWS
    return count * box.groups * ROWS, extra


def unpack(box, refs, stack, tails, at=0):
    count = 0
    for ref in refs:
        for p in range(ref.shape[0] // ROWS):
            for g in range(box.groups):
                stack[at : at + ROWS, :] = ref[p * ROWS : (p + 1) * ROWS, box.group(g)]
                at += ROWS
            if box.extra:
                tails[count * ROWS : (count + 1) * ROWS, :] = ref[
                    p * ROWS : (p + 1) * ROWS, box.tail()
                ]
            count += 1
    if box.extra:
        extra = heights(box, count)[1]
        r = iota((extra, count * ROWS), 0)
        c = iota((extra, count * ROWS), 1)
        mine = (r // box.extra == c // ROWS) & (r % box.extra == c % ROWS // box.cuts)
        for i in range(box.pieces):
            start, size = box.piece(i)
            sel = jnp.where(mine & (c % ROWS % box.cuts == i), 1.0, 0.0).astype(BF)
            stack[at : at + extra, start : start + size] = dot(sel, tails[:, :size]).astype(BF)


def repack(box, rows, refs):
    rows = rows.astype(BF)
    at = 0
    count = 0
    for ref in refs:
        for p in range(ref.shape[0] // ROWS):
            for g in range(box.groups):
                ref[p * ROWS : (p + 1) * ROWS, box.group(g)] = rows[at : at + ROWS]
                at += ROWS
            count += 1
    if box.extra:
        extra = heights(box, count)[1]
        r = iota((count * ROWS, extra), 0)
        c = iota((count * ROWS, extra), 1)
        mine = (c // box.extra == r // ROWS) & (c % box.extra == r % ROWS // box.cuts)
        total = jnp.zeros((count * ROWS, box.wide), F32)
        for i in range(box.pieces):
            start, size = box.piece(i)
            sel = jnp.where(mine & (r % ROWS % box.cuts == i), 1.0, 0.0).astype(BF)
            got = dot(sel, rows[at:, start : start + size])
            if size < box.wide:
                pad = jnp.zeros((count * ROWS, box.wide - size), F32)
                got = jnp.concatenate([got, pad], axis=1)
            total = total + got
        total = total.astype(BF)
        count = 0
        for ref in refs:
            tall = ref.shape[0]
            ref[:, box.tail()] = total[count : count + tall]
            count += tall


def inv_rms(wide):
    return lax.rsqrt(jnp.mean(wide * wide, axis=-1, keepdims=True) + EPSILON)


def total_of(refs):
    return sum(ref[...].astype(F32) for ref in refs).astype(BF)


def start_kernel(box, experts, tokens, cot, gain, ids, mix, ahead, notes0, notes1, *boxes):
    n, width = tokens.shape
    mine = lax.axis_index("expert") // SPLIT
    for k, notes in enumerate((notes0, notes1)):
        rel = ids[k : k + 1, :] - mine
        rel = jnp.where(rel < 0, rel + experts, rel).astype(F32)
        slots = slots_of(rel, experts, box.capacity)
        notes[...] = notes_of(slots, mix[k : k + 1, :], gain[...], n, width)
    ahead[:n] = tokens[...]
    ahead[n:] = notes0[...]
    wide = tokens[...].astype(F32)
    normed = (wide * inv_rms(wide) * gain[...]).astype(BF)
    crossing = boxes[2:]
    firsts = [boxes[0]] + [ref.at[:ROWS] for ref in crossing]
    pack_rows(box, slots_in(notes0[...], n), normed, firsts)
    seconds = [boxes[1]] + [ref.at[ROWS:] for ref in crossing]
    pack_rows(box, slots_in(notes1[...], n), cot[...], seconds)


def combine(box, notes, n, own, back, picked):
    sums = [total_of(own)] + [ref[...].astype(BF) for ref in back]
    pick_rows(box, slots_in(notes, n), sums, n, picked)
    return mix_in(notes, n) * picked[...]


def split_refs(refs, experts, outs):
    ins = refs[:-outs]
    return ins[experts - 1 :], ins[: experts - 1], refs[-outs:]


def middle_kernel(box, experts, arrived, cot, notes1, gain, *refs):
    boxes, picked = refs[-1 - experts : -1], refs[-1]
    own, back, (after, behind) = split_refs(refs[: -1 - experts], experts, 2)
    n = cot.shape[0]
    update = combine(box, arrived[n:], n, own, back, picked)
    later = (arrived[:n].astype(F32) + update).astype(BF)
    after[...] = later
    behind[:n] = later
    behind[n : 2 * n] = cot[...]
    behind[2 * n :] = notes1[...]
    wide = later.astype(F32)
    normed = (wide * inv_rms(wide) * gain[...]).astype(BF)
    pack_rows(box, slots_in(notes1[...], n), normed, boxes)


def final_kernel(box, experts, hidden, notes, *refs):
    picked = refs[-1]
    own, back, (out,) = split_refs(refs[:-1], experts, 1)
    n = hidden.shape[0]
    update = combine(box, notes[...], n, own, back, picked)
    out[...] = (hidden[...].astype(F32) + update).astype(BF)


def norm_back(hidden, gain, grad):
    wide = hidden.astype(F32)
    inv = inv_rms(wide)
    scaled = grad * gain
    along = jnp.mean(scaled * wide, axis=-1, keepdims=True)
    return inv * scaled - wide * (inv * inv * inv * along)


def turn_kernel(box, experts, arrived, notes0, *refs):
    boxes, picked = refs[-1 - experts : -1], refs[-1]
    own, back, (out,) = split_refs(refs[: -1 - experts], experts, 1)
    n = out.shape[0]
    notes = arrived[2 * n :]
    d_normed = combine(box, notes, n, own, back, picked)
    change = norm_back(arrived[:n], gain_in(notes), d_normed)
    now = (arrived[n : 2 * n].astype(F32) + change).astype(BF)
    out[...] = now
    pack_rows(box, slots_in(notes0[...], n), now, boxes)


def last_kernel(box, experts, grad, hidden, notes0, gain, *refs):
    picked = refs[-1]
    own, back, (out,) = split_refs(refs[:-1], experts, 1)
    n = hidden.shape[0]
    d_normed = combine(box, notes0[...], n, own, back, picked)
    change = norm_back(hidden[...], gain[...], d_normed)
    out[...] = (grad[...].astype(F32) + change).astype(BF)


def spans(tall):
    return pl.ds(0, 2 * tall), pl.ds(tall, 2 * tall)


def gate_up(rows, pack):
    return dot(rows, pack[: 2 * (pack.shape[0] // 3)], NT)


def parts_of(both):
    units = both.shape[1] // 2
    return both[:, :units], both[:, units:]


def down_rows(both, pack):
    g, u = parts_of(both)
    return dot((jax.nn.silu(g) * u).astype(BF), pack[2 * g.shape[1] :])


def inner_of(rows, pack):
    return dot(rows, pack[2 * (pack.shape[0] // 3) :], NT)


def part_rows(d_inner, both, pack):
    g, u = parts_of(both)
    r = jax.nn.sigmoid(g)
    d_gate = d_inner * u * r * (1.0 + g * (1.0 - r))
    d_up = d_inner * g * r
    return dot(jnp.concatenate([d_gate, d_up], axis=1).astype(BF), pack[: both.shape[1]])


def read_rows(box, rows, stack, tails):
    tall = stack.shape[0] // 3
    for at, ref in enumerate(rows):
        unpack(box, [ref], stack, tails, at * tall)
    return [stack[span, :] for span in spans(tall)]


def write_rows(box, top, bottom, outs):
    tall = top.shape[0] // 2
    for ref, value in zip(outs, (top[:tall], top[tall:] + bottom[:tall], bottom[tall:])):
        repack(box, value, [ref])


def forward_kernel(box, packs, saved, rows, outs, kept, stack, tails):
    sides = read_rows(box, rows, stack, tails)
    total = []
    for side, values in enumerate(sides):
        total.append(0.0)
        for at in (2 * side, 2 * side + 1):
            both = gate_up(values, packs[at])
            kept[at][...] = both
            total[side] = total[side] + down_rows(both, packs[at])
    write_rows(box, *total, outs)


def inner_kernel(box, packs, saved, rows, outs, kept, stack, tails):
    for side, values in enumerate(read_rows(box, rows, stack, tails)):
        for at in (2 * side, 2 * side + 1):
            kept[at][...] = inner_of(values, packs[at])


def gate_back_kernel(box, packs, saved, rows, outs, kept, stack, tails):
    sides = read_rows(box, rows, stack, tails)
    total = []
    for side, values in enumerate(sides):
        total.append(0.0)
        for at in (2 * side, 2 * side + 1):
            both = gate_up(values, packs[at])
            kept[at][...] = both
            total[side] = total[side] + part_rows(saved[at][...], both, packs[at])
    write_rows(box, *total, outs)


def back_kernel(box, packs, saved, rows, outs, kept, stack, tails):
    sides = read_rows(box, rows, stack, tails)
    total = []
    for side, values in enumerate(sides):
        total.append(0.0)
        for at in (2 * side, 2 * side + 1):
            d_inner = inner_of(values, packs[at])
            total[side] = total[side] + part_rows(d_inner, saved[at][...], packs[at])
    write_rows(box, *total, outs)


def down_kernel(box, packs, saved, rows, outs, kept, stack, tails):
    total = []
    for side in range(2):
        at = 2 * side
        total.append(sum(down_rows(saved[i][...], packs[i]) for i in (at, at + 1)))
    write_rows(box, *total, outs)


def expert_call(kernel, box, packs, rows, saved=(), outs=True, kept=0, reads=True, after=(), window=None):
    width = packs[0].shape[1]
    first, size = window or (0, rows[0].shape[0])
    count = size // ROWS
    tall = sum(heights(box, count))
    boxes = jax.ShapeDtypeStruct((count * ROWS, box.lanes), BF)
    results = [boxes] * len(rows) if outs else []
    if kept:
        units = [pack.shape[0] // 3 for pack in packs]
        results += [jax.ShapeDtypeStruct((2 * tall, kept * u), F32) for u in units]
    inputs = list(packs) + list(saved) + (list(rows) if reads else [])
    n_in, n_p, n_s, n_out = len(inputs), len(packs), len(saved), len(rows) if outs else 0

    def body(*refs):
        results_refs = refs[n_in:-2]
        kernel(
            box,
            refs[:n_p],
            refs[n_p : n_p + n_s],
            [ref.at[pl.ds(first, size)] for ref in refs[n_p + n_s : n_in]],
            results_refs[:n_out],
            results_refs[n_out:],
            refs[-2],
            refs[-1],
        )

    scratch = [
        pltpu.VMEM((3 * tall, width), BF),
        pltpu.VMEM((count * ROWS, max(box.wide, LANES)), BF),
    ]
    flops = sum(2 * 2 * tall * pack.size for pack in packs)
    results = call(body, results, *inputs, scratch=scratch, flops=flops, after=after)
    return results[:n_out], results[n_out:]


def local(tokens, norm_gain, w_gate, w_up, w_down, routes, mix_weights, cotangent):
    experts = lax.axis_size("expert") // SPLIT
    n, width = tokens.shape[1:]
    capacity = n // experts + max(1, n // (16 * experts))
    box = Box(capacity, width)
    gain = norm_gain
    gate_w, up_w, down_w = w_gate[0, 0].T, w_up[0, 0].T, w_down[0, 0]
    boxed = jax.ShapeDtypeStruct((ROWS, box.lanes), BF)
    picked = pltpu.VMEM((n, width), F32)
    bind = functools.partial

    def joined(arrays):
        return arrays[0] if len(arrays) == 1 else jnp.concatenate(arrays, axis=0)

    fence = lax.optimization_barrier

    def crossing_of(boxes):
        return joined([shift(boxes[j - 1], experts=j) for j in range(1, experts)])

    def around(boxes):
        return [shift(boxes, flip=2), boxes, shift(boxes, flip=1)]

    def add(*values):
        return sum(v.astype(F32) for v in values).astype(BF)

    def sums(parts):
        return add(parts[1], shift(parts[0], flip=2), shift(parts[2], flip=1))

    def home(total, sections):
        return [
            shift(total[(j - 1) * ROWS : j * ROWS], sections=sections, experts=-j)
            for j in range(1, experts)
        ]

    def own_home(parts, sections):
        return [
            shift(parts[0], sections=sections, flip=2),
            shift(parts[2], sections=sections, flip=1),
            shift(parts[1], sections=sections),
        ]

    def give_back(cross, own, sections, others=()):
        total = sums(cross)
        back = home(total, sections)
        own, _, others = fence((own, total, others))
        return back + own_home(own, sections), others

    units = w_gate.shape[3]
    cut = -(-units * 7 // 12 // ROWS) * ROWS
    top = jnp.concatenate([gate_w[:cut], up_w[:cut], down_w[:cut]], axis=0)
    bottom = jnp.concatenate([gate_w[cut:], up_w[cut:], down_w[cut:]], axis=0)
    packs = [top, shift(top, flip=1), bottom, shift(bottom, flip=2)]

    def rows_of(count):
        return jax.ShapeDtypeStruct((count, width), BF)

    both = jax.ShapeDtypeStruct((2 * ROWS, box.lanes), BF)
    ahead, notes0, notes1, own_tok, own_cot, *crossing = call(
        bind(start_kernel, box, experts),
        [rows_of(n + ROWS), rows_of(ROWS), rows_of(ROWS), boxed, boxed] + [both] * (experts - 1),
        tokens[0],
        cotangent[0],
        gain,
        routes[0, :, :, 0],
        mix_weights[0, :, :, 0],
        after=[top, bottom],
    )
    crossed = [shift(crossing[j - 1], experts=j) for j in range(1, experts)]
    own0 = around(own_tok)
    packs, crossed, own0 = fence((packs, crossed, own0))
    cross0 = around(joined([c[:ROWS] for c in crossed]))
    cots = joined([own_cot] + [c[ROWS:] for c in crossed])
    cross0, cots = fence((cross0, cots))
    cots = around(cots)

    cross_out, cross_kept0 = expert_call(forward_kernel, box, packs, cross0, kept=2)
    own_out, own_kept0 = expert_call(
        forward_kernel, box, packs, own0, kept=2, after=cross_out[:1]
    )
    cross_out, ahead = fence((cross_out, ahead))
    arrived0 = shift(ahead, sections=1)
    got, cots = give_back(cross_out, own_out, 1, cots)
    h1, behind, own1, *boxes1 = call(
        bind(middle_kernel, box, experts),
        [rows_of(n), rows_of(2 * n + ROWS)] + [boxed] * experts,
        arrived0,
        cotangent[0],
        notes1,
        gain,
        *got,
        scratch=[picked],
    )
    cross1, own_z, own_x = fence(
        (crossing_of(boxes1), shift(own1, flip=2), shift(own1, flip=1))
    )
    cross1, own1 = around(cross1), [own_z, own1, own_x]
    inner = bind(expert_call, inner_kernel, box, packs, cots, outs=False, kept=1)
    own_di = inner(window=(0, ROWS))[1]
    cross_di = inner(window=(ROWS, (experts - 1) * ROWS))[1]

    gate_back = bind(expert_call, gate_back_kernel, box, packs, kept=2)
    own_grad, own_kept1 = gate_back(own1, own_di)
    cross_grad, cross_kept1 = gate_back(cross1, cross_di, after=own_grad[:1])
    down = bind(expert_call, down_kernel, box, packs, reads=False)
    cross_fin = down(cross1, cross_kept1)[0]
    arrived1 = shift(behind, sections=-1)
    got, _ = give_back(cross_grad, own_grad, -1)
    got[: experts - 1], fin_sums = fence((got[: experts - 1], sums(cross_fin)))
    fin_back = home(fin_sums, 0)
    own_fin = down(own1, own_kept1)[0]
    g1, own_g, *boxes_g = call(
        bind(turn_kernel, box, experts),
        [rows_of(n)] + [boxed] * experts,
        arrived1,
        notes0,
        *got,
        scratch=[picked],
    )

    cross_g, own_z, own_x, fin_back = fence(
        (crossing_of(boxes_g), shift(own_g, flip=2), shift(own_g, flip=1), fin_back)
    )
    cross_g, own_g = around(cross_g), [own_z, own_g, own_x]
    back = bind(expert_call, back_kernel, box, packs)
    own_grad = back(own_g, own_kept0)[0]
    cross_grad = back(cross_g, cross_kept0, after=own_grad[:1])[0]
    total = sums(cross_grad)
    own_grad, own_fin, _ = fence((own_grad, own_fin, total))
    got = [array.astype(F32) for array in home(total, 0)] + own_home(own_grad, 0)
    fin_own = own_home(own_fin, 0)
    (g0,) = call(
        bind(last_kernel, box, experts),
        [rows_of(n)],
        g1,
        tokens[0],
        notes0,
        gain,
        *got,
        scratch=[picked],
    )
    (final,) = call(
        bind(final_kernel, box, experts),
        [rows_of(n)],
        h1,
        notes1,
        *fin_back,
        *fin_own,
        scratch=[picked],
    )
    return (final[None], g0[None])


def solution(mesh):
    in_specs = (
        P("section", "expert", None),
        P("section", None),
        P("section", "expert", None, None),
        P("section", "expert", None, None),
        P("section", "expert", None, None),
        P("section", None, "expert", None),
        P("section", None, "expert", None),
        P("section", "expert", None),
    )
    out_specs = (P("section", "expert", None), P("section", "expert", None))
    return jax.shard_map(local, mesh=mesh, in_specs=in_specs, out_specs=out_specs, check_vma=False)
```

```python
import functools

import jax
import jax.numpy as jnp
from jax import lax
from jax.experimental import pallas as pl
from jax.experimental.pallas import tpu as pltpu
from jax.sharding import PartitionSpec as P

SPLIT = 4
EPSILON = 1e-06
BF = jnp.bfloat16
F32 = jnp.float32
ROWS = 16
LANES = 128


def dot(left, right, dims=((1,), (0,))):
    return lax.dot_general(left, right, (dims, ((), ())), preferred_element_type=F32)


NT = ((1,), (1,))


def iota(shape, axis):
    return lax.broadcasted_iota(jnp.int32, shape, axis)


class Box:
    def __init__(self, capacity, width):
        self.capacity, self.width = capacity, width
        self.groups, self.extra = capacity // ROWS, capacity % ROWS
        self.cuts = ROWS // self.extra if self.extra else 1
        self.wide = -(-width // (LANES * self.cuts)) * LANES if self.extra else 0
        self.lanes = self.groups * width + self.wide
        self.pieces = -(-width // self.wide) if self.extra else 0

    def group(self, g):
        return pl.ds(g * self.width, self.width)

    def tail(self):
        return pl.ds(self.groups * self.width, self.wide)

    def piece(self, i):
        return i * self.wide, min(self.wide, self.width - i * self.wide)


def shift(value, sections=0, experts=0, flip=0):
    n_sec, n_own = lax.axis_size("section"), lax.axis_size("expert")
    n_exp = n_own // SPLIT
    if sections % n_sec == 0 and experts % n_exp == 0 and flip == 0:
        return value
    pairs = []
    for sec in range(n_sec):
        for own in range(n_own):
            exp, sl = own // SPLIT, own % SPLIT
            to = ((exp + experts) % n_exp) * SPLIT + (sl ^ flip)
            pairs.append((sec * n_own + own, ((sec + sections) % n_sec) * n_own + to))
    return lax.ppermute(value, ("section", "expert"), pairs)


def call(body, outs, *operands, scratch=(), flops=0, after=()):
    moved = sum(a.size * a.dtype.itemsize for a in operands)
    moved += sum(o.size * o.dtype.itemsize for o in outs)
    vmem = pl.BlockSpec(memory_space=pltpu.VMEM)
    read = len(operands)

    def reading(*refs):
        body(*refs[:read], *refs[read + len(after) :])

    return pl.pallas_call(
        reading,
        out_shape=list(outs),
        in_specs=[vmem] * read + [pl.BlockSpec(memory_space=pl.ANY)] * len(after),
        out_specs=[vmem] * len(outs),
        scratch_shapes=list(scratch),
        compiler_params=pltpu.CompilerParams(vmem_limit_bytes=40 * 2**20),
        cost_estimate=pl.CostEstimate(flops=flops, bytes_accessed=moved, transcendentals=0),
    )(*operands, *after)


def column_of(row):
    n = row.shape[1]
    eye = iota((n, n), 0) == iota((n, n), 1)
    return jnp.sum(jnp.where(eye, row, 0.0), axis=1, keepdims=True)


def slots_of(rel, experts, capacity):
    n = rel.shape[1]
    same = jnp.broadcast_to(column_of(rel), (n, n)) == jnp.broadcast_to(rel, (n, n))
    before = iota((n, n), 0) < iota((n, n), 1)
    rank = jnp.sum(jnp.where(same & before, 1.0, 0.0), axis=0, keepdims=True)
    return rel * capacity + rank


def terms(value):
    high = value.astype(BF).astype(F32)
    middle = (value - high).astype(BF).astype(F32)
    return high, middle, value - high - middle


def notes_of(slots, mix, gain, n, width):
    r = iota((ROWS, n), 0)
    left = jnp.where(r == 0, slots, 0.0)
    for at, term in enumerate(terms(mix)):
        left = jnp.where(r == 1 + at, term, left)
    r = iota((ROWS, width), 0)
    wide = jnp.concatenate([left, jnp.zeros((ROWS, width - n), F32)], axis=1)
    for at, term in enumerate(terms(gain)):
        wide = jnp.where(r == 4 + at, term, wide)
    return wide.astype(BF)


def slots_in(notes, n):
    return notes[:, :n].astype(F32)[0:1]


def mix_in(notes, n):
    left = notes[:, :n].astype(F32)
    return column_of(left[1:2] + left[2:3] + left[3:4])


def gain_in(notes):
    wide = notes.astype(F32)
    return wide[4:5] + wide[5:6] + wide[6:7]


def pack_rows(box, slots, values, out_refs):
    n = values.shape[0]
    line = jnp.broadcast_to(slots.astype(jnp.int32), (ROWS, n))
    r = iota((ROWS, n), 0)
    for j, out in enumerate(out_refs):
        first = j * box.capacity
        for g in range(box.groups):
            sel = jnp.where(line == first + g * ROWS + r, 1.0, 0.0).astype(BF)
            out[:, box.group(g)] = dot(sel, values).astype(BF)
        if box.extra:
            total = jnp.zeros((ROWS, box.wide), F32)
            for i in range(box.pieces):
                at, size = box.piece(i)
                hit = (line == first + box.groups * ROWS + r // box.cuts) & (r % box.cuts == i)
                hit &= r // box.cuts < box.extra
                got = dot(jnp.where(hit, 1.0, 0.0).astype(BF), values[:, at : at + size])
                if size < box.wide:
                    got = jnp.concatenate([got, jnp.zeros((ROWS, box.wide - size), F32)], axis=1)
                total = total + got
            out[:, box.tail()] = total.astype(BF)


def pick_rows(box, slots, boxes, n, picked):
    count = len(boxes)
    slots = column_of(slots)
    if box.groups:
        stack = jnp.concatenate(
            [b[:, g * box.width : (g + 1) * box.width] for b in boxes for g in range(box.groups)],
            axis=0,
        )
        tall = count * box.groups * ROWS
        c = iota((n, tall), 1)
        slot = c // (box.groups * ROWS) * box.capacity + c % (box.groups * ROWS)
        sel = jnp.where(slots.astype(jnp.int32) == slot, 1.0, 0.0).astype(BF)
        picked[...] = dot(sel, stack)
    else:
        picked[...] = jnp.zeros(picked.shape, F32)
    if box.extra:
        tails = jnp.concatenate([b[:, box.groups * box.width :] for b in boxes], axis=0)
        c = iota((n, count * ROWS), 1)
        r = c % ROWS
        slot = c // ROWS * box.capacity + box.groups * ROWS + r // box.cuts
        mine = (slots.astype(jnp.int32) == slot) & (r // box.cuts < box.extra)
        for i in range(box.pieces):
            at, size = box.piece(i)
            sel = jnp.where(mine & (r % box.cuts == i), 1.0, 0.0).astype(BF)
            picked[:, at : at + size] += dot(sel, tails[:, :size])


def heights(box, count):
    extra = -(-count * box.extra // ROWS) * ROWS
    return count * box.groups * ROWS, extra


def unpack(box, refs, stack, tails, at=0):
    count = 0
    for ref in refs:
        for p in range(ref.shape[0] // ROWS):
            for g in range(box.groups):
                stack[at : at + ROWS, :] = ref[p * ROWS : (p + 1) * ROWS, box.group(g)]
                at += ROWS
            if box.extra:
                tails[count * ROWS : (count + 1) * ROWS, :] = ref[
                    p * ROWS : (p + 1) * ROWS, box.tail()
                ]
            count += 1
    if box.extra:
        extra = heights(box, count)[1]
        r = iota((extra, count * ROWS), 0)
        c = iota((extra, count * ROWS), 1)
        mine = (r // box.extra == c // ROWS) & (r % box.extra == c % ROWS // box.cuts)
        for i in range(box.pieces):
            start, size = box.piece(i)
            sel = jnp.where(mine & (c % ROWS % box.cuts == i), 1.0, 0.0).astype(BF)
            stack[at : at + extra, start : start + size] = dot(sel, tails[:, :size]).astype(BF)


def repack(box, rows, refs):
    rows = rows.astype(BF)
    at = 0
    count = 0
    for ref in refs:
        for p in range(ref.shape[0] // ROWS):
            for g in range(box.groups):
                ref[p * ROWS : (p + 1) * ROWS, box.group(g)] = rows[at : at + ROWS]
                at += ROWS
            count += 1
    if box.extra:
        extra = heights(box, count)[1]
        r = iota((count * ROWS, extra), 0)
        c = iota((count * ROWS, extra), 1)
        mine = (c // box.extra == r // ROWS) & (c % box.extra == r % ROWS // box.cuts)
        total = jnp.zeros((count * ROWS, box.wide), F32)
        for i in range(box.pieces):
            start, size = box.piece(i)
            sel = jnp.where(mine & (r % ROWS % box.cuts == i), 1.0, 0.0).astype(BF)
            got = dot(sel, rows[at:, start : start + size])
            if size < box.wide:
                pad = jnp.zeros((count * ROWS, box.wide - size), F32)
                got = jnp.concatenate([got, pad], axis=1)
            total = total + got
        total = total.astype(BF)
        count = 0
        for ref in refs:
            tall = ref.shape[0]
            ref[:, box.tail()] = total[count : count + tall]
            count += tall


def inv_rms(wide):
    return lax.rsqrt(jnp.mean(wide * wide, axis=-1, keepdims=True) + EPSILON)


def total_of(refs):
    return sum(ref[...].astype(F32) for ref in refs).astype(BF)


def start_kernel(box, experts, tokens, cot, gain, ids, mix, ahead, notes0, notes1, *boxes):
    n, width = tokens.shape
    mine = lax.axis_index("expert") // SPLIT
    for k, notes in enumerate((notes0, notes1)):
        rel = ids[k : k + 1, :] - mine
        rel = jnp.where(rel < 0, rel + experts, rel).astype(F32)
        slots = slots_of(rel, experts, box.capacity)
        notes[...] = notes_of(slots, mix[k : k + 1, :], gain[...], n, width)
    ahead[:n] = tokens[...]
    ahead[n:] = notes0[...]
    wide = tokens[...].astype(F32)
    normed = (wide * inv_rms(wide) * gain[...]).astype(BF)
    crossing = boxes[2:]
    firsts = [boxes[0]] + [ref.at[:ROWS] for ref in crossing]
    pack_rows(box, slots_in(notes0[...], n), normed, firsts)
    seconds = [boxes[1]] + [ref.at[ROWS:] for ref in crossing]
    pack_rows(box, slots_in(notes1[...], n), cot[...], seconds)


def combine(box, notes, n, own, back, picked):
    sums = [total_of(own)] + [ref[...].astype(BF) for ref in back]
    pick_rows(box, slots_in(notes, n), sums, n, picked)
    return mix_in(notes, n) * picked[...]


def split_refs(refs, experts, outs):
    ins = refs[:-outs]
    return ins[experts - 1 :], ins[: experts - 1], refs[-outs:]


def middle_kernel(box, experts, arrived, cot, notes1, gain, *refs):
    boxes, picked = refs[-1 - experts : -1], refs[-1]
    own, back, (after, behind) = split_refs(refs[: -1 - experts], experts, 2)
    n = cot.shape[0]
    update = combine(box, arrived[n:], n, own, back, picked)
    later = (arrived[:n].astype(F32) + update).astype(BF)
    after[...] = later
    behind[:n] = later
    behind[n : 2 * n] = cot[...]
    behind[2 * n :] = notes1[...]
    wide = later.astype(F32)
    normed = (wide * inv_rms(wide) * gain[...]).astype(BF)
    pack_rows(box, slots_in(notes1[...], n), normed, boxes)


def final_kernel(box, experts, hidden, notes, *refs):
    picked = refs[-1]
    own, back, (out,) = split_refs(refs[:-1], experts, 1)
    n = hidden.shape[0]
    update = combine(box, notes[...], n, own, back, picked)
    out[...] = (hidden[...].astype(F32) + update).astype(BF)


def norm_back(hidden, gain, grad):
    wide = hidden.astype(F32)
    inv = inv_rms(wide)
    scaled = grad * gain
    along = jnp.mean(scaled * wide, axis=-1, keepdims=True)
    return inv * scaled - wide * (inv * inv * inv * along)


def turn_kernel(box, experts, arrived, notes0, *refs):
    boxes, picked = refs[-1 - experts : -1], refs[-1]
    own, back, (out,) = split_refs(refs[: -1 - experts], experts, 1)
    n = out.shape[0]
    notes = arrived[2 * n :]
    d_normed = combine(box, notes, n, own, back, picked)
    change = norm_back(arrived[:n], gain_in(notes), d_normed)
    now = (arrived[n : 2 * n].astype(F32) + change).astype(BF)
    out[...] = now
    pack_rows(box, slots_in(notes0[...], n), now, boxes)


def last_kernel(box, experts, grad, hidden, notes0, gain, *refs):
    picked = refs[-1]
    own, back, (out,) = split_refs(refs[:-1], experts, 1)
    n = hidden.shape[0]
    d_normed = combine(box, notes0[...], n, own, back, picked)
    change = norm_back(hidden[...], gain[...], d_normed)
    out[...] = (grad[...].astype(F32) + change).astype(BF)


def spans(tall):
    return pl.ds(0, 2 * tall), pl.ds(tall, 2 * tall)


def gate_up(rows, pack):
    return dot(rows, pack[: 2 * (pack.shape[0] // 3)], NT)


def parts_of(both):
    units = both.shape[1] // 2
    return both[:, :units], both[:, units:]


def down_rows(both, pack):
    g, u = parts_of(both)
    return dot((jax.nn.silu(g) * u).astype(BF), pack[2 * g.shape[1] :])


def inner_of(rows, pack):
    return dot(rows, pack[2 * (pack.shape[0] // 3) :], NT)


def part_rows(d_inner, both, pack):
    g, u = parts_of(both)
    r = jax.nn.sigmoid(g)
    d_gate = d_inner * u * r * (1.0 + g * (1.0 - r))
    d_up = d_inner * g * r
    return dot(jnp.concatenate([d_gate, d_up], axis=1).astype(BF), pack[: both.shape[1]])


def read_rows(box, rows, stack, tails):
    tall = stack.shape[0] // 3
    for at, ref in enumerate(rows):
        unpack(box, [ref], stack, tails, at * tall)
    return [stack[span, :] for span in spans(tall)]


def write_rows(box, top, bottom, outs):
    tall = top.shape[0] // 2
    for ref, value in zip(outs, (top[:tall], top[tall:] + bottom[:tall], bottom[tall:])):
        repack(box, value, [ref])


def forward_kernel(box, packs, saved, rows, outs, kept, stack, tails):
    sides = read_rows(box, rows, stack, tails)
    total = []
    for side, values in enumerate(sides):
        total.append(0.0)
        for at in (2 * side, 2 * side + 1):
            both = gate_up(values, packs[at])
            kept[at][...] = both
            total[side] = total[side] + down_rows(both, packs[at])
    write_rows(box, *total, outs)


def inner_kernel(box, packs, saved, rows, outs, kept, stack, tails):
    for side, values in enumerate(read_rows(box, rows, stack, tails)):
        for at in (2 * side, 2 * side + 1):
            kept[at][...] = inner_of(values, packs[at])


def gate_back_kernel(box, packs, saved, rows, outs, kept, stack, tails):
    sides = read_rows(box, rows, stack, tails)
    total = []
    for side, values in enumerate(sides):
        total.append(0.0)
        for at in (2 * side, 2 * side + 1):
            both = gate_up(values, packs[at])
            kept[at][...] = both
            total[side] = total[side] + part_rows(saved[at][...], both, packs[at])
    write_rows(box, *total, outs)


def back_kernel(box, packs, saved, rows, outs, kept, stack, tails):
    sides = read_rows(box, rows, stack, tails)
    total = []
    for side, values in enumerate(sides):
        total.append(0.0)
        for at in (2 * side, 2 * side + 1):
            d_inner = inner_of(values, packs[at])
            total[side] = total[side] + part_rows(d_inner, saved[at][...], packs[at])
    write_rows(box, *total, outs)


def down_kernel(box, packs, saved, rows, outs, kept, stack, tails):
    total = []
    for side in range(2):
        at = 2 * side
        total.append(sum(down_rows(saved[i][...], packs[i]) for i in (at, at + 1)))
    write_rows(box, *total, outs)


def expert_call(kernel, box, packs, rows, saved=(), outs=True, kept=0, reads=True, after=(), window=None):
    width = packs[0].shape[1]
    first, size = window or (0, rows[0].shape[0])
    count = size // ROWS
    tall = sum(heights(box, count))
    boxes = jax.ShapeDtypeStruct((count * ROWS, box.lanes), BF)
    results = [boxes] * len(rows) if outs else []
    if kept:
        units = [pack.shape[0] // 3 for pack in packs]
        results += [jax.ShapeDtypeStruct((2 * tall, kept * u), F32) for u in units]
    inputs = list(packs) + list(saved) + (list(rows) if reads else [])
    n_in, n_p, n_s, n_out = len(inputs), len(packs), len(saved), len(rows) if outs else 0

    def body(*refs):
        results_refs = refs[n_in:-2]
        kernel(
            box,
            refs[:n_p],
            refs[n_p : n_p + n_s],
            [ref.at[pl.ds(first, size)] for ref in refs[n_p + n_s : n_in]],
            results_refs[:n_out],
            results_refs[n_out:],
            refs[-2],
            refs[-1],
        )

    scratch = [
        pltpu.VMEM((3 * tall, width), BF),
        pltpu.VMEM((count * ROWS, max(box.wide, LANES)), BF),
    ]
    flops = sum(2 * 2 * tall * pack.size for pack in packs)
    results = call(body, results, *inputs, scratch=scratch, flops=flops, after=after)
    return results[:n_out], results[n_out:]


def local(tokens, norm_gain, w_gate, w_up, w_down, routes, mix_weights, cotangent):
    experts = lax.axis_size("expert") // SPLIT
    n, width = tokens.shape[1:]
    capacity = n // experts + max(1, n // (16 * experts))
    box = Box(capacity, width)
    gain = norm_gain
    gate_w, up_w, down_w = w_gate[0, 0].T, w_up[0, 0].T, w_down[0, 0]
    boxed = jax.ShapeDtypeStruct((ROWS, box.lanes), BF)
    picked = pltpu.VMEM((n, width), F32)
    bind = functools.partial

    def joined(arrays):
        return arrays[0] if len(arrays) == 1 else jnp.concatenate(arrays, axis=0)

    fence = lax.optimization_barrier

    def crossing_of(boxes):
        return joined([shift(boxes[j - 1], experts=j) for j in range(1, experts)])

    def around(boxes):
        return [shift(boxes, flip=2), boxes, shift(boxes, flip=1)]

    def add(*values):
        return sum(v.astype(F32) for v in values).astype(BF)

    def sums(parts):
        return add(parts[1], shift(parts[0], flip=2), shift(parts[2], flip=1))

    def home(total, sections):
        return [
            shift(total[(j - 1) * ROWS : j * ROWS], sections=sections, experts=-j)
            for j in range(1, experts)
        ]

    def own_home(parts, sections):
        return [
            shift(parts[0], sections=sections, flip=2),
            shift(parts[2], sections=sections, flip=1),
            shift(parts[1], sections=sections),
        ]

    def give_back(cross, own, sections, others=()):
        total = sums(cross)
        back = home(total, sections)
        own, _, others = fence((own, total, others))
        return back + own_home(own, sections), others

    units = w_gate.shape[3]
    cut = -(-units * 7 // 12 // ROWS) * ROWS
    top = jnp.concatenate([gate_w[:cut], up_w[:cut], down_w[:cut]], axis=0)
    bottom = jnp.concatenate([gate_w[cut:], up_w[cut:], down_w[cut:]], axis=0)
    packs = [top, shift(top, flip=1), bottom, shift(bottom, flip=2)]

    def rows_of(count):
        return jax.ShapeDtypeStruct((count, width), BF)

    both = jax.ShapeDtypeStruct((2 * ROWS, box.lanes), BF)
    ahead, notes0, notes1, own_tok, own_cot, *crossing = call(
        bind(start_kernel, box, experts),
        [rows_of(n + ROWS), rows_of(ROWS), rows_of(ROWS), boxed, boxed] + [both] * (experts - 1),
        tokens[0],
        cotangent[0],
        gain,
        routes[0, :, :, 0],
        mix_weights[0, :, :, 0],
        after=[top, bottom],
    )
    crossed = [shift(crossing[j - 1], experts=j) for j in range(1, experts)]
    own0 = around(own_tok)
    packs, crossed, own0 = fence((packs, crossed, own0))
    cross0 = around(joined([c[:ROWS] for c in crossed]))
    cots = joined([own_cot] + [c[ROWS:] for c in crossed])
    cross0, cots = fence((cross0, cots))
    cots = around(cots)

    cross_out, cross_kept0 = expert_call(forward_kernel, box, packs, cross0, kept=2)
    own_out, own_kept0 = expert_call(
        forward_kernel, box, packs, own0, kept=2, after=cross_out[:1]
    )
    cross_out, ahead = fence((cross_out, ahead))
    arrived0 = shift(ahead, sections=1)
    got, cots = give_back(cross_out, own_out, 1, cots)
    h1, behind, own1, *boxes1 = call(
        bind(middle_kernel, box, experts),
        [rows_of(n), rows_of(2 * n + ROWS)] + [boxed] * experts,
        arrived0,
        cotangent[0],
        notes1,
        gain,
        *got,
        scratch=[picked],
    )
    cross1, own_z, own_x = fence(
        (crossing_of(boxes1), shift(own1, flip=2), shift(own1, flip=1))
    )
    cross1, own1 = around(cross1), [own_z, own1, own_x]
    inner = bind(expert_call, inner_kernel, box, packs, cots, outs=False, kept=1)
    own_di = inner(window=(0, ROWS))[1]
    cross_di = inner(window=(ROWS, (experts - 1) * ROWS))[1]

    gate_back = bind(expert_call, gate_back_kernel, box, packs, kept=2)
    own_grad, own_kept1 = gate_back(own1, own_di)
    cross_grad, cross_kept1 = gate_back(cross1, cross_di, after=own_grad[:1])
    down = bind(expert_call, down_kernel, box, packs, reads=False)
    cross_fin = down(cross1, cross_kept1)[0]
    arrived1 = shift(behind, sections=-1)
    got, _ = give_back(cross_grad, own_grad, -1)
    got[: experts - 1], fin_sums = fence((got[: experts - 1], sums(cross_fin)))
    own_fin = down(own1, own_kept1)[0]
    g1, own_g, *boxes_g = call(
        bind(turn_kernel, box, experts),
        [rows_of(n)] + [boxed] * experts,
        arrived1,
        notes0,
        *got,
        scratch=[picked],
    )

    cross_g, own_z, own_x = fence(
        (crossing_of(boxes_g), shift(own_g, flip=2), shift(own_g, flip=1))
    )
    cross_g, own_g = around(cross_g), [own_z, own_g, own_x]
    back = bind(expert_call, back_kernel, box, packs)
    own_grad = back(own_g, own_kept0)[0]
    cross_grad = back(cross_g, cross_kept0, after=own_grad[:1])[0]
    total = sums(cross_grad)
    own_grad, own_fin, fin_sums, _ = fence((own_grad, own_fin, fin_sums, total))
    got = [array.astype(F32) for array in home(total, 0)] + own_home(own_grad, 0)
    fin_back = [array.astype(F32) for array in home(fin_sums, 0)]
    fin_own = own_home(own_fin, 0)
    (g0,) = call(
        bind(last_kernel, box, experts),
        [rows_of(n)],
        g1,
        tokens[0],
        notes0,
        gain,
        *got,
        scratch=[picked],
    )
    (final,) = call(
        bind(final_kernel, box, experts),
        [rows_of(n)],
        h1,
        notes1,
        *fin_back,
        *fin_own,
        scratch=[picked],
        after=[g0],
    )
    return (final[None], g0[None])


def solution(mesh):
    in_specs = (
        P("section", "expert", None),
        P("section", None),
        P("section", "expert", None, None),
        P("section", "expert", None, None),
        P("section", "expert", None, None),
        P("section", None, "expert", None),
        P("section", None, "expert", None),
        P("section", "expert", None),
    )
    out_specs = (P("section", "expert", None), P("section", "expert", None))
    return jax.shard_map(local, mesh=mesh, in_specs=in_specs, out_specs=out_specs, check_vma=False)
```

```python
import functools

import jax
import jax.numpy as jnp
from jax import lax
from jax.experimental import pallas as pl
from jax.experimental.pallas import tpu as pltpu
from jax.sharding import PartitionSpec as P

SPLIT = 4
EPSILON = 1e-06
BF = jnp.bfloat16
F32 = jnp.float32
ROWS = 16
LANES = 128


def dot(left, right, dims=((1,), (0,))):
    return lax.dot_general(left, right, (dims, ((), ())), preferred_element_type=F32)


NT = ((1,), (1,))


def iota(shape, axis):
    return lax.broadcasted_iota(jnp.int32, shape, axis)


class Box:
    def __init__(self, capacity, width):
        self.capacity, self.width = capacity, width
        self.groups, self.extra = capacity // ROWS, capacity % ROWS
        self.cuts = ROWS // self.extra if self.extra else 1
        self.wide = -(-width // (LANES * self.cuts)) * LANES if self.extra else 0
        self.lanes = self.groups * width + self.wide
        self.pieces = -(-width // self.wide) if self.extra else 0

    def group(self, g):
        return pl.ds(g * self.width, self.width)

    def tail(self):
        return pl.ds(self.groups * self.width, self.wide)

    def piece(self, i):
        return i * self.wide, min(self.wide, self.width - i * self.wide)


def shift(value, sections=0, experts=0, flip=0):
    n_sec, n_own = lax.axis_size("section"), lax.axis_size("expert")
    n_exp = n_own // SPLIT
    if sections % n_sec == 0 and experts % n_exp == 0 and flip == 0:
        return value
    pairs = []
    for sec in range(n_sec):
        for own in range(n_own):
            exp, sl = own // SPLIT, own % SPLIT
            to = ((exp + experts) % n_exp) * SPLIT + (sl ^ flip)
            pairs.append((sec * n_own + own, ((sec + sections) % n_sec) * n_own + to))
    return lax.ppermute(value, ("section", "expert"), pairs)


def call(body, outs, *operands, scratch=(), flops=0, after=()):
    moved = sum(a.size * a.dtype.itemsize for a in operands)
    moved += sum(o.size * o.dtype.itemsize for o in outs)
    vmem = pl.BlockSpec(memory_space=pltpu.VMEM)
    read = len(operands)

    def reading(*refs):
        body(*refs[:read], *refs[read + len(after) :])

    return pl.pallas_call(
        reading,
        out_shape=list(outs),
        in_specs=[vmem] * read + [pl.BlockSpec(memory_space=pl.ANY)] * len(after),
        out_specs=[vmem] * len(outs),
        scratch_shapes=list(scratch),
        compiler_params=pltpu.CompilerParams(vmem_limit_bytes=40 * 2**20),
        cost_estimate=pl.CostEstimate(flops=flops, bytes_accessed=moved, transcendentals=0),
    )(*operands, *after)


def column_of(row):
    n = row.shape[1]
    eye = iota((n, n), 0) == iota((n, n), 1)
    return jnp.sum(jnp.where(eye, row, 0.0), axis=1, keepdims=True)


def slots_of(rel, experts, capacity):
    n = rel.shape[1]
    same = jnp.broadcast_to(column_of(rel), (n, n)) == jnp.broadcast_to(rel, (n, n))
    before = iota((n, n), 0) < iota((n, n), 1)
    rank = jnp.sum(jnp.where(same & before, 1.0, 0.0), axis=0, keepdims=True)
    return rel * capacity + rank


def terms(value):
    high = value.astype(BF).astype(F32)
    middle = (value - high).astype(BF).astype(F32)
    return high, middle, value - high - middle


def notes_of(slots, mix, gain, n, width):
    r = iota((ROWS, n), 0)
    left = jnp.where(r == 0, slots, 0.0)
    for at, term in enumerate(terms(mix)):
        left = jnp.where(r == 1 + at, term, left)
    r = iota((ROWS, width), 0)
    wide = jnp.concatenate([left, jnp.zeros((ROWS, width - n), F32)], axis=1)
    for at, term in enumerate(terms(gain)):
        wide = jnp.where(r == 4 + at, term, wide)
    return wide.astype(BF)


def slots_in(notes, n):
    return notes[:, :n].astype(F32)[0:1]


def mix_in(notes, n):
    left = notes[:, :n].astype(F32)
    return column_of(left[1:2] + left[2:3] + left[3:4])


def gain_in(notes):
    wide = notes.astype(F32)
    return wide[4:5] + wide[5:6] + wide[6:7]


def pack_rows(box, slots, values, out_refs):
    n = values.shape[0]
    line = jnp.broadcast_to(slots.astype(jnp.int32), (ROWS, n))
    r = iota((ROWS, n), 0)
    for j, out in enumerate(out_refs):
        first = j * box.capacity
        for g in range(box.groups):
            sel = jnp.where(line == first + g * ROWS + r, 1.0, 0.0).astype(BF)
            out[:, box.group(g)] = dot(sel, values).astype(BF)
        if box.extra:
            total = jnp.zeros((ROWS, box.wide), F32)
            for i in range(box.pieces):
                at, size = box.piece(i)
                hit = (line == first + box.groups * ROWS + r // box.cuts) & (r % box.cuts == i)
                hit &= r // box.cuts < box.extra
                got = dot(jnp.where(hit, 1.0, 0.0).astype(BF), values[:, at : at + size])
                if size < box.wide:
                    got = jnp.concatenate([got, jnp.zeros((ROWS, box.wide - size), F32)], axis=1)
                total = total + got
            out[:, box.tail()] = total.astype(BF)


def pick_rows(box, slots, boxes, n, picked):
    count = len(boxes)
    slots = column_of(slots)
    if box.groups:
        stack = jnp.concatenate(
            [b[:, g * box.width : (g + 1) * box.width] for b in boxes for g in range(box.groups)],
            axis=0,
        )
        tall = count * box.groups * ROWS
        c = iota((n, tall), 1)
        slot = c // (box.groups * ROWS) * box.capacity + c % (box.groups * ROWS)
        sel = jnp.where(slots.astype(jnp.int32) == slot, 1.0, 0.0).astype(BF)
        picked[...] = dot(sel, stack)
    else:
        picked[...] = jnp.zeros(picked.shape, F32)
    if box.extra:
        tails = jnp.concatenate([b[:, box.groups * box.width :] for b in boxes], axis=0)
        c = iota((n, count * ROWS), 1)
        r = c % ROWS
        slot = c // ROWS * box.capacity + box.groups * ROWS + r // box.cuts
        mine = (slots.astype(jnp.int32) == slot) & (r // box.cuts < box.extra)
        for i in range(box.pieces):
            at, size = box.piece(i)
            sel = jnp.where(mine & (r % box.cuts == i), 1.0, 0.0).astype(BF)
            picked[:, at : at + size] += dot(sel, tails[:, :size])


def heights(box, count):
    extra = -(-count * box.extra // ROWS) * ROWS
    return count * box.groups * ROWS, extra


def unpack(box, refs, stack, tails, at=0):
    count = 0
    for ref in refs:
        for p in range(ref.shape[0] // ROWS):
            for g in range(box.groups):
                stack[at : at + ROWS, :] = ref[p * ROWS : (p + 1) * ROWS, box.group(g)]
                at += ROWS
            if box.extra:
                tails[count * ROWS : (count + 1) * ROWS, :] = ref[
                    p * ROWS : (p + 1) * ROWS, box.tail()
                ]
            count += 1
    if box.extra:
        extra = heights(box, count)[1]
        r = iota((extra, count * ROWS), 0)
        c = iota((extra, count * ROWS), 1)
        mine = (r // box.extra == c // ROWS) & (r % box.extra == c % ROWS // box.cuts)
        for i in range(box.pieces):
            start, size = box.piece(i)
            sel = jnp.where(mine & (c % ROWS % box.cuts == i), 1.0, 0.0).astype(BF)
            stack[at : at + extra, start : start + size] = dot(sel, tails[:, :size]).astype(BF)


def repack(box, rows, refs):
    rows = rows.astype(BF)
    at = 0
    count = 0
    for ref in refs:
        for p in range(ref.shape[0] // ROWS):
            for g in range(box.groups):
                ref[p * ROWS : (p + 1) * ROWS, box.group(g)] = rows[at : at + ROWS]
                at += ROWS
            count += 1
    if box.extra:
        extra = heights(box, count)[1]
        r = iota((count * ROWS, extra), 0)
        c = iota((count * ROWS, extra), 1)
        mine = (c // box.extra == r // ROWS) & (c % box.extra == r % ROWS // box.cuts)
        total = jnp.zeros((count * ROWS, box.wide), F32)
        for i in range(box.pieces):
            start, size = box.piece(i)
            sel = jnp.where(mine & (r % ROWS % box.cuts == i), 1.0, 0.0).astype(BF)
            got = dot(sel, rows[at:, start : start + size])
            if size < box.wide:
                pad = jnp.zeros((count * ROWS, box.wide - size), F32)
                got = jnp.concatenate([got, pad], axis=1)
            total = total + got
        total = total.astype(BF)
        count = 0
        for ref in refs:
            tall = ref.shape[0]
            ref[:, box.tail()] = total[count : count + tall]
            count += tall


def inv_rms(wide):
    return lax.rsqrt(jnp.mean(wide * wide, axis=-1, keepdims=True) + EPSILON)


def total_of(refs):
    return sum(ref[...].astype(F32) for ref in refs).astype(BF)


def start_kernel(box, experts, tokens, cot, gain, ids, mix, ahead, notes0, notes1, *boxes):
    n, width = tokens.shape
    mine = lax.axis_index("expert") // SPLIT
    for k, notes in enumerate((notes0, notes1)):
        rel = ids[k : k + 1, :] - mine
        rel = jnp.where(rel < 0, rel + experts, rel).astype(F32)
        slots = slots_of(rel, experts, box.capacity)
        notes[...] = notes_of(slots, mix[k : k + 1, :], gain[...], n, width)
    ahead[:n] = tokens[...]
    ahead[n:] = notes0[...]
    wide = tokens[...].astype(F32)
    normed = (wide * inv_rms(wide) * gain[...]).astype(BF)
    crossing = boxes[2:]
    firsts = [boxes[0]] + [ref.at[:ROWS] for ref in crossing]
    pack_rows(box, slots_in(notes0[...], n), normed, firsts)
    seconds = [boxes[1]] + [ref.at[ROWS:] for ref in crossing]
    pack_rows(box, slots_in(notes1[...], n), cot[...], seconds)


def combine(box, notes, n, own, back, picked):
    sums = [total_of(own)] + [ref[...].astype(BF) for ref in back]
    pick_rows(box, slots_in(notes, n), sums, n, picked)
    return mix_in(notes, n) * picked[...]


def split_refs(refs, experts, outs):
    ins = refs[:-outs]
    return ins[experts - 1 :], ins[: experts - 1], refs[-outs:]


def middle_kernel(box, experts, arrived, cot, notes1, gain, *refs):
    boxes, picked = refs[-1 - experts : -1], refs[-1]
    own, back, (after, behind) = split_refs(refs[: -1 - experts], experts, 2)
    n = cot.shape[0]
    update = combine(box, arrived[n:], n, own, back, picked)
    later = (arrived[:n].astype(F32) + update).astype(BF)
    after[...] = later
    behind[:n] = later
    behind[n : 2 * n] = cot[...]
    behind[2 * n :] = notes1[...]
    wide = later.astype(F32)
    normed = (wide * inv_rms(wide) * gain[...]).astype(BF)
    pack_rows(box, slots_in(notes1[...], n), normed, boxes)


def final_kernel(box, experts, hidden, notes, *refs):
    picked = refs[-1]
    own, back, (out,) = split_refs(refs[:-1], experts, 1)
    n = hidden.shape[0]
    update = combine(box, notes[...], n, own, back, picked)
    out[...] = (hidden[...].astype(F32) + update).astype(BF)


def norm_back(hidden, gain, grad):
    wide = hidden.astype(F32)
    inv = inv_rms(wide)
    scaled = grad * gain
    along = jnp.mean(scaled * wide, axis=-1, keepdims=True)
    return inv * scaled - wide * (inv * inv * inv * along)


def turn_kernel(box, experts, arrived, notes0, *refs):
    boxes, picked = refs[-1 - experts : -1], refs[-1]
    own, back, (out,) = split_refs(refs[: -1 - experts], experts, 1)
    n = out.shape[0]
    notes = arrived[2 * n :]
    d_normed = combine(box, notes, n, own, back, picked)
    change = norm_back(arrived[:n], gain_in(notes), d_normed)
    now = (arrived[n : 2 * n].astype(F32) + change).astype(BF)
    out[...] = now
    pack_rows(box, slots_in(notes0[...], n), now, boxes)


def last_kernel(box, experts, grad, hidden, notes0, gain, *refs):
    picked = refs[-1]
    own, back, (out,) = split_refs(refs[:-1], experts, 1)
    n = hidden.shape[0]
    d_normed = combine(box, notes0[...], n, own, back, picked)
    change = norm_back(hidden[...], gain[...], d_normed)
    out[...] = (grad[...].astype(F32) + change).astype(BF)


def spans(tall):
    return pl.ds(0, 2 * tall), pl.ds(tall, 2 * tall)


def gate_up(rows, pack):
    return dot(rows, pack[: 2 * (pack.shape[0] // 3)], NT)


def parts_of(both):
    units = both.shape[1] // 2
    return both[:, :units], both[:, units:]


def down_rows(both, pack):
    g, u = parts_of(both)
    return dot((jax.nn.silu(g) * u).astype(BF), pack[2 * g.shape[1] :])


def inner_of(rows, pack):
    return dot(rows, pack[2 * (pack.shape[0] // 3) :], NT)


def part_rows(d_inner, both, pack):
    g, u = parts_of(both)
    r = jax.nn.sigmoid(g)
    d_gate = d_inner * u * r * (1.0 + g * (1.0 - r))
    d_up = d_inner * g * r
    return dot(jnp.concatenate([d_gate, d_up], axis=1).astype(BF), pack[: both.shape[1]])


def read_rows(box, rows, stack, tails):
    tall = stack.shape[0] // 3
    for at, ref in enumerate(rows):
        unpack(box, [ref], stack, tails, at * tall)
    return [stack[span, :] for span in spans(tall)]


def write_rows(box, top, bottom, outs):
    tall = top.shape[0] // 2
    for ref, value in zip(outs, (top[:tall], top[tall:] + bottom[:tall], bottom[tall:])):
        repack(box, value, [ref])


def forward_kernel(box, packs, saved, rows, outs, kept, stack, tails):
    sides = read_rows(box, rows, stack, tails)
    total = []
    for side, values in enumerate(sides):
        total.append(0.0)
        for at in (2 * side, 2 * side + 1):
            both = gate_up(values, packs[at])
            kept[at][...] = both
            total[side] = total[side] + down_rows(both, packs[at])
    write_rows(box, *total, outs)


def inner_kernel(box, packs, saved, rows, outs, kept, stack, tails):
    for side, values in enumerate(read_rows(box, rows, stack, tails)):
        for at in (2 * side, 2 * side + 1):
            kept[at][...] = inner_of(values, packs[at])


def gate_back_kernel(box, packs, saved, rows, outs, kept, stack, tails):
    sides = read_rows(box, rows, stack, tails)
    total = []
    for side, values in enumerate(sides):
        total.append(0.0)
        for at in (2 * side, 2 * side + 1):
            both = gate_up(values, packs[at])
            kept[at][...] = both
            total[side] = total[side] + part_rows(saved[at][...], both, packs[at])
    write_rows(box, *total, outs)


def back_kernel(box, packs, saved, rows, outs, kept, stack, tails):
    sides = read_rows(box, rows, stack, tails)
    total = []
    for side, values in enumerate(sides):
        total.append(0.0)
        for at in (2 * side, 2 * side + 1):
            d_inner = inner_of(values, packs[at])
            total[side] = total[side] + part_rows(d_inner, saved[at][...], packs[at])
    write_rows(box, *total, outs)


def down_kernel(box, packs, saved, rows, outs, kept, stack, tails):
    total = []
    for side in range(2):
        at = 2 * side
        total.append(sum(down_rows(saved[i][...], packs[i]) for i in (at, at + 1)))
    write_rows(box, *total, outs)


def expert_call(kernel, box, packs, rows, saved=(), outs=True, kept=0, reads=True, after=(), window=None):
    width = packs[0].shape[1]
    first, size = window or (0, rows[0].shape[0])
    count = size // ROWS
    tall = sum(heights(box, count))
    boxes = jax.ShapeDtypeStruct((count * ROWS, box.lanes), BF)
    results = [boxes] * len(rows) if outs else []
    if kept:
        units = [pack.shape[0] // 3 for pack in packs]
        results += [jax.ShapeDtypeStruct((2 * tall, kept * u), F32) for u in units]
    inputs = list(packs) + list(saved) + (list(rows) if reads else [])
    n_in, n_p, n_s, n_out = len(inputs), len(packs), len(saved), len(rows) if outs else 0

    def body(*refs):
        results_refs = refs[n_in:-2]
        kernel(
            box,
            refs[:n_p],
            refs[n_p : n_p + n_s],
            [ref.at[pl.ds(first, size)] for ref in refs[n_p + n_s : n_in]],
            results_refs[:n_out],
            results_refs[n_out:],
            refs[-2],
            refs[-1],
        )

    scratch = [
        pltpu.VMEM((3 * tall, width), BF),
        pltpu.VMEM((count * ROWS, max(box.wide, LANES)), BF),
    ]
    flops = sum(2 * 2 * tall * pack.size for pack in packs)
    results = call(body, results, *inputs, scratch=scratch, flops=flops, after=after)
    return results[:n_out], results[n_out:]


def local(tokens, norm_gain, w_gate, w_up, w_down, routes, mix_weights, cotangent):
    experts = lax.axis_size("expert") // SPLIT
    n, width = tokens.shape[1:]
    capacity = n // experts + max(1, n // (16 * experts))
    box = Box(capacity, width)
    gain = norm_gain
    gate_w, up_w, down_w = w_gate[0, 0].T, w_up[0, 0].T, w_down[0, 0]
    boxed = jax.ShapeDtypeStruct((ROWS, box.lanes), BF)
    picked = pltpu.VMEM((n, width), F32)
    bind = functools.partial

    def joined(arrays):
        return arrays[0] if len(arrays) == 1 else jnp.concatenate(arrays, axis=0)

    fence = lax.optimization_barrier

    def crossing_of(boxes):
        return joined([shift(boxes[j - 1], experts=j) for j in range(1, experts)])

    def around(boxes):
        return [shift(boxes, flip=2), boxes, shift(boxes, flip=1)]

    def add(*values):
        return sum(v.astype(F32) for v in values).astype(BF)

    def sums(parts):
        return add(parts[1], shift(parts[0], flip=2), shift(parts[2], flip=1))

    def home(total, sections):
        return [
            shift(total[(j - 1) * ROWS : j * ROWS], sections=sections, experts=-j)
            for j in range(1, experts)
        ]

    def own_home(parts, sections):
        return [
            shift(parts[0], sections=sections, flip=2),
            shift(parts[2], sections=sections, flip=1),
            shift(parts[1], sections=sections),
        ]

    def give_back(cross, own, sections, others=()):
        total = sums(cross)
        back = home(total, sections)
        own, _, others = fence((own, total, others))
        return back + own_home(own, sections), others

    units = w_gate.shape[3]
    cut = -(-units * 7 // 12 // ROWS) * ROWS
    top = jnp.concatenate([gate_w[:cut], up_w[:cut], down_w[:cut]], axis=0)
    bottom = jnp.concatenate([gate_w[cut:], up_w[cut:], down_w[cut:]], axis=0)
    packs = [top, shift(top, flip=1), bottom, shift(bottom, flip=2)]

    def rows_of(count):
        return jax.ShapeDtypeStruct((count, width), BF)

    both = jax.ShapeDtypeStruct((2 * ROWS, box.lanes), BF)
    ahead, notes0, notes1, own_tok, own_cot, *crossing = call(
        bind(start_kernel, box, experts),
        [rows_of(n + ROWS), rows_of(ROWS), rows_of(ROWS), boxed, boxed] + [both] * (experts - 1),
        tokens[0],
        cotangent[0],
        gain,
        routes[0, :, :, 0],
        mix_weights[0, :, :, 0],
        after=[top, bottom],
    )
    crossed = [shift(crossing[j - 1], experts=j) for j in range(1, experts)]
    own0 = around(own_tok)
    packs, crossed, own0 = fence((packs, crossed, own0))
    cross0 = around(joined([c[:ROWS] for c in crossed]))
    cots = joined([own_cot] + [c[ROWS:] for c in crossed])
    cross0, cots = fence((cross0, cots))
    cots = around(cots)

    cross_out, cross_kept0 = expert_call(forward_kernel, box, packs, cross0, kept=2)
    own_out, own_kept0 = expert_call(
        forward_kernel, box, packs, own0, kept=2, after=cross_out[:1]
    )
    cross_out, ahead = fence((cross_out, ahead))
    arrived0 = shift(ahead, sections=1)
    got, cots = give_back(cross_out, own_out, 1, cots)
    h1, behind, own1, *boxes1 = call(
        bind(middle_kernel, box, experts),
        [rows_of(n), rows_of(2 * n + ROWS)] + [boxed] * experts,
        arrived0,
        cotangent[0],
        notes1,
        gain,
        *got,
        scratch=[picked],
    )
    cross1, own_z, own_x = fence(
        (crossing_of(boxes1), shift(own1, flip=2), shift(own1, flip=1))
    )
    cross1, own1 = around(cross1), [own_z, own1, own_x]
    inner = bind(expert_call, inner_kernel, box, packs, cots, outs=False, kept=1)
    own_di = inner(window=(0, ROWS))[1]
    cross_di = inner(window=(ROWS, (experts - 1) * ROWS))[1]

    gate_back = bind(expert_call, gate_back_kernel, box, packs, kept=2)
    own_grad, own_kept1 = gate_back(own1, own_di)
    cross_grad, cross_kept1 = gate_back(cross1, cross_di, after=own_grad[:1])
    down = bind(expert_call, down_kernel, box, packs, reads=False)
    cross_fin = down(cross1, cross_kept1)[0]
    arrived1 = shift(behind, sections=-1)
    got, _ = give_back(cross_grad, own_grad, -1)
    got[: experts - 1], fin_sums = fence((got[: experts - 1], sums(cross_fin)))
    own_fin = down(own1, own_kept1)[0]
    g1, own_g, *boxes_g = call(
        bind(turn_kernel, box, experts),
        [rows_of(n)] + [boxed] * experts,
        arrived1,
        notes0,
        *got,
        scratch=[picked],
    )

    cross_g, own_z, own_x = fence(
        (crossing_of(boxes_g), shift(own_g, flip=2), shift(own_g, flip=1))
    )
    cross_g, own_g = around(cross_g), [own_z, own_g, own_x]
    back = bind(expert_call, back_kernel, box, packs)
    own_grad = back(own_g, own_kept0)[0]
    cross_grad = back(cross_g, cross_kept0, after=own_grad[:1])[0]
    total = sums(cross_grad)
    own_grad, own_fin, fin_sums, _ = fence((own_grad, own_fin, fin_sums, total))
    got = [array.astype(F32) for array in home(total, 0)] + own_home(own_grad, 0)
    fin_back = home(fin_sums, 0)
    fin_own = own_home(own_fin, 0)
    (g0,) = call(
        bind(last_kernel, box, experts),
        [rows_of(n)],
        g1,
        tokens[0],
        notes0,
        gain,
        *got,
        scratch=[picked],
    )
    (final,) = call(
        bind(final_kernel, box, experts),
        [rows_of(n)],
        h1,
        notes1,
        *fin_back,
        *fin_own,
        scratch=[picked],
        after=[g0],
    )
    return (final[None], g0[None])


def solution(mesh):
    in_specs = (
        P("section", "expert", None),
        P("section", None),
        P("section", "expert", None, None),
        P("section", "expert", None, None),
        P("section", "expert", None, None),
        P("section", None, "expert", None),
        P("section", None, "expert", None),
        P("section", "expert", None),
    )
    out_specs = (P("section", "expert", None), P("section", "expert", None))
    return jax.shard_map(local, mesh=mesh, in_specs=in_specs, out_specs=out_specs, check_vma=False)
```

```python
import functools

import jax
import jax.numpy as jnp
from jax import lax
from jax.experimental import pallas as pl
from jax.experimental.pallas import tpu as pltpu
from jax.sharding import PartitionSpec as P

SPLIT = 4
EPSILON = 1e-06
BF = jnp.bfloat16
F32 = jnp.float32
ROWS = 16
LANES = 128


def dot(left, right, dims=((1,), (0,))):
    return lax.dot_general(left, right, (dims, ((), ())), preferred_element_type=F32)


NT = ((1,), (1,))


def iota(shape, axis):
    return lax.broadcasted_iota(jnp.int32, shape, axis)


class Box:
    def __init__(self, capacity, width):
        self.capacity, self.width = capacity, width
        self.groups, self.extra = capacity // ROWS, capacity % ROWS
        self.cuts = ROWS // self.extra if self.extra else 1
        self.wide = -(-width // (LANES * self.cuts)) * LANES if self.extra else 0
        self.lanes = self.groups * width + self.wide
        self.pieces = -(-width // self.wide) if self.extra else 0

    def group(self, g):
        return pl.ds(g * self.width, self.width)

    def tail(self):
        return pl.ds(self.groups * self.width, self.wide)

    def piece(self, i):
        return i * self.wide, min(self.wide, self.width - i * self.wide)


def shift(value, sections=0, experts=0, flip=0):
    n_sec, n_own = lax.axis_size("section"), lax.axis_size("expert")
    n_exp = n_own // SPLIT
    if sections % n_sec == 0 and experts % n_exp == 0 and flip == 0:
        return value
    pairs = []
    for sec in range(n_sec):
        for own in range(n_own):
            exp, sl = own // SPLIT, own % SPLIT
            to = ((exp + experts) % n_exp) * SPLIT + (sl ^ flip)
            pairs.append((sec * n_own + own, ((sec + sections) % n_sec) * n_own + to))
    return lax.ppermute(value, ("section", "expert"), pairs)


def call(body, outs, *operands, scratch=(), flops=0, after=()):
    moved = sum(a.size * a.dtype.itemsize for a in operands)
    moved += sum(o.size * o.dtype.itemsize for o in outs)
    vmem = pl.BlockSpec(memory_space=pltpu.VMEM)
    read = len(operands)

    def reading(*refs):
        body(*refs[:read], *refs[read + len(after) :])

    return pl.pallas_call(
        reading,
        out_shape=list(outs),
        in_specs=[vmem] * read + [pl.BlockSpec(memory_space=pl.ANY)] * len(after),
        out_specs=[vmem] * len(outs),
        scratch_shapes=list(scratch),
        compiler_params=pltpu.CompilerParams(vmem_limit_bytes=40 * 2**20),
        cost_estimate=pl.CostEstimate(flops=flops, bytes_accessed=moved, transcendentals=0),
    )(*operands, *after)


def column_of(row):
    n = row.shape[1]
    eye = iota((n, n), 0) == iota((n, n), 1)
    return jnp.sum(jnp.where(eye, row, 0.0), axis=1, keepdims=True)


def slots_of(rel, experts, capacity):
    n = rel.shape[1]
    same = jnp.broadcast_to(column_of(rel), (n, n)) == jnp.broadcast_to(rel, (n, n))
    before = iota((n, n), 0) < iota((n, n), 1)
    rank = jnp.sum(jnp.where(same & before, 1.0, 0.0), axis=0, keepdims=True)
    return rel * capacity + rank


def terms(value):
    high = value.astype(BF).astype(F32)
    middle = (value - high).astype(BF).astype(F32)
    return high, middle, value - high - middle


def notes_of(slots, mix, gain, n, width):
    r = iota((ROWS, n), 0)
    left = jnp.where(r == 0, slots, 0.0)
    for at, term in enumerate(terms(mix)):
        left = jnp.where(r == 1 + at, term, left)
    r = iota((ROWS, width), 0)
    wide = jnp.concatenate([left, jnp.zeros((ROWS, width - n), F32)], axis=1)
    for at, term in enumerate(terms(gain)):
        wide = jnp.where(r == 4 + at, term, wide)
    return wide.astype(BF)


def slots_in(notes, n):
    return notes[:, :n].astype(F32)[0:1]


def mix_in(notes, n):
    left = notes[:, :n].astype(F32)
    return column_of(left[1:2] + left[2:3] + left[3:4])


def gain_in(notes):
    wide = notes.astype(F32)
    return wide[4:5] + wide[5:6] + wide[6:7]


def pack_rows(box, slots, values, out_refs):
    n = values.shape[0]
    line = jnp.broadcast_to(slots.astype(jnp.int32), (ROWS, n))
    r = iota((ROWS, n), 0)
    for j, out in enumerate(out_refs):
        first = j * box.capacity
        for g in range(box.groups):
            sel = jnp.where(line == first + g * ROWS + r, 1.0, 0.0).astype(BF)
            out[:, box.group(g)] = dot(sel, values).astype(BF)
        if box.extra:
            total = jnp.zeros((ROWS, box.wide), F32)
            for i in range(box.pieces):
                at, size = box.piece(i)
                hit = (line == first + box.groups * ROWS + r // box.cuts) & (r % box.cuts == i)
                hit &= r // box.cuts < box.extra
                got = dot(jnp.where(hit, 1.0, 0.0).astype(BF), values[:, at : at + size])
                if size < box.wide:
                    got = jnp.concatenate([got, jnp.zeros((ROWS, box.wide - size), F32)], axis=1)
                total = total + got
            out[:, box.tail()] = total.astype(BF)


def pick_rows(box, slots, boxes, n, picked):
    count = len(boxes)
    slots = column_of(slots)
    if box.groups:
        stack = jnp.concatenate(
            [b[:, g * box.width : (g + 1) * box.width] for b in boxes for g in range(box.groups)],
            axis=0,
        )
        tall = count * box.groups * ROWS
        c = iota((n, tall), 1)
        slot = c // (box.groups * ROWS) * box.capacity + c % (box.groups * ROWS)
        sel = jnp.where(slots.astype(jnp.int32) == slot, 1.0, 0.0).astype(BF)
        picked[...] = dot(sel, stack)
    else:
        picked[...] = jnp.zeros(picked.shape, F32)
    if box.extra:
        tails = jnp.concatenate([b[:, box.groups * box.width :] for b in boxes], axis=0)
        c = iota((n, count * ROWS), 1)
        r = c % ROWS
        slot = c // ROWS * box.capacity + box.groups * ROWS + r // box.cuts
        mine = (slots.astype(jnp.int32) == slot) & (r // box.cuts < box.extra)
        for i in range(box.pieces):
            at, size = box.piece(i)
            sel = jnp.where(mine & (r % box.cuts == i), 1.0, 0.0).astype(BF)
            picked[:, at : at + size] += dot(sel, tails[:, :size])


def heights(box, count):
    extra = -(-count * box.extra // ROWS) * ROWS
    return count * box.groups * ROWS, extra


def unpack(box, refs, stack, tails, at=0):
    count = 0
    for ref in refs:
        for p in range(ref.shape[0] // ROWS):
            for g in range(box.groups):
                stack[at : at + ROWS, :] = ref[p * ROWS : (p + 1) * ROWS, box.group(g)]
                at += ROWS
            if box.extra:
                tails[count * ROWS : (count + 1) * ROWS, :] = ref[
                    p * ROWS : (p + 1) * ROWS, box.tail()
                ]
            count += 1
    if box.extra:
        extra = heights(box, count)[1]
        r = iota((extra, count * ROWS), 0)
        c = iota((extra, count * ROWS), 1)
        mine = (r // box.extra == c // ROWS) & (r % box.extra == c % ROWS // box.cuts)
        for i in range(box.pieces):
            start, size = box.piece(i)
            sel = jnp.where(mine & (c % ROWS % box.cuts == i), 1.0, 0.0).astype(BF)
            stack[at : at + extra, start : start + size] = dot(sel, tails[:, :size]).astype(BF)


def repack(box, rows, refs):
    rows = rows.astype(BF)
    at = 0
    count = 0
    for ref in refs:
        for p in range(ref.shape[0] // ROWS):
            for g in range(box.groups):
                ref[p * ROWS : (p + 1) * ROWS, box.group(g)] = rows[at : at + ROWS]
                at += ROWS
            count += 1
    if box.extra:
        extra = heights(box, count)[1]
        r = iota((count * ROWS, extra), 0)
        c = iota((count * ROWS, extra), 1)
        mine = (c // box.extra == r // ROWS) & (c % box.extra == r % ROWS // box.cuts)
        total = jnp.zeros((count * ROWS, box.wide), F32)
        for i in range(box.pieces):
            start, size = box.piece(i)
            sel = jnp.where(mine & (r % ROWS % box.cuts == i), 1.0, 0.0).astype(BF)
            got = dot(sel, rows[at:, start : start + size])
            if size < box.wide:
                pad = jnp.zeros((count * ROWS, box.wide - size), F32)
                got = jnp.concatenate([got, pad], axis=1)
            total = total + got
        total = total.astype(BF)
        count = 0
        for ref in refs:
            tall = ref.shape[0]
            ref[:, box.tail()] = total[count : count + tall]
            count += tall


def inv_rms(wide):
    return lax.rsqrt(jnp.mean(wide * wide, axis=-1, keepdims=True) + EPSILON)


def total_of(refs):
    return sum(ref[...].astype(F32) for ref in refs).astype(BF)


def start_kernel(box, experts, tokens, cot, gain, ids, mix, ahead, notes0, notes1, *boxes):
    n, width = tokens.shape
    mine = lax.axis_index("expert") // SPLIT
    for k, notes in enumerate((notes0, notes1)):
        rel = ids[k : k + 1, :] - mine
        rel = jnp.where(rel < 0, rel + experts, rel).astype(F32)
        slots = slots_of(rel, experts, box.capacity)
        notes[...] = notes_of(slots, mix[k : k + 1, :], gain[...], n, width)
    ahead[:n] = tokens[...]
    ahead[n:] = notes0[...]
    wide = tokens[...].astype(F32)
    normed = (wide * inv_rms(wide) * gain[...]).astype(BF)
    crossing = boxes[2:]
    firsts = [boxes[0]] + [ref.at[:ROWS] for ref in crossing]
    pack_rows(box, slots_in(notes0[...], n), normed, firsts)
    seconds = [boxes[1]] + [ref.at[ROWS:] for ref in crossing]
    pack_rows(box, slots_in(notes1[...], n), cot[...], seconds)


def combine(box, notes, n, own, back, picked):
    sums = [total_of(own)] + [ref[...].astype(BF) for ref in back]
    pick_rows(box, slots_in(notes, n), sums, n, picked)
    return mix_in(notes, n) * picked[...]


def split_refs(refs, experts, outs):
    ins = refs[:-outs]
    return ins[experts - 1 :], ins[: experts - 1], refs[-outs:]


def middle_kernel(box, experts, arrived, cot, notes1, gain, *refs):
    boxes, picked = refs[-1 - experts : -1], refs[-1]
    own, back, (after, behind) = split_refs(refs[: -1 - experts], experts, 2)
    n = cot.shape[0]
    update = combine(box, arrived[n:], n, own, back, picked)
    later = (arrived[:n].astype(F32) + update).astype(BF)
    after[...] = later
    behind[:n] = later
    behind[n : 2 * n] = cot[...]
    behind[2 * n :] = notes1[...]
    wide = later.astype(F32)
    normed = (wide * inv_rms(wide) * gain[...]).astype(BF)
    pack_rows(box, slots_in(notes1[...], n), normed, boxes)


def final_kernel(box, experts, hidden, notes, *refs):
    picked = refs[-1]
    own, back, (out,) = split_refs(refs[:-1], experts, 1)
    n = hidden.shape[0]
    update = combine(box, notes[...], n, own, back, picked)
    out[...] = (hidden[...].astype(F32) + update).astype(BF)


def norm_back(hidden, gain, grad):
    wide = hidden.astype(F32)
    inv = inv_rms(wide)
    scaled = grad * gain
    along = jnp.mean(scaled * wide, axis=-1, keepdims=True)
    return inv * scaled - wide * (inv * inv * inv * along)


def turn_kernel(box, experts, arrived, notes0, *refs):
    boxes, picked = refs[-1 - experts : -1], refs[-1]
    own, back, (out,) = split_refs(refs[: -1 - experts], experts, 1)
    n = out.shape[0]
    notes = arrived[2 * n :]
    d_normed = combine(box, notes, n, own, back, picked)
    change = norm_back(arrived[:n], gain_in(notes), d_normed)
    now = (arrived[n : 2 * n].astype(F32) + change).astype(BF)
    out[...] = now
    pack_rows(box, slots_in(notes0[...], n), now, boxes)


def last_kernel(box, experts, grad, hidden, notes0, gain, *refs):
    picked = refs[-1]
    own, back, (out,) = split_refs(refs[:-1], experts, 1)
    n = hidden.shape[0]
    d_normed = combine(box, notes0[...], n, own, back, picked)
    change = norm_back(hidden[...], gain[...], d_normed)
    out[...] = (grad[...].astype(F32) + change).astype(BF)


def spans(tall):
    return pl.ds(0, 2 * tall), pl.ds(tall, 2 * tall)


def gate_up(rows, pack):
    return dot(rows, pack[: 2 * (pack.shape[0] // 3)], NT)


def parts_of(both):
    units = both.shape[1] // 2
    return both[:, :units], both[:, units:]


def down_rows(both, pack):
    g, u = parts_of(both)
    return dot((jax.nn.silu(g) * u).astype(BF), pack[2 * g.shape[1] :])


def inner_of(rows, pack):
    return dot(rows, pack[2 * (pack.shape[0] // 3) :], NT)


def part_rows(d_inner, both, pack):
    g, u = parts_of(both)
    r = jax.nn.sigmoid(g)
    d_gate = d_inner * u * r * (1.0 + g * (1.0 - r))
    d_up = d_inner * g * r
    return dot(jnp.concatenate([d_gate, d_up], axis=1).astype(BF), pack[: both.shape[1]])


def read_rows(box, rows, stack, tails):
    tall = stack.shape[0] // 3
    for at, ref in enumerate(rows):
        unpack(box, [ref], stack, tails, at * tall)
    return [stack[span, :] for span in spans(tall)]


def write_rows(box, top, bottom, outs):
    tall = top.shape[0] // 2
    for ref, value in zip(outs, (top[:tall], top[tall:] + bottom[:tall], bottom[tall:])):
        repack(box, value, [ref])


def forward_kernel(box, packs, saved, rows, outs, kept, stack, tails):
    sides = read_rows(box, rows, stack, tails)
    total = []
    for side, values in enumerate(sides):
        total.append(0.0)
        for at in (2 * side, 2 * side + 1):
            both = gate_up(values, packs[at])
            kept[at][...] = both
            total[side] = total[side] + down_rows(both, packs[at])
    write_rows(box, *total, outs)


def inner_kernel(box, packs, saved, rows, outs, kept, stack, tails):
    for side, values in enumerate(read_rows(box, rows, stack, tails)):
        for at in (2 * side, 2 * side + 1):
            kept[at][...] = inner_of(values, packs[at])


def gate_back_kernel(box, packs, saved, rows, outs, kept, stack, tails):
    sides = read_rows(box, rows, stack, tails)
    total = []
    for side, values in enumerate(sides):
        total.append(0.0)
        for at in (2 * side, 2 * side + 1):
            both = gate_up(values, packs[at])
            kept[at][...] = both
            total[side] = total[side] + part_rows(saved[at][...], both, packs[at])
    write_rows(box, *total, outs)


def back_kernel(box, packs, saved, rows, outs, kept, stack, tails):
    sides = read_rows(box, rows, stack, tails)
    total = []
    for side, values in enumerate(sides):
        total.append(0.0)
        for at in (2 * side, 2 * side + 1):
            d_inner = inner_of(values, packs[at])
            total[side] = total[side] + part_rows(d_inner, saved[at][...], packs[at])
    write_rows(box, *total, outs)


def down_kernel(box, packs, saved, rows, outs, kept, stack, tails):
    total = []
    for side in range(2):
        at = 2 * side
        total.append(sum(down_rows(saved[i][...], packs[i]) for i in (at, at + 1)))
    write_rows(box, *total, outs)


def expert_call(kernel, box, packs, rows, saved=(), outs=True, kept=0, reads=True, after=(), window=None):
    width = packs[0].shape[1]
    first, size = window or (0, rows[0].shape[0])
    count = size // ROWS
    tall = sum(heights(box, count))
    boxes = jax.ShapeDtypeStruct((count * ROWS, box.lanes), BF)
    results = [boxes] * len(rows) if outs else []
    if kept:
        units = [pack.shape[0] // 3 for pack in packs]
        results += [jax.ShapeDtypeStruct((2 * tall, kept * u), F32) for u in units]
    inputs = list(packs) + list(saved) + (list(rows) if reads else [])
    n_in, n_p, n_s, n_out = len(inputs), len(packs), len(saved), len(rows) if outs else 0

    def body(*refs):
        results_refs = refs[n_in:-2]
        kernel(
            box,
            refs[:n_p],
            refs[n_p : n_p + n_s],
            [ref.at[pl.ds(first, size)] for ref in refs[n_p + n_s : n_in]],
            results_refs[:n_out],
            results_refs[n_out:],
            refs[-2],
            refs[-1],
        )

    scratch = [
        pltpu.VMEM((3 * tall, width), BF),
        pltpu.VMEM((count * ROWS, max(box.wide, LANES)), BF),
    ]
    flops = sum(2 * 2 * tall * pack.size for pack in packs)
    results = call(body, results, *inputs, scratch=scratch, flops=flops, after=after)
    return results[:n_out], results[n_out:]


def local(tokens, norm_gain, w_gate, w_up, w_down, routes, mix_weights, cotangent):
    experts = lax.axis_size("expert") // SPLIT
    n, width = tokens.shape[1:]
    capacity = n // experts + max(1, n // (16 * experts))
    box = Box(capacity, width)
    gain = norm_gain
    gate_w, up_w, down_w = w_gate[0, 0].T, w_up[0, 0].T, w_down[0, 0]
    boxed = jax.ShapeDtypeStruct((ROWS, box.lanes), BF)
    picked = pltpu.VMEM((n, width), F32)
    bind = functools.partial

    def joined(arrays):
        return arrays[0] if len(arrays) == 1 else jnp.concatenate(arrays, axis=0)

    fence = lax.optimization_barrier

    def crossing_of(boxes):
        return joined([shift(boxes[j - 1], experts=j) for j in range(1, experts)])

    def around(boxes):
        return [shift(boxes, flip=2), boxes, shift(boxes, flip=1)]

    def add(*values):
        return sum(v.astype(F32) for v in values).astype(BF)

    def sums(parts):
        return add(parts[1], shift(parts[0], flip=2), shift(parts[2], flip=1))

    def home(total, sections):
        return [
            shift(total[(j - 1) * ROWS : j * ROWS], sections=sections, experts=-j)
            for j in range(1, experts)
        ]

    def own_home(parts, sections):
        return [
            shift(parts[0], sections=sections, flip=2),
            shift(parts[2], sections=sections, flip=1),
            shift(parts[1], sections=sections),
        ]

    def give_back(cross, own, sections, others=()):
        total = sums(cross)
        back = home(total, sections)
        own, _, others = fence((own, total, others))
        return back + own_home(own, sections), others

    units = w_gate.shape[3]
    cut = -(-units * 7 // 12 // ROWS) * ROWS
    top = jnp.concatenate([gate_w[:cut], up_w[:cut], down_w[:cut]], axis=0)
    bottom = jnp.concatenate([gate_w[cut:], up_w[cut:], down_w[cut:]], axis=0)
    packs = [top, shift(top, flip=1), bottom, shift(bottom, flip=2)]

    def rows_of(count):
        return jax.ShapeDtypeStruct((count, width), BF)

    both = jax.ShapeDtypeStruct((2 * ROWS, box.lanes), BF)
    ahead, notes0, notes1, own_tok, own_cot, *crossing = call(
        bind(start_kernel, box, experts),
        [rows_of(n + ROWS), rows_of(ROWS), rows_of(ROWS), boxed, boxed] + [both] * (experts - 1),
        tokens[0],
        cotangent[0],
        gain,
        routes[0, :, :, 0],
        mix_weights[0, :, :, 0],
        after=[top, bottom],
    )
    crossed = [shift(crossing[j - 1], experts=j) for j in range(1, experts)]
    own0 = around(own_tok)
    packs, crossed, own0 = fence((packs, crossed, own0))
    cross0 = around(joined([c[:ROWS] for c in crossed]))
    cots = joined([own_cot] + [c[ROWS:] for c in crossed])
    cross0, cots = fence((cross0, cots))
    cots = around(cots)

    cross_out, cross_kept0 = expert_call(forward_kernel, box, packs, cross0, kept=2)
    own_out, own_kept0 = expert_call(
        forward_kernel, box, packs, own0, kept=2, after=cross_out[:1]
    )
    cross_out, ahead = fence((cross_out, ahead))
    arrived0 = shift(ahead, sections=1)
    got, cots = give_back(cross_out, own_out, 1, cots)
    h1, behind, own1, *boxes1 = call(
        bind(middle_kernel, box, experts),
        [rows_of(n), rows_of(2 * n + ROWS)] + [boxed] * experts,
        arrived0,
        cotangent[0],
        notes1,
        gain,
        *got,
        scratch=[picked],
    )
    cross1, own_z, own_x = fence(
        (crossing_of(boxes1), shift(own1, flip=2), shift(own1, flip=1))
    )
    cross1, own1 = around(cross1), [own_z, own1, own_x]
    inner = bind(expert_call, inner_kernel, box, packs, cots, outs=False, kept=1)
    own_di = inner(window=(0, ROWS))[1]
    cross_di = inner(window=(ROWS, (experts - 1) * ROWS))[1]

    gate_back = bind(expert_call, gate_back_kernel, box, packs, kept=2)
    own_grad, own_kept1 = gate_back(own1, own_di)
    cross_grad, cross_kept1 = gate_back(cross1, cross_di, after=own_grad[:1])
    down = bind(expert_call, down_kernel, box, packs, reads=False)
    cross_fin = down(cross1, cross_kept1)[0]
    arrived1 = shift(behind, sections=-1)
    got, _ = give_back(cross_grad, own_grad, -1)
    got[: experts - 1], fin_sums = fence((got[: experts - 1], sums(cross_fin)))
    fin_back = home(fin_sums, 0)
    own_fin = down(own1, own_kept1)[0]
    g1, own_g, *boxes_g = call(
        bind(turn_kernel, box, experts),
        [rows_of(n)] + [boxed] * experts,
        arrived1,
        notes0,
        *got,
        scratch=[picked],
    )

    cross_g, own_z, own_x, fin_back = fence(
        (crossing_of(boxes_g), shift(own_g, flip=2), shift(own_g, flip=1), fin_back)
    )
    cross_g, own_g = around(cross_g), [own_z, own_g, own_x]
    back = bind(expert_call, back_kernel, box, packs)
    own_grad = back(own_g, own_kept0)[0]
    cross_grad = back(cross_g, cross_kept0, after=own_grad[:1])[0]
    total = sums(cross_grad)
    own_grad, own_fin, _ = fence((own_grad, own_fin, total))
    got = [array.astype(F32) for array in home(total, 0)] + own_home(own_grad, 0)
    fin_own = own_home(own_fin, 0)
    (g0,) = call(
        bind(last_kernel, box, experts),
        [rows_of(n)],
        g1,
        tokens[0],
        notes0,
        gain,
        *got,
        scratch=[picked],
    )
    (final,) = call(
        bind(final_kernel, box, experts),
        [rows_of(n)],
        h1,
        notes1,
        *fin_back,
        *fin_own,
        scratch=[picked],
        after=[g0],
    )
    return (final[None], g0[None])


def solution(mesh):
    in_specs = (
        P("section", "expert", None),
        P("section", None),
        P("section", "expert", None, None),
        P("section", "expert", None, None),
        P("section", "expert", None, None),
        P("section", None, "expert", None),
        P("section", None, "expert", None),
        P("section", "expert", None),
    )
    out_specs = (P("section", "expert", None), P("section", "expert", None))
    return jax.shard_map(local, mesh=mesh, in_specs=in_specs, out_specs=out_specs, check_vma=False)
```
